128 devices in a mesh: ctx: 32 (over z, y, core), head: 4 (over x).
Axes of the slice: x: 4, y: 4, z: 4, core: 2. Of those that a mesh axis runs over, the one named last changes fastest.
Arguments:
- tokens: bfloat16 [16384, 4096], P('ctx'), may hold values from -6 to 6
- x_weight: bfloat16 [4096, 8192], P('ctx', 'head'), may hold values from -0.09375 to 0.09375
- z_weight: bfloat16 [4096, 8192], P('ctx', 'head'), may hold values from -0.09375 to 0.09375
- bc_weight: bfloat16 [4096, 256], P('ctx'), may hold values from -0.09375 to 0.09375
- dt_weight: bfloat16 [4096, 128], P('ctx', 'head'), may hold values from -0.09375 to 0.09375
- conv_x: float32 [4, 8192], P(None, 'head'), may hold values from -3 to 3
- conv_bc: float32 [4, 256], replicated, may hold values from -3 to 3
- dt_bias: float32 [128], P('head'), may hold values from -1 to 1
- decay_rate: float32 [128], P('head'), may hold values from 3.0517578e-06 to 0.05
- skip: float32 [128], P('head'), may hold values from 0.5 to 1.5
- norm_gain: float32 [8192], P('head'), may hold values from 0.5 to 1.5
Outputs:
- mixed: bfloat16 [16384, 8192], P('ctx', 'head')
The draws below stay inside these ranges and needn't reach their ends.
All inputs are finite; a program needn't handle non-finite values.
Results may differ from the reference program's by a relative error of at most 0.013.
Values may be sent and summed in bfloat16 or wider, within the bound.
No kernel may reach another device: no remote copies, remote signals or barrier semaphores. Data moves between devices by JAX's collectives and lax.ppermute only.
A program may use at most 192 MiB of HBM per device.

```python
import math
import jax
import jax.numpy as jnp
from jax import lax

D = 4096
HEADS = 128
HEAD_DIM = 64
STATE = 128
GROUP = 256
CONV = 4
TOKENS = 16384
INNER = 8192


def draw_decay_rate(key, part):
    key = jax.random.fold_in(key, 7)
    key_pick, key_slow, key_fast = jax.random.split(key, 3)
    share = 0.5
    chosen = jax.random.uniform(key_pick, (HEADS,), jnp.float32) < share
    slow_rate = jnp.exp(jax.random.uniform(key_slow, (HEADS,), jnp.float32, math.log(0.05), 0.0)) / TOKENS
    fast_rate = jnp.exp(jax.random.uniform(key_fast, (HEADS,), jnp.float32, math.log(0.02), math.log(0.05)))
    return jnp.where(chosen, slow_rate, fast_rate).astype(jnp.float32)


def block_levels(key, dims, cuts, low, top_value):
    level, own = 1.0, jax.random.fold_in(key, 6)
    for axis_at, shards_of in cuts:
        draws = jnp.exp(jax.random.uniform(jax.random.fold_in(own, axis_at), (shards_of,), jnp.float32, low / len(cuts), top_value / len(cuts)))
        level = level * jnp.repeat(draws, dims[axis_at] // shards_of).reshape([-1 if axis == axis_at else 1 for axis in range(len(dims))])
    return level


def gaussian(key, dims, deviation, most, cuts=(), dtype=jnp.bfloat16):
    result = jax.random.normal(key, dims, jnp.float32) * deviation
    if len(cuts) > 0:
        result = block_levels(key, dims, cuts, -0.22, 0.18) * result
    return jnp.clip(result, min=-most, max=most).astype(dtype)


def setup_inputs(seed: int = 0) -> dict:
    arg_keys = jax.random.split(jax.random.key(seed), 12)
    return {
        "tokens": gaussian(arg_keys[0], (TOKENS, D), 1.0, 6.0, ((0, 32),)),
        "x_weight": gaussian(arg_keys[1], (D, INNER), D ** -0.5, 0.09375, ((0, 32), (1, 4))),
        "z_weight": gaussian(arg_keys[2], (D, INNER), D ** -0.5, 0.09375, ((0, 32), (1, 4))),
        "bc_weight": gaussian(arg_keys[3], (D, 2 * STATE), D ** -0.5, 0.09375, ((0, 32),)),
        "dt_weight": gaussian(arg_keys[4], (D, HEADS), D ** -0.5, 0.09375, ((0, 32), (1, 4))),
        "conv_x": gaussian(arg_keys[5], (CONV, INNER), 0.6, 3.0, ((1, 4),), jnp.float32),
        "conv_bc": gaussian(arg_keys[6], (CONV, 2 * STATE), 0.6, 3.0, (), jnp.float32),
        "dt_bias": jnp.clip(jax.random.uniform(arg_keys[7], (HEADS,), jnp.float32, -1.0, 1.0) * block_levels(arg_keys[7], (HEADS,), ((0, 4),), -0.4, 0.0), -1.0, 1.0),
        "decay_rate": draw_decay_rate(jax.random.fold_in(arg_keys[11], 71), 0),
        "skip": jnp.clip(0.5 + 1.0 * jax.random.uniform(arg_keys[9], (HEADS,), jnp.float32) ** block_levels(arg_keys[9], (HEADS,), ((0, 4),), -0.2, 0.2), 0.5, 1.5),
        "norm_gain": jnp.clip(1.0 + 0.1 * jax.random.normal(arg_keys[10], (INNER,), jnp.float32), 0.5, 1.5),
    }


def causal_conv(pre_rows, kernel):
    width = kernel.shape[0]
    padded = jnp.concatenate([jnp.zeros((width - 1, pre_rows.shape[1]), jnp.bfloat16), pre_rows], axis=0)
    accum = jnp.zeros(pre_rows.shape, jnp.float32)
    for offset in range(width):
        accum = accum + kernel[offset][None, :] * padded[offset:offset + pre_rows.shape[0]].astype(jnp.float32)
    return jax.nn.silu(accum).astype(jnp.bfloat16)

def block_step(carried, pieces, skip):
    inputs, b_rows, c_rows, step_size, log_decay = pieces
    length = inputs.shape[0]
    cumul = jnp.cumsum(log_decay, axis=0)
    scores = jnp.dot(c_rows, b_rows.T, preferred_element_type=jnp.float32)
    log_gaps = cumul.T[:, :, None] - cumul.T[:, None, :]
    causal = jnp.arange(length)[:, None] >= jnp.arange(length)[None, :]
    mixing = (scores[None] * jnp.exp(jnp.where(causal[None], log_gaps, -1e+30)) * step_size.T[:, None, :]).astype(jnp.bfloat16)
    inputs_f = inputs.astype(jnp.float32)
    output = jnp.einsum('hts,shp->thp', mixing.astype(jnp.float32), inputs_f, precision=lax.Precision.HIGHEST)
    output = output + jnp.exp(cumul)[:, :, None] * jnp.einsum('tn,hpn->thp', c_rows.astype(jnp.float32), carried, precision=lax.Precision.HIGHEST)
    output = output + skip[None, :, None] * inputs_f
    weights_in = jnp.exp(cumul[-1][None, :] - cumul) * step_size
    weighted = (weights_in[:, :, None] * inputs_f).astype(jnp.bfloat16)
    contrib = jnp.einsum('shp,sn->hpn', weighted.astype(jnp.float32), b_rows.astype(jnp.float32), precision=lax.Precision.HIGHEST)
    return (jnp.exp(cumul[-1])[:, None, None] * carried + contrib, output)

def reference(tokens, x_weight, z_weight, bc_weight, dt_weight, conv_x, conv_bc, dt_bias, decay_rate, skip, norm_gain):
    x_in = jnp.dot(tokens, x_weight, preferred_element_type=jnp.float32).astype(jnp.bfloat16)
    gate = jnp.dot(tokens, z_weight, preferred_element_type=jnp.float32).astype(jnp.bfloat16)
    bc_in = jnp.dot(tokens, bc_weight, preferred_element_type=jnp.float32).astype(jnp.bfloat16)
    dt_raw = jnp.dot(tokens, dt_weight, preferred_element_type=jnp.float32)
    x_conv = causal_conv(x_in, conv_x)
    bc_conv = causal_conv(bc_in, conv_bc)
    b_rows = bc_conv[:, :STATE]
    c_rows = bc_conv[:, STATE:]
    step_size = jax.nn.softplus(dt_raw + dt_bias[None, :])
    log_decay = -decay_rate[None, :] * step_size
    blocks = TOKENS // GROUP
    pieces = (x_conv.reshape(blocks, GROUP, HEADS, HEAD_DIM), b_rows.reshape(blocks, GROUP, STATE), c_rows.reshape(blocks, GROUP, STATE), step_size.reshape(blocks, GROUP, HEADS), log_decay.reshape(blocks, GROUP, HEADS))
    start = jnp.zeros((HEADS, HEAD_DIM, STATE), jnp.float32)
    final_state, outputs = lax.scan(lambda carried, piece: block_step(carried, piece, skip), start, pieces)
    ssm_out = outputs.reshape(TOKENS, INNER)
    gated = ssm_out * jax.nn.silu(gate.astype(jnp.float32))
    scale = lax.rsqrt(lax.optimization_barrier(jnp.mean(gated * gated, axis=1)) + 1e-05)
    return (gated * scale[:, None] * norm_gain[None, :]).astype(jnp.bfloat16)
```

```python
import jax
import jax.numpy as jnp
from jax import lax
from jax.experimental import pallas as pl
from jax.experimental.pallas import tpu as pltpu
from jax.sharding import Mesh, PartitionSpec as P

GROUP = 256
HALO = 16
LANES = 128
HEAD = 64
F32 = jnp.float32
BF16 = jnp.bfloat16


def swap_cores(a):
    return lax.ppermute(a, "core", [(0, 1), (1, 0)])


def along_chips(a, distance):
    chips = lax.axis_size("z") * lax.axis_size("y")
    return lax.ppermute(a, ("z", "y"), [(i, i + distance) for i in range(chips - distance)])


def in_core_order(core, mine, other, axis):
    first = jnp.where(core == 0, mine, other)
    second = jnp.where(core == 0, other, mine)
    return jnp.concatenate([first, second], axis=axis)


def expand_heads(values, width):
    high = values.astype(BF16)
    rest = values - high.astype(F32)
    middle = rest.astype(BF16)
    low = (rest - middle.astype(F32)).astype(BF16)
    row = lax.broadcasted_iota(jnp.int32, (LANES, width), 0)
    col = lax.broadcasted_iota(jnp.int32, (LANES, width), 1)
    spread = ((col >= row * HEAD) & (col < row * HEAD + HEAD)).astype(BF16)
    dot = lambda part: jnp.dot(part, spread, preferred_element_type=F32)
    return dot(high) + dot(middle) + dot(low)


def silu(a):
    return a * (1.0 / (1.0 + jnp.exp(-a)))


def conv_block(ref, kernel_ref, start):
    taps = kernel_ref.shape[0]
    rows = ref[pl.ds(start, GROUP + HALO), :].astype(F32)
    first = HALO - (taps - 1)
    accum = kernel_ref[0:1, :] * rows[first : first + GROUP]
    for tap in range(1, taps):
        accum = accum + kernel_ref[tap : tap + 1, :] * rows[first + tap : first + tap + GROUP]
    return silu(accum).astype(BF16)


def states_kernel(
    x_ref, bc_ref, dt_ref, conv_x_ref, conv_bc_ref, bias_ref, rate_ref,
    xc_ref, bcc_ref, cum_ref, cum_slab_ref, cum_t_ref, step_t_ref, entering_ref, final_ref,
    state, total,
):
    block = pl.program_id(0)
    start = pl.multiple_of(block * GROUP, GROUP)
    width = x_ref.shape[1]
    heads = cum_t_ref.shape[0]

    @pl.when(block == 0)
    def _():
        state[...] = jnp.zeros_like(state)
        total[...] = jnp.zeros_like(total)

    xc = conv_block(x_ref, conv_x_ref, start)
    xc_ref[...] = xc
    bcc = conv_block(bc_ref, conv_bc_ref, start)
    bcc_ref[...] = bcc
    raw = dt_ref[pl.ds(start + HALO, GROUP), :] + bias_ref[...]
    step = jnp.maximum(raw, 0.0) + jnp.log1p(jnp.exp(-jnp.abs(raw)))
    log_decay = -rate_ref[...] * step
    row = lax.broadcasted_iota(jnp.int32, (GROUP, GROUP), 0)
    col = lax.broadcasted_iota(jnp.int32, (GROUP, GROUP), 1)
    lower = (row >= col).astype(F32)
    cum = jnp.dot(lower, log_decay, preferred_element_type=F32, precision=lax.Precision.HIGHEST)
    last = cum[GROUP - 1 : GROUP, :]
    cum_ref[...] = cum
    cum_slab_ref[...] = cum + total[0:1, :]
    cum_t_ref[...] = cum.T[:heads, :]
    step_t_ref[...] = step.T[:heads, :]
    entering_ref[0] = state[...].astype(BF16)
    weights_in = expand_heads(jnp.exp(last - cum) * step, width)
    weighted = (weights_in * xc.astype(F32)).astype(BF16)
    contrib = lax.dot_general(
        bcc[:, :LANES], weighted, (((0,), (0,)), ((), ())), preferred_element_type=F32
    )
    decay = expand_heads(jnp.broadcast_to(jnp.exp(last), (8, LANES)), width)
    state[...] = state[...] * decay[0:1] + contrib
    total[...] = total[...] + jnp.broadcast_to(last, total.shape)

    @pl.when(block == pl.num_programs(0) - 1)
    def _():
        final_ref[:LANES, :] = state[...]
        final_ref[LANES:, :] = expand_heads(jnp.exp(total[...]), width)


def outputs_kernel(xc_ref, bcc_ref, cum_ref, cum_t_ref, step_t_ref, entering_ref, skip_ref, out_ref):
    width = xc_ref.shape[1]
    b_rows, c_rows = bcc_ref[:, :LANES], bcc_ref[:, LANES:]
    scores = lax.dot_general(c_rows, b_rows, (((1,), (1,)), ((), ())), preferred_element_type=F32)
    row = lax.broadcasted_iota(jnp.int32, (GROUP, GROUP), 0)
    col = lax.broadcasted_iota(jnp.int32, (GROUP, GROUP), 1)
    scores = jnp.where(row >= col, scores, 0.0)
    cum = cum_ref[...]
    grown = expand_heads(jnp.exp(cum), width)
    out_ref[...] = grown * jnp.dot(c_rows, entering_ref[0], preferred_element_type=F32)
    lane = lax.broadcasted_iota(jnp.int32, (GROUP, LANES), 1)

    def mixing(head):
        gaps = cum[:, head : head + 1] - cum_t_ref[head : head + 1, :]
        return (
            scores * jnp.exp(jnp.minimum(gaps, 0.0)) * step_t_ref[head : head + 1, :]
        ).astype(BF16)

    for pair in range(width // LANES):
        lanes = slice(pair * LANES, (pair + 1) * LANES)
        inputs = xc_ref[:, lanes]
        zero = jnp.zeros_like(inputs)
        both = jnp.concatenate([mixing(2 * pair), mixing(2 * pair + 1)], axis=1)
        stacked = jnp.concatenate(
            [jnp.where(lane < HEAD, inputs, zero), jnp.where(lane < HEAD, zero, inputs)], axis=0
        )
        out_ref[:, lanes] = (
            out_ref[:, lanes]
            + jnp.dot(both, stacked, preferred_element_type=F32)
            + skip_ref[:, lanes] * inputs.astype(F32)
        )


def gate_kernel(
    tokens_ref, weight_ref, local_ref, bcc_ref, cum_ref, incoming_ref, gated_ref, squares_ref, accum
):
    step = pl.program_id(0)
    rows, width = accum.shape
    product = jnp.dot(tokens_ref[HALO:, :], weight_ref[...], preferred_element_type=F32)

    @pl.when(step == 0)
    def _():
        accum[...] = product

    @pl.when(step > 0)
    def _():
        accum[...] = accum[...] + product

    @pl.when(step == pl.num_programs(0) - 1)
    def _():
        for block in range(rows // GROUP):
            part = slice(block * GROUP, (block + 1) * GROUP)
            gate = accum[part, :].astype(BF16).astype(F32)
            grown = expand_heads(jnp.exp(cum_ref[part, :]), width)
            carried = jnp.dot(bcc_ref[part, LANES:], incoming_ref[...], preferred_element_type=F32)
            gated = (local_ref[part, :] + grown * carried) * silu(gate)
            gated_ref[part, :] = gated.astype(BF16)
            squares_ref[part, :] = jnp.sum(gated * gated, axis=1, keepdims=True)


def whole(shape):
    return pl.BlockSpec(shape, lambda i: (0,) * len(shape))


def rows_of(width):
    return pl.BlockSpec((GROUP, width), lambda i: (i, 0))


def local_states(x_in, bc_in, dt_raw, conv_x, conv_bc, bias, rate, heads):
    rows, width = x_in.shape[0] - HALO, x_in.shape[1]
    blocks = rows // GROUP
    shape = jax.ShapeDtypeStruct
    by_lane = pl.BlockSpec((heads, GROUP), lambda i: (0, i))
    return pl.pallas_call(
        states_kernel,
        grid=(blocks,),
        in_specs=[whole(a.shape) for a in (x_in, bc_in, dt_raw, conv_x, conv_bc, bias, rate)],
        out_specs=[
            rows_of(width), rows_of(2 * LANES), rows_of(LANES), rows_of(LANES), by_lane, by_lane,
            pl.BlockSpec((1, LANES, width), lambda i: (i, 0, 0)), whole((LANES + 8, width)),
        ],
        out_shape=[
            shape((rows, width), BF16), shape((rows, 2 * LANES), BF16),
            shape((rows, LANES), F32), shape((rows, LANES), F32),
            shape((heads, rows), F32), shape((heads, rows), F32),
            shape((blocks, LANES, width), BF16), shape((LANES + 8, width), F32),
        ],
        scratch_shapes=[pltpu.VMEM((LANES, width), F32), pltpu.VMEM((8, LANES), F32)],
        compiler_params=pltpu.CompilerParams(vmem_limit_bytes=40 * 2**20),
        cost_estimate=pl.CostEstimate(flops=4 * 10**9, bytes_accessed=10 * 2**20, transcendentals=0),
        name="states",
    )(x_in, bc_in, dt_raw, conv_x, conv_bc, bias, rate)


def local_outputs(xc, bcc, cum, cum_t, step_t, entering, skip):
    rows, width = xc.shape
    heads = cum_t.shape[0]
    by_lane = pl.BlockSpec((heads, GROUP), lambda i: (0, i))
    return pl.pallas_call(
        outputs_kernel,
        grid=(rows // GROUP,),
        in_specs=[
            rows_of(width), rows_of(2 * LANES), rows_of(LANES), by_lane, by_lane,
            pl.BlockSpec((1, LANES, width), lambda i: (i, 0, 0)), whole((1, width)),
        ],
        out_specs=rows_of(width),
        out_shape=jax.ShapeDtypeStruct((rows, width), F32),
        compiler_params=pltpu.CompilerParams(vmem_limit_bytes=40 * 2**20),
        cost_estimate=pl.CostEstimate(flops=10**10, bytes_accessed=10 * 2**20, transcendentals=4 * 2**20),
        name="outputs",
    )(xc, bcc, cum, cum_t, step_t, entering, skip)


def gate_outputs(tokens, weight, local, bcc, cum_slab, incoming):
    rows, width = local.shape
    depth = 512
    return pl.pallas_call(
        gate_kernel,
        grid=(weight.shape[0] // depth,),
        in_specs=[
            pl.BlockSpec((tokens.shape[0], depth), lambda i: (0, i)),
            pl.BlockSpec((depth, width), lambda i: (i, 0)),
            whole(local.shape), whole(bcc.shape), whole(cum_slab.shape), whole(incoming.shape),
        ],
        out_specs=[whole((rows, width)), whole((rows, 1))],
        out_shape=[
            jax.ShapeDtypeStruct((rows, width), BF16), jax.ShapeDtypeStruct((rows, 1), F32),
        ],
        scratch_shapes=[pltpu.VMEM((rows, width), F32)],
        compiler_params=pltpu.CompilerParams(vmem_limit_bytes=48 * 2**20),
        cost_estimate=pl.CostEstimate(flops=10**10, bytes_accessed=20 * 2**20, transcendentals=0),
        name="gate",
    )(tokens, weight, local, bcc, cum_slab, incoming)


def entering_state(final):
    window, decay = final[:LANES], final[LANES : LANES + 1]
    state, state_decay = None, None
    chips = lax.axis_size("z") * lax.axis_size("y")
    distance = 1
    while distance < chips:
        high = decay.astype(BF16)
        low = (decay - high.astype(F32)).astype(BF16)
        pad = jnp.zeros((HALO - 2, decay.shape[1]), BF16)
        sent = jnp.concatenate([window.astype(BF16), high, low, pad], axis=0)
        got = along_chips(sent, distance).astype(F32)
        got_decay = got[LANES : LANES + 1] + got[LANES + 1 : LANES + 2]
        got = got[:LANES]
        if state is None:
            state, state_decay = got, got_decay
        else:
            state, state_decay = got * state_decay + state, got_decay * state_decay
        window, decay = got * decay + window, got_decay * decay
        distance *= 2
    return state.astype(BF16)


def shards(
    tokens, x_weight, z_weight, bc_weight, dt_weight, conv_x, conv_bc, dt_bias, decay_rate, skip,
    norm_gain,
):
    core = lax.axis_index("core")
    width = x_weight.shape[1] // 2
    heads = dt_weight.shape[1] // 2

    def mine(a, axis):
        size = a.shape[axis] // 2
        return lax.dynamic_slice_in_dim(a, core * size, size, axis)

    def others(a, axis):
        size = a.shape[axis] // 2
        return lax.dynamic_slice_in_dim(a, (1 - core) * size, size, axis)

    def paired(a):
        return in_core_order(core, mine(a, 1), swap_cores(others(a, 1)), 0)

    gather = lambda a: lax.all_gather(a, ("z", "y"), axis=0, tiled=True)
    early = jnp.concatenate(
        [paired(x_weight), paired(bc_weight), jnp.pad(paired(dt_weight), ((0, 0), (0, LANES - heads)))],
        axis=1,
    )
    early = gather(early)
    z_whole = gather(paired(z_weight))
    slabs = in_core_order(core, tokens, swap_cores(tokens), 0)
    extended = jnp.concatenate([along_chips(slabs[-HALO:], 1), slabs], axis=0)

    x_in = jnp.dot(extended, early[:, :width], preferred_element_type=F32).astype(BF16)
    small = jnp.dot(extended, early[:, width:], preferred_element_type=F32)
    bc_half = small[:, :LANES].astype(BF16)
    bc_in = in_core_order(core, bc_half, swap_cores(bc_half), 1)
    dt_raw = small[:, LANES:]

    def per_lane(a):
        return jnp.pad(mine(a, 0), (0, LANES - heads))[None, :]

    xc, bcc, cum, cum_slab, cum_t, step_t, entering, final = local_states(
        x_in, bc_in, dt_raw, mine(conv_x, 1), conv_bc, per_lane(dt_bias), per_lane(decay_rate), heads
    )
    incoming = entering_state(final)
    skip_lanes = jnp.repeat(mine(skip, 0), HEAD)[None, :]
    local = local_outputs(xc, bcc, cum, cum_t, step_t, entering, skip_lanes)
    gated, squares = gate_outputs(extended, z_whole, local, bcc, cum_slab, incoming)

    summed = lax.psum(squares[:, 0], ("core", "x"))
    inner = 2 * width * lax.axis_size("x")
    scale = lax.rsqrt(mine(summed, 0) / inner + 1e-05)
    full = in_core_order(core, mine(gated, 0), swap_cores(others(gated, 0)), 1)
    return (full.astype(F32) * scale[:, None] * norm_gain[None, :]).astype(BF16)


def solution(mesh):
    fine = Mesh(mesh.devices.reshape(4, 4, 2, 4), ("z", "y", "core", "x"))
    ctx = ("z", "y", "core")
    placed = (
        P(ctx, None),
        P(ctx, "x"),
        P(ctx, "x"),
        P(ctx, None),
        P(ctx, "x"),
        P(None, "x"),
        P(),
        P("x"),
        P("x"),
        P("x"),
        P("x"),
    )
    return jax.shard_map(
        shards, mesh=fine, in_specs=placed, out_specs=P(ctx, "x"), check_vma=False
    )
```

```python
import functools

import jax
import jax.numpy as jnp
from jax import lax
from jax.experimental import pallas as pl
from jax.experimental.pallas import tpu as pltpu
from jax.sharding import Mesh, PartitionSpec as P

GROUP = 256
HALO = 16
LANES = 128
HEAD = 64
F32 = jnp.float32
BF16 = jnp.bfloat16


def swap_cores(a):
    return lax.ppermute(a, "core", [(0, 1), (1, 0)])


def round_ring(a, axis, distance):
    size = lax.axis_size(axis)
    return lax.ppermute(a, axis, [(i, (i + distance) % size) for i in range(size)])


def along_chips(a, distance):
    chips = lax.axis_size("z") * lax.axis_size("y")
    return lax.ppermute(a, ("z", "y"), [(i, i + distance) for i in range(chips - distance)])


def in_core_order(core, mine, other, axis):
    first = jnp.where(core == 0, mine, other)
    second = jnp.where(core == 0, other, mine)
    return jnp.concatenate([first, second], axis=axis)


def expand_heads(values, width):
    high = values.astype(BF16)
    rest = values - high.astype(F32)
    middle = rest.astype(BF16)
    low = (rest - middle.astype(F32)).astype(BF16)
    row = lax.broadcasted_iota(jnp.int32, (LANES, width), 0)
    col = lax.broadcasted_iota(jnp.int32, (LANES, width), 1)
    spread = ((col >= row * HEAD) & (col < row * HEAD + HEAD)).astype(BF16)
    dot = lambda part: jnp.dot(part, spread, preferred_element_type=F32)
    return dot(high) + dot(middle) + dot(low)


def silu(a):
    half = 0.5 * a
    return half + half * jnp.tanh(half)


def conv_block(ref, kernel_ref, start):
    taps = kernel_ref.shape[0]
    rows = ref[pl.ds(start, GROUP + HALO), :].astype(F32)
    first = HALO - (taps - 1)
    accum = kernel_ref[0:1, :] * rows[first : first + GROUP]
    for tap in range(1, taps):
        accum = accum + kernel_ref[tap : tap + 1, :] * rows[first + tap : first + tap + GROUP]
    return silu(accum).astype(BF16)


def states_kernel(
    x_ref, bc_ref, dt_ref, conv_x_ref, conv_bc_ref, bias_ref, rate_ref,
    xc_ref, bcc_ref, cum_ref, cum_slab_ref, cum_t_ref, step_t_ref, entering_ref, final_ref,
    state, total,
):
    block = pl.program_id(0)
    start = pl.multiple_of(block * GROUP, GROUP)
    width = x_ref.shape[1]
    heads = cum_t_ref.shape[0]

    @pl.when(block == 0)
    def _():
        state[...] = jnp.zeros_like(state)
        total[...] = jnp.zeros_like(total)

    xc = conv_block(x_ref, conv_x_ref, start)
    xc_ref[...] = xc
    bcc = conv_block(bc_ref, conv_bc_ref, start)
    bcc_ref[...] = bcc
    raw = dt_ref[pl.ds(start + HALO, GROUP), :] + bias_ref[...]
    step = jnp.maximum(raw, 0.0) + jnp.log1p(jnp.exp(-jnp.abs(raw)))
    log_decay = -rate_ref[...] * step
    row = lax.broadcasted_iota(jnp.int32, (GROUP, GROUP), 0)
    col = lax.broadcasted_iota(jnp.int32, (GROUP, GROUP), 1)
    lower = (row >= col).astype(F32)
    cum = jnp.dot(lower, log_decay, preferred_element_type=F32, precision=lax.Precision.HIGHEST)
    last = cum[GROUP - 1 : GROUP, :]
    cum_ref[...] = cum
    cum_slab_ref[...] = cum + total[0:1, :]
    cum_t_ref[...] = cum.T[:heads, :]
    step_t_ref[...] = step.T[:heads, :]
    entering_ref[0] = state[...].astype(BF16)
    weights_in = expand_heads(jnp.exp(last - cum) * step, width)
    weighted = (weights_in * xc.astype(F32)).astype(BF16)
    contrib = lax.dot_general(
        bcc[:, :LANES], weighted, (((0,), (0,)), ((), ())), preferred_element_type=F32
    )
    decay = expand_heads(jnp.broadcast_to(jnp.exp(last), (8, LANES)), width)
    state[...] = state[...] * decay[0:1] + contrib
    total[...] = total[...] + jnp.broadcast_to(last, total.shape)

    @pl.when(block == pl.num_programs(0) - 1)
    def _():
        final_ref[:LANES, :] = state[...]
        final_ref[LANES:, :] = expand_heads(jnp.exp(total[...]), width)


def outputs_kernel(xc_ref, bcc_ref, cum_ref, cum_t_ref, step_t_ref, entering_ref, skip_ref, out_ref):
    width = xc_ref.shape[1]
    b_rows, c_rows = bcc_ref[:, :LANES], bcc_ref[:, LANES:]
    scores = lax.dot_general(c_rows, b_rows, (((1,), (1,)), ((), ())), preferred_element_type=F32)
    row = lax.broadcasted_iota(jnp.int32, (GROUP, GROUP), 0)
    col = lax.broadcasted_iota(jnp.int32, (GROUP, GROUP), 1)
    scores = jnp.where(row >= col, scores, 0.0)
    cum = cum_ref[...]
    grown = expand_heads(jnp.exp(cum), width)
    out_ref[...] = grown * jnp.dot(c_rows, entering_ref[0], preferred_element_type=F32)
    lane = lax.broadcasted_iota(jnp.int32, (GROUP, LANES), 1)

    def mixing(head):
        gaps = cum[:, head : head + 1] - cum_t_ref[head : head + 1, :]
        return (
            scores * jnp.exp(jnp.minimum(gaps, 0.0)) * step_t_ref[head : head + 1, :]
        ).astype(BF16)

    for pair in range(width // LANES):
        lanes = slice(pair * LANES, (pair + 1) * LANES)
        inputs = xc_ref[:, lanes]
        zero = jnp.zeros_like(inputs)
        both = jnp.concatenate([mixing(2 * pair), mixing(2 * pair + 1)], axis=1)
        stacked = jnp.concatenate(
            [jnp.where(lane < HEAD, inputs, zero), jnp.where(lane < HEAD, zero, inputs)], axis=0
        )
        out_ref[:, lanes] = (
            out_ref[:, lanes]
            + jnp.dot(both, stacked, preferred_element_type=F32)
            + skip_ref[:, lanes] * inputs.astype(F32)
        )


def staged_kernel(sources, count, order_ref, tokens_ref, *refs):
    weights, before, accum = refs[:count], refs[count:-1], refs[-1]
    step = pl.program_id(0)
    for place, source in enumerate(sources):

        @pl.when(step == place)
        def _():
            parts = [weights[ref][first : first + size, :] for ref, first, size in source]
            block = parts[0] if len(parts) == 1 else jnp.concatenate(parts, axis=0)
            product = jnp.dot(tokens_ref[...], block, preferred_element_type=F32)
            if place == 0:
                accum[...] = before[0][...] + product if before else product
            else:
                accum[...] = accum[...] + product


def z_kernel(tokens_ref, weight_ref, gate_ref, accum):
    step = pl.program_id(0)
    product = jnp.dot(tokens_ref[HALO:, :], weight_ref[...], preferred_element_type=F32)

    @pl.when(step == 0)
    def _():
        accum[...] = product

    @pl.when((step > 0) & (step < pl.num_programs(0) - 1))
    def _():
        accum[...] = accum[...] + product

    @pl.when(step == pl.num_programs(0) - 1)
    def _():
        gate_ref[...] = (accum[...] + product).astype(BF16)


def gate_kernel(gate_ref, local_ref, bcc_ref, cum_ref, incoming_ref, gated_ref, squares_ref):
    width = local_ref.shape[1]
    grown = expand_heads(jnp.exp(cum_ref[...]), width)
    carried = jnp.dot(bcc_ref[:, LANES:], incoming_ref[...], preferred_element_type=F32)
    gated = (local_ref[...] + grown * carried) * silu(gate_ref[...].astype(F32))
    gated_ref[...] = gated.astype(BF16)
    squares = gated * gated
    high = squares.astype(BF16)
    low = (squares - high.astype(F32)).astype(BF16)
    ones = jnp.ones((8, width), BF16)
    across = (((1,), (1,)), ((), ()))
    summed = lax.dot_general(ones, high, across, preferred_element_type=F32) + lax.dot_general(
        ones, low, across, preferred_element_type=F32
    )
    squares_ref[...] = summed[0:1, :]


def norm_kernel(core_ref, mine_ref, other_ref, squares_ref, gain_ref, out_ref):
    half = pl.program_id(0)
    across = jnp.broadcast_to(squares_ref[...], (8, squares_ref.shape[1]))
    scale = lax.rsqrt(across + 1e-05).T[:, 0:1]

    @pl.when(half == core_ref[0])
    def _():
        out_ref[...] = (mine_ref[...].astype(F32) * scale * gain_ref[...]).astype(BF16)

    @pl.when(half != core_ref[0])
    def _():
        out_ref[...] = (other_ref[...].astype(F32) * scale * gain_ref[...]).astype(BF16)


def whole(shape):
    return pl.BlockSpec(shape, lambda i: (0,) * len(shape))


def rows_of(width):
    return pl.BlockSpec((GROUP, width), lambda i: (i, 0))


def local_states(x_in, bc_in, dt_raw, conv_x, conv_bc, bias, rate, heads):
    rows, width = x_in.shape[0] - HALO, x_in.shape[1]
    blocks = rows // GROUP
    shape = jax.ShapeDtypeStruct
    by_lane = pl.BlockSpec((heads, GROUP), lambda i: (0, i))
    return pl.pallas_call(
        states_kernel,
        grid=(blocks,),
        in_specs=[whole(a.shape) for a in (x_in, bc_in, dt_raw, conv_x, conv_bc, bias, rate)],
        out_specs=[
            rows_of(width), rows_of(2 * LANES), rows_of(LANES), rows_of(LANES), by_lane, by_lane,
            pl.BlockSpec((1, LANES, width), lambda i: (i, 0, 0)), whole((LANES + 8, width)),
        ],
        out_shape=[
            shape((rows, width), BF16), shape((rows, 2 * LANES), BF16),
            shape((rows, LANES), F32), shape((rows, LANES), F32),
            shape((heads, rows), F32), shape((heads, rows), F32),
            shape((blocks, LANES, width), BF16), shape((LANES + 8, width), F32),
        ],
        scratch_shapes=[pltpu.VMEM((LANES, width), F32), pltpu.VMEM((8, LANES), F32)],
        compiler_params=pltpu.CompilerParams(vmem_limit_bytes=40 * 2**20),
        cost_estimate=pl.CostEstimate(flops=4 * 10**9, bytes_accessed=10 * 2**20, transcendentals=0),
        name="states",
    )(x_in, bc_in, dt_raw, conv_x, conv_bc, bias, rate)


def local_outputs(xc, bcc, cum, cum_t, step_t, entering, skip):
    rows, width = xc.shape
    heads = cum_t.shape[0]
    by_lane = pl.BlockSpec((heads, GROUP), lambda i: (0, i))
    return pl.pallas_call(
        outputs_kernel,
        grid=(rows // GROUP,),
        in_specs=[
            rows_of(width), rows_of(2 * LANES), rows_of(LANES), by_lane, by_lane,
            pl.BlockSpec((1, LANES, width), lambda i: (i, 0, 0)), whole((1, width)),
        ],
        out_specs=rows_of(width),
        out_shape=jax.ShapeDtypeStruct((rows, width), F32),
        compiler_params=pltpu.CompilerParams(vmem_limit_bytes=40 * 2**20),
        cost_estimate=pl.CostEstimate(flops=10**10, bytes_accessed=10 * 2**20, transcendentals=4 * 2**20),
        name="outputs",
    )(xc, bcc, cum, cum_t, step_t, entering, skip)


def project(tokens, order, weights, sources, before=None):
    rows, width, depth = tokens.shape[0], weights[0].shape[1], 256
    fixed = lambda a: pl.BlockSpec(a.shape, lambda i, order: (0,) * a.ndim)
    operands = list(weights) + ([] if before is None else [before])
    accum = jax.ShapeDtypeStruct((rows, width), F32)
    return pl.pallas_call(
        functools.partial(staged_kernel, sources, len(weights)),
        grid_spec=pltpu.PrefetchScalarGridSpec(
            num_scalar_prefetch=1,
            grid=(len(sources),),
            in_specs=[pl.BlockSpec((rows, depth), lambda i, order: (0, order[i]))]
            + [fixed(a) for a in operands],
            out_specs=fixed(accum),
        ),
        out_shape=accum,
        compiler_params=pltpu.CompilerParams(vmem_limit_bytes=48 * 2**20),
        cost_estimate=pl.CostEstimate(
            flops=2 * rows * width * depth * len(sources), bytes_accessed=12 * 2**20, transcendentals=0
        ),
        name="project",
    )(order, tokens, *operands)


def project_gate(tokens, weight):
    rows, width, depth = tokens.shape[0] - HALO, weight.shape[1], 1024
    return pl.pallas_call(
        z_kernel,
        grid=(weight.shape[0] // depth,),
        in_specs=[
            pl.BlockSpec((tokens.shape[0], depth), lambda i: (0, i)),
            pl.BlockSpec((depth, width), lambda i: (i, 0)),
        ],
        out_specs=whole((rows, width)),
        out_shape=jax.ShapeDtypeStruct((rows, width), BF16),
        scratch_shapes=[pltpu.VMEM((rows, width), F32)],
        compiler_params=pltpu.CompilerParams(vmem_limit_bytes=48 * 2**20),
        cost_estimate=pl.CostEstimate(flops=10**10, bytes_accessed=20 * 2**20, transcendentals=0),
        name="project_gate",
    )(tokens, weight)


def gate_outputs(gate, local, bcc, cum_slab, incoming):
    rows, width = local.shape
    return pl.pallas_call(
        gate_kernel,
        grid=(rows // GROUP,),
        in_specs=[
            rows_of(width), rows_of(width), rows_of(2 * LANES), rows_of(LANES), whole(incoming.shape),
        ],
        out_specs=[rows_of(width), pl.BlockSpec((1, GROUP), lambda i: (0, i))],
        out_shape=[
            jax.ShapeDtypeStruct((rows, width), BF16), jax.ShapeDtypeStruct((1, rows), F32),
        ],
        compiler_params=pltpu.CompilerParams(vmem_limit_bytes=40 * 2**20),
        cost_estimate=pl.CostEstimate(flops=10**9, bytes_accessed=10 * 2**20, transcendentals=0),
        name="gate",
    )(gate, local, bcc, cum_slab, incoming)


def normalized(core, gated, other, mean_squares, gain):
    rows, width = other.shape
    return pl.pallas_call(
        norm_kernel,
        grid_spec=pltpu.PrefetchScalarGridSpec(
            num_scalar_prefetch=1,
            grid=(2,),
            in_specs=[
                pl.BlockSpec((rows, width), lambda j, core: (core[0], 0)),
                pl.BlockSpec((rows, width), lambda j, core: (0, 0)),
                pl.BlockSpec((1, rows), lambda j, core: (0, 0)),
                pl.BlockSpec((1, width), lambda j, core: (0, j)),
            ],
            out_specs=pl.BlockSpec((rows, width), lambda j, core: (0, j)),
        ),
        out_shape=jax.ShapeDtypeStruct((rows, 2 * width), BF16),
        compiler_params=pltpu.CompilerParams(vmem_limit_bytes=40 * 2**20),
        cost_estimate=pl.CostEstimate(flops=10**7, bytes_accessed=4 * 2**20, transcendentals=0),
        name="normalized",
    )(core[None], gated, other, mean_squares, gain)


def packed(state, decay):
    high = decay.astype(BF16)
    low = (decay - high.astype(F32)).astype(BF16)
    pad = jnp.zeros((HALO - 2, decay.shape[1]), BF16)
    return jnp.concatenate([state.astype(BF16), high, low, pad], axis=0)


def unpacked(sent):
    sent = sent.astype(F32)
    return sent[:LANES], sent[LANES : LANES + 1] + sent[LANES + 1 : LANES + 2]


def entering_state(final):
    size = lax.axis_size("y")
    place = lax.axis_index("y")
    own = packed(final[:LANES], final[LANES : LANES + 1])
    parts = [own] + [round_ring(own, "y", distance) for distance in range(1, size)]
    total = jnp.zeros((LANES, final.shape[1]), F32)
    decay = jnp.ones((1, final.shape[1]), F32)
    before, before_decay = total, decay
    for index in range(size):
        chosen = parts[0]
        for distance in range(1, size):
            chosen = jnp.where((place - index) % size == distance, parts[distance], chosen)
        state, state_decay = unpacked(chosen)
        before = jnp.where(place == index, total, before)
        before_decay = jnp.where(place == index, decay, before_decay)
        total = total * state_decay + state
        decay = decay * state_decay
    sent = packed(total, decay)
    rows = lax.axis_size("z")
    earlier = jnp.zeros_like(total)
    for distance in range(rows - 1, 0, -1):
        got = lax.ppermute(sent, "z", [(i, i + distance) for i in range(rows - distance)])
        state, state_decay = unpacked(got)
        earlier = earlier * state_decay + state
    return (earlier * before_decay + before).astype(BF16)


def project_early(tokens, own):
    y, z = lax.axis_index("y"), lax.axis_index("z")
    block = own.shape[0]
    half = block // 2

    def order(*places):
        return jnp.stack([(z + dz) % 4 * 4 + (y + dy) % 4 for dy, dz in places]).astype(jnp.int32)

    y_less, y_more = round_ring(own, "y", 1), round_ring(own, "y", -1)
    z_less, z_more = round_ring(own, "z", 1), round_ring(own, "z", -1)
    join = lambda *parts: jnp.concatenate(parts, axis=0)
    from_y_less = round_ring(join(z_less, y_less[:half]), "y", 1)
    from_y_more = round_ring(join(z_more, y_more[half:]), "y", -1)
    from_z_less = round_ring(join(y_more, z_less[:half]), "z", 1)
    from_z_more = round_ring(join(y_less, z_more[half:]), "z", -1)
    y_far = join(from_y_less[block:], from_y_more[block:])
    z_far = join(from_z_less[block:], from_z_more[block:])
    far_y_less, far_y_more = round_ring(z_far, "y", 1), round_ring(z_far, "y", -1)
    far_z_less, far_z_more = round_ring(y_far, "z", 1), round_ring(y_far, "z", -1)
    far_top = round_ring(far_y_less[:half], "y", 1)
    far_low = round_ring(far_z_more[half:], "z", -1)

    full = lambda count: [((i, 0, block),) for i in range(count)]
    accum = project(
        tokens,
        order((0, 0), (-1, 0), (1, 0), (0, -1), (0, 1)),
        [own, y_less, y_more, z_less, z_more],
        full(5),
    )
    accum = project(
        tokens,
        order((-1, -1), (1, 1), (1, -1), (-1, 1), (2, 0), (0, 2)),
        [from_y_less, from_y_more, from_z_less, from_z_more],
        full(4) + [((0, block, half), (1, block, half)), ((2, block, half), (3, block, half))],
        accum,
    )
    accum = project(
        tokens,
        order((-1, 2), (1, 2), (2, -1), (2, 1)),
        [far_y_less, far_y_more, far_z_less, far_z_more],
        full(4),
        accum,
    )
    return project(tokens, order((2, 2)), [far_top, far_low], [((0, 0, half), (1, 0, half))], accum)


def shards(
    tokens, x_weight, z_weight, bc_weight, dt_weight, conv_x, conv_bc, dt_bias, decay_rate, skip,
    norm_gain,
):
    core = lax.axis_index("core")
    width = x_weight.shape[1] // 2
    heads = dt_weight.shape[1] // 2

    def mine(a, axis):
        size = a.shape[axis] // 2
        return lax.dynamic_slice_in_dim(a, core * size, size, axis)

    def others(a, axis):
        size = a.shape[axis] // 2
        return lax.dynamic_slice_in_dim(a, (1 - core) * size, size, axis)

    def paired(a):
        return in_core_order(core, mine(a, 1), swap_cores(others(a, 1)), 0)

    early = jnp.concatenate(
        [paired(x_weight), paired(bc_weight), jnp.pad(paired(dt_weight), ((0, 0), (0, LANES - heads)))],
        axis=1,
    )
    z_whole = lax.all_gather(paired(z_weight), ("z", "y"), axis=0, tiled=True)
    slabs = in_core_order(core, tokens, swap_cores(tokens), 0)
    extended = jnp.concatenate([along_chips(slabs[-HALO:], 1), slabs], axis=0)

    projected = project_early(extended, early)
    x_in = projected[:, :width].astype(BF16)
    small = projected[:, width:]
    bc_half = small[:, :LANES].astype(BF16)
    bc_in = in_core_order(core, bc_half, swap_cores(bc_half), 1)
    dt_raw = small[:, LANES:]

    def per_lane(a):
        return jnp.pad(mine(a, 0), (0, LANES - heads))[None, :]

    xc, bcc, cum, cum_slab, cum_t, step_t, entering, final = local_states(
        x_in, bc_in, dt_raw, mine(conv_x, 1), conv_bc, per_lane(dt_bias), per_lane(decay_rate), heads
    )
    incoming = entering_state(final)
    skip_lanes = jnp.repeat(mine(skip, 0), HEAD)[None, :]
    local = local_outputs(xc, bcc, cum, cum_t, step_t, entering, skip_lanes)
    gate = project_gate(extended, z_whole)
    gated, squares = gate_outputs(gate, local, bcc, cum_slab, incoming)

    other = swap_cores(others(gated, 0))
    summed = mine(squares + swap_cores(squares), 1)
    across = [round_ring(summed, "x", distance) for distance in range(1, lax.axis_size("x"))]
    mean_squares = (summed + sum(across)) / (2 * width * lax.axis_size("x"))
    return normalized(core, gated, other, mean_squares, norm_gain[None, :])


def solution(mesh):
    fine = Mesh(mesh.devices.reshape(4, 4, 2, 4), ("z", "y", "core", "x"))
    ctx = ("z", "y", "core")
    placed = (
        P(ctx, None),
        P(ctx, "x"),
        P(ctx, "x"),
        P(ctx, None),
        P(ctx, "x"),
        P(None, "x"),
        P(),
        P("x"),
        P("x"),
        P("x"),
        P("x"),
    )
    return jax.shard_map(
        shards, mesh=fine, in_specs=placed, out_specs=P(ctx, "x"), check_vma=False
    )
```

```python
import functools

import jax
import jax.numpy as jnp
from jax import lax
from jax.experimental import pallas as pl
from jax.experimental.pallas import tpu as pltpu
from jax.sharding import Mesh, PartitionSpec as P

GROUP = 256
HALO = 16
LANES = 128
HEAD = 64
F32 = jnp.float32
BF16 = jnp.bfloat16


def swap_cores(a):
    return lax.ppermute(a, "core", [(0, 1), (1, 0)])


def round_ring(a, axis, distance):
    size = lax.axis_size(axis)
    return lax.ppermute(a, axis, [(i, (i + distance) % size) for i in range(size)])


def along_chips(a, distance):
    chips = lax.axis_size("z") * lax.axis_size("y")
    return lax.ppermute(a, ("z", "y"), [(i, i + distance) for i in range(chips - distance)])


def in_core_order(core, mine, other, axis):
    first = jnp.where(core == 0, mine, other)
    second = jnp.where(core == 0, other, mine)
    return jnp.concatenate([first, second], axis=axis)


def expand_heads(values, width):
    high = values.astype(BF16)
    rest = values - high.astype(F32)
    middle = rest.astype(BF16)
    low = (rest - middle.astype(F32)).astype(BF16)
    row = lax.broadcasted_iota(jnp.int32, (LANES, width), 0)
    col = lax.broadcasted_iota(jnp.int32, (LANES, width), 1)
    spread = ((col >= row * HEAD) & (col < row * HEAD + HEAD)).astype(BF16)
    dot = lambda part: jnp.dot(part, spread, preferred_element_type=F32)
    return dot(high) + dot(middle) + dot(low)


def silu(a):
    half = 0.5 * a
    return half + half * jnp.tanh(half)


def conv_rows(rows, kernel_ref):
    taps, count = kernel_ref.shape[0], rows.shape[0] - HALO
    first = HALO - (taps - 1)
    accum = kernel_ref[0:1, :] * rows[first : first + count]
    for tap in range(1, taps):
        accum = accum + kernel_ref[tap : tap + 1, :] * rows[first + tap : first + tap + count]
    return silu(accum).astype(BF16)


def prepare_kernel(
    place_ref, own_ref, other_ref, before_ref, weight_ref, conv_ref, bias_ref, rate_ref,
    bcc_ref, cum_ref, cum_slab_ref, cum_t_ref, step_t_ref, weights_in_ref, decays_ref,
    accum,
):
    step = pl.program_id(0)
    core = place_ref[0]
    slab = own_ref.shape[0]
    heads = cum_t_ref.shape[0]
    rows_own = pl.ds(pl.multiple_of(HALO + slab * core, HALO), slab)
    rows_other = pl.ds(pl.multiple_of(HALO + slab * (1 - core), HALO), slab)

    @pl.when(step == 0)
    def _():
        accum[...] = jnp.zeros_like(accum)

    weight = weight_ref[...]
    for rows, ref in ((slice(0, HALO), before_ref), (rows_own, own_ref), (rows_other, other_ref)):
        accum[rows, :] = accum[rows, :] + jnp.dot(ref[...], weight, preferred_element_type=F32)

    @pl.when(step == pl.num_programs(0) - 1)
    def _():
        total = jnp.zeros((1, LANES), F32)
        row = lax.broadcasted_iota(jnp.int32, (GROUP, GROUP), 0)
        col = lax.broadcasted_iota(jnp.int32, (GROUP, GROUP), 1)
        lower = (row >= col).astype(F32)
        for block in range(2 * slab // GROUP):
            part = slice(block * GROUP, (block + 1) * GROUP)
            narrow = accum[block * GROUP : (block + 1) * GROUP + HALO, : 2 * LANES]
            bcc_ref[part, :] = conv_rows(narrow.astype(BF16).astype(F32), conv_ref)
            raw = accum[block * GROUP + HALO : (block + 1) * GROUP + HALO, 2 * LANES :]
            raw = jnp.where(core == 0, raw, pltpu.roll(raw, LANES - heads, axis=1))
            raw = raw + bias_ref[...]
            step_size = jnp.maximum(raw, 0.0) + jnp.log1p(jnp.exp(-jnp.abs(raw)))
            log_decay = -rate_ref[...] * step_size
            cum = jnp.dot(
                lower, log_decay, preferred_element_type=F32, precision=lax.Precision.HIGHEST
            )
            last = cum[GROUP - 1 : GROUP, :]
            cum_ref[part, :] = cum
            cum_slab_ref[part, :] = cum + total
            cum_t_ref[:, part] = cum.T[:heads, :]
            step_t_ref[:, part] = step_size.T[:heads, :]
            weights_in_ref[part, :] = jnp.exp(last - cum) * step_size
            decays_ref[block * 8 : block * 8 + 8, :] = jnp.broadcast_to(jnp.exp(last), (8, LANES))
            total = total + last
        end = decays_ref.shape[0] - 8
        decays_ref[end:, :] = jnp.broadcast_to(jnp.exp(total), (8, LANES))


def block_columns(ref, place_ref, first, count):
    core = place_ref[0]
    parts = []
    for index in range(first, first + count):
        base = place_ref[1 + index] * (2 * LANES)
        for start in (base + LANES * core, base + LANES * (1 - core)):
            parts.append(ref[:, pl.ds(pl.multiple_of(start, LANES), LANES)])
    return jnp.concatenate(parts, axis=1)


def stacked(sources, refs):
    return jnp.concatenate([refs[ref][first : first + size, :] for ref, first, size in sources], axis=0)


def first_kernel(sources, count, place_ref, own_ref, other_ref, before_ref, *refs):
    weights, (out_ref, out_before_ref) = refs[:-2], refs[-2:]
    block = pl.program_id(0)
    is_own = block // 2 == place_ref[0]

    def product(ref):
        columns = block_columns(ref, place_ref, 0, count)
        return jnp.dot(columns, stacked(sources, weights), preferred_element_type=F32)

    @pl.when(block == 0)
    def _():
        out_before_ref[...] = product(before_ref)

    @pl.when(is_own)
    def _():
        out_ref[...] = product(own_ref)

    @pl.when(jnp.logical_not(is_own))
    def _():
        out_ref[...] = product(other_ref)


def states_kernel(
    sources, done, count, place_ref, own_ref, other_ref, before_ref, *refs
):
    weights = refs[:-12]
    (
        sum_ref, sum_before_ref, bcc_ref, weights_in_ref, decays_ref, conv_ref,
        xc_ref, entering_ref, final_ref,
        state, x_in, tail,
    ) = refs[-12:]
    block = pl.program_id(0)
    width = x_in.shape[1]
    is_own = block // 2 == place_ref[0]

    def product(ref):
        columns = block_columns(ref, place_ref, done, count)
        return jnp.dot(columns, stacked(sources, weights), preferred_element_type=F32)

    @pl.when(block == 0)
    def _():
        state[...] = jnp.zeros_like(state)
        tail[...] = (sum_before_ref[...] + product(before_ref)).astype(BF16).astype(F32)

    @pl.when(is_own)
    def _():
        x_in[...] = (sum_ref[...] + product(own_ref)).astype(BF16).astype(F32)

    @pl.when(jnp.logical_not(is_own))
    def _():
        x_in[...] = (sum_ref[...] + product(other_ref)).astype(BF16).astype(F32)

    rows = jnp.concatenate([tail[...], x_in[...]], axis=0)
    tail[...] = rows[GROUP:]
    xc = conv_rows(rows, conv_ref)
    xc_ref[...] = xc
    entering_ref[0] = state[...].astype(BF16)
    weighted = (expand_heads(weights_in_ref[...], width) * xc.astype(F32)).astype(BF16)
    contrib = lax.dot_general(
        bcc_ref[:, :LANES], weighted, (((0,), (0,)), ((), ())), preferred_element_type=F32
    )
    decay = expand_heads(decays_ref[pl.ds(pl.multiple_of(block * 8, 8), 8), :], width)
    state[...] = state[...] * decay[0:1] + contrib

    @pl.when(block == pl.num_programs(0) - 1)
    def _():
        end = decays_ref.shape[0] - 8
        final_ref[:LANES, :] = state[...].astype(BF16)
        final_ref[LANES:, :] = split_decay(expand_heads(decays_ref[end:, :], width)[0:1])


def split_decay(decay):
    high = decay.astype(BF16)
    low = decay - high.astype(F32)
    row = lax.broadcasted_iota(jnp.int32, (HALO, decay.shape[1]), 0)
    return jnp.where(row == 0, high.astype(F32), jnp.where(row == 1, low, 0.0)).astype(BF16)


def unpacked(sent):
    sent = sent.astype(F32)
    return sent[:LANES], sent[LANES : LANES + 1] + sent[LANES + 1 : LANES + 2]


def row_kernel(place_ref, *refs):
    size = len(refs) - 3
    parts, (total_ref, before_ref, before_decay_ref) = refs[:size], refs[size:]
    place = place_ref[0]
    width = total_ref.shape[1]
    total, decay = jnp.zeros((LANES, width), F32), jnp.ones((1, width), F32)
    before_ref[...] = total
    before_decay_ref[...] = jnp.broadcast_to(decay, before_decay_ref.shape)
    for index in range(size):
        if index > 0:

            @pl.when(place == index)
            def _():
                before_ref[...] = total
                before_decay_ref[...] = jnp.broadcast_to(decay, before_decay_ref.shape)

        distance = (place - index + size) % size
        chosen = parts[0][...]
        for other in range(1, size):
            chosen = jnp.where(distance == other, parts[other][...], chosen)
        state, state_decay = unpacked(chosen)
        total = total * state_decay + state
        decay = decay * state_decay
    total_ref[:LANES, :] = total.astype(BF16)
    total_ref[LANES:, :] = split_decay(decay)


def outputs_kernel(xc_ref, bcc_ref, cum_ref, cum_t_ref, step_t_ref, entering_ref, skip_ref, out_ref):
    width = xc_ref.shape[1]
    b_rows, c_rows = bcc_ref[:, :LANES], bcc_ref[:, LANES:]
    scores = lax.dot_general(c_rows, b_rows, (((1,), (1,)), ((), ())), preferred_element_type=F32)
    row = lax.broadcasted_iota(jnp.int32, (GROUP, GROUP), 0)
    col = lax.broadcasted_iota(jnp.int32, (GROUP, GROUP), 1)
    scores = jnp.where(row >= col, scores, 0.0)
    cum = cum_ref[...]
    grown = expand_heads(jnp.exp(cum), width)
    out_ref[...] = grown * jnp.dot(c_rows, entering_ref[0], preferred_element_type=F32)
    lane = lax.broadcasted_iota(jnp.int32, (GROUP, LANES), 1)

    def mixing(head):
        gaps = cum[:, head : head + 1] - cum_t_ref[head : head + 1, :]
        return (
            scores * jnp.exp(jnp.minimum(gaps, 0.0)) * step_t_ref[head : head + 1, :]
        ).astype(BF16)

    for pair in range(width // LANES):
        lanes = slice(pair * LANES, (pair + 1) * LANES)
        inputs = xc_ref[:, lanes]
        zero = jnp.zeros_like(inputs)
        both = jnp.concatenate([mixing(2 * pair), mixing(2 * pair + 1)], axis=1)
        stacked = jnp.concatenate(
            [jnp.where(lane < HEAD, inputs, zero), jnp.where(lane < HEAD, zero, inputs)], axis=0
        )
        out_ref[:, lanes] = (
            out_ref[:, lanes]
            + jnp.dot(both, stacked, preferred_element_type=F32)
            + skip_ref[:, lanes] * inputs.astype(F32)
        )


def z_kernel(place_ref, own_ref, other_ref, weight_ref, gate_ref, accum):
    step = pl.program_id(0)
    slab = own_ref.shape[0]
    core = place_ref[0]

    def product(ref):
        return jnp.dot(ref[...], weight_ref[...], preferred_element_type=F32)

    for index, ref in enumerate((own_ref, other_ref)):
        rows = slice(index * slab, (index + 1) * slab)
        target = pl.ds(pl.multiple_of(slab * (core if index == 0 else 1 - core), slab), slab)

        @pl.when(step == 0)
        def _():
            accum[rows, :] = product(ref)

        @pl.when((step > 0) & (step < pl.num_programs(0) - 1))
        def _():
            accum[rows, :] = accum[rows, :] + product(ref)

        @pl.when(step == pl.num_programs(0) - 1)
        def _():
            gate_ref[target, :] = (accum[rows, :] + product(ref)).astype(BF16)


def gate_kernel(
    gate_ref, local_ref, bcc_ref, cum_ref, before_ref, before_decay_ref, *refs
):
    earlier, (gated_ref, squares_ref, incoming) = refs[:-3], refs[-3:]
    width = local_ref.shape[1]

    @pl.when(pl.program_id(0) == 0)
    def _():
        carried = jnp.zeros((LANES, width), F32)
        for part in earlier:
            state, decay = unpacked(part[...])
            carried = carried * decay + state
        incoming[...] = (carried * before_decay_ref[0:1, :] + before_ref[...]).astype(BF16)

    grown = expand_heads(jnp.exp(cum_ref[...]), width)
    carried = jnp.dot(bcc_ref[:, LANES:], incoming[...], preferred_element_type=F32)
    gated = (local_ref[...] + grown * carried) * silu(gate_ref[...].astype(F32))
    gated_ref[...] = gated.astype(BF16)
    squares = gated * gated
    high = squares.astype(BF16)
    low = (squares - high.astype(F32)).astype(BF16)
    ones = jnp.ones((8, width), BF16)
    across = (((1,), (1,)), ((), ()))
    summed = lax.dot_general(ones, high, across, preferred_element_type=F32) + lax.dot_general(
        ones, low, across, preferred_element_type=F32
    )
    squares_ref[...] = summed[0:1, :]


def norm_kernel(core_ref, mine_ref, other_ref, squares_ref, gain_ref, out_ref):
    half = pl.program_id(0)
    across = jnp.broadcast_to(squares_ref[...], (8, squares_ref.shape[1]))
    scale = lax.rsqrt(across + 1e-05).T[:, 0:1]

    @pl.when(half == core_ref[0])
    def _():
        out_ref[...] = (mine_ref[...].astype(F32) * scale * gain_ref[...]).astype(BF16)

    @pl.when(half != core_ref[0])
    def _():
        out_ref[...] = (other_ref[...].astype(F32) * scale * gain_ref[...]).astype(BF16)


def whole(shape):
    return pl.BlockSpec(shape, lambda i: (0,) * len(shape))


def rows_of(width):
    return pl.BlockSpec((GROUP, width), lambda i: (i, 0))


def params(flops, megabytes):
    return dict(
        compiler_params=pltpu.CompilerParams(vmem_limit_bytes=48 * 2**20),
        cost_estimate=pl.CostEstimate(
            flops=int(flops), bytes_accessed=megabytes * 2**20, transcendentals=0
        ),
    )


def fixed(a):
    return pl.BlockSpec(a.shape, lambda i, place: (0,) * len(a.shape))


def row_block(width):
    return pl.BlockSpec((GROUP, width), lambda i, place: (i, 0))


def slab_blocks(depth):
    own = pl.BlockSpec((GROUP, depth), lambda i, place: (jnp.clip(i - 2 * place[0], 0, 1), 0))
    other = pl.BlockSpec((GROUP, depth), lambda i, place: (jnp.clip(i - 2 + 2 * place[0], 0, 1), 0))
    return [own, other]


def prepared(place, slabs, weight, conv_bc, bias, rate, heads):
    own, other, before = slabs
    slab, rows, depth = own.shape[0], 2 * own.shape[0], 512
    shape = jax.ShapeDtypeStruct
    outs = [
        shape((rows, 2 * LANES), BF16), shape((rows, LANES), F32), shape((rows, LANES), F32),
        shape((heads, rows), F32), shape((heads, rows), F32), shape((rows, LANES), F32),
        shape((rows // GROUP * 8 + 8, LANES), F32),
    ]
    columns = lambda a: pl.BlockSpec((a.shape[0], depth), lambda i, place: (0, i))
    return pl.pallas_call(
        prepare_kernel,
        grid_spec=pltpu.PrefetchScalarGridSpec(
            num_scalar_prefetch=1,
            grid=(own.shape[1] // depth,),
            in_specs=[columns(a) for a in slabs]
            + [pl.BlockSpec((depth, weight.shape[1]), lambda i, place: (i, 0))]
            + [fixed(a) for a in (conv_bc, bias, rate)],
            out_specs=[fixed(a) for a in outs],
            scratch_shapes=[pltpu.VMEM((HALO + rows, weight.shape[1]), F32)],
        ),
        out_shape=outs,
        name="prepared",
        **params(4e9, 14),
    )(place, *slabs, weight, conv_bc, bias, rate)


def first_products(place, slabs, weights, sources, count):
    own, other, before = slabs
    width = weights[0].shape[1]
    outs = [
        jax.ShapeDtypeStruct((2 * own.shape[0], width), F32), jax.ShapeDtypeStruct((HALO, width), F32),
    ]
    return pl.pallas_call(
        functools.partial(first_kernel, sources, count),
        grid_spec=pltpu.PrefetchScalarGridSpec(
            num_scalar_prefetch=1,
            grid=(2 * own.shape[0] // GROUP,),
            in_specs=slab_blocks(own.shape[1]) + [fixed(a) for a in (before, *weights)],
            out_specs=[row_block(width), fixed(outs[1])],
        ),
        out_shape=outs,
        name="first_products",
        **params(6e9, 18),
    )(place, *slabs, *weights)


def local_states(place, slabs, weights, sources, done, count, sums, bcc, weights_in, decays, conv_x):
    own, other, before = slabs
    rows, width = sums[0].shape
    blocks = rows // GROUP
    outs = [
        jax.ShapeDtypeStruct((rows, width), BF16),
        jax.ShapeDtypeStruct((blocks, LANES, width), BF16),
        jax.ShapeDtypeStruct((LANES + HALO, width), BF16),
    ]
    return pl.pallas_call(
        functools.partial(states_kernel, sources, done, count),
        grid_spec=pltpu.PrefetchScalarGridSpec(
            num_scalar_prefetch=1,
            grid=(blocks,),
            in_specs=slab_blocks(own.shape[1])
            + [fixed(a) for a in (before, *weights)]
            + [
                row_block(width), fixed(sums[1]), row_block(2 * LANES), row_block(LANES),
                fixed(decays), fixed(conv_x),
            ],
            out_specs=[
                row_block(width),
                pl.BlockSpec((1, LANES, width), lambda i, place: (i, 0, 0)),
                fixed(outs[2]),
            ],
            scratch_shapes=[
                pltpu.VMEM((LANES, width), F32), pltpu.VMEM((GROUP, width), F32),
                pltpu.VMEM((HALO, width), F32),
            ],
        ),
        out_shape=outs,
        name="states",
        **params(8e9, 16),
    )(place, *slabs, *weights, *sums, bcc, weights_in, decays, conv_x)


def local_outputs(xc, bcc, cum, cum_t, step_t, entering, skip):
    rows, width = xc.shape
    heads = cum_t.shape[0]
    by_lane = pl.BlockSpec((heads, GROUP), lambda i: (0, i))
    return pl.pallas_call(
        outputs_kernel,
        grid=(rows // GROUP,),
        in_specs=[
            rows_of(width), rows_of(2 * LANES), rows_of(LANES), by_lane, by_lane,
            pl.BlockSpec((1, LANES, width), lambda i: (i, 0, 0)), whole((1, width)),
        ],
        out_specs=rows_of(width),
        out_shape=jax.ShapeDtypeStruct((rows, width), F32),
        compiler_params=pltpu.CompilerParams(vmem_limit_bytes=40 * 2**20),
        cost_estimate=pl.CostEstimate(flops=10**10, bytes_accessed=10 * 2**20, transcendentals=4 * 2**20),
        name="outputs",
    )(xc, bcc, cum, cum_t, step_t, entering, skip)


def project_gate(place, slabs, weight):
    own, other, _ = slabs
    rows, width, depth = 2 * own.shape[0], weight.shape[1], 1024
    columns = pl.BlockSpec((own.shape[0], depth), lambda i, place: (0, i))
    out = jax.ShapeDtypeStruct((rows, width), BF16)
    return pl.pallas_call(
        z_kernel,
        grid_spec=pltpu.PrefetchScalarGridSpec(
            num_scalar_prefetch=1,
            grid=(weight.shape[0] // depth,),
            in_specs=[columns, columns, pl.BlockSpec((depth, width), lambda i, place: (i, 0))],
            out_specs=fixed(out),
            scratch_shapes=[pltpu.VMEM((rows, width), F32)],
        ),
        out_shape=out,
        name="project_gate",
        **params(9e9, 20),
    )(place, own, other, weight)


def gate_outputs(gate, local, bcc, cum_slab, before, before_decay, earlier):
    rows, width = local.shape
    return pl.pallas_call(
        gate_kernel,
        grid=(rows // GROUP,),
        in_specs=[rows_of(width), rows_of(width), rows_of(2 * LANES), rows_of(LANES)]
        + [whole(a.shape) for a in (before, before_decay, *earlier)],
        out_specs=[rows_of(width), pl.BlockSpec((1, GROUP), lambda i: (0, i))],
        out_shape=[
            jax.ShapeDtypeStruct((rows, width), BF16), jax.ShapeDtypeStruct((1, rows), F32),
        ],
        scratch_shapes=[pltpu.VMEM((LANES, width), BF16)],
        name="gate",
        **params(1e9, 10),
    )(gate, local, bcc, cum_slab, before, before_decay, *earlier)


def normalized(core, gated, other, mean_squares, gain):
    rows, width = other.shape
    return pl.pallas_call(
        norm_kernel,
        grid_spec=pltpu.PrefetchScalarGridSpec(
            num_scalar_prefetch=1,
            grid=(2,),
            in_specs=[
                pl.BlockSpec((rows, width), lambda j, core: (core[0], 0)),
                pl.BlockSpec((rows, width), lambda j, core: (0, 0)),
                pl.BlockSpec((1, rows), lambda j, core: (0, 0)),
                pl.BlockSpec((1, width), lambda j, core: (0, j)),
            ],
            out_specs=pl.BlockSpec((rows, width), lambda j, core: (0, j)),
        ),
        out_shape=jax.ShapeDtypeStruct((rows, 2 * width), BF16),
        compiler_params=pltpu.CompilerParams(vmem_limit_bytes=40 * 2**20),
        cost_estimate=pl.CostEstimate(flops=10**7, bytes_accessed=4 * 2**20, transcendentals=0),
        name="normalized",
    )(core.astype(jnp.int32)[None], gated, other, mean_squares, gain)


def earlier_states(final):
    size = lax.axis_size("y")
    parts = [final] + [round_ring(final, "y", distance) for distance in range(1, size)]
    width = final.shape[1]
    outs = [
        jax.ShapeDtypeStruct(final.shape, BF16),
        jax.ShapeDtypeStruct((LANES, width), F32),
        jax.ShapeDtypeStruct((8, width), F32),
    ]
    total, before, before_decay = pl.pallas_call(
        row_kernel,
        grid_spec=pltpu.PrefetchScalarGridSpec(
            num_scalar_prefetch=1,
            grid=(1,),
            in_specs=[fixed(a) for a in parts],
            out_specs=[fixed(a) for a in outs],
        ),
        out_shape=outs,
        name="row_states",
        **params(1e7, 2),
    )(lax.axis_index("y").astype(jnp.int32)[None], *parts)
    rows = lax.axis_size("z")
    earlier = [
        lax.ppermute(total, "z", [(i, i + distance) for i in range(rows - distance)])
        for distance in range(rows - 1, 0, -1)
    ]
    return before, before_decay, earlier


def travelling(own):
    block = own.shape[0]
    half = block // 2
    y_less, y_more = round_ring(own, "y", 1), round_ring(own, "y", -1)
    z_less, z_more = round_ring(own, "z", 1), round_ring(own, "z", -1)
    join = lambda *parts: jnp.concatenate(parts, axis=0)
    from_y_less = round_ring(join(z_less, y_less[:half]), "y", 1)
    from_y_more = round_ring(join(z_more, y_more[half:]), "y", -1)
    from_z_less = round_ring(join(y_more, z_less[:half]), "z", 1)
    from_z_more = round_ring(join(y_less, z_more[half:]), "z", -1)
    y_far = join(from_y_less[block:], from_y_more[block:])
    z_far = join(from_z_less[block:], from_z_more[block:])
    far_y_less, far_y_more = round_ring(z_far, "y", 1), round_ring(z_far, "y", -1)
    far_z_less, far_z_more = round_ring(y_far, "z", 1), round_ring(y_far, "z", -1)
    far_top = round_ring(far_y_less[:half], "y", 1)
    far_low = round_ring(far_z_more[half:], "z", -1)

    full = lambda indices: [(i, 0, block) for i in indices]
    near = [own, y_less, y_more, z_less, z_more, from_y_less, from_y_more, from_z_less, from_z_more]
    near_sources = full(range(9)) + [(i, block, half) for i in (5, 6, 7, 8)]
    far = [far_y_less, far_y_more, far_z_less, far_z_more, far_top, far_low]
    far_sources = full(range(4)) + [(4, 0, half), (5, 0, half)]
    places = (
        ((0, 0), (-1, 0), (1, 0), (0, -1), (0, 1), (-1, -1), (1, 1), (1, -1), (-1, 1), (2, 0), (0, 2))
        + ((-1, 2), (1, 2), (2, -1), (2, 1), (2, 2))
    )
    y, z = lax.axis_index("y"), lax.axis_index("z")
    order = [(z + dz) % 4 * 4 + (y + dy) % 4 for dy, dz in places]
    return near, near_sources, far, far_sources, order


def shards(
    tokens, x_weight, z_weight, bc_weight, dt_weight, conv_x, conv_bc, dt_bias, decay_rate, skip,
    norm_gain,
):
    core = lax.axis_index("core")
    width = x_weight.shape[1] // 2
    heads = dt_weight.shape[1] // 2

    def mine(a, axis):
        size = a.shape[axis] // 2
        return lax.dynamic_slice_in_dim(a, core * size, size, axis)

    def others(a, axis):
        size = a.shape[axis] // 2
        return lax.dynamic_slice_in_dim(a, (1 - core) * size, size, axis)

    def per_lane(a):
        return jnp.pad(mine(a, 0), (0, LANES - heads))[None, :]

    narrow = jnp.concatenate(
        [bc_weight, dt_weight, jnp.zeros((bc_weight.shape[0], LANES - 2 * heads), BF16)], axis=1
    )
    narrow = lax.all_gather(narrow, ("z", "y", "core"), axis=0, tiled=True)
    own_block = jnp.concatenate([mine(x_weight, 1), swap_cores(others(x_weight, 1))], axis=0)
    near, near_sources, far, far_sources, order = travelling(own_block)
    place = jnp.stack([core, *order]).astype(jnp.int32)

    tokens, z_weight, _ = lax.optimization_barrier((tokens, z_weight, own_block))
    other = swap_cores(tokens)
    last = jnp.where(core == 0, other[-HALO:], tokens[-HALO:])
    slabs = (tokens, other, along_chips(last, 1))
    z_block = in_core_order(core, mine(z_weight, 1), swap_cores(others(z_weight, 1)), 0)
    z_block, _ = lax.optimization_barrier((z_block, near[1]))
    z_whole = lax.all_gather(z_block, ("z", "y"), axis=0, tiled=True)

    bcc, cum, cum_slab, cum_t, step_t, weights_in, decays = prepared(
        place, slabs, narrow, conv_bc, per_lane(dt_bias), per_lane(decay_rate), heads
    )
    sums = first_products(place, slabs, near, near_sources, 11)
    xc, entering, final = local_states(
        place, slabs, far, far_sources, 11, 5, sums, bcc, weights_in, decays, mine(conv_x, 1)
    )
    before, before_decay, earlier = earlier_states(final)
    skip_lanes = jnp.repeat(mine(skip, 0), HEAD)[None, :]
    local = local_outputs(xc, bcc, cum, cum_t, step_t, entering, skip_lanes)
    gate = project_gate(place, slabs, z_whole)
    gated, squares = gate_outputs(gate, local, bcc, cum_slab, before, before_decay, earlier)

    other = swap_cores(others(gated, 0))
    summed = mine(squares + swap_cores(squares), 1)
    across = [round_ring(summed, "x", distance) for distance in range(1, lax.axis_size("x"))]
    mean_squares = (summed + sum(across)) / (2 * width * lax.axis_size("x"))
    return normalized(core, gated, other, mean_squares, norm_gain[None, :])


def solution(mesh):
    fine = Mesh(mesh.devices.reshape(4, 4, 2, 4), ("z", "y", "core", "x"))
    ctx = ("z", "y", "core")
    placed = (
        P(ctx, None),
        P(ctx, "x"),
        P(ctx, "x"),
        P(ctx, None),
        P(ctx, "x"),
        P(None, "x"),
        P(),
        P("x"),
        P("x"),
        P("x"),
        P("x"),
    )
    return jax.shard_map(
        shards, mesh=fine, in_specs=placed, out_specs=P(ctx, "x"), check_vma=False
    )
```

```python
import functools

import jax
import jax.numpy as jnp
from jax import lax
from jax.experimental import pallas as pl
from jax.experimental.pallas import tpu as pltpu
from jax.sharding import Mesh, PartitionSpec as P

GROUP = 256
HALO = 16
LANES = 128
HEAD = 64
VMEM = 60 * 2**20
F32 = jnp.float32
BF16 = jnp.bfloat16


def swap_cores(a):
    return lax.ppermute(a, "core", [(0, 1), (1, 0)])


def round_ring(a, axis, distance):
    size = lax.axis_size(axis)
    return lax.ppermute(a, axis, [(i, (i + distance) % size) for i in range(size)])


def along_chips(a, distance):
    chips = lax.axis_size("z") * lax.axis_size("y")
    return lax.ppermute(a, ("z", "y"), [(i, i + distance) for i in range(chips - distance)])


def in_core_order(core, mine, other, axis):
    first = jnp.where(core == 0, mine, other)
    second = jnp.where(core == 0, other, mine)
    return jnp.concatenate([first, second], axis=axis)


def expand_heads(values, width):
    high = values.astype(BF16)
    rest = values - high.astype(F32)
    middle = rest.astype(BF16)
    low = (rest - middle.astype(F32)).astype(BF16)
    row = lax.broadcasted_iota(jnp.int32, (LANES, width), 0)
    col = lax.broadcasted_iota(jnp.int32, (LANES, width), 1)
    spread = ((col >= row * HEAD) & (col < row * HEAD + HEAD)).astype(BF16)
    dot = lambda part: jnp.dot(part, spread, preferred_element_type=F32)
    return dot(high) + dot(middle) + dot(low)


def silu(a):
    half = 0.5 * a
    return half + half * jnp.tanh(half)


def conv_rows(rows, kernel_ref):
    taps, count = kernel_ref.shape[0], rows.shape[0] - HALO
    first = HALO - (taps - 1)
    accum = kernel_ref[0:1, :] * rows[first : first + count]
    for tap in range(1, taps):
        accum = accum + kernel_ref[tap : tap + 1, :] * rows[first + tap : first + tap + count]
    return silu(accum).astype(BF16)


def pack_kernel(core_ref, x_ref, bc_ref, dt_ref, mine_ref, send_ref):
    width, heads = x_ref.shape[1] // 2, dt_ref.shape[0] // 2
    rows = x_ref.shape[0]
    for ref, core in ((mine_ref, core_ref[0]), (send_ref, 1 - core_ref[0])):
        for panel in range(width // LANES):
            lanes = pl.ds(pl.multiple_of(core * width + panel * LANES, LANES), LANES)
            ref[panel * rows : (panel + 1) * rows, :] = x_ref[:, lanes]
        lanes = pl.ds(pl.multiple_of(core * LANES, LANES), LANES)
        ref[width // LANES * rows : width // LANES * rows + rows, :] = bc_ref[:, lanes]
        ref[width // LANES * rows + rows :, :] = dt_ref[pl.ds(pl.multiple_of(core * heads, heads), heads), :]


def block_columns(ref, place_ref, first, count):
    core = place_ref[0]
    parts = []
    for index in range(first, first + count):
        base = place_ref[1 + index] * (2 * LANES)
        for start in (base + LANES * core, base + LANES * (1 - core)):
            parts.append(ref[:, pl.ds(pl.multiple_of(start, LANES), LANES)])
    return jnp.concatenate(parts, axis=1)


def unpack_wide(chunks, refs, target):
    for index, (ref, base) in enumerate(chunks):
        for panel in range(target.shape[1] // LANES):
            start = base + panel * LANES
            target[index * LANES : (index + 1) * LANES, panel * LANES : (panel + 1) * LANES] = refs[
                ref
            ][start : start + LANES, :]


def unpack_narrow(chunks, refs, width, bc, dt):
    for index, (ref, base) in enumerate(chunks):
        rows = slice(index * LANES, (index + 1) * LANES)
        bc[rows, :] = refs[ref][base + width : base + width + LANES, :]
        dt[:, rows] = refs[ref][base + width + LANES : base + width + LANES + dt.shape[0], :]


def narrow_products(columns, bc, dt):
    turned = (((1,), (1,)), ((), ()))
    return (
        jnp.dot(columns, bc[...], preferred_element_type=F32),
        lax.dot_general(columns, dt[...], turned, preferred_element_type=F32),
    )


def first_kernel(chunks, count, place_ref, own_ref, other_ref, before_ref, *refs):
    weights = refs[:-8]
    x_ref, x_before_ref, bc_ref, bc_before_ref, dt_ref, wide, bc, dt = refs[-8:]
    block = pl.program_id(0)
    is_own = block // 2 == place_ref[0]

    @pl.when(block == 0)
    def _():
        unpack_wide(chunks, weights, wide)
        unpack_narrow(chunks, weights, wide.shape[1], bc, dt)
        columns = block_columns(before_ref, place_ref, 0, count)
        x_before_ref[...] = jnp.dot(columns, wide[...], preferred_element_type=F32)
        bc_before_ref[...] = narrow_products(columns, bc, dt)[0]

    def products(ref):
        columns = block_columns(ref, place_ref, 0, count)
        x_ref[...] = jnp.dot(columns, wide[...], preferred_element_type=F32)
        bc_ref[...], dt_ref[...] = narrow_products(columns, bc, dt)

    @pl.when(is_own)
    def _():
        products(own_ref)

    @pl.when(jnp.logical_not(is_own))
    def _():
        products(other_ref)


def narrow_kernel(chunks, width, done, count, place_ref, own_ref, other_ref, before_ref, *refs):
    weights = refs[:-7]
    sum_ref, sum_before_ref, sum_dt_ref, out_ref, raw_ref, bc, dt = refs[-7:]
    block = pl.program_id(0)
    is_own = block // 2 == place_ref[0]
    rows = pl.ds(pl.multiple_of(HALO + block * GROUP, HALO), GROUP)

    @pl.when(block == 0)
    def _():
        unpack_narrow(chunks, weights, width, bc, dt)
        columns = block_columns(before_ref, place_ref, done, count)
        out_ref[:HALO, :] = (sum_before_ref[...] + narrow_products(columns, bc, dt)[0]).astype(BF16)

    def products(ref):
        added, raw = narrow_products(block_columns(ref, place_ref, done, count), bc, dt)
        out_ref[rows, :] = (sum_ref[...] + added).astype(BF16)
        raw_ref[...] = sum_dt_ref[...] + raw

    @pl.when(is_own)
    def _():
        products(own_ref)

    @pl.when(jnp.logical_not(is_own))
    def _():
        products(other_ref)


def inputs_kernel(chunks, done, count, place_ref, own_ref, other_ref, before_ref, *refs):
    weights = refs[:-7]
    sum_ref, sum_before_ref, conv_ref, xc_ref, wide, x_in, tail = refs[-7:]
    block = pl.program_id(0)
    is_own = block // 2 == place_ref[0]

    def product(ref):
        columns = block_columns(ref, place_ref, done, count)
        return jnp.dot(columns, wide[...], preferred_element_type=F32)

    @pl.when(block == 0)
    def _():
        unpack_wide(chunks, weights, wide)
        tail[...] = (sum_before_ref[...] + product(before_ref)).astype(BF16).astype(F32)

    @pl.when(is_own)
    def _():
        x_in[...] = (sum_ref[...] + product(own_ref)).astype(BF16).astype(F32)

    @pl.when(jnp.logical_not(is_own))
    def _():
        x_in[...] = (sum_ref[...] + product(other_ref)).astype(BF16).astype(F32)

    rows = jnp.concatenate([tail[...], x_in[...]], axis=0)
    tail[...] = rows[GROUP:]
    xc_ref[...] = conv_rows(rows, conv_ref)


def states_kernel(
    core_ref, xc_ref, bc_mine_ref, bc_other_ref, raw_ref, conv_ref, bias_ref, rate_ref,
    bcc_ref, cum_ref, cum_slab_ref, cum_t_ref, step_t_ref, entering_ref, final_ref,
    state, total,
):
    block = pl.program_id(0)
    width, heads = xc_ref.shape[1], cum_t_ref.shape[0]
    start = pl.multiple_of(block * GROUP, GROUP)

    @pl.when(block == 0)
    def _():
        state[...] = jnp.zeros_like(state)
        total[...] = jnp.zeros_like(total)

    mine = bc_mine_ref[pl.ds(start, GROUP + HALO), :].astype(F32)
    other = bc_other_ref[pl.ds(start, GROUP + HALO), :].astype(F32)
    first = core_ref[0] == 0
    b_rows = conv_rows(jnp.where(first, mine, other), conv_ref.at[:, :LANES])
    c_rows = conv_rows(jnp.where(first, other, mine), conv_ref.at[:, LANES:])
    bcc_ref[:, :LANES] = b_rows
    bcc_ref[:, LANES:] = c_rows
    raw = jnp.concatenate([raw_ref[...], jnp.zeros((GROUP, LANES - heads), F32)], axis=1)
    raw = raw + bias_ref[...]
    step_size = jnp.maximum(raw, 0.0) + jnp.log1p(jnp.exp(-jnp.abs(raw)))
    log_decay = -rate_ref[...] * step_size
    row = lax.broadcasted_iota(jnp.int32, (GROUP, GROUP), 0)
    col = lax.broadcasted_iota(jnp.int32, (GROUP, GROUP), 1)
    lower = (row >= col).astype(F32)
    cum = jnp.dot(lower, log_decay, preferred_element_type=F32, precision=lax.Precision.HIGHEST)
    last = cum[GROUP - 1 : GROUP, :]
    cum_ref[...] = cum
    cum_slab_ref[...] = cum + total[0:1, :]
    cum_t_ref[...] = cum.T[:heads, :]
    step_t_ref[...] = step_size.T[:heads, :]
    entering_ref[0] = state[...].astype(BF16)
    weights_in = expand_heads(jnp.exp(last - cum) * step_size, width)
    weighted = (weights_in * xc_ref[...].astype(F32)).astype(BF16)
    contrib = lax.dot_general(
        b_rows, weighted, (((0,), (0,)), ((), ())), preferred_element_type=F32
    )
    decay = expand_heads(jnp.broadcast_to(jnp.exp(last), (8, LANES)), width)
    state[...] = state[...] * decay[0:1] + contrib
    total[...] = total[...] + jnp.broadcast_to(last, total.shape)

    @pl.when(block == pl.num_programs(0) - 1)
    def _():
        final_ref[:LANES, :] = state[...].astype(BF16)
        final_ref[LANES:, :] = split_decay(expand_heads(jnp.exp(total[...]), width)[0:1])


def split_decay(decay):
    high = decay.astype(BF16)
    low = decay - high.astype(F32)
    row = lax.broadcasted_iota(jnp.int32, (HALO, decay.shape[1]), 0)
    return jnp.where(row == 0, high.astype(F32), jnp.where(row == 1, low, 0.0)).astype(BF16)


def unpacked(sent):
    sent = sent.astype(F32)
    return sent[:LANES], sent[LANES : LANES + 1] + sent[LANES + 1 : LANES + 2]


def row_kernel(place_ref, *refs):
    size = len(refs) - 3
    parts, (total_ref, before_ref, before_decay_ref) = refs[:size], refs[size:]
    place = place_ref[0]
    width = total_ref.shape[1]
    total, decay = jnp.zeros((LANES, width), F32), jnp.ones((1, width), F32)
    before_ref[...] = total
    before_decay_ref[...] = jnp.broadcast_to(decay, before_decay_ref.shape)
    for index in range(size):
        if index > 0:

            @pl.when(place == index)
            def _():
                before_ref[...] = total
                before_decay_ref[...] = jnp.broadcast_to(decay, before_decay_ref.shape)

        distance = (place - index + size) % size
        chosen = parts[0][...]
        for other in range(1, size):
            chosen = jnp.where(distance == other, parts[other][...], chosen)
        state, state_decay = unpacked(chosen)
        total = total * state_decay + state
        decay = decay * state_decay
    total_ref[:LANES, :] = total.astype(BF16)
    total_ref[LANES:, :] = split_decay(decay)


def outputs_kernel(xc_ref, bcc_ref, cum_ref, cum_t_ref, step_t_ref, entering_ref, skip_ref, out_ref):
    width = xc_ref.shape[1]
    b_rows, c_rows = bcc_ref[:, :LANES], bcc_ref[:, LANES:]
    scores = lax.dot_general(c_rows, b_rows, (((1,), (1,)), ((), ())), preferred_element_type=F32)
    row = lax.broadcasted_iota(jnp.int32, (GROUP, GROUP), 0)
    col = lax.broadcasted_iota(jnp.int32, (GROUP, GROUP), 1)
    scores = jnp.where(row >= col, scores, 0.0)
    cum = cum_ref[...]
    grown = expand_heads(jnp.exp(cum), width)
    out_ref[...] = grown * jnp.dot(c_rows, entering_ref[0], preferred_element_type=F32)
    lane = lax.broadcasted_iota(jnp.int32, (GROUP, LANES), 1)

    def mixing(head):
        gaps = cum[:, head : head + 1] - cum_t_ref[head : head + 1, :]
        return (
            scores * jnp.exp(jnp.minimum(gaps, 0.0)) * step_t_ref[head : head + 1, :]
        ).astype(BF16)

    for pair in range(width // LANES):
        lanes = slice(pair * LANES, (pair + 1) * LANES)
        inputs = xc_ref[:, lanes]
        zero = jnp.zeros_like(inputs)
        both = jnp.concatenate([mixing(2 * pair), mixing(2 * pair + 1)], axis=1)
        stacked = jnp.concatenate(
            [jnp.where(lane < HEAD, inputs, zero), jnp.where(lane < HEAD, zero, inputs)], axis=0
        )
        out_ref[:, lanes] = (
            out_ref[:, lanes]
            + jnp.dot(both, stacked, preferred_element_type=F32)
            + skip_ref[:, lanes] * inputs.astype(F32)
        )


def z_kernel(place_ref, own_ref, other_ref, weight_ref, gate_ref, accum):
    step = pl.program_id(0)
    slab = own_ref.shape[0]
    core = place_ref[0]

    def product(ref):
        return jnp.dot(ref[...], weight_ref[...], preferred_element_type=F32)

    for index, ref in enumerate((own_ref, other_ref)):
        rows = slice(index * slab, (index + 1) * slab)
        target = pl.ds(pl.multiple_of(slab * (core if index == 0 else 1 - core), slab), slab)

        @pl.when(step == 0)
        def _():
            accum[rows, :] = product(ref)

        @pl.when((step > 0) & (step < pl.num_programs(0) - 1))
        def _():
            accum[rows, :] = accum[rows, :] + product(ref)

        @pl.when(step == pl.num_programs(0) - 1)
        def _():
            gate_ref[target, :] = (accum[rows, :] + product(ref)).astype(BF16)


def gate_kernel(
    gate_ref, local_ref, bcc_ref, cum_ref, before_ref, before_decay_ref, *refs
):
    earlier, (gated_ref, squares_ref, incoming) = refs[:-3], refs[-3:]
    width = local_ref.shape[1]

    @pl.when(pl.program_id(0) == 0)
    def _():
        carried = jnp.zeros((LANES, width), F32)
        for part in earlier:
            state, decay = unpacked(part[...])
            carried = carried * decay + state
        incoming[...] = (carried * before_decay_ref[0:1, :] + before_ref[...]).astype(BF16)

    grown = expand_heads(jnp.exp(cum_ref[...]), width)
    carried = jnp.dot(bcc_ref[:, LANES:], incoming[...], preferred_element_type=F32)
    gated = (local_ref[...] + grown * carried) * silu(gate_ref[...].astype(F32))
    gated_ref[...] = gated.astype(BF16)
    squares = gated * gated
    high = squares.astype(BF16)
    low = (squares - high.astype(F32)).astype(BF16)
    ones = jnp.ones((8, width), BF16)
    across = (((1,), (1,)), ((), ()))
    summed = lax.dot_general(ones, high, across, preferred_element_type=F32) + lax.dot_general(
        ones, low, across, preferred_element_type=F32
    )
    squares_ref[...] = summed[0:1, :]


def norm_kernel(core_ref, mine_ref, other_ref, squares_ref, gain_ref, out_ref):
    half = pl.program_id(0)
    across = jnp.broadcast_to(squares_ref[...], (8, squares_ref.shape[1]))
    scale = lax.rsqrt(across + 1e-05).T[:, 0:1]

    @pl.when(half == core_ref[0])
    def _():
        out_ref[...] = (mine_ref[...].astype(F32) * scale * gain_ref[...]).astype(BF16)

    @pl.when(half != core_ref[0])
    def _():
        out_ref[...] = (other_ref[...].astype(F32) * scale * gain_ref[...]).astype(BF16)


def whole(shape):
    return pl.BlockSpec(shape, lambda i: (0,) * len(shape))


def rows_of(width):
    return pl.BlockSpec((GROUP, width), lambda i: (i, 0))


def params(flops, megabytes):
    return dict(
        compiler_params=pltpu.CompilerParams(vmem_limit_bytes=VMEM),
        cost_estimate=pl.CostEstimate(
            flops=int(flops), bytes_accessed=megabytes * 2**20, transcendentals=0
        ),
    )


def fixed(a):
    return pl.BlockSpec(a.shape, lambda i, place: (0,) * len(a.shape))


def row_block(width):
    return pl.BlockSpec((GROUP, width), lambda i, place: (i, 0))


def slab_blocks(depth):
    own = pl.BlockSpec((GROUP, depth), lambda i, place: (jnp.clip(i - 2 * place[0], 0, 1), 0))
    other = pl.BlockSpec((GROUP, depth), lambda i, place: (jnp.clip(i - 2 + 2 * place[0], 0, 1), 0))
    return [own, other]


def packed_weights(core, x_weight, bc_weight, dt_turned):
    out = jax.ShapeDtypeStruct(
        (x_weight.shape[1] // 2 + bc_weight.shape[0] + dt_turned.shape[0] // 2, LANES), BF16
    )
    return pl.pallas_call(
        pack_kernel,
        grid_spec=pltpu.PrefetchScalarGridSpec(
            num_scalar_prefetch=1,
            grid=(1,),
            in_specs=[fixed(a) for a in (x_weight, bc_weight, dt_turned)],
            out_specs=[fixed(out), fixed(out)],
        ),
        out_shape=[out, out],
        name="packed_weights",
        **params(1e6, 1),
    )(core, x_weight, bc_weight, dt_turned)


def by_blocks(kernel, name, cost, place, slabs, weights, extras, extra_specs, outs, out_specs, scratch):
    own, other, before = slabs
    return pl.pallas_call(
        kernel,
        grid_spec=pltpu.PrefetchScalarGridSpec(
            num_scalar_prefetch=1,
            grid=(2 * own.shape[0] // GROUP,),
            in_specs=slab_blocks(own.shape[1]) + [fixed(a) for a in (before, *weights)] + extra_specs,
            out_specs=out_specs,
            scratch_shapes=scratch,
        ),
        out_shape=outs,
        name=name,
        **cost,
    )(place, *slabs, *weights, *extras)


def first_products(place, slabs, weights, chunks, width, heads):
    shape, rows = jax.ShapeDtypeStruct, 2 * slabs[0].shape[0]
    outs = [
        shape((rows, width), F32), shape((HALO, width), F32),
        shape((rows, LANES), F32), shape((HALO, LANES), F32), shape((rows, heads), F32),
    ]
    specs = [row_block(width), fixed(outs[1]), row_block(LANES), fixed(outs[3]), row_block(heads)]
    depth = len(chunks) * LANES
    scratch = [
        pltpu.VMEM((depth, width), BF16), pltpu.VMEM((depth, LANES), BF16), pltpu.VMEM((heads, depth), BF16),
    ]
    kernel = functools.partial(first_kernel, chunks, len(chunks) // 2)
    return by_blocks(
        kernel, "first_products", params(9e9, 20), place, slabs, weights, [], [], outs, specs, scratch
    )


def narrow_inputs(place, slabs, weights, chunks, done, sums):
    sum_bc, sum_before, sum_dt = sums
    rows, heads = sum_dt.shape
    width = weights[0].shape[0] // 2 - LANES - heads
    outs = [jax.ShapeDtypeStruct((HALO + rows, LANES), BF16), jax.ShapeDtypeStruct((rows, heads), F32)]
    depth = len(chunks) * LANES
    return by_blocks(
        functools.partial(narrow_kernel, chunks, width, done, len(chunks) // 2),
        "narrow_inputs", params(2e9, 12), place, slabs, weights,
        [sum_bc, sum_before, sum_dt], [row_block(LANES), fixed(sum_before), row_block(heads)],
        outs, [fixed(outs[0]), row_block(heads)],
        [pltpu.VMEM((depth, LANES), BF16), pltpu.VMEM((heads, depth), BF16)],
    )


def head_inputs(place, slabs, weights, chunks, done, sums, conv_x):
    sum_x, sum_before = sums
    rows, width = sum_x.shape
    return by_blocks(
        functools.partial(inputs_kernel, chunks, done, len(chunks) // 2),
        "head_inputs", params(5e9, 18), place, slabs, weights,
        [sum_x, sum_before, conv_x], [row_block(width), fixed(sum_before), fixed(conv_x)],
        jax.ShapeDtypeStruct((rows, width), BF16), row_block(width),
        [
            pltpu.VMEM((len(chunks) * LANES, width), BF16), pltpu.VMEM((GROUP, width), F32),
            pltpu.VMEM((HALO, width), F32),
        ],
    )


def local_states(core, xc, bc_mine, bc_other, raw, conv_bc, bias, rate):
    rows, width = xc.shape
    heads, blocks = raw.shape[1], rows // GROUP
    shape = jax.ShapeDtypeStruct
    by_lane = pl.BlockSpec((heads, GROUP), lambda i, core: (0, i))
    outs = [
        shape((rows, 2 * LANES), BF16), shape((rows, LANES), F32), shape((rows, LANES), F32),
        shape((heads, rows), F32), shape((heads, rows), F32),
        shape((blocks, LANES, width), BF16), shape((LANES + HALO, width), BF16),
    ]
    return pl.pallas_call(
        states_kernel,
        grid_spec=pltpu.PrefetchScalarGridSpec(
            num_scalar_prefetch=1,
            grid=(blocks,),
            in_specs=[row_block(width), fixed(bc_mine), fixed(bc_other), row_block(heads)]
            + [fixed(a) for a in (conv_bc, bias, rate)],
            out_specs=[
                row_block(2 * LANES), row_block(LANES), row_block(LANES), by_lane, by_lane,
                pl.BlockSpec((1, LANES, width), lambda i, core: (i, 0, 0)), fixed(outs[6]),
            ],
            scratch_shapes=[pltpu.VMEM((LANES, width), F32), pltpu.VMEM((8, LANES), F32)],
        ),
        out_shape=outs,
        name="states",
        **params(5e9, 8),
    )(core, xc, bc_mine, bc_other, raw, conv_bc, bias, rate)


def local_outputs(xc, bcc, cum, cum_t, step_t, entering, skip):
    rows, width = xc.shape
    heads = cum_t.shape[0]
    by_lane = pl.BlockSpec((heads, GROUP), lambda i: (0, i))
    return pl.pallas_call(
        outputs_kernel,
        grid=(rows // GROUP,),
        in_specs=[
            rows_of(width), rows_of(2 * LANES), rows_of(LANES), by_lane, by_lane,
            pl.BlockSpec((1, LANES, width), lambda i: (i, 0, 0)), whole((1, width)),
        ],
        out_specs=rows_of(width),
        out_shape=jax.ShapeDtypeStruct((rows, width), F32),
        compiler_params=pltpu.CompilerParams(vmem_limit_bytes=VMEM),
        cost_estimate=pl.CostEstimate(flops=10**10, bytes_accessed=10 * 2**20, transcendentals=4 * 2**20),
        name="outputs",
    )(xc, bcc, cum, cum_t, step_t, entering, skip)


def project_gate(place, slabs, weight):
    own, other, _ = slabs
    rows, width, depth = 2 * own.shape[0], weight.shape[1], 1024
    columns = pl.BlockSpec((own.shape[0], depth), lambda i, place: (0, i))
    out = jax.ShapeDtypeStruct((rows, width), BF16)
    return pl.pallas_call(
        z_kernel,
        grid_spec=pltpu.PrefetchScalarGridSpec(
            num_scalar_prefetch=1,
            grid=(weight.shape[0] // depth,),
            in_specs=[columns, columns, pl.BlockSpec((depth, width), lambda i, place: (i, 0))],
            out_specs=fixed(out),
            scratch_shapes=[pltpu.VMEM((rows, width), F32)],
        ),
        out_shape=out,
        name="project_gate",
        **params(9e9, 20),
    )(place, own, other, weight)


def gate_outputs(gate, local, bcc, cum_slab, before, before_decay, earlier):
    rows, width = local.shape
    return pl.pallas_call(
        gate_kernel,
        grid=(rows // GROUP,),
        in_specs=[rows_of(width), rows_of(width), rows_of(2 * LANES), rows_of(LANES)]
        + [whole(a.shape) for a in (before, before_decay, *earlier)],
        out_specs=[rows_of(width), pl.BlockSpec((1, GROUP), lambda i: (0, i))],
        out_shape=[
            jax.ShapeDtypeStruct((rows, width), BF16), jax.ShapeDtypeStruct((1, rows), F32),
        ],
        scratch_shapes=[pltpu.VMEM((LANES, width), BF16)],
        name="gate",
        **params(1e9, 10),
    )(gate, local, bcc, cum_slab, before, before_decay, *earlier)


def normalized(core, gated, other, mean_squares, gain):
    rows, width = other.shape
    return pl.pallas_call(
        norm_kernel,
        grid_spec=pltpu.PrefetchScalarGridSpec(
            num_scalar_prefetch=1,
            grid=(2,),
            in_specs=[
                pl.BlockSpec((rows, width), lambda j, core: (core[0], 0)),
                pl.BlockSpec((rows, width), lambda j, core: (0, 0)),
                pl.BlockSpec((1, rows), lambda j, core: (0, 0)),
                pl.BlockSpec((1, width), lambda j, core: (0, j)),
            ],
            out_specs=pl.BlockSpec((rows, width), lambda j, core: (0, j)),
        ),
        out_shape=jax.ShapeDtypeStruct((rows, 2 * width), BF16),
        compiler_params=pltpu.CompilerParams(vmem_limit_bytes=VMEM),
        cost_estimate=pl.CostEstimate(flops=10**7, bytes_accessed=4 * 2**20, transcendentals=0),
        name="normalized",
    )(core.astype(jnp.int32)[None], gated, other, mean_squares, gain)


def earlier_states(final):
    size = lax.axis_size("y")
    parts = [final] + [round_ring(final, "y", distance) for distance in range(1, size)]
    width = final.shape[1]
    outs = [
        jax.ShapeDtypeStruct(final.shape, BF16),
        jax.ShapeDtypeStruct((LANES, width), F32),
        jax.ShapeDtypeStruct((8, width), F32),
    ]
    total, before, before_decay = pl.pallas_call(
        row_kernel,
        grid_spec=pltpu.PrefetchScalarGridSpec(
            num_scalar_prefetch=1,
            grid=(1,),
            in_specs=[fixed(a) for a in parts],
            out_specs=[fixed(a) for a in outs],
        ),
        out_shape=outs,
        name="row_states",
        **params(1e7, 2),
    )(lax.axis_index("y").astype(jnp.int32)[None], *parts)
    rows = lax.axis_size("z")
    earlier = [
        lax.ppermute(total, "z", [(i, i + distance) for i in range(rows - distance)])
        for distance in range(rows - 1, 0, -1)
    ]
    return before, before_decay, earlier


def near_blocks(own):
    block = own.shape[0]
    half = block // 2
    y_less, y_more = round_ring(own, "y", 1), round_ring(own, "y", -1)
    z_less, z_more = round_ring(own, "z", 1), round_ring(own, "z", -1)
    join = lambda *parts: jnp.concatenate(parts, axis=0)
    from_y_less = round_ring(join(z_less, y_less[:half]), "y", 1)
    from_y_more = round_ring(join(z_more, y_more[half:]), "y", -1)
    from_z_less = round_ring(join(y_more, z_less[:half]), "z", 1)
    from_z_more = round_ring(join(y_less, z_more[half:]), "z", -1)
    y_far = join(from_y_less[block:], from_y_more[block:])
    z_far = join(from_z_less[block:], from_z_more[block:])
    near = [own, y_less, y_more, z_less, z_more, from_y_less, from_y_more, from_z_less, from_z_more]
    chunks = [(i, base) for i in range(9) for base in (0, half)] + [(i, block) for i in (5, 6, 7, 8)]
    return near, chunks, y_far, z_far


def far_blocks(y_far, z_far, hold):
    half = y_far.shape[0] // 2
    far_y_less, far_y_more = round_ring(z_far, "y", 1), round_ring(z_far, "y", -1)
    far_z_less, far_z_more = round_ring(y_far, "z", 1), round_ring(y_far, "z", -1)
    top, low = hold(far_y_less[:half], far_z_more[half:])
    far_top, far_low = round_ring(top, "y", 1), round_ring(low, "z", -1)
    far = [far_y_less, far_y_more, far_z_less, far_z_more, far_top, far_low]
    chunks = [(i, base) for i in range(4) for base in (0, half)] + [(4, 0), (5, 0)]
    return far, chunks


def block_order():
    places = (
        ((0, 0), (-1, 0), (1, 0), (0, -1), (0, 1), (-1, -1), (1, 1), (1, -1), (-1, 1), (2, 0), (0, 2))
        + ((-1, 2), (1, 2), (2, -1), (2, 1), (2, 2))
    )
    y, z = lax.axis_index("y"), lax.axis_index("z")
    return [(z + dz) % 4 * 4 + (y + dy) % 4 for dy, dz in places]


def shards(
    tokens, x_weight, z_weight, bc_weight, dt_weight, conv_x, conv_bc, dt_bias, decay_rate, skip,
    norm_gain,
):
    core = lax.axis_index("core")
    width = x_weight.shape[1] // 2
    heads = dt_weight.shape[1] // 2

    def mine(a, axis):
        size = a.shape[axis] // 2
        return lax.dynamic_slice_in_dim(a, core * size, size, axis)

    def others(a, axis):
        size = a.shape[axis] // 2
        return lax.dynamic_slice_in_dim(a, (1 - core) * size, size, axis)

    def per_lane(a):
        return jnp.pad(mine(a, 0), (0, LANES - heads))[None, :]

    place = jnp.stack([core, *block_order()]).astype(jnp.int32)
    this_core = place[:1]
    packed, send = packed_weights(this_core, x_weight, bc_weight, dt_weight.T)
    own_block = jnp.concatenate([packed, swap_cores(send)], axis=0)
    near, near_chunks, y_far, z_far = near_blocks(own_block)

    tokens, z_weight, _ = lax.optimization_barrier((tokens, z_weight, own_block))
    other = swap_cores(tokens)
    last = jnp.where(core == 0, other[-HALO:], tokens[-HALO:])
    slabs = (tokens, other, along_chips(last, 1))
    z_block = in_core_order(core, mine(z_weight, 1), swap_cores(others(z_weight, 1)), 0)
    z_block, *_ = lax.optimization_barrier((z_block, *near[1:5]))
    z_whole = lax.all_gather(z_block, ("z", "y"), axis=0, tiled=True)

    y_far, z_far, _ = lax.optimization_barrier((y_far, z_far, slabs[2]))
    sum_x, sum_x_before, *narrow_sums = first_products(place, slabs, near, near_chunks, width, heads)
    hold = lambda top, low: lax.optimization_barrier((top, low, sum_x))[:2]
    far, far_chunks = far_blocks(y_far, z_far, hold)
    bc_mine, raw = narrow_inputs(place, slabs, far, far_chunks, 11, narrow_sums)
    bc_other = swap_cores(bc_mine)
    xc = head_inputs(place, slabs, far, far_chunks, 11, (sum_x, sum_x_before), mine(conv_x, 1))
    bcc, cum, cum_slab, cum_t, step_t, entering, final = local_states(
        this_core, xc, bc_mine, bc_other, raw, conv_bc, per_lane(dt_bias), per_lane(decay_rate)
    )
    before, before_decay, earlier = earlier_states(final)
    skip_lanes = jnp.repeat(mine(skip, 0), HEAD)[None, :]
    local = local_outputs(xc, bcc, cum, cum_t, step_t, entering, skip_lanes)
    gate = project_gate(place, slabs, z_whole)
    gated, squares = gate_outputs(gate, local, bcc, cum_slab, before, before_decay, earlier)

    other = swap_cores(others(gated, 0))
    summed = mine(squares + swap_cores(squares), 1)
    across = [round_ring(summed, "x", distance) for distance in range(1, lax.axis_size("x"))]
    mean_squares = (summed + sum(across)) / (2 * width * lax.axis_size("x"))
    return normalized(core, gated, other, mean_squares, norm_gain[None, :])


def solution(mesh):
    fine = Mesh(mesh.devices.reshape(4, 4, 2, 4), ("z", "y", "core", "x"))
    ctx = ("z", "y", "core")
    placed = (
        P(ctx, None),
        P(ctx, "x"),
        P(ctx, "x"),
        P(ctx, None),
        P(ctx, "x"),
        P(None, "x"),
        P(),
        P("x"),
        P("x"),
        P("x"),
        P("x"),
    )
    return jax.shard_map(
        shards, mesh=fine, in_specs=placed, out_specs=P(ctx, "x"), check_vma=False
    )
```

```python
import functools

import jax
import jax.numpy as jnp
from jax import lax
from jax.experimental import pallas as pl
from jax.experimental.pallas import tpu as pltpu
from jax.sharding import Mesh, PartitionSpec as P

GROUP = 256
HALO = 16
LANES = 128
HEAD = 64
VMEM = 44 * 2**20
F32 = jnp.float32
BF16 = jnp.bfloat16


def swap_cores(a):
    return lax.ppermute(a, "core", [(0, 1), (1, 0)])


def round_ring(a, axis, distance):
    size = lax.axis_size(axis)
    return lax.ppermute(a, axis, [(i, (i + distance) % size) for i in range(size)])


def along_chips(a, distance):
    chips = lax.axis_size("z") * lax.axis_size("y")
    return lax.ppermute(a, ("z", "y"), [(i, i + distance) for i in range(chips - distance)])


def in_core_order(core, mine, other, axis):
    first = jnp.where(core == 0, mine, other)
    second = jnp.where(core == 0, other, mine)
    return jnp.concatenate([first, second], axis=axis)


def expand_heads(values, width):
    high = values.astype(BF16)
    rest = values - high.astype(F32)
    middle = rest.astype(BF16)
    low = (rest - middle.astype(F32)).astype(BF16)
    row = lax.broadcasted_iota(jnp.int32, (LANES, width), 0)
    col = lax.broadcasted_iota(jnp.int32, (LANES, width), 1)
    spread = ((col >= row * HEAD) & (col < row * HEAD + HEAD)).astype(BF16)
    dot = lambda part: jnp.dot(part, spread, preferred_element_type=F32)
    return dot(high) + dot(middle) + dot(low)


def silu(a):
    half = 0.5 * a
    return half + half * jnp.tanh(half)


def conv_rows(rows, kernel_ref):
    taps, count = kernel_ref.shape[0], rows.shape[0] - HALO
    first = HALO - (taps - 1)
    accum = kernel_ref[0:1, :] * rows[first : first + count]
    for tap in range(1, taps):
        accum = accum + kernel_ref[tap : tap + 1, :] * rows[first + tap : first + tap + count]
    return silu(accum).astype(BF16)


def pack_kernel(core_ref, x_ref, bc_ref, dt_ref, mine_ref, send_ref):
    width, heads = x_ref.shape[1] // 2, dt_ref.shape[0] // 2
    rows = x_ref.shape[0]
    for ref, core in ((mine_ref, core_ref[0]), (send_ref, 1 - core_ref[0])):
        for panel in range(width // LANES):
            lanes = pl.ds(pl.multiple_of(core * width + panel * LANES, LANES), LANES)
            ref[panel * rows : (panel + 1) * rows, :] = x_ref[:, lanes]
        lanes = pl.ds(pl.multiple_of(core * LANES, LANES), LANES)
        ref[width // LANES * rows : width // LANES * rows + rows, :] = bc_ref[:, lanes]
        ref[width // LANES * rows + rows :, :] = dt_ref[pl.ds(pl.multiple_of(core * heads, heads), heads), :]


def block_columns(ref, place_ref, first, count):
    core = place_ref[0]
    parts = []
    for index in range(first, first + count):
        base = place_ref[1 + index] * (2 * LANES)
        for start in (base + LANES * core, base + LANES * (1 - core)):
            parts.append(ref[:, pl.ds(pl.multiple_of(start, LANES), LANES)])
    return jnp.concatenate(parts, axis=1)


def unpack_wide(chunks, refs, target):
    for index, (ref, base) in enumerate(chunks):
        rows = slice(index * LANES, (index + 1) * LANES)
        if refs[ref].shape[1] == target.shape[1]:
            target[rows, :] = refs[ref][base : base + LANES, :]
            continue
        for panel in range(target.shape[1] // LANES):
            start = base + panel * LANES
            target[rows, panel * LANES : (panel + 1) * LANES] = refs[ref][start : start + LANES, :]


def unpack_narrow(chunks, refs, width, bc, dt):
    for index, (ref, base) in enumerate(chunks):
        rows = slice(index * LANES, (index + 1) * LANES)
        bc[rows, :] = refs[ref][base + width : base + width + LANES, :]
        dt[:, rows] = refs[ref][base + width + LANES : base + width + LANES + dt.shape[0], :]


def narrow_products(columns, bc, dt):
    turned = (((1,), (1,)), ((), ()))
    return (
        jnp.dot(columns, bc[...], preferred_element_type=F32),
        lax.dot_general(columns, dt[...], turned, preferred_element_type=F32),
    )


def first_kernel(chunks, count, place_ref, own_ref, other_ref, before_ref, *refs):
    weights = refs[:-8]
    x_ref, x_before_ref, bc_ref, bc_before_ref, dt_ref, wide, bc, dt = refs[-8:]
    block = pl.program_id(0)
    is_own = block // 2 == place_ref[0]

    @pl.when(block == 0)
    def _():
        unpack_wide(chunks, weights, wide)
        unpack_narrow(chunks, weights, wide.shape[1], bc, dt)
        columns = block_columns(before_ref, place_ref, 0, count)
        x_before_ref[...] = jnp.dot(columns, wide[...], preferred_element_type=F32)
        bc_before_ref[...] = narrow_products(columns, bc, dt)[0]

    def products(ref):
        columns = block_columns(ref, place_ref, 0, count)
        x_ref[...] = jnp.dot(columns, wide[...], preferred_element_type=F32)
        bc_ref[...], dt_ref[...] = narrow_products(columns, bc, dt)

    @pl.when(is_own)
    def _():
        products(own_ref)

    @pl.when(jnp.logical_not(is_own))
    def _():
        products(other_ref)


def inputs_kernel(chunks, done, count, place_ref, own_ref, other_ref, before_ref, *refs):
    weights = refs[:-14]
    (
        sum_ref, sum_before_ref, sum_bc_ref, sum_bc_before_ref, sum_dt_ref, conv_ref,
        xc_ref, out_bc_ref, raw_ref,
        wide, bc, dt, x_in, tail,
    ) = refs[-14:]
    block = pl.program_id(0)
    is_own = block // 2 == place_ref[0]
    rows_out = pl.ds(pl.multiple_of(HALO + block * GROUP, HALO), GROUP)

    @pl.when(block == 0)
    def _():
        unpack_wide(chunks, weights, wide)
        unpack_narrow(chunks, weights, wide.shape[1], bc, dt)
        columns = block_columns(before_ref, place_ref, done, count)
        product = jnp.dot(columns, wide[...], preferred_element_type=F32)
        tail[...] = (sum_before_ref[...] + product).astype(BF16).astype(F32)
        narrow = narrow_products(columns, bc, dt)[0]
        out_bc_ref[:HALO, :] = (sum_bc_before_ref[...] + narrow).astype(BF16)

    def products(ref):
        columns = block_columns(ref, place_ref, done, count)
        product = jnp.dot(columns, wide[...], preferred_element_type=F32)
        x_in[...] = (sum_ref[...] + product).astype(BF16).astype(F32)
        added, raw = narrow_products(columns, bc, dt)
        out_bc_ref[rows_out, :] = (sum_bc_ref[...] + added).astype(BF16)
        raw_ref[...] = sum_dt_ref[...] + raw

    @pl.when(is_own)
    def _():
        products(own_ref)

    @pl.when(jnp.logical_not(is_own))
    def _():
        products(other_ref)

    rows = jnp.concatenate([tail[...], x_in[...]], axis=0)
    tail[...] = rows[GROUP:]
    xc_ref[...] = conv_rows(rows, conv_ref)


def gate_first_kernel(chunks, count, place_ref, own_ref, other_ref, before_ref, *refs):
    weights, (out_ref, wide) = refs[:-2], refs[-2:]
    block = pl.program_id(0)
    is_own = block // 2 == place_ref[0]

    @pl.when(block == 0)
    def _():
        unpack_wide(chunks, weights, wide)

    def product(ref):
        columns = block_columns(ref, place_ref, 0, count)
        out_ref[...] = jnp.dot(columns, wide[...], preferred_element_type=F32)

    @pl.when(is_own)
    def _():
        product(own_ref)

    @pl.when(jnp.logical_not(is_own))
    def _():
        product(other_ref)


def states_kernel(
    core_ref, xc_ref, bc_mine_ref, bc_other_ref, raw_ref, conv_ref, bias_ref, rate_ref,
    bcc_ref, cum_ref, cum_slab_ref, cum_t_ref, step_t_ref, entering_ref, final_ref,
    state, total,
):
    block = pl.program_id(0)
    width, heads = xc_ref.shape[1], cum_t_ref.shape[0]
    start = pl.multiple_of(block * GROUP, GROUP)

    @pl.when(block == 0)
    def _():
        state[...] = jnp.zeros_like(state)
        total[...] = jnp.zeros_like(total)

    mine = bc_mine_ref[pl.ds(start, GROUP + HALO), :].astype(F32)
    other = bc_other_ref[pl.ds(start, GROUP + HALO), :].astype(F32)
    first = core_ref[0] == 0
    b_rows = conv_rows(jnp.where(first, mine, other), conv_ref.at[:, :LANES])
    c_rows = conv_rows(jnp.where(first, other, mine), conv_ref.at[:, LANES:])
    bcc_ref[:, :LANES] = b_rows
    bcc_ref[:, LANES:] = c_rows
    raw = jnp.concatenate([raw_ref[...], jnp.zeros((GROUP, LANES - heads), F32)], axis=1)
    raw = raw + bias_ref[...]
    step_size = jnp.maximum(raw, 0.0) + jnp.log1p(jnp.exp(-jnp.abs(raw)))
    log_decay = -rate_ref[...] * step_size
    row = lax.broadcasted_iota(jnp.int32, (GROUP, GROUP), 0)
    col = lax.broadcasted_iota(jnp.int32, (GROUP, GROUP), 1)
    lower = (row >= col).astype(F32)
    cum = jnp.dot(lower, log_decay, preferred_element_type=F32, precision=lax.Precision.HIGHEST)
    last = cum[GROUP - 1 : GROUP, :]
    cum_ref[...] = cum
    cum_slab_ref[...] = cum + total[0:1, :]
    cum_t_ref[...] = cum.T[:heads, :]
    step_t_ref[...] = step_size.T[:heads, :]
    entering_ref[0] = state[...].astype(BF16)
    weights_in = expand_heads(jnp.exp(last - cum) * step_size, width)
    weighted = (weights_in * xc_ref[...].astype(F32)).astype(BF16)
    contrib = lax.dot_general(
        b_rows, weighted, (((0,), (0,)), ((), ())), preferred_element_type=F32
    )
    decay = expand_heads(jnp.broadcast_to(jnp.exp(last), (8, LANES)), width)
    state[...] = state[...] * decay[0:1] + contrib
    total[...] = total[...] + jnp.broadcast_to(last, total.shape)

    @pl.when(block == pl.num_programs(0) - 1)
    def _():
        final_ref[:LANES, :] = state[...].astype(BF16)
        final_ref[LANES:, :] = split_decay(expand_heads(jnp.exp(total[...]), width)[0:1])


def split_decay(decay):
    high = decay.astype(BF16)
    low = decay - high.astype(F32)
    row = lax.broadcasted_iota(jnp.int32, (HALO, decay.shape[1]), 0)
    return jnp.where(row == 0, high.astype(F32), jnp.where(row == 1, low, 0.0)).astype(BF16)


def unpacked(sent):
    sent = sent.astype(F32)
    return sent[:LANES], sent[LANES : LANES + 1] + sent[LANES + 1 : LANES + 2]


def row_kernel(place_ref, *refs):
    size = len(refs) - 3
    parts, (total_ref, before_ref, before_decay_ref) = refs[:size], refs[size:]
    place = place_ref[0]
    width = total_ref.shape[1]
    total, decay = jnp.zeros((LANES, width), F32), jnp.ones((1, width), F32)
    before_ref[...] = total
    before_decay_ref[...] = jnp.broadcast_to(decay, before_decay_ref.shape)
    for index in range(size):
        if index > 0:

            @pl.when(place == index)
            def _():
                before_ref[...] = total
                before_decay_ref[...] = jnp.broadcast_to(decay, before_decay_ref.shape)

        distance = (place - index + size) % size
        chosen = parts[0][...]
        for other in range(1, size):
            chosen = jnp.where(distance == other, parts[other][...], chosen)
        state, state_decay = unpacked(chosen)
        total = total * state_decay + state
        decay = decay * state_decay
    total_ref[:LANES, :] = total.astype(BF16)
    total_ref[LANES:, :] = split_decay(decay)


def outputs_kernel(xc_ref, bcc_ref, cum_ref, cum_t_ref, step_t_ref, entering_ref, skip_ref, out_ref):
    width = xc_ref.shape[1]
    b_rows, c_rows = bcc_ref[:, :LANES], bcc_ref[:, LANES:]
    scores = lax.dot_general(c_rows, b_rows, (((1,), (1,)), ((), ())), preferred_element_type=F32)
    row = lax.broadcasted_iota(jnp.int32, (GROUP, GROUP), 0)
    col = lax.broadcasted_iota(jnp.int32, (GROUP, GROUP), 1)
    scores = jnp.where(row >= col, scores, 0.0)
    cum = cum_ref[...]
    grown = expand_heads(jnp.exp(cum), width)
    out_ref[...] = grown * jnp.dot(c_rows, entering_ref[0], preferred_element_type=F32)
    lane = lax.broadcasted_iota(jnp.int32, (GROUP, LANES), 1)

    def mixing(head):
        gaps = cum[:, head : head + 1] - cum_t_ref[head : head + 1, :]
        return (
            scores * jnp.exp(jnp.minimum(gaps, 0.0)) * step_t_ref[head : head + 1, :]
        ).astype(BF16)

    for pair in range(width // LANES):
        lanes = slice(pair * LANES, (pair + 1) * LANES)
        inputs = xc_ref[:, lanes]
        zero = jnp.zeros_like(inputs)
        both = jnp.concatenate([mixing(2 * pair), mixing(2 * pair + 1)], axis=1)
        stacked = jnp.concatenate(
            [jnp.where(lane < HEAD, inputs, zero), jnp.where(lane < HEAD, zero, inputs)], axis=0
        )
        out_ref[:, lanes] = (
            out_ref[:, lanes]
            + jnp.dot(both, stacked, preferred_element_type=F32)
            + skip_ref[:, lanes] * inputs.astype(F32)
        )


def gate_kernel(chunks, done, count, place_ref, own_ref, other_ref, before_rows_ref, *refs):
    weights, refs = refs[: len(chunks) // 2], refs[len(chunks) // 2 :]
    sum_ref, local_ref, bcc_ref, cum_ref, before_ref, before_decay_ref = refs[:6]
    earlier, (gated_ref, squares_ref, wide, incoming, gate) = refs[6:-5], refs[-5:]
    width = local_ref.shape[1]
    is_own = pl.program_id(0) // 2 == place_ref[0]

    @pl.when(pl.program_id(0) == 0)
    def _():
        unpack_wide(chunks, weights, wide)
        carried = jnp.zeros((LANES, width), F32)
        for part in earlier:
            state, decay = unpacked(part[...])
            carried = carried * decay + state
        incoming[...] = (carried * before_decay_ref[0:1, :] + before_ref[...]).astype(BF16)

    def product(ref):
        columns = block_columns(ref, place_ref, done, count)
        product = jnp.dot(columns, wide[...], preferred_element_type=F32)
        gate[...] = (sum_ref[...] + product).astype(BF16)

    @pl.when(is_own)
    def _():
        product(own_ref)

    @pl.when(jnp.logical_not(is_own))
    def _():
        product(other_ref)

    grown = expand_heads(jnp.exp(cum_ref[...]), width)
    carried = jnp.dot(bcc_ref[:, LANES:], incoming[...], preferred_element_type=F32)
    gated = (local_ref[...] + grown * carried) * silu(gate[...].astype(F32))
    gated_ref[...] = gated.astype(BF16)
    squares = gated * gated
    high = squares.astype(BF16)
    low = (squares - high.astype(F32)).astype(BF16)
    ones = jnp.ones((8, width), BF16)
    across = (((1,), (1,)), ((), ()))
    summed = lax.dot_general(ones, high, across, preferred_element_type=F32) + lax.dot_general(
        ones, low, across, preferred_element_type=F32
    )
    squares_ref[...] = summed[0:1, :]


def norm_kernel(core_ref, mine_ref, other_ref, squares_ref, gain_ref, out_ref):
    half = pl.program_id(0)
    across = jnp.broadcast_to(squares_ref[...], (8, squares_ref.shape[1]))
    scale = lax.rsqrt(across + 1e-05).T[:, 0:1]

    @pl.when(half == core_ref[0])
    def _():
        out_ref[...] = (mine_ref[...].astype(F32) * scale * gain_ref[...]).astype(BF16)

    @pl.when(half != core_ref[0])
    def _():
        out_ref[...] = (other_ref[...].astype(F32) * scale * gain_ref[...]).astype(BF16)


def whole(shape):
    return pl.BlockSpec(shape, lambda i: (0,) * len(shape))


def rows_of(width):
    return pl.BlockSpec((GROUP, width), lambda i: (i, 0))


def params(flops, megabytes):
    return dict(
        compiler_params=pltpu.CompilerParams(vmem_limit_bytes=VMEM),
        cost_estimate=pl.CostEstimate(
            flops=int(flops), bytes_accessed=megabytes * 2**20, transcendentals=0
        ),
    )


def fixed(a):
    return pl.BlockSpec(a.shape, lambda i, place: (0,) * len(a.shape))


def row_block(width):
    return pl.BlockSpec((GROUP, width), lambda i, place: (i, 0))


def slab_blocks(depth):
    own = pl.BlockSpec((GROUP, depth), lambda i, place: (jnp.clip(i - 2 * place[0], 0, 1), 0))
    other = pl.BlockSpec((GROUP, depth), lambda i, place: (jnp.clip(i - 2 + 2 * place[0], 0, 1), 0))
    return [own, other]


def packed_weights(core, x_weight, bc_weight, dt_turned):
    out = jax.ShapeDtypeStruct(
        (x_weight.shape[1] // 2 + bc_weight.shape[0] + dt_turned.shape[0] // 2, LANES), BF16
    )
    return pl.pallas_call(
        pack_kernel,
        grid_spec=pltpu.PrefetchScalarGridSpec(
            num_scalar_prefetch=1,
            grid=(1,),
            in_specs=[fixed(a) for a in (x_weight, bc_weight, dt_turned)],
            out_specs=[fixed(out), fixed(out)],
        ),
        out_shape=[out, out],
        name="packed_weights",
        **params(1e6, 1),
    )(core, x_weight, bc_weight, dt_turned)


def by_blocks(kernel, name, cost, place, slabs, weights, extras, extra_specs, outs, out_specs, scratch):
    own, other, before = slabs
    return pl.pallas_call(
        kernel,
        grid_spec=pltpu.PrefetchScalarGridSpec(
            num_scalar_prefetch=1,
            grid=(2 * own.shape[0] // GROUP,),
            in_specs=slab_blocks(own.shape[1]) + [fixed(a) for a in (before, *weights)] + extra_specs,
            out_specs=out_specs,
            scratch_shapes=scratch,
        ),
        out_shape=outs,
        name=name,
        **cost,
    )(place, *slabs, *weights, *extras)


def first_products(place, slabs, weights, chunks, width, heads):
    shape, rows = jax.ShapeDtypeStruct, 2 * slabs[0].shape[0]
    outs = [
        shape((rows, width), F32), shape((HALO, width), F32),
        shape((rows, LANES), F32), shape((HALO, LANES), F32), shape((rows, heads), F32),
    ]
    specs = [row_block(width), fixed(outs[1]), row_block(LANES), fixed(outs[3]), row_block(heads)]
    depth = len(chunks) * LANES
    scratch = [
        pltpu.VMEM((depth, width), BF16), pltpu.VMEM((depth, LANES), BF16), pltpu.VMEM((heads, depth), BF16),
    ]
    kernel = functools.partial(first_kernel, chunks, len(chunks) // 2)
    return by_blocks(
        kernel, "first_products", params(9e9, 20), place, slabs, weights, [], [], outs, specs, scratch
    )


def head_inputs(place, slabs, weights, chunks, done, sums, conv_x):
    shape = jax.ShapeDtypeStruct
    (rows, width), heads, depth = sums[0].shape, sums[4].shape[1], len(chunks) * LANES
    sum_specs = [row_block(width), fixed(sums[1]), row_block(LANES), fixed(sums[3]), row_block(heads)]
    outs = [shape((rows, width), BF16), shape((HALO + rows, LANES), BF16), shape((rows, heads), F32)]
    return by_blocks(
        functools.partial(inputs_kernel, chunks, done, len(chunks) // 2),
        "head_inputs", params(6e9, 18), place, slabs, weights,
        [*sums, conv_x], sum_specs + [fixed(conv_x)],
        outs, [row_block(width), fixed(outs[1]), row_block(heads)],
        [
            pltpu.VMEM((depth, width), BF16), pltpu.VMEM((depth, LANES), BF16),
            pltpu.VMEM((heads, depth), BF16), pltpu.VMEM((GROUP, width), F32),
            pltpu.VMEM((HALO, width), F32),
        ],
    )


def gate_first(place, slabs, weights, chunks):
    rows, width = 2 * slabs[0].shape[0], weights[0].shape[1]
    return by_blocks(
        functools.partial(gate_first_kernel, chunks, len(chunks) // 2),
        "gate_first", params(7e9, 18), place, slabs, weights, [], [],
        jax.ShapeDtypeStruct((rows, width), F32), row_block(width),
        [pltpu.VMEM((len(chunks) * LANES, width), BF16)],
    )


def local_states(core, xc, bc_mine, bc_other, raw, conv_bc, bias, rate):
    rows, width = xc.shape
    heads, blocks = raw.shape[1], rows // GROUP
    shape = jax.ShapeDtypeStruct
    by_lane = pl.BlockSpec((heads, GROUP), lambda i, core: (0, i))
    outs = [
        shape((rows, 2 * LANES), BF16), shape((rows, LANES), F32), shape((rows, LANES), F32),
        shape((heads, rows), F32), shape((heads, rows), F32),
        shape((blocks, LANES, width), BF16), shape((LANES + HALO, width), BF16),
    ]
    return pl.pallas_call(
        states_kernel,
        grid_spec=pltpu.PrefetchScalarGridSpec(
            num_scalar_prefetch=1,
            grid=(blocks,),
            in_specs=[row_block(width), fixed(bc_mine), fixed(bc_other), row_block(heads)]
            + [fixed(a) for a in (conv_bc, bias, rate)],
            out_specs=[
                row_block(2 * LANES), row_block(LANES), row_block(LANES), by_lane, by_lane,
                pl.BlockSpec((1, LANES, width), lambda i, core: (i, 0, 0)), fixed(outs[6]),
            ],
            scratch_shapes=[pltpu.VMEM((LANES, width), F32), pltpu.VMEM((8, LANES), F32)],
        ),
        out_shape=outs,
        name="states",
        **params(5e9, 8),
    )(core, xc, bc_mine, bc_other, raw, conv_bc, bias, rate)


def local_outputs(xc, bcc, cum, cum_t, step_t, entering, skip):
    rows, width = xc.shape
    heads = cum_t.shape[0]
    by_lane = pl.BlockSpec((heads, GROUP), lambda i: (0, i))
    return pl.pallas_call(
        outputs_kernel,
        grid=(rows // GROUP,),
        in_specs=[
            rows_of(width), rows_of(2 * LANES), rows_of(LANES), by_lane, by_lane,
            pl.BlockSpec((1, LANES, width), lambda i: (i, 0, 0)), whole((1, width)),
        ],
        out_specs=rows_of(width),
        out_shape=jax.ShapeDtypeStruct((rows, width), F32),
        compiler_params=pltpu.CompilerParams(vmem_limit_bytes=VMEM),
        cost_estimate=pl.CostEstimate(flops=10**10, bytes_accessed=10 * 2**20, transcendentals=4 * 2**20),
        name="outputs",
    )(xc, bcc, cum, cum_t, step_t, entering, skip)


def gate_outputs(place, slabs, weights, chunks, done, gate_sum, local, bcc, cum_slab, before, before_decay, earlier):
    rows, width = local.shape
    whole_ones = [before, before_decay, *earlier]
    return by_blocks(
        functools.partial(gate_kernel, chunks, done, len(chunks) // 2),
        "gate", params(4e9, 18), place, slabs, weights,
        [gate_sum, local, bcc, cum_slab, *whole_ones],
        [row_block(width), row_block(width), row_block(2 * LANES), row_block(LANES)]
        + [fixed(a) for a in whole_ones],
        [jax.ShapeDtypeStruct((rows, width), BF16), jax.ShapeDtypeStruct((1, rows), F32)],
        [row_block(width), pl.BlockSpec((1, GROUP), lambda i, place: (0, i))],
        [
            pltpu.VMEM((len(chunks) * LANES, width), BF16), pltpu.VMEM((LANES, width), BF16),
            pltpu.VMEM((GROUP, width), BF16),
        ],
    )


def normalized(core, gated, other, mean_squares, gain):
    rows, width = other.shape
    return pl.pallas_call(
        norm_kernel,
        grid_spec=pltpu.PrefetchScalarGridSpec(
            num_scalar_prefetch=1,
            grid=(2,),
            in_specs=[
                pl.BlockSpec((rows, width), lambda j, core: (core[0], 0)),
                pl.BlockSpec((rows, width), lambda j, core: (0, 0)),
                pl.BlockSpec((1, rows), lambda j, core: (0, 0)),
                pl.BlockSpec((1, width), lambda j, core: (0, j)),
            ],
            out_specs=pl.BlockSpec((rows, width), lambda j, core: (0, j)),
        ),
        out_shape=jax.ShapeDtypeStruct((rows, 2 * width), BF16),
        compiler_params=pltpu.CompilerParams(vmem_limit_bytes=VMEM),
        cost_estimate=pl.CostEstimate(flops=10**7, bytes_accessed=4 * 2**20, transcendentals=0),
        name="normalized",
    )(core.astype(jnp.int32)[None], gated, other, mean_squares, gain)


def earlier_states(final):
    size = lax.axis_size("y")
    parts = [final] + [round_ring(final, "y", distance) for distance in range(1, size)]
    width = final.shape[1]
    outs = [
        jax.ShapeDtypeStruct(final.shape, BF16),
        jax.ShapeDtypeStruct((LANES, width), F32),
        jax.ShapeDtypeStruct((8, width), F32),
    ]
    total, before, before_decay = pl.pallas_call(
        row_kernel,
        grid_spec=pltpu.PrefetchScalarGridSpec(
            num_scalar_prefetch=1,
            grid=(1,),
            in_specs=[fixed(a) for a in parts],
            out_specs=[fixed(a) for a in outs],
        ),
        out_shape=outs,
        name="row_states",
        **params(1e7, 2),
    )(lax.axis_index("y").astype(jnp.int32)[None], *parts)
    rows = lax.axis_size("z")
    earlier = [
        lax.ppermute(total, "z", [(i, i + distance) for i in range(rows - distance)])
        for distance in range(rows - 1, 0, -1)
    ]
    return before, before_decay, earlier


def travelling(own, way, after_first, after_far, before_last):
    y_less, y_more = round_ring(own, "y", 1), round_ring(own, "y", -1)
    z_less, z_more = round_ring(own, "z", 1), round_ring(own, "z", -1)
    y_less, y_more, z_less, z_more = after_first(y_less, y_more, z_less, z_more)
    if way > 0:
        y_far, z_far = round_ring(y_less, "y", 1), round_ring(z_more, "z", -1)
    else:
        y_far, z_far = round_ring(y_more, "y", -1), round_ring(z_less, "z", 1)
    diagonal = [
        round_ring(z_less, "y", 1), round_ring(z_more, "y", -1),
        round_ring(y_more, "z", 1), round_ring(y_less, "z", -1),
    ]
    y_far, z_far = after_far(y_far, z_far)
    near = [own, y_less, y_more, z_less, z_more, *diagonal, y_far, z_far]
    far = [
        round_ring(z_far, "y", 1), round_ring(z_far, "y", -1),
        round_ring(y_far, "z", 1), round_ring(y_far, "z", -1),
    ]
    last = before_last(near, far[1] if way > 0 else far[0])
    far.append(round_ring(last, "y", -1 if way > 0 else 1))
    return near, far


def chunks_of(blocks):
    half = blocks[0].shape[0] // 2
    return [(i, base) for i in range(len(blocks)) for base in (0, half)]


def block_order():
    places = (
        ((0, 0), (-1, 0), (1, 0), (0, -1), (0, 1), (-1, -1), (1, 1), (1, -1), (-1, 1), (2, 0), (0, 2))
        + ((-1, 2), (1, 2), (2, -1), (2, 1), (2, 2))
    )
    y, z = lax.axis_index("y"), lax.axis_index("z")
    return [(z + dz) % 4 * 4 + (y + dy) % 4 for dy, dz in places]


def tied(values, *to):
    return lax.optimization_barrier((*values, *to))[: len(values)]


def shards(
    tokens, x_weight, z_weight, bc_weight, dt_weight, conv_x, conv_bc, dt_bias, decay_rate, skip,
    norm_gain,
):
    core = lax.axis_index("core")
    width = x_weight.shape[1] // 2
    heads = dt_weight.shape[1] // 2

    def mine(a, axis):
        size = a.shape[axis] // 2
        return lax.dynamic_slice_in_dim(a, core * size, size, axis)

    def others(a, axis):
        size = a.shape[axis] // 2
        return lax.dynamic_slice_in_dim(a, (1 - core) * size, size, axis)

    def per_lane(a):
        return jnp.pad(mine(a, 0), (0, LANES - heads))[None, :]

    place = jnp.stack([core, *block_order()]).astype(jnp.int32)
    this_core = place[:1]
    packed, send = packed_weights(this_core, x_weight, bc_weight, dt_weight.T)
    own_block = jnp.concatenate([packed, swap_cores(send)], axis=0)
    chips = lax.axis_size("z") * lax.axis_size("y")
    to_next = lambda target: lax.ppermute(
        tokens[-HALO:], ("z", "y", "core"),
        [(2 * i + 1, 2 * i + 2 + target) for i in range(chips - 1)],
    )
    before_rows = to_next(0) + to_next(1)
    tokens, z_weight = tied((tokens, z_weight), own_block)
    slabs = (tokens, swap_cores(tokens), before_rows)
    z_own = jnp.concatenate([mine(z_weight, 1), swap_cores(others(z_weight, 1))], axis=0)

    first = []

    def run_first(near, last):
        first.extend(first_products(place, slabs, near, chunks_of(near), width, heads))
        return tied((last,), first[0])[0]

    x_far = []

    def note_far(*far):
        x_far.extend(far)
        return tied(far, slabs[1], z_own)

    near, far = travelling(own_block, 1, lambda *got: tied(got, before_rows), note_far, run_first)
    xc, bc_mine, raw = head_inputs(place, slabs, far, chunks_of(far), 11, first, mine(conv_x, 1))
    bc_other = swap_cores(bc_mine)
    bcc, cum, cum_slab, cum_t, step_t, entering, final = local_states(
        this_core, xc, bc_mine, bc_other, raw, conv_bc, per_lane(dt_bias), per_lane(decay_rate)
    )
    (z_own,) = tied((z_own,), *x_far)
    same = lambda *got: got
    z_near, z_far = travelling(z_own, -1, same, same, lambda near, last: last)
    before, before_decay, earlier = earlier_states(final)
    skip_lanes = jnp.repeat(mine(skip, 0), HEAD)[None, :]
    local = local_outputs(xc, bcc, cum, cum_t, step_t, entering, skip_lanes)
    gate_sum = gate_first(place, slabs, tied(z_near, final), chunks_of(z_near))
    gated, squares = gate_outputs(
        place, slabs, z_far, chunks_of(z_far), 11,
        gate_sum, local, bcc, cum_slab, before, before_decay, earlier,
    )

    other = swap_cores(others(gated, 0))
    summed = mine(squares + swap_cores(squares), 1)
    across = [round_ring(summed, "x", distance) for distance in range(1, lax.axis_size("x"))]
    mean_squares = (summed + sum(across)) / (2 * width * lax.axis_size("x"))
    return normalized(core, gated, other, mean_squares, norm_gain[None, :])


def solution(mesh):
    fine = Mesh(mesh.devices.reshape(4, 4, 2, 4), ("z", "y", "core", "x"))
    ctx = ("z", "y", "core")
    placed = (
        P(ctx, None),
        P(ctx, "x"),
        P(ctx, "x"),
        P(ctx, None),
        P(ctx, "x"),
        P(None, "x"),
        P(),
        P("x"),
        P("x"),
        P("x"),
        P("x"),
    )
    return jax.shard_map(
        shards, mesh=fine, in_specs=placed, out_specs=P(ctx, "x"), check_vma=False
    )
```

```python
import functools

import jax
import jax.numpy as jnp
from jax import lax
from jax.experimental import pallas as pl
from jax.experimental.pallas import tpu as pltpu
from jax.sharding import Mesh, PartitionSpec as P

GROUP = 256
HALO = 16
LANES = 128
HEAD = 64
F32 = jnp.float32
BF16 = jnp.bfloat16


def swap_cores(a):
    return lax.ppermute(a, "core", [(0, 1), (1, 0)])


def round_ring(a, axis, distance):
    size = lax.axis_size(axis)
    return lax.ppermute(a, axis, [(i, (i + distance) % size) for i in range(size)])


def along_chips(a, distance):
    chips = lax.axis_size("z") * lax.axis_size("y")
    return lax.ppermute(a, ("z", "y"), [(i, i + distance) for i in range(chips - distance)])


def in_core_order(core, mine, other, axis):
    first = jnp.where(core == 0, mine, other)
    second = jnp.where(core == 0, other, mine)
    return jnp.concatenate([first, second], axis=axis)


def expand_heads(values, width):
    high = values.astype(BF16)
    rest = values - high.astype(F32)
    middle = rest.astype(BF16)
    low = (rest - middle.astype(F32)).astype(BF16)
    row = lax.broadcasted_iota(jnp.int32, (LANES, width), 0)
    col = lax.broadcasted_iota(jnp.int32, (LANES, width), 1)
    spread = ((col >= row * HEAD) & (col < row * HEAD + HEAD)).astype(BF16)
    dot = lambda part: jnp.dot(part, spread, preferred_element_type=F32)
    return dot(high) + dot(middle) + dot(low)


def silu(a):
    half = 0.5 * a
    return half + half * jnp.tanh(half)


def conv_rows(rows, kernel_ref):
    taps, count = kernel_ref.shape[0], rows.shape[0] - HALO
    first = HALO - (taps - 1)
    accum = kernel_ref[0:1, :] * rows[first : first + count]
    for tap in range(1, taps):
        accum = accum + kernel_ref[tap : tap + 1, :] * rows[first + tap : first + tap + count]
    return silu(accum).astype(BF16)


def prepare_kernel(
    place_ref, own_ref, other_ref, before_ref, weight_ref, conv_ref, bias_ref, rate_ref,
    bcc_ref, cum_ref, cum_slab_ref, cum_t_ref, step_t_ref, weights_in_ref, decays_ref,
    accum,
):
    step = pl.program_id(0)
    core = place_ref[0]
    slab = own_ref.shape[0]
    heads = cum_t_ref.shape[0]
    rows_own = pl.ds(pl.multiple_of(HALO + slab * core, HALO), slab)
    rows_other = pl.ds(pl.multiple_of(HALO + slab * (1 - core), HALO), slab)

    @pl.when(step == 0)
    def _():
        accum[...] = jnp.zeros_like(accum)

    weight = weight_ref[...]
    for rows, ref in ((slice(0, HALO), before_ref), (rows_own, own_ref), (rows_other, other_ref)):
        accum[rows, :] = accum[rows, :] + jnp.dot(ref[...], weight, preferred_element_type=F32)

    @pl.when(step == pl.num_programs(0) - 1)
    def _():
        total = jnp.zeros((1, LANES), F32)
        row = lax.broadcasted_iota(jnp.int32, (GROUP, GROUP), 0)
        col = lax.broadcasted_iota(jnp.int32, (GROUP, GROUP), 1)
        lower = (row >= col).astype(F32)
        for block in range(2 * slab // GROUP):
            part = slice(block * GROUP, (block + 1) * GROUP)
            narrow = accum[block * GROUP : (block + 1) * GROUP + HALO, : 2 * LANES]
            bcc_ref[part, :] = conv_rows(narrow.astype(BF16).astype(F32), conv_ref)
            raw = accum[block * GROUP + HALO : (block + 1) * GROUP + HALO, 2 * LANES :]
            raw = jnp.where(core == 0, raw, pltpu.roll(raw, LANES - heads, axis=1))
            raw = raw + bias_ref[...]
            step_size = jnp.maximum(raw, 0.0) + jnp.log1p(jnp.exp(-jnp.abs(raw)))
            log_decay = -rate_ref[...] * step_size
            cum = jnp.dot(
                lower, log_decay, preferred_element_type=F32, precision=lax.Precision.HIGHEST
            )
            last = cum[GROUP - 1 : GROUP, :]
            cum_ref[part, :] = cum
            cum_slab_ref[part, :] = cum + total
            cum_t_ref[:, part] = cum.T[:heads, :]
            step_t_ref[:, part] = step_size.T[:heads, :]
            weights_in_ref[part, :] = jnp.exp(last - cum) * step_size
            decays_ref[block * 8 : block * 8 + 8, :] = jnp.broadcast_to(jnp.exp(last), (8, LANES))
            total = total + last
        end = decays_ref.shape[0] - 8
        decays_ref[end:, :] = jnp.broadcast_to(jnp.exp(total), (8, LANES))


def block_columns(ref, place_ref, first, count):
    core = place_ref[0]
    parts = []
    for index in range(first, first + count):
        base = place_ref[1 + index] * (2 * LANES)
        for start in (base + LANES * core, base + LANES * (1 - core)):
            parts.append(ref[:, pl.ds(pl.multiple_of(start, LANES), LANES)])
    return jnp.concatenate(parts, axis=1)


def stacked(sources, refs):
    return jnp.concatenate([refs[ref][first : first + size, :] for ref, first, size in sources], axis=0)


def first_kernel(sources, count, place_ref, own_ref, other_ref, before_ref, *refs):
    weights, (out_ref, out_before_ref) = refs[:-2], refs[-2:]
    block = pl.program_id(0)
    is_own = block // 2 == place_ref[0]

    def product(ref):
        columns = block_columns(ref, place_ref, 0, count)
        return jnp.dot(columns, stacked(sources, weights), preferred_element_type=F32)

    @pl.when(block == 0)
    def _():
        out_before_ref[...] = product(before_ref)

    @pl.when(is_own)
    def _():
        out_ref[...] = product(own_ref)

    @pl.when(jnp.logical_not(is_own))
    def _():
        out_ref[...] = product(other_ref)


def states_kernel(
    sources, done, count, place_ref, own_ref, other_ref, before_ref, *refs
):
    weights = refs[:-12]
    (
        sum_ref, sum_before_ref, bcc_ref, weights_in_ref, decays_ref, conv_ref,
        xc_ref, entering_ref, final_ref,
        state, x_in, tail,
    ) = refs[-12:]
    block = pl.program_id(0)
    width = x_in.shape[1]
    is_own = block // 2 == place_ref[0]

    def product(ref):
        columns = block_columns(ref, place_ref, done, count)
        return jnp.dot(columns, stacked(sources, weights), preferred_element_type=F32)

    @pl.when(block == 0)
    def _():
        state[...] = jnp.zeros_like(state)
        tail[...] = (sum_before_ref[...] + product(before_ref)).astype(BF16).astype(F32)

    @pl.when(is_own)
    def _():
        x_in[...] = (sum_ref[...] + product(own_ref)).astype(BF16).astype(F32)

    @pl.when(jnp.logical_not(is_own))
    def _():
        x_in[...] = (sum_ref[...] + product(other_ref)).astype(BF16).astype(F32)

    rows = jnp.concatenate([tail[...], x_in[...]], axis=0)
    tail[...] = rows[GROUP:]
    xc = conv_rows(rows, conv_ref)
    xc_ref[...] = xc
    entering_ref[0] = state[...].astype(BF16)
    weighted = (expand_heads(weights_in_ref[...], width) * xc.astype(F32)).astype(BF16)
    contrib = lax.dot_general(
        bcc_ref[:, :LANES], weighted, (((0,), (0,)), ((), ())), preferred_element_type=F32
    )
    decay = expand_heads(decays_ref[pl.ds(pl.multiple_of(block * 8, 8), 8), :], width)
    state[...] = state[...] * decay[0:1] + contrib

    @pl.when(block == pl.num_programs(0) - 1)
    def _():
        end = decays_ref.shape[0] - 8
        final_ref[:LANES, :] = state[...].astype(BF16)
        final_ref[LANES:, :] = split_decay(expand_heads(decays_ref[end:, :], width)[0:1])


def split_decay(decay):
    high = decay.astype(BF16)
    low = decay - high.astype(F32)
    row = lax.broadcasted_iota(jnp.int32, (HALO, decay.shape[1]), 0)
    return jnp.where(row == 0, high.astype(F32), jnp.where(row == 1, low, 0.0)).astype(BF16)


def unpacked(sent):
    sent = sent.astype(F32)
    return sent[:LANES], sent[LANES : LANES + 1] + sent[LANES + 1 : LANES + 2]


def row_kernel(place_ref, *refs):
    size = len(refs) - 3
    parts, (total_ref, before_ref, before_decay_ref) = refs[:size], refs[size:]
    place = place_ref[0]
    width = total_ref.shape[1]
    total, decay = jnp.zeros((LANES, width), F32), jnp.ones((1, width), F32)
    before_ref[...] = total
    before_decay_ref[...] = jnp.broadcast_to(decay, before_decay_ref.shape)
    for index in range(size):
        if index > 0:

            @pl.when(place == index)
            def _():
                before_ref[...] = total
                before_decay_ref[...] = jnp.broadcast_to(decay, before_decay_ref.shape)

        distance = (place - index + size) % size
        chosen = parts[0][...]
        for other in range(1, size):
            chosen = jnp.where(distance == other, parts[other][...], chosen)
        state, state_decay = unpacked(chosen)
        total = total * state_decay + state
        decay = decay * state_decay
    total_ref[:LANES, :] = total.astype(BF16)
    total_ref[LANES:, :] = split_decay(decay)


def outputs_kernel(xc_ref, bcc_ref, cum_ref, cum_t_ref, step_t_ref, entering_ref, skip_ref, out_ref):
    width = xc_ref.shape[1]
    b_rows, c_rows = bcc_ref[:, :LANES], bcc_ref[:, LANES:]
    scores = lax.dot_general(c_rows, b_rows, (((1,), (1,)), ((), ())), preferred_element_type=F32)
    row = lax.broadcasted_iota(jnp.int32, (GROUP, GROUP), 0)
    col = lax.broadcasted_iota(jnp.int32, (GROUP, GROUP), 1)
    scores = jnp.where(row >= col, scores, 0.0)
    cum = cum_ref[...]
    grown = expand_heads(jnp.exp(cum), width)
    out_ref[...] = grown * jnp.dot(c_rows, entering_ref[0], preferred_element_type=F32)
    lane = lax.broadcasted_iota(jnp.int32, (GROUP, LANES), 1)

    def mixing(head):
        gaps = cum[:, head : head + 1] - cum_t_ref[head : head + 1, :]
        return (
            scores * jnp.exp(jnp.minimum(gaps, 0.0)) * step_t_ref[head : head + 1, :]
        ).astype(BF16)

    for pair in range(width // LANES):
        lanes = slice(pair * LANES, (pair + 1) * LANES)
        inputs = xc_ref[:, lanes]
        zero = jnp.zeros_like(inputs)
        both = jnp.concatenate([mixing(2 * pair), mixing(2 * pair + 1)], axis=1)
        stacked = jnp.concatenate(
            [jnp.where(lane < HEAD, inputs, zero), jnp.where(lane < HEAD, zero, inputs)], axis=0
        )
        out_ref[:, lanes] = (
            out_ref[:, lanes]
            + jnp.dot(both, stacked, preferred_element_type=F32)
            + skip_ref[:, lanes] * inputs.astype(F32)
        )


def z_kernel(place_ref, own_ref, other_ref, weight_ref, gate_ref, accum):
    step = pl.program_id(0)
    slab = own_ref.shape[0]
    core = place_ref[0]

    def product(ref):
        return jnp.dot(ref[...], weight_ref[...], preferred_element_type=F32)

    for index, ref in enumerate((own_ref, other_ref)):
        rows = slice(index * slab, (index + 1) * slab)
        target = pl.ds(pl.multiple_of(slab * (core if index == 0 else 1 - core), slab), slab)

        @pl.when(step == 0)
        def _():
            accum[rows, :] = product(ref)

        @pl.when((step > 0) & (step < pl.num_programs(0) - 1))
        def _():
            accum[rows, :] = accum[rows, :] + product(ref)

        @pl.when(step == pl.num_programs(0) - 1)
        def _():
            gate_ref[target, :] = (accum[rows, :] + product(ref)).astype(BF16)


def gate_kernel(
    gate_ref, local_ref, bcc_ref, cum_ref, before_ref, before_decay_ref, *refs
):
    earlier, (gated_ref, squares_ref, incoming) = refs[:-3], refs[-3:]
    width = local_ref.shape[1]

    @pl.when(pl.program_id(0) == 0)
    def _():
        carried = jnp.zeros((LANES, width), F32)
        for part in earlier:
            state, decay = unpacked(part[...])
            carried = carried * decay + state
        incoming[...] = (carried * before_decay_ref[0:1, :] + before_ref[...]).astype(BF16)

    grown = expand_heads(jnp.exp(cum_ref[...]), width)
    carried = jnp.dot(bcc_ref[:, LANES:], incoming[...], preferred_element_type=F32)
    gated = (local_ref[...] + grown * carried) * silu(gate_ref[...].astype(F32))
    gated_ref[...] = gated.astype(BF16)
    squares = gated * gated
    high = squares.astype(BF16)
    low = (squares - high.astype(F32)).astype(BF16)
    ones = jnp.ones((8, width), BF16)
    across = (((1,), (1,)), ((), ()))
    summed = lax.dot_general(ones, high, across, preferred_element_type=F32) + lax.dot_general(
        ones, low, across, preferred_element_type=F32
    )
    squares_ref[...] = summed[0:1, :]


def norm_kernel(core_ref, mine_ref, other_ref, squares_ref, gain_ref, out_ref):
    half = pl.program_id(0)
    across = jnp.broadcast_to(squares_ref[...], (8, squares_ref.shape[1]))
    scale = lax.rsqrt(across + 1e-05).T[:, 0:1]

    @pl.when(half == core_ref[0])
    def _():
        out_ref[...] = (mine_ref[...].astype(F32) * scale * gain_ref[...]).astype(BF16)

    @pl.when(half != core_ref[0])
    def _():
        out_ref[...] = (other_ref[...].astype(F32) * scale * gain_ref[...]).astype(BF16)


def whole(shape):
    return pl.BlockSpec(shape, lambda i: (0,) * len(shape))


def rows_of(width):
    return pl.BlockSpec((GROUP, width), lambda i: (i, 0))


def params(flops, megabytes, vmem=48):
    return dict(
        compiler_params=pltpu.CompilerParams(vmem_limit_bytes=vmem * 2**20),
        cost_estimate=pl.CostEstimate(
            flops=int(flops), bytes_accessed=megabytes * 2**20, transcendentals=0
        ),
    )


def fixed(a):
    return pl.BlockSpec(a.shape, lambda i, place: (0,) * len(a.shape))


def row_block(width):
    return pl.BlockSpec((GROUP, width), lambda i, place: (i, 0))


def slab_blocks(depth):
    own = pl.BlockSpec((GROUP, depth), lambda i, place: (jnp.clip(i - 2 * place[0], 0, 1), 0))
    other = pl.BlockSpec((GROUP, depth), lambda i, place: (jnp.clip(i - 2 + 2 * place[0], 0, 1), 0))
    return [own, other]


def prepared(place, slabs, weight, conv_bc, bias, rate, heads):
    own, other, before = slabs
    slab, rows, depth = own.shape[0], 2 * own.shape[0], 512
    shape = jax.ShapeDtypeStruct
    outs = [
        shape((rows, 2 * LANES), BF16), shape((rows, LANES), F32), shape((rows, LANES), F32),
        shape((heads, rows), F32), shape((heads, rows), F32), shape((rows, LANES), F32),
        shape((rows // GROUP * 8 + 8, LANES), F32),
    ]
    columns = lambda a: pl.BlockSpec((a.shape[0], depth), lambda i, place: (0, i))
    return pl.pallas_call(
        prepare_kernel,
        grid_spec=pltpu.PrefetchScalarGridSpec(
            num_scalar_prefetch=1,
            grid=(own.shape[1] // depth,),
            in_specs=[columns(a) for a in slabs]
            + [pl.BlockSpec((depth, weight.shape[1]), lambda i, place: (i, 0))]
            + [fixed(a) for a in (conv_bc, bias, rate)],
            out_specs=[fixed(a) for a in outs],
            scratch_shapes=[pltpu.VMEM((HALO + rows, weight.shape[1]), F32)],
        ),
        out_shape=outs,
        name="prepared",
        **params(4e9, 14),
    )(place, *slabs, weight, conv_bc, bias, rate)


def first_products(place, slabs, weights, sources, count):
    own, other, before = slabs
    width = weights[0].shape[1]
    outs = [
        jax.ShapeDtypeStruct((2 * own.shape[0], width), F32), jax.ShapeDtypeStruct((HALO, width), F32),
    ]
    return pl.pallas_call(
        functools.partial(first_kernel, sources, count),
        grid_spec=pltpu.PrefetchScalarGridSpec(
            num_scalar_prefetch=1,
            grid=(2 * own.shape[0] // GROUP,),
            in_specs=slab_blocks(own.shape[1]) + [fixed(a) for a in (before, *weights)],
            out_specs=[row_block(width), fixed(outs[1])],
        ),
        out_shape=outs,
        name="first_products",
        **params(6e9, 18),
    )(place, *slabs, *weights)


def local_states(place, slabs, weights, sources, done, count, sums, bcc, weights_in, decays, conv_x):
    own, other, before = slabs
    rows, width = sums[0].shape
    blocks = rows // GROUP
    outs = [
        jax.ShapeDtypeStruct((rows, width), BF16),
        jax.ShapeDtypeStruct((blocks, LANES, width), BF16),
        jax.ShapeDtypeStruct((LANES + HALO, width), BF16),
    ]
    return pl.pallas_call(
        functools.partial(states_kernel, sources, done, count),
        grid_spec=pltpu.PrefetchScalarGridSpec(
            num_scalar_prefetch=1,
            grid=(blocks,),
            in_specs=slab_blocks(own.shape[1])
            + [fixed(a) for a in (before, *weights)]
            + [
                row_block(width), fixed(sums[1]), row_block(2 * LANES), row_block(LANES),
                fixed(decays), fixed(conv_x),
            ],
            out_specs=[
                row_block(width),
                pl.BlockSpec((1, LANES, width), lambda i, place: (i, 0, 0)),
                fixed(outs[2]),
            ],
            scratch_shapes=[
                pltpu.VMEM((LANES, width), F32), pltpu.VMEM((GROUP, width), F32),
                pltpu.VMEM((HALO, width), F32),
            ],
        ),
        out_shape=outs,
        name="states",
        **params(8e9, 16),
    )(place, *slabs, *weights, *sums, bcc, weights_in, decays, conv_x)


def local_outputs(xc, bcc, cum, cum_t, step_t, entering, skip):
    rows, width = xc.shape
    heads = cum_t.shape[0]
    by_lane = pl.BlockSpec((heads, GROUP), lambda i: (0, i))
    return pl.pallas_call(
        outputs_kernel,
        grid=(rows // GROUP,),
        in_specs=[
            rows_of(width), rows_of(2 * LANES), rows_of(LANES), by_lane, by_lane,
            pl.BlockSpec((1, LANES, width), lambda i: (i, 0, 0)), whole((1, width)),
        ],
        out_specs=rows_of(width),
        out_shape=jax.ShapeDtypeStruct((rows, width), F32),
        compiler_params=pltpu.CompilerParams(vmem_limit_bytes=40 * 2**20),
        cost_estimate=pl.CostEstimate(flops=10**10, bytes_accessed=10 * 2**20, transcendentals=4 * 2**20),
        name="outputs",
    )(xc, bcc, cum, cum_t, step_t, entering, skip)


def project_gate(place, slabs, weight):
    own, other, _ = slabs
    rows, width, depth = 2 * own.shape[0], weight.shape[1], 1024
    columns = pl.BlockSpec((own.shape[0], depth), lambda i, place: (0, i))
    out = jax.ShapeDtypeStruct((rows, width), BF16)
    return pl.pallas_call(
        z_kernel,
        grid_spec=pltpu.PrefetchScalarGridSpec(
            num_scalar_prefetch=1,
            grid=(weight.shape[0] // depth,),
            in_specs=[columns, columns, pl.BlockSpec((depth, width), lambda i, place: (i, 0))],
            out_specs=fixed(out),
            scratch_shapes=[pltpu.VMEM((rows, width), F32)],
        ),
        out_shape=out,
        name="project_gate",
        **params(9e9, 20),
    )(place, own, other, weight)


def gate_outputs(gate, local, bcc, cum_slab, before, before_decay, earlier):
    rows, width = local.shape
    return pl.pallas_call(
        gate_kernel,
        grid=(rows // GROUP,),
        in_specs=[rows_of(width), rows_of(width), rows_of(2 * LANES), rows_of(LANES)]
        + [whole(a.shape) for a in (before, before_decay, *earlier)],
        out_specs=[rows_of(width), pl.BlockSpec((1, GROUP), lambda i: (0, i))],
        out_shape=[
            jax.ShapeDtypeStruct((rows, width), BF16), jax.ShapeDtypeStruct((1, rows), F32),
        ],
        scratch_shapes=[pltpu.VMEM((LANES, width), BF16)],
        name="gate",
        **params(1e9, 10, 60),
    )(gate, local, bcc, cum_slab, before, before_decay, *earlier)


def normalized(core, gated, other, mean_squares, gain):
    rows, width = other.shape
    return pl.pallas_call(
        norm_kernel,
        grid_spec=pltpu.PrefetchScalarGridSpec(
            num_scalar_prefetch=1,
            grid=(2,),
            in_specs=[
                pl.BlockSpec((rows, width), lambda j, core: (core[0], 0)),
                pl.BlockSpec((rows, width), lambda j, core: (0, 0)),
                pl.BlockSpec((1, rows), lambda j, core: (0, 0)),
                pl.BlockSpec((1, width), lambda j, core: (0, j)),
            ],
            out_specs=pl.BlockSpec((rows, width), lambda j, core: (0, j)),
        ),
        out_shape=jax.ShapeDtypeStruct((rows, 2 * width), BF16),
        compiler_params=pltpu.CompilerParams(vmem_limit_bytes=40 * 2**20),
        cost_estimate=pl.CostEstimate(flops=10**7, bytes_accessed=4 * 2**20, transcendentals=0),
        name="normalized",
    )(core.astype(jnp.int32)[None], gated, other, mean_squares, gain)


def earlier_states(final):
    size = lax.axis_size("y")
    parts = [final] + [round_ring(final, "y", distance) for distance in range(1, size)]
    width = final.shape[1]
    outs = [
        jax.ShapeDtypeStruct(final.shape, BF16),
        jax.ShapeDtypeStruct((LANES, width), F32),
        jax.ShapeDtypeStruct((8, width), F32),
    ]
    total, before, before_decay = pl.pallas_call(
        row_kernel,
        grid_spec=pltpu.PrefetchScalarGridSpec(
            num_scalar_prefetch=1,
            grid=(1,),
            in_specs=[fixed(a) for a in parts],
            out_specs=[fixed(a) for a in outs],
        ),
        out_shape=outs,
        name="row_states",
        **params(1e7, 2),
    )(lax.axis_index("y").astype(jnp.int32)[None], *parts)
    rows = lax.axis_size("z")
    earlier = [
        lax.ppermute(total, "z", [(i, i + distance) for i in range(rows - distance)])
        for distance in range(rows - 1, 0, -1)
    ]
    return before, before_decay, earlier


def tied(values, *to):
    return lax.optimization_barrier((*values, *to))[: len(values)]


def near_blocks(own):
    block = own.shape[0]
    half = block // 2
    y_less, y_more = round_ring(own, "y", 1), round_ring(own, "y", -1)
    z_less, z_more = round_ring(own, "z", 1), round_ring(own, "z", -1)
    join = lambda *parts: jnp.concatenate(parts, axis=0)
    from_y_less = round_ring(join(z_less, y_less[:half]), "y", 1)
    from_y_more = round_ring(join(z_more, y_more[half:]), "y", -1)
    from_z_less = round_ring(join(y_more, z_less[:half]), "z", 1)
    from_z_more = round_ring(join(y_less, z_more[half:]), "z", -1)
    y_far = join(from_y_less[block:], from_y_more[block:])
    z_far = join(from_z_less[block:], from_z_more[block:])
    near = [own, y_less, y_more, z_less, z_more, from_y_less, from_y_more, from_z_less, from_z_more]
    sources = [(i, 0, block) for i in range(9)] + [(i, block, half) for i in (5, 6, 7, 8)]
    return near, sources, y_far, z_far


def far_blocks(y_far, z_far, before_last):
    block = y_far.shape[0]
    half = block // 2
    far_y_less, far_y_more = round_ring(z_far, "y", 1), round_ring(z_far, "y", -1)
    far_z_less, far_z_more = round_ring(y_far, "z", 1), round_ring(y_far, "z", -1)
    top, low = tied((far_y_less[:half], far_z_more[half:]), before_last)
    far = [far_y_less, far_y_more, far_z_less, far_z_more, round_ring(top, "y", 1), round_ring(low, "z", -1)]
    sources = [(i, 0, block) for i in range(4)] + [(4, 0, half), (5, 0, half)]
    return far, sources


def block_order():
    places = (
        ((0, 0), (-1, 0), (1, 0), (0, -1), (0, 1), (-1, -1), (1, 1), (1, -1), (-1, 1), (2, 0), (0, 2))
        + ((-1, 2), (1, 2), (2, -1), (2, 1), (2, 2))
    )
    y, z = lax.axis_index("y"), lax.axis_index("z")
    return [(z + dz) % 4 * 4 + (y + dy) % 4 for dy, dz in places]


def shards(
    tokens, x_weight, z_weight, bc_weight, dt_weight, conv_x, conv_bc, dt_bias, decay_rate, skip,
    norm_gain,
):
    core = lax.axis_index("core")
    width = x_weight.shape[1] // 2
    heads = dt_weight.shape[1] // 2

    def mine(a, axis):
        size = a.shape[axis] // 2
        return lax.dynamic_slice_in_dim(a, core * size, size, axis)

    def others(a, axis):
        size = a.shape[axis] // 2
        return lax.dynamic_slice_in_dim(a, (1 - core) * size, size, axis)

    def per_lane(a):
        return jnp.pad(mine(a, 0), (0, LANES - heads))[None, :]

    narrow = jnp.concatenate(
        [bc_weight, dt_weight, jnp.zeros((bc_weight.shape[0], LANES - 2 * heads), BF16)], axis=1
    )
    narrow = lax.all_gather(narrow, ("z", "y", "core"), axis=0, tiled=True)
    own_block = jnp.concatenate([mine(x_weight, 1), swap_cores(others(x_weight, 1))], axis=0)
    near, near_sources, y_far, z_far = near_blocks(own_block)
    place = jnp.stack([core, *block_order()]).astype(jnp.int32)

    (z_weight,) = tied((z_weight,), own_block)
    z_block = in_core_order(core, mine(z_weight, 1), swap_cores(others(z_weight, 1)), 0)
    z_whole = lax.all_gather(z_block, ("z", "y"), axis=0, tiled=True)
    (tokens,) = tied((tokens,), *near[1:5])
    chips = lax.axis_size("z") * lax.axis_size("y")
    to_next = lambda target: lax.ppermute(
        tokens[-HALO:], ("z", "y", "core"),
        [(2 * i + 1, 2 * i + 2 + target) for i in range(chips - 1)],
    )
    slabs = (tokens, swap_cores(tokens), to_next(0) + to_next(1))

    y_far, z_far = tied((y_far, z_far), *slabs[1:])
    sums = first_products(place, slabs, near, near_sources, 11)
    far, far_sources = far_blocks(y_far, z_far, sums[0])
    bcc, cum, cum_slab, cum_t, step_t, weights_in, decays = prepared(
        place, slabs, narrow, conv_bc, per_lane(dt_bias), per_lane(decay_rate), heads
    )
    xc, entering, final = local_states(
        place, slabs, far, far_sources, 11, 5, sums, bcc, weights_in, decays, mine(conv_x, 1)
    )
    before, before_decay, earlier = earlier_states(final)
    skip_lanes = jnp.repeat(mine(skip, 0), HEAD)[None, :]
    local = local_outputs(xc, bcc, cum, cum_t, step_t, entering, skip_lanes)
    gate = project_gate(place, slabs, z_whole)
    gated, squares = gate_outputs(gate, local, bcc, cum_slab, before, before_decay, earlier)

    other = swap_cores(others(gated, 0))
    summed = mine(squares + swap_cores(squares), 1)
    across = [round_ring(summed, "x", distance) for distance in range(1, lax.axis_size("x"))]
    mean_squares = (summed + sum(across)) / (2 * width * lax.axis_size("x"))
    return normalized(core, gated, other, mean_squares, norm_gain[None, :])


def solution(mesh):
    fine = Mesh(mesh.devices.reshape(4, 4, 2, 4), ("z", "y", "core", "x"))
    ctx = ("z", "y", "core")
    placed = (
        P(ctx, None),
        P(ctx, "x"),
        P(ctx, "x"),
        P(ctx, None),
        P(ctx, "x"),
        P(None, "x"),
        P(),
        P("x"),
        P("x"),
        P("x"),
        P("x"),
    )
    return jax.shard_map(
        shards, mesh=fine, in_specs=placed, out_specs=P(ctx, "x"), check_vma=False
    )
```

```python
import functools

import jax
import jax.numpy as jnp
from jax import lax
from jax.experimental import pallas as pl
from jax.experimental.pallas import tpu as pltpu
from jax.sharding import Mesh, PartitionSpec as P

GROUP = 256
HALO = 16
LANES = 128
HEAD = 64
F32 = jnp.float32
BF16 = jnp.bfloat16


def swap_cores(a):
    return lax.ppermute(a, "core", [(0, 1), (1, 0)])


def round_ring(a, axis, distance):
    size = lax.axis_size(axis)
    return lax.ppermute(a, axis, [(i, (i + distance) % size) for i in range(size)])


def along_chips(a, distance):
    chips = lax.axis_size("z") * lax.axis_size("y")
    return lax.ppermute(a, ("z", "y"), [(i, i + distance) for i in range(chips - distance)])


def in_core_order(core, mine, other, axis):
    first = jnp.where(core == 0, mine, other)
    second = jnp.where(core == 0, other, mine)
    return jnp.concatenate([first, second], axis=axis)


def expand_heads(values, width):
    high = values.astype(BF16)
    rest = values - high.astype(F32)
    middle = rest.astype(BF16)
    low = (rest - middle.astype(F32)).astype(BF16)
    row = lax.broadcasted_iota(jnp.int32, (LANES, width), 0)
    col = lax.broadcasted_iota(jnp.int32, (LANES, width), 1)
    spread = ((col >= row * HEAD) & (col < row * HEAD + HEAD)).astype(BF16)
    dot = lambda part: jnp.dot(part, spread, preferred_element_type=F32)
    return dot(high) + dot(middle) + dot(low)


def silu(a):
    half = 0.5 * a
    return half + half * jnp.tanh(half)


def conv_rows(rows, kernel_ref):
    taps, count = kernel_ref.shape[0], rows.shape[0] - HALO
    first = HALO - (taps - 1)
    accum = kernel_ref[0:1, :] * rows[first : first + count]
    for tap in range(1, taps):
        accum = accum + kernel_ref[tap : tap + 1, :] * rows[first + tap : first + tap + count]
    return silu(accum).astype(BF16)


def prepare_kernel(
    place_ref, own_ref, other_ref, before_ref, weight_ref, conv_ref, bias_ref, rate_ref,
    bcc_ref, cum_ref, cum_slab_ref, cum_t_ref, step_t_ref, weights_in_ref, decays_ref,
    accum,
):
    step = pl.program_id(0)
    core = place_ref[0]
    slab = own_ref.shape[0]
    heads = cum_t_ref.shape[0]
    rows_own = pl.ds(pl.multiple_of(HALO + slab * core, HALO), slab)
    rows_other = pl.ds(pl.multiple_of(HALO + slab * (1 - core), HALO), slab)

    @pl.when(step == 0)
    def _():
        accum[...] = jnp.zeros_like(accum)

    weight = weight_ref[...]
    for rows, ref in ((slice(0, HALO), before_ref), (rows_own, own_ref), (rows_other, other_ref)):
        accum[rows, :] = accum[rows, :] + jnp.dot(ref[...], weight, preferred_element_type=F32)

    @pl.when(step == pl.num_programs(0) - 1)
    def _():
        total = jnp.zeros((1, LANES), F32)
        row = lax.broadcasted_iota(jnp.int32, (GROUP, GROUP), 0)
        col = lax.broadcasted_iota(jnp.int32, (GROUP, GROUP), 1)
        lower = (row >= col).astype(F32)
        for block in range(2 * slab // GROUP):
            part = slice(block * GROUP, (block + 1) * GROUP)
            narrow = accum[block * GROUP : (block + 1) * GROUP + HALO, : 2 * LANES]
            bcc_ref[part, :] = conv_rows(narrow.astype(BF16).astype(F32), conv_ref)
            raw = accum[block * GROUP + HALO : (block + 1) * GROUP + HALO, 2 * LANES :]
            raw = jnp.where(core == 0, raw, pltpu.roll(raw, LANES - heads, axis=1))
            raw = raw + bias_ref[...]
            step_size = jnp.maximum(raw, 0.0) + jnp.log1p(jnp.exp(-jnp.abs(raw)))
            log_decay = -rate_ref[...] * step_size
            cum = jnp.dot(
                lower, log_decay, preferred_element_type=F32, precision=lax.Precision.HIGHEST
            )
            last = cum[GROUP - 1 : GROUP, :]
            cum_ref[part, :] = cum
            cum_slab_ref[part, :] = cum + total
            cum_t_ref[:, part] = cum.T[:heads, :]
            step_t_ref[:, part] = step_size.T[:heads, :]
            weights_in_ref[part, :] = jnp.exp(last - cum) * step_size
            decays_ref[block * 8 : block * 8 + 8, :] = jnp.broadcast_to(jnp.exp(last), (8, LANES))
            total = total + last
        end = decays_ref.shape[0] - 8
        decays_ref[end:, :] = jnp.broadcast_to(jnp.exp(total), (8, LANES))


def block_columns(ref, place_ref, first, count):
    core = place_ref[0]
    parts = []
    for index in range(first, first + count):
        base = place_ref[1 + index] * (2 * LANES)
        for start in (base + LANES * core, base + LANES * (1 - core)):
            parts.append(ref[:, pl.ds(pl.multiple_of(start, LANES), LANES)])
    return jnp.concatenate(parts, axis=1)


def stacked(sources, refs):
    return jnp.concatenate([refs[ref][first : first + size, :] for ref, first, size in sources], axis=0)


def first_kernel(sources, count, place_ref, own_ref, other_ref, before_ref, *refs):
    weights, (out_ref, out_before_ref) = refs[:-2], refs[-2:]
    block = pl.program_id(0)
    is_own = block // 2 == place_ref[0]

    def product(ref):
        columns = block_columns(ref, place_ref, 0, count)
        return jnp.dot(columns, stacked(sources, weights), preferred_element_type=F32)

    @pl.when(block == 0)
    def _():
        out_before_ref[...] = product(before_ref)

    @pl.when(is_own)
    def _():
        out_ref[...] = product(own_ref)

    @pl.when(jnp.logical_not(is_own))
    def _():
        out_ref[...] = product(other_ref)


def states_kernel(
    sources, done, count, place_ref, own_ref, other_ref, before_ref, *refs
):
    weights = refs[:-12]
    (
        sum_ref, sum_before_ref, bcc_ref, weights_in_ref, decays_ref, conv_ref,
        xc_ref, entering_ref, final_ref,
        state, x_in, tail,
    ) = refs[-12:]
    block = pl.program_id(0)
    width = x_in.shape[1]
    is_own = block // 2 == place_ref[0]

    def product(ref):
        columns = block_columns(ref, place_ref, done, count)
        return jnp.dot(columns, stacked(sources, weights), preferred_element_type=F32)

    @pl.when(block == 0)
    def _():
        state[...] = jnp.zeros_like(state)
        tail[...] = (sum_before_ref[...] + product(before_ref)).astype(BF16).astype(F32)

    @pl.when(is_own)
    def _():
        x_in[...] = (sum_ref[...] + product(own_ref)).astype(BF16).astype(F32)

    @pl.when(jnp.logical_not(is_own))
    def _():
        x_in[...] = (sum_ref[...] + product(other_ref)).astype(BF16).astype(F32)

    rows = jnp.concatenate([tail[...], x_in[...]], axis=0)
    tail[...] = rows[GROUP:]
    xc = conv_rows(rows, conv_ref)
    xc_ref[...] = xc
    entering_ref[0] = state[...].astype(BF16)
    weighted = (expand_heads(weights_in_ref[...], width) * xc.astype(F32)).astype(BF16)
    contrib = lax.dot_general(
        bcc_ref[:, :LANES], weighted, (((0,), (0,)), ((), ())), preferred_element_type=F32
    )
    decay = expand_heads(decays_ref[pl.ds(pl.multiple_of(block * 8, 8), 8), :], width)
    state[...] = state[...] * decay[0:1] + contrib

    @pl.when(block == pl.num_programs(0) - 1)
    def _():
        end = decays_ref.shape[0] - 8
        final_ref[:LANES, :] = state[...].astype(BF16)
        final_ref[LANES:, :] = split_decay(expand_heads(decays_ref[end:, :], width)[0:1])


def split_decay(decay):
    high = decay.astype(BF16)
    low = decay - high.astype(F32)
    row = lax.broadcasted_iota(jnp.int32, (HALO, decay.shape[1]), 0)
    return jnp.where(row == 0, high.astype(F32), jnp.where(row == 1, low, 0.0)).astype(BF16)


def unpacked(sent):
    sent = sent.astype(F32)
    return sent[:LANES], sent[LANES : LANES + 1] + sent[LANES + 1 : LANES + 2]


def row_kernel(place_ref, *refs):
    size = len(refs) - 3
    parts, (total_ref, before_ref, before_decay_ref) = refs[:size], refs[size:]
    place = place_ref[0]
    width = total_ref.shape[1]
    total, decay = jnp.zeros((LANES, width), F32), jnp.ones((1, width), F32)
    before_ref[...] = total
    before_decay_ref[...] = jnp.broadcast_to(decay, before_decay_ref.shape)
    for index in range(size):
        if index > 0:

            @pl.when(place == index)
            def _():
                before_ref[...] = total
                before_decay_ref[...] = jnp.broadcast_to(decay, before_decay_ref.shape)

        distance = (place - index + size) % size
        chosen = parts[0][...]
        for other in range(1, size):
            chosen = jnp.where(distance == other, parts[other][...], chosen)
        state, state_decay = unpacked(chosen)
        total = total * state_decay + state
        decay = decay * state_decay
    total_ref[:LANES, :] = total.astype(BF16)
    total_ref[LANES:, :] = split_decay(decay)


def outputs_kernel(xc_ref, bcc_ref, cum_ref, cum_t_ref, step_t_ref, entering_ref, skip_ref, out_ref, carried):
    width = xc_ref.shape[1]
    b_rows, c_rows = bcc_ref[:, :LANES], bcc_ref[:, LANES:]
    scores = lax.dot_general(c_rows, b_rows, (((1,), (1,)), ((), ())), preferred_element_type=F32)
    row = lax.broadcasted_iota(jnp.int32, (GROUP, GROUP), 0)
    col = lax.broadcasted_iota(jnp.int32, (GROUP, GROUP), 1)
    scores = jnp.where(row >= col, scores, 0.0)
    cum = cum_ref[...]
    grown = expand_heads(jnp.exp(cum), width)
    carried[...] = grown * jnp.dot(c_rows, entering_ref[0], preferred_element_type=F32)
    lane = lax.broadcasted_iota(jnp.int32, (GROUP, LANES), 1)

    def mixing(head):
        gaps = cum[:, head : head + 1] - cum_t_ref[head : head + 1, :]
        return (
            scores * jnp.exp(jnp.minimum(gaps, 0.0)) * step_t_ref[head : head + 1, :]
        ).astype(BF16)

    for pair in range(width // LANES):
        lanes = slice(pair * LANES, (pair + 1) * LANES)
        inputs = xc_ref[:, lanes]
        zero = jnp.zeros_like(inputs)
        both = jnp.concatenate([mixing(2 * pair), mixing(2 * pair + 1)], axis=1)
        stacked = jnp.concatenate(
            [jnp.where(lane < HEAD, inputs, zero), jnp.where(lane < HEAD, zero, inputs)], axis=0
        )
        out_ref[:, lanes] = (
            carried[:, lanes]
            + jnp.dot(both, stacked, preferred_element_type=F32)
            + skip_ref[:, lanes] * inputs.astype(F32)
        ).astype(BF16)


def z_kernel(place_ref, own_ref, other_ref, weight_ref, gate_ref, accum):
    step = pl.program_id(0)
    slab = own_ref.shape[0]
    core = place_ref[0]

    def product(ref):
        return jnp.dot(ref[...], weight_ref[...], preferred_element_type=F32)

    for index, ref in enumerate((own_ref, other_ref)):
        rows = slice(index * slab, (index + 1) * slab)
        target = pl.ds(pl.multiple_of(slab * (core if index == 0 else 1 - core), slab), slab)

        @pl.when(step == 0)
        def _():
            accum[rows, :] = product(ref)

        @pl.when((step > 0) & (step < pl.num_programs(0) - 1))
        def _():
            accum[rows, :] = accum[rows, :] + product(ref)

        @pl.when(step == pl.num_programs(0) - 1)
        def _():
            gate_ref[target, :] = (accum[rows, :] + product(ref)).astype(BF16)


def gate_kernel(
    core_ref, gate_ref, local_ref, bcc_ref, cum_ref, before_ref, before_decay_ref, *refs
):
    earlier, (mine_ref, send_ref, squares_ref, incoming) = refs[:-4], refs[-4:]
    width = local_ref.shape[1]

    @pl.when(pl.program_id(0) == 0)
    def _():
        carried = jnp.zeros((LANES, width), F32)
        for part in earlier:
            state, decay = unpacked(part[...])
            carried = carried * decay + state
        incoming[...] = (carried * before_decay_ref[0:1, :] + before_ref[...]).astype(BF16)

    grown = expand_heads(jnp.exp(cum_ref[...]), width)
    carried = jnp.dot(bcc_ref[:, LANES:], incoming[...], preferred_element_type=F32)
    gated = (local_ref[...].astype(F32) + grown * carried) * silu(gate_ref[...].astype(F32))
    is_own = pl.program_id(0) // 2 == core_ref[0]

    @pl.when(is_own)
    def _():
        mine_ref[...] = gated.astype(BF16)

    @pl.when(jnp.logical_not(is_own))
    def _():
        send_ref[...] = gated.astype(BF16)

    squares = gated * gated
    high = squares.astype(BF16)
    low = (squares - high.astype(F32)).astype(BF16)
    ones = jnp.ones((8, width), BF16)
    across = (((1,), (1,)), ((), ()))
    summed = lax.dot_general(ones, high, across, preferred_element_type=F32) + lax.dot_general(
        ones, low, across, preferred_element_type=F32
    )
    squares_ref[...] = summed[0:1, :]


def norm_kernel(core_ref, mine_ref, other_ref, squares_ref, gain_ref, out_ref):
    half = pl.program_id(0)
    across = jnp.broadcast_to(squares_ref[...], (8, squares_ref.shape[1]))
    scale = lax.rsqrt(across + 1e-05).T[:, 0:1]

    @pl.when(half == core_ref[0])
    def _():
        out_ref[...] = (mine_ref[...].astype(F32) * scale * gain_ref[...]).astype(BF16)

    @pl.when(half != core_ref[0])
    def _():
        out_ref[...] = (other_ref[...].astype(F32) * scale * gain_ref[...]).astype(BF16)


def whole(shape):
    return pl.BlockSpec(shape, lambda i: (0,) * len(shape))


def rows_of(width):
    return pl.BlockSpec((GROUP, width), lambda i: (i, 0))


def params(flops, megabytes, vmem=32):
    return dict(
        compiler_params=pltpu.CompilerParams(vmem_limit_bytes=vmem * 2**20),
        cost_estimate=pl.CostEstimate(
            flops=int(flops), bytes_accessed=megabytes * 2**20, transcendentals=0
        ),
    )


def fixed(a):
    return pl.BlockSpec(a.shape, lambda i, place: (0,) * len(a.shape))


def row_block(width):
    return pl.BlockSpec((GROUP, width), lambda i, place: (i, 0))


def slab_blocks(depth):
    own = pl.BlockSpec((GROUP, depth), lambda i, place: (jnp.clip(i - 2 * place[0], 0, 1), 0))
    other = pl.BlockSpec((GROUP, depth), lambda i, place: (jnp.clip(i - 2 + 2 * place[0], 0, 1), 0))
    return [own, other]


def prepared(place, slabs, weight, conv_bc, bias, rate, heads):
    own, other, before = slabs
    slab, rows, depth = own.shape[0], 2 * own.shape[0], 512
    shape = jax.ShapeDtypeStruct
    outs = [
        shape((rows, 2 * LANES), BF16), shape((rows, LANES), F32), shape((rows, LANES), F32),
        shape((heads, rows), F32), shape((heads, rows), F32), shape((rows, LANES), F32),
        shape((rows // GROUP * 8 + 8, LANES), F32),
    ]
    columns = lambda a: pl.BlockSpec((a.shape[0], depth), lambda i, place: (0, i))
    return pl.pallas_call(
        prepare_kernel,
        grid_spec=pltpu.PrefetchScalarGridSpec(
            num_scalar_prefetch=1,
            grid=(own.shape[1] // depth,),
            in_specs=[columns(a) for a in slabs]
            + [pl.BlockSpec((depth, weight.shape[1]), lambda i, place: (i, 0))]
            + [fixed(a) for a in (conv_bc, bias, rate)],
            out_specs=[fixed(a) for a in outs],
            scratch_shapes=[pltpu.VMEM((HALO + rows, weight.shape[1]), F32)],
        ),
        out_shape=outs,
        name="prepared",
        **params(4e9, 14),
    )(place, *slabs, weight, conv_bc, bias, rate)


def first_products(place, slabs, weights, sources, count):
    own, other, before = slabs
    width = weights[0].shape[1]
    outs = [
        jax.ShapeDtypeStruct((2 * own.shape[0], width), F32), jax.ShapeDtypeStruct((HALO, width), F32),
    ]
    return pl.pallas_call(
        functools.partial(first_kernel, sources, count),
        grid_spec=pltpu.PrefetchScalarGridSpec(
            num_scalar_prefetch=1,
            grid=(2 * own.shape[0] // GROUP,),
            in_specs=slab_blocks(own.shape[1]) + [fixed(a) for a in (before, *weights)],
            out_specs=[row_block(width), fixed(outs[1])],
        ),
        out_shape=outs,
        name="first_products",
        **params(6e9, 18),
    )(place, *slabs, *weights)


def local_states(place, slabs, weights, sources, done, count, sums, bcc, weights_in, decays, conv_x):
    own, other, before = slabs
    rows, width = sums[0].shape
    blocks = rows // GROUP
    outs = [
        jax.ShapeDtypeStruct((rows, width), BF16),
        jax.ShapeDtypeStruct((blocks, LANES, width), BF16),
        jax.ShapeDtypeStruct((LANES + HALO, width), BF16),
    ]
    return pl.pallas_call(
        functools.partial(states_kernel, sources, done, count),
        grid_spec=pltpu.PrefetchScalarGridSpec(
            num_scalar_prefetch=1,
            grid=(blocks,),
            in_specs=slab_blocks(own.shape[1])
            + [fixed(a) for a in (before, *weights)]
            + [
                row_block(width), fixed(sums[1]), row_block(2 * LANES), row_block(LANES),
                fixed(decays), fixed(conv_x),
            ],
            out_specs=[
                row_block(width),
                pl.BlockSpec((1, LANES, width), lambda i, place: (i, 0, 0)),
                fixed(outs[2]),
            ],
            scratch_shapes=[
                pltpu.VMEM((LANES, width), F32), pltpu.VMEM((GROUP, width), F32),
                pltpu.VMEM((HALO, width), F32),
            ],
        ),
        out_shape=outs,
        name="states",
        **params(8e9, 16),
    )(place, *slabs, *weights, *sums, bcc, weights_in, decays, conv_x)


def local_outputs(xc, bcc, cum, cum_t, step_t, entering, skip):
    rows, width = xc.shape
    heads = cum_t.shape[0]
    by_lane = pl.BlockSpec((heads, GROUP), lambda i: (0, i))
    return pl.pallas_call(
        outputs_kernel,
        grid=(rows // GROUP,),
        in_specs=[
            rows_of(width), rows_of(2 * LANES), rows_of(LANES), by_lane, by_lane,
            pl.BlockSpec((1, LANES, width), lambda i: (i, 0, 0)), whole((1, width)),
        ],
        out_specs=rows_of(width),
        out_shape=jax.ShapeDtypeStruct((rows, width), BF16),
        scratch_shapes=[pltpu.VMEM((GROUP, width), F32)],
        compiler_params=pltpu.CompilerParams(vmem_limit_bytes=32 * 2**20),
        cost_estimate=pl.CostEstimate(flops=10**10, bytes_accessed=10 * 2**20, transcendentals=4 * 2**20),
        name="outputs",
    )(xc, bcc, cum, cum_t, step_t, entering, skip)


def project_gate(place, slabs, weight):
    own, other, _ = slabs
    rows, width, depth = 2 * own.shape[0], weight.shape[1], 1024
    columns = pl.BlockSpec((own.shape[0], depth), lambda i, place: (0, i))
    out = jax.ShapeDtypeStruct((rows, width), BF16)
    return pl.pallas_call(
        z_kernel,
        grid_spec=pltpu.PrefetchScalarGridSpec(
            num_scalar_prefetch=1,
            grid=(weight.shape[0] // depth,),
            in_specs=[columns, columns, pl.BlockSpec((depth, width), lambda i, place: (i, 0))],
            out_specs=fixed(out),
            scratch_shapes=[pltpu.VMEM((rows, width), F32)],
        ),
        out_shape=out,
        name="project_gate",
        **params(9e9, 20),
    )(place, own, other, weight)


def gate_outputs(core, gate, local, bcc, cum_slab, before, before_decay, earlier):
    rows, width = local.shape
    half = jax.ShapeDtypeStruct((rows // 2, width), BF16)
    return pl.pallas_call(
        gate_kernel,
        grid_spec=pltpu.PrefetchScalarGridSpec(
            num_scalar_prefetch=1,
            grid=(rows // GROUP,),
            in_specs=[row_block(width), row_block(width), row_block(2 * LANES), row_block(LANES)]
            + [fixed(a) for a in (before, before_decay, *earlier)],
            out_specs=slab_blocks(width) + [pl.BlockSpec((1, GROUP), lambda i, place: (0, i))],
            scratch_shapes=[pltpu.VMEM((LANES, width), BF16)],
        ),
        out_shape=[half, half, jax.ShapeDtypeStruct((1, rows), F32)],
        name="gate",
        **params(1e9, 10),
    )(core, gate, local, bcc, cum_slab, before, before_decay, *earlier)


def normalized(core, gated, other, mean_squares, gain):
    rows, width = other.shape
    return pl.pallas_call(
        norm_kernel,
        grid_spec=pltpu.PrefetchScalarGridSpec(
            num_scalar_prefetch=1,
            grid=(2,),
            in_specs=[
                pl.BlockSpec((rows, width), lambda j, core: (0, 0)),
                pl.BlockSpec((rows, width), lambda j, core: (0, 0)),
                pl.BlockSpec((1, rows), lambda j, core: (0, 0)),
                pl.BlockSpec((1, width), lambda j, core: (0, j)),
            ],
            out_specs=pl.BlockSpec((rows, width), lambda j, core: (0, j)),
        ),
        out_shape=jax.ShapeDtypeStruct((rows, 2 * width), BF16),
        compiler_params=pltpu.CompilerParams(vmem_limit_bytes=32 * 2**20),
        cost_estimate=pl.CostEstimate(flops=10**7, bytes_accessed=4 * 2**20, transcendentals=0),
        name="normalized",
    )(core.astype(jnp.int32)[None], gated, other, mean_squares, gain)


def earlier_states(final):
    size = lax.axis_size("y")
    parts = [final] + [round_ring(final, "y", distance) for distance in range(1, size)]
    width = final.shape[1]
    outs = [
        jax.ShapeDtypeStruct(final.shape, BF16),
        jax.ShapeDtypeStruct((LANES, width), F32),
        jax.ShapeDtypeStruct((8, width), F32),
    ]
    total, before, before_decay = pl.pallas_call(
        row_kernel,
        grid_spec=pltpu.PrefetchScalarGridSpec(
            num_scalar_prefetch=1,
            grid=(1,),
            in_specs=[fixed(a) for a in parts],
            out_specs=[fixed(a) for a in outs],
        ),
        out_shape=outs,
        name="row_states",
        **params(1e7, 2),
    )(lax.axis_index("y").astype(jnp.int32)[None], *parts)
    rows = lax.axis_size("z")
    earlier = [
        lax.ppermute(total, "z", [(i, i + distance) for i in range(rows - distance)])
        for distance in range(rows - 1, 0, -1)
    ]
    return before, before_decay, earlier


def tied(values, *to):
    return lax.optimization_barrier((*values, *to))[: len(values)]


def near_blocks(own):
    block = own.shape[0]
    half = block // 2
    y_less, y_more = round_ring(own, "y", 1), round_ring(own, "y", -1)
    z_less, z_more = round_ring(own, "z", 1), round_ring(own, "z", -1)
    join = lambda *parts: jnp.concatenate(parts, axis=0)
    from_y_less = round_ring(join(z_less, y_less[:half]), "y", 1)
    from_y_more = round_ring(join(z_more, y_more[half:]), "y", -1)
    from_z_less = round_ring(join(y_more, z_less[:half]), "z", 1)
    from_z_more = round_ring(join(y_less, z_more[half:]), "z", -1)
    y_far = join(from_y_less[block:], from_y_more[block:])
    z_far = join(from_z_less[block:], from_z_more[block:])
    near = [own, y_less, y_more, z_less, z_more, from_y_less, from_y_more, from_z_less, from_z_more]
    sources = [(i, 0, block) for i in range(9)] + [(i, block, half) for i in (5, 6, 7, 8)]
    return near, sources, y_far, z_far


def far_blocks(y_far, z_far, before_last):
    block = y_far.shape[0]
    half = block // 2
    far_y_less, far_y_more = round_ring(z_far, "y", 1), round_ring(z_far, "y", -1)
    far_z_less, far_z_more = round_ring(y_far, "z", 1), round_ring(y_far, "z", -1)
    top, low = tied((far_y_less[:half], far_z_more[half:]), before_last)
    far = [far_y_less, far_y_more, far_z_less, far_z_more, round_ring(top, "y", 1), round_ring(low, "z", -1)]
    sources = [(i, 0, block) for i in range(4)] + [(4, 0, half), (5, 0, half)]
    return far, sources


def block_order():
    places = (
        ((0, 0), (-1, 0), (1, 0), (0, -1), (0, 1), (-1, -1), (1, 1), (1, -1), (-1, 1), (2, 0), (0, 2))
        + ((-1, 2), (1, 2), (2, -1), (2, 1), (2, 2))
    )
    y, z = lax.axis_index("y"), lax.axis_index("z")
    return [(z + dz) % 4 * 4 + (y + dy) % 4 for dy, dz in places]


def shards(
    tokens, x_weight, z_weight, bc_weight, dt_weight, conv_x, conv_bc, dt_bias, decay_rate, skip,
    norm_gain,
):
    core = lax.axis_index("core")
    width = x_weight.shape[1] // 2
    heads = dt_weight.shape[1] // 2

    def mine(a, axis):
        size = a.shape[axis] // 2
        return lax.dynamic_slice_in_dim(a, core * size, size, axis)

    def others(a, axis):
        size = a.shape[axis] // 2
        return lax.dynamic_slice_in_dim(a, (1 - core) * size, size, axis)

    def per_lane(a):
        return jnp.pad(mine(a, 0), (0, LANES - heads))[None, :]

    narrow = jnp.concatenate(
        [bc_weight, dt_weight, jnp.zeros((bc_weight.shape[0], LANES - 2 * heads), BF16)], axis=1
    )
    narrow = lax.all_gather(narrow, ("z", "y", "core"), axis=0, tiled=True)
    own_block = jnp.concatenate([mine(x_weight, 1), swap_cores(others(x_weight, 1))], axis=0)
    near, near_sources, y_far, z_far = near_blocks(own_block)
    place = jnp.stack([core, *block_order()]).astype(jnp.int32)

    (z_weight,) = tied((z_weight,), own_block)
    z_block = in_core_order(core, mine(z_weight, 1), swap_cores(others(z_weight, 1)), 0)
    z_whole = lax.all_gather(z_block, ("z", "y"), axis=0, tiled=True)
    (tokens,) = tied((tokens,), *near[1:5])
    chips = lax.axis_size("z") * lax.axis_size("y")
    to_next = lambda target: lax.ppermute(
        tokens[-HALO:], ("z", "y", "core"),
        [(2 * i + 1, 2 * i + 2 + target) for i in range(chips - 1)],
    )
    slabs = (tokens, swap_cores(tokens), to_next(0) + to_next(1))

    y_far, z_far = tied((y_far, z_far), *slabs[1:])
    sums = first_products(place, slabs, near, near_sources, 11)
    far, far_sources = far_blocks(y_far, z_far, sums[0])
    bcc, cum, cum_slab, cum_t, step_t, weights_in, decays = prepared(
        place, slabs, narrow, conv_bc, per_lane(dt_bias), per_lane(decay_rate), heads
    )
    xc, entering, final = local_states(
        place, slabs, far, far_sources, 11, 5, sums, bcc, weights_in, decays, mine(conv_x, 1)
    )
    before, before_decay, earlier = earlier_states(final)
    skip_lanes = jnp.repeat(mine(skip, 0), HEAD)[None, :]
    local = local_outputs(xc, bcc, cum, cum_t, step_t, entering, skip_lanes)
    gate = project_gate(place, slabs, z_whole)
    gated, send, squares = gate_outputs(place[:1], gate, local, bcc, cum_slab, before, before_decay, earlier)

    other = swap_cores(send)
    summed = mine(squares + swap_cores(squares), 1)
    across = [round_ring(summed, "x", distance) for distance in range(1, lax.axis_size("x"))]
    mean_squares = (summed + sum(across)) / (2 * width * lax.axis_size("x"))
    return normalized(core, gated, other, mean_squares, norm_gain[None, :])


def solution(mesh):
    fine = Mesh(mesh.devices.reshape(4, 4, 2, 4), ("z", "y", "core", "x"))
    ctx = ("z", "y", "core")
    placed = (
        P(ctx, None),
        P(ctx, "x"),
        P(ctx, "x"),
        P(ctx, None),
        P(ctx, "x"),
        P(None, "x"),
        P(),
        P("x"),
        P("x"),
        P("x"),
        P("x"),
    )
    return jax.shard_map(
        shards, mesh=fine, in_specs=placed, out_specs=P(ctx, "x"), check_vma=False
    )
```

```python
import functools

import jax
import jax.numpy as jnp
from jax import lax
from jax.experimental import pallas as pl
from jax.experimental.pallas import tpu as pltpu
from jax.sharding import Mesh, PartitionSpec as P

GROUP = 256
HALO = 16
LANES = 128
HEAD = 64
F32 = jnp.float32
BF16 = jnp.bfloat16


def swap_cores(a):
    return lax.ppermute(a, "core", [(0, 1), (1, 0)])


def round_ring(a, axis, distance):
    size = lax.axis_size(axis)
    return lax.ppermute(a, axis, [(i, (i + distance) % size) for i in range(size)])


def along_chips(a, distance):
    chips = lax.axis_size("z") * lax.axis_size("y")
    return lax.ppermute(a, ("z", "y"), [(i, i + distance) for i in range(chips - distance)])


def in_core_order(core, mine, other, axis):
    first = jnp.where(core == 0, mine, other)
    second = jnp.where(core == 0, other, mine)
    return jnp.concatenate([first, second], axis=axis)


def expand_heads(values, width):
    high = values.astype(BF16)
    rest = values - high.astype(F32)
    middle = rest.astype(BF16)
    low = (rest - middle.astype(F32)).astype(BF16)
    row = lax.broadcasted_iota(jnp.int32, (LANES, width), 0)
    col = lax.broadcasted_iota(jnp.int32, (LANES, width), 1)
    spread = ((col >= row * HEAD) & (col < row * HEAD + HEAD)).astype(BF16)
    dot = lambda part: jnp.dot(part, spread, preferred_element_type=F32)
    return dot(high) + dot(middle) + dot(low)


def silu(a):
    half = 0.5 * a
    return half + half * jnp.tanh(half)


def conv_rows(rows, kernel_ref):
    taps, count = kernel_ref.shape[0], rows.shape[0] - HALO
    first = HALO - (taps - 1)
    accum = kernel_ref[0:1, :] * rows[first : first + count]
    for tap in range(1, taps):
        accum = accum + kernel_ref[tap : tap + 1, :] * rows[first + tap : first + tap + count]
    return silu(accum).astype(BF16)


def prepare_kernel(
    place_ref, own_ref, other_ref, before_ref, weight_ref, conv_ref, bias_ref, rate_ref,
    bcc_ref, cum_ref, cum_slab_ref, cum_t_ref, step_t_ref, weights_in_ref, decays_ref,
    accum,
):
    step = pl.program_id(0)
    core = place_ref[0]
    slab = own_ref.shape[0]
    heads = cum_t_ref.shape[0]
    rows_own = pl.ds(pl.multiple_of(HALO + slab * core, HALO), slab)
    rows_other = pl.ds(pl.multiple_of(HALO + slab * (1 - core), HALO), slab)

    @pl.when(step == 0)
    def _():
        accum[...] = jnp.zeros_like(accum)

    weight = weight_ref[...]
    for rows, ref in ((slice(0, HALO), before_ref), (rows_own, own_ref), (rows_other, other_ref)):
        accum[rows, :] = accum[rows, :] + jnp.dot(ref[...], weight, preferred_element_type=F32)

    @pl.when(step == pl.num_programs(0) - 1)
    def _():
        total = jnp.zeros((1, LANES), F32)
        row = lax.broadcasted_iota(jnp.int32, (GROUP, GROUP), 0)
        col = lax.broadcasted_iota(jnp.int32, (GROUP, GROUP), 1)
        lower = (row >= col).astype(F32)
        for block in range(2 * slab // GROUP):
            part = slice(block * GROUP, (block + 1) * GROUP)
            narrow = accum[block * GROUP : (block + 1) * GROUP + HALO, : 2 * LANES]
            bcc_ref[part, :] = conv_rows(narrow.astype(BF16).astype(F32), conv_ref)
            raw = accum[block * GROUP + HALO : (block + 1) * GROUP + HALO, 2 * LANES :]
            raw = jnp.where(core == 0, raw, pltpu.roll(raw, LANES - heads, axis=1))
            raw = raw + bias_ref[...]
            step_size = jnp.maximum(raw, 0.0) + jnp.log1p(jnp.exp(-jnp.abs(raw)))
            log_decay = -rate_ref[...] * step_size
            cum = jnp.dot(
                lower, log_decay, preferred_element_type=F32, precision=lax.Precision.HIGHEST
            )
            last = cum[GROUP - 1 : GROUP, :]
            cum_ref[part, :] = cum
            cum_slab_ref[part, :] = cum + total
            cum_t_ref[:, part] = cum.T[:heads, :]
            step_t_ref[:, part] = step_size.T[:heads, :]
            weights_in_ref[part, :] = jnp.exp(last - cum) * step_size
            decays_ref[block * 8 : block * 8 + 8, :] = jnp.broadcast_to(jnp.exp(last), (8, LANES))
            total = total + last
        end = decays_ref.shape[0] - 8
        decays_ref[end:, :] = jnp.broadcast_to(jnp.exp(total), (8, LANES))


def block_columns(ref, place_ref, first, count):
    core = place_ref[0]
    parts = []
    for index in range(first, first + count):
        base = place_ref[1 + index] * (2 * LANES)
        for start in (base + LANES * core, base + LANES * (1 - core)):
            parts.append(ref[:, pl.ds(pl.multiple_of(start, LANES), LANES)])
    return jnp.concatenate(parts, axis=1)


def stacked(sources, refs):
    return jnp.concatenate([refs[ref][first : first + size, :] for ref, first, size in sources], axis=0)


def first_kernel(sources, count, place_ref, own_ref, other_ref, before_ref, *refs):
    weights, (out_ref, out_before_ref) = refs[:-2], refs[-2:]
    block = pl.program_id(0)
    is_own = block // 2 == place_ref[0]

    def product(ref):
        columns = block_columns(ref, place_ref, 0, count)
        return jnp.dot(columns, stacked(sources, weights), preferred_element_type=F32)

    @pl.when(block == 0)
    def _():
        out_before_ref[...] = product(before_ref)

    @pl.when(is_own)
    def _():
        out_ref[...] = product(own_ref)

    @pl.when(jnp.logical_not(is_own))
    def _():
        out_ref[...] = product(other_ref)


def states_kernel(
    sources, done, count, place_ref, own_ref, other_ref, before_ref, *refs
):
    weights = refs[:-13]
    (
        sum_ref, sum_before_ref, bcc_ref, weights_in_ref, decays_ref, conv_ref,
        xc_ref, entering_ref, final_ref,
        state, x_in, tail, wide,
    ) = refs[-13:]
    block = pl.program_id(0)
    width = x_in.shape[1]
    is_own = block // 2 == place_ref[0]

    def product(ref):
        columns = block_columns(ref, place_ref, done, count)
        return jnp.dot(columns, wide[...], preferred_element_type=F32)

    @pl.when(block == 0)
    def _():
        state[...] = jnp.zeros_like(state)
        row = 0
        for ref, first, size in sources:
            wide[row : row + size, :] = weights[ref][first : first + size, :]
            row += size
        tail[...] = (sum_before_ref[...] + product(before_ref)).astype(BF16).astype(F32)

    @pl.when(is_own)
    def _():
        x_in[...] = (sum_ref[...] + product(own_ref)).astype(BF16).astype(F32)

    @pl.when(jnp.logical_not(is_own))
    def _():
        x_in[...] = (sum_ref[...] + product(other_ref)).astype(BF16).astype(F32)

    rows = jnp.concatenate([tail[...], x_in[...]], axis=0)
    tail[...] = rows[GROUP:]
    xc = conv_rows(rows, conv_ref)
    xc_ref[...] = xc
    entering_ref[0] = state[...].astype(BF16)
    weighted = (expand_heads(weights_in_ref[...], width) * xc.astype(F32)).astype(BF16)
    contrib = lax.dot_general(
        bcc_ref[:, :LANES], weighted, (((0,), (0,)), ((), ())), preferred_element_type=F32
    )
    decay = expand_heads(decays_ref[pl.ds(pl.multiple_of(block * 8, 8), 8), :], width)
    state[...] = state[...] * decay[0:1] + contrib

    @pl.when(block == pl.num_programs(0) - 1)
    def _():
        end = decays_ref.shape[0] - 8
        final_ref[:LANES, :] = state[...].astype(BF16)
        final_ref[LANES:, :] = split_decay(expand_heads(decays_ref[end:, :], width)[0:1])


def split_decay(decay):
    high = decay.astype(BF16)
    low = decay - high.astype(F32)
    row = lax.broadcasted_iota(jnp.int32, (HALO, decay.shape[1]), 0)
    return jnp.where(row == 0, high.astype(F32), jnp.where(row == 1, low, 0.0)).astype(BF16)


def unpacked(sent):
    sent = sent.astype(F32)
    return sent[:LANES], sent[LANES : LANES + 1] + sent[LANES + 1 : LANES + 2]


def row_kernel(place_ref, *refs):
    size = len(refs) - 3
    parts, (total_ref, before_ref, before_decay_ref) = refs[:size], refs[size:]
    place = place_ref[0]
    width = total_ref.shape[1]
    total, decay = jnp.zeros((LANES, width), F32), jnp.ones((1, width), F32)
    before_ref[...] = total
    before_decay_ref[...] = jnp.broadcast_to(decay, before_decay_ref.shape)
    for index in range(size):
        if index > 0:

            @pl.when(place == index)
            def _():
                before_ref[...] = total
                before_decay_ref[...] = jnp.broadcast_to(decay, before_decay_ref.shape)

        distance = (place - index + size) % size
        chosen = parts[0][...]
        for other in range(1, size):
            chosen = jnp.where(distance == other, parts[other][...], chosen)
        state, state_decay = unpacked(chosen)
        total = total * state_decay + state
        decay = decay * state_decay
    total_ref[:LANES, :] = total.astype(BF16)
    total_ref[LANES:, :] = split_decay(decay)


def outputs_kernel(xc_ref, bcc_ref, cum_ref, cum_t_ref, step_t_ref, entering_ref, skip_ref, out_ref, carried):
    width = xc_ref.shape[1]
    b_rows, c_rows = bcc_ref[:, :LANES], bcc_ref[:, LANES:]
    scores = lax.dot_general(c_rows, b_rows, (((1,), (1,)), ((), ())), preferred_element_type=F32)
    row = lax.broadcasted_iota(jnp.int32, (GROUP, GROUP), 0)
    col = lax.broadcasted_iota(jnp.int32, (GROUP, GROUP), 1)
    scores = jnp.where(row >= col, scores, 0.0)
    cum = cum_ref[...]
    grown = expand_heads(jnp.exp(cum), width)
    carried[...] = grown * jnp.dot(c_rows, entering_ref[0], preferred_element_type=F32)
    lane = lax.broadcasted_iota(jnp.int32, (GROUP, LANES), 1)

    def mixing(head):
        gaps = cum[:, head : head + 1] - cum_t_ref[head : head + 1, :]
        return (
            scores * jnp.exp(jnp.minimum(gaps, 0.0)) * step_t_ref[head : head + 1, :]
        ).astype(BF16)

    for pair in range(width // LANES):
        lanes = slice(pair * LANES, (pair + 1) * LANES)
        inputs = xc_ref[:, lanes]
        zero = jnp.zeros_like(inputs)
        both = jnp.concatenate([mixing(2 * pair), mixing(2 * pair + 1)], axis=1)
        stacked = jnp.concatenate(
            [jnp.where(lane < HEAD, inputs, zero), jnp.where(lane < HEAD, zero, inputs)], axis=0
        )
        out_ref[:, lanes] = (
            carried[:, lanes]
            + jnp.dot(both, stacked, preferred_element_type=F32)
            + skip_ref[:, lanes] * inputs.astype(F32)
        ).astype(BF16)


def z_kernel(place_ref, own_ref, other_ref, weight_ref, gate_ref, accum):
    step = pl.program_id(0)
    slab = own_ref.shape[0]
    core = place_ref[0]

    def product(ref):
        return jnp.dot(ref[...], weight_ref[...], preferred_element_type=F32)

    for index, ref in enumerate((own_ref, other_ref)):
        rows = slice(index * slab, (index + 1) * slab)
        target = pl.ds(pl.multiple_of(slab * (core if index == 0 else 1 - core), slab), slab)

        @pl.when(step == 0)
        def _():
            accum[rows, :] = product(ref)

        @pl.when((step > 0) & (step < pl.num_programs(0) - 1))
        def _():
            accum[rows, :] = accum[rows, :] + product(ref)

        @pl.when(step == pl.num_programs(0) - 1)
        def _():
            gate_ref[target, :] = (accum[rows, :] + product(ref)).astype(BF16)


def gate_kernel(
    core_ref, gate_ref, local_ref, bcc_ref, cum_ref, before_ref, before_decay_ref, *refs
):
    earlier, (mine_ref, send_ref, squares_ref, incoming) = refs[:-4], refs[-4:]
    width = local_ref.shape[1]

    @pl.when(pl.program_id(0) == 0)
    def _():
        carried = jnp.zeros((LANES, width), F32)
        for part in earlier:
            state, decay = unpacked(part[...])
            carried = carried * decay + state
        incoming[...] = (carried * before_decay_ref[0:1, :] + before_ref[...]).astype(BF16)

    grown = expand_heads(jnp.exp(cum_ref[...]), width)
    carried = jnp.dot(bcc_ref[:, LANES:], incoming[...], preferred_element_type=F32)
    gated = (local_ref[...].astype(F32) + grown * carried) * silu(gate_ref[...].astype(F32))
    is_own = pl.program_id(0) // 2 == core_ref[0]

    @pl.when(is_own)
    def _():
        mine_ref[...] = gated.astype(BF16)

    @pl.when(jnp.logical_not(is_own))
    def _():
        send_ref[...] = gated.astype(BF16)

    squares = gated * gated
    high = squares.astype(BF16)
    low = (squares - high.astype(F32)).astype(BF16)
    ones = jnp.ones((8, width), BF16)
    across = (((1,), (1,)), ((), ()))
    summed = lax.dot_general(ones, high, across, preferred_element_type=F32) + lax.dot_general(
        ones, low, across, preferred_element_type=F32
    )
    squares_ref[...] = summed[0:1, :]


def norm_kernel(core_ref, mine_ref, other_ref, squares_ref, gain_ref, out_ref):
    half = pl.program_id(0)
    across = jnp.broadcast_to(squares_ref[...], (8, squares_ref.shape[1]))
    scale = lax.rsqrt(across + 1e-05).T[:, 0:1]

    @pl.when(half == core_ref[0])
    def _():
        out_ref[...] = (mine_ref[...].astype(F32) * scale * gain_ref[...]).astype(BF16)

    @pl.when(half != core_ref[0])
    def _():
        out_ref[...] = (other_ref[...].astype(F32) * scale * gain_ref[...]).astype(BF16)


def whole(shape):
    return pl.BlockSpec(shape, lambda i: (0,) * len(shape))


def rows_of(width):
    return pl.BlockSpec((GROUP, width), lambda i: (i, 0))


def params(flops, megabytes, vmem=60):
    return dict(
        compiler_params=pltpu.CompilerParams(vmem_limit_bytes=vmem * 2**20),
        cost_estimate=pl.CostEstimate(
            flops=int(flops), bytes_accessed=megabytes * 2**20, transcendentals=0
        ),
    )


def fixed(a):
    return pl.BlockSpec(a.shape, lambda i, place: (0,) * len(a.shape))


def row_block(width):
    return pl.BlockSpec((GROUP, width), lambda i, place: (i, 0))


def slab_blocks(depth):
    own = pl.BlockSpec((GROUP, depth), lambda i, place: (jnp.clip(i - 2 * place[0], 0, 1), 0))
    other = pl.BlockSpec((GROUP, depth), lambda i, place: (jnp.clip(i - 2 + 2 * place[0], 0, 1), 0))
    return [own, other]


def prepared(place, slabs, weight, conv_bc, bias, rate, heads):
    own, other, before = slabs
    slab, rows, depth = own.shape[0], 2 * own.shape[0], 512
    shape = jax.ShapeDtypeStruct
    outs = [
        shape((rows, 2 * LANES), BF16), shape((rows, LANES), F32), shape((rows, LANES), F32),
        shape((heads, rows), F32), shape((heads, rows), F32), shape((rows, LANES), F32),
        shape((rows // GROUP * 8 + 8, LANES), F32),
    ]
    columns = lambda a: pl.BlockSpec((a.shape[0], depth), lambda i, place: (0, i))
    return pl.pallas_call(
        prepare_kernel,
        grid_spec=pltpu.PrefetchScalarGridSpec(
            num_scalar_prefetch=1,
            grid=(own.shape[1] // depth,),
            in_specs=[columns(a) for a in slabs]
            + [pl.BlockSpec((depth, weight.shape[1]), lambda i, place: (i, 0))]
            + [fixed(a) for a in (conv_bc, bias, rate)],
            out_specs=[fixed(a) for a in outs],
            scratch_shapes=[pltpu.VMEM((HALO + rows, weight.shape[1]), F32)],
        ),
        out_shape=outs,
        name="prepared",
        **params(4e9, 14),
    )(place, *slabs, weight, conv_bc, bias, rate)


def first_products(place, slabs, weights, sources, count):
    own, other, before = slabs
    width = weights[0].shape[1]
    outs = [
        jax.ShapeDtypeStruct((2 * own.shape[0], width), F32), jax.ShapeDtypeStruct((HALO, width), F32),
    ]
    return pl.pallas_call(
        functools.partial(first_kernel, sources, count),
        grid_spec=pltpu.PrefetchScalarGridSpec(
            num_scalar_prefetch=1,
            grid=(2 * own.shape[0] // GROUP,),
            in_specs=slab_blocks(own.shape[1]) + [fixed(a) for a in (before, *weights)],
            out_specs=[row_block(width), fixed(outs[1])],
        ),
        out_shape=outs,
        name="first_products",
        **params(6e9, 18),
    )(place, *slabs, *weights)


def local_states(place, slabs, weights, sources, done, count, sums, bcc, weights_in, decays, conv_x):
    own, other, before = slabs
    rows, width = sums[0].shape
    blocks = rows // GROUP
    outs = [
        jax.ShapeDtypeStruct((rows, width), BF16),
        jax.ShapeDtypeStruct((blocks, LANES, width), BF16),
        jax.ShapeDtypeStruct((LANES + HALO, width), BF16),
    ]
    return pl.pallas_call(
        functools.partial(states_kernel, sources, done, count),
        grid_spec=pltpu.PrefetchScalarGridSpec(
            num_scalar_prefetch=1,
            grid=(blocks,),
            in_specs=slab_blocks(own.shape[1])
            + [fixed(a) for a in (before, *weights)]
            + [
                row_block(width), fixed(sums[1]), row_block(2 * LANES), row_block(LANES),
                fixed(decays), fixed(conv_x),
            ],
            out_specs=[
                row_block(width),
                pl.BlockSpec((1, LANES, width), lambda i, place: (i, 0, 0)),
                fixed(outs[2]),
            ],
            scratch_shapes=[
                pltpu.VMEM((LANES, width), F32), pltpu.VMEM((GROUP, width), F32),
                pltpu.VMEM((HALO, width), F32),
                pltpu.VMEM((sum(size for _, _, size in sources), width), BF16),
            ],
        ),
        out_shape=outs,
        name="states",
        **params(11e9, 18, 48),
    )(place, *slabs, *weights, *sums, bcc, weights_in, decays, conv_x)


def local_outputs(xc, bcc, cum, cum_t, step_t, entering, skip):
    rows, width = xc.shape
    heads = cum_t.shape[0]
    by_lane = pl.BlockSpec((heads, GROUP), lambda i: (0, i))
    return pl.pallas_call(
        outputs_kernel,
        grid=(rows // GROUP,),
        in_specs=[
            rows_of(width), rows_of(2 * LANES), rows_of(LANES), by_lane, by_lane,
            pl.BlockSpec((1, LANES, width), lambda i: (i, 0, 0)), whole((1, width)),
        ],
        out_specs=rows_of(width),
        out_shape=jax.ShapeDtypeStruct((rows, width), BF16),
        scratch_shapes=[pltpu.VMEM((GROUP, width), F32)],
        compiler_params=pltpu.CompilerParams(vmem_limit_bytes=60 * 2**20),
        cost_estimate=pl.CostEstimate(flops=10**10, bytes_accessed=10 * 2**20, transcendentals=4 * 2**20),
        name="outputs",
    )(xc, bcc, cum, cum_t, step_t, entering, skip)


def project_gate(place, slabs, weight):
    own, other, _ = slabs
    rows, width, depth = 2 * own.shape[0], weight.shape[1], 1024
    columns = pl.BlockSpec((own.shape[0], depth), lambda i, place: (0, i))
    out = jax.ShapeDtypeStruct((rows, width), BF16)
    return pl.pallas_call(
        z_kernel,
        grid_spec=pltpu.PrefetchScalarGridSpec(
            num_scalar_prefetch=1,
            grid=(weight.shape[0] // depth,),
            in_specs=[columns, columns, pl.BlockSpec((depth, width), lambda i, place: (i, 0))],
            out_specs=fixed(out),
            scratch_shapes=[pltpu.VMEM((rows, width), F32)],
        ),
        out_shape=out,
        name="project_gate",
        **params(9e9, 20),
    )(place, own, other, weight)


def gate_outputs(core, gate, local, bcc, cum_slab, before, before_decay, earlier):
    rows, width = local.shape
    half = jax.ShapeDtypeStruct((rows // 2, width), BF16)
    return pl.pallas_call(
        gate_kernel,
        grid_spec=pltpu.PrefetchScalarGridSpec(
            num_scalar_prefetch=1,
            grid=(rows // GROUP,),
            in_specs=[row_block(width), row_block(width), row_block(2 * LANES), row_block(LANES)]
            + [fixed(a) for a in (before, before_decay, *earlier)],
            out_specs=slab_blocks(width) + [pl.BlockSpec((1, GROUP), lambda i, place: (0, i))],
            scratch_shapes=[pltpu.VMEM((LANES, width), BF16)],
        ),
        out_shape=[half, half, jax.ShapeDtypeStruct((1, rows), F32)],
        name="gate",
        **params(1e9, 10),
    )(core, gate, local, bcc, cum_slab, before, before_decay, *earlier)


def normalized(core, gated, other, mean_squares, gain):
    rows, width = other.shape
    return pl.pallas_call(
        norm_kernel,
        grid_spec=pltpu.PrefetchScalarGridSpec(
            num_scalar_prefetch=1,
            grid=(2,),
            in_specs=[
                pl.BlockSpec((rows, width), lambda j, core: (0, 0)),
                pl.BlockSpec((rows, width), lambda j, core: (0, 0)),
                pl.BlockSpec((1, rows), lambda j, core: (0, 0)),
                pl.BlockSpec((1, width), lambda j, core: (0, j)),
            ],
            out_specs=pl.BlockSpec((rows, width), lambda j, core: (0, j)),
        ),
        out_shape=jax.ShapeDtypeStruct((rows, 2 * width), BF16),
        compiler_params=pltpu.CompilerParams(vmem_limit_bytes=60 * 2**20),
        cost_estimate=pl.CostEstimate(flops=10**7, bytes_accessed=4 * 2**20, transcendentals=0),
        name="normalized",
    )(core.astype(jnp.int32)[None], gated, other, mean_squares, gain)


def earlier_states(final):
    size = lax.axis_size("y")
    parts = [final] + [round_ring(final, "y", distance) for distance in range(1, size)]
    width = final.shape[1]
    outs = [
        jax.ShapeDtypeStruct(final.shape, BF16),
        jax.ShapeDtypeStruct((LANES, width), F32),
        jax.ShapeDtypeStruct((8, width), F32),
    ]
    total, before, before_decay = pl.pallas_call(
        row_kernel,
        grid_spec=pltpu.PrefetchScalarGridSpec(
            num_scalar_prefetch=1,
            grid=(1,),
            in_specs=[fixed(a) for a in parts],
            out_specs=[fixed(a) for a in outs],
        ),
        out_shape=outs,
        name="row_states",
        **params(1e7, 2),
    )(lax.axis_index("y").astype(jnp.int32)[None], *parts)
    rows = lax.axis_size("z")
    earlier = [
        lax.ppermute(total, "z", [(i, i + distance) for i in range(rows - distance)])
        for distance in range(rows - 1, 0, -1)
    ]
    return before, before_decay, earlier


def tied(values, *to):
    return lax.optimization_barrier((*values, *to))[: len(values)]


def travelling(own, after_first, before_third, before_last):
    block = own.shape[0]
    half = block // 2
    y_less, y_more = round_ring(own, "y", 1), round_ring(own, "y", -1)
    z_less, z_more = round_ring(own, "z", 1), round_ring(own, "z", -1)
    after_first([own, y_less, y_more, z_less, z_more])
    join = lambda *parts: jnp.concatenate(parts, axis=0)
    from_y_less = round_ring(join(z_less, y_less[:half]), "y", 1)
    from_y_more = round_ring(join(z_more, y_more[half:]), "y", -1)
    from_z_less = round_ring(join(y_more, z_less[:half]), "z", 1)
    from_z_more = round_ring(join(y_less, z_more[half:]), "z", -1)
    halves = tied((from_y_less, from_y_more, from_z_less, from_z_more), *before_third())
    y_far = join(halves[0][block:], halves[1][block:])
    z_far = join(halves[2][block:], halves[3][block:])
    far_y_less, far_y_more = round_ring(z_far, "y", 1), round_ring(z_far, "y", -1)
    far_z_less, far_z_more = round_ring(y_far, "z", 1), round_ring(y_far, "z", -1)
    top, low = tied((far_y_less, far_z_more), *before_last(halves))
    blocks = [
        from_y_less, from_y_more, from_z_less, from_z_more,
        far_y_less, far_y_more, far_z_less, far_z_more,
        round_ring(top[:half], "y", 1), round_ring(low[half:], "z", -1),
    ]
    sources = [(i, 0, block) for i in range(4)] + [(i, block, half) for i in range(4)]
    sources += [(i, 0, block) for i in range(4, 8)] + [(8, 0, half), (9, 0, half)]
    return blocks, sources


def block_order():
    places = (
        ((0, 0), (-1, 0), (1, 0), (0, -1), (0, 1), (-1, -1), (1, 1), (1, -1), (-1, 1), (2, 0), (0, 2))
        + ((-1, 2), (1, 2), (2, -1), (2, 1), (2, 2))
    )
    y, z = lax.axis_index("y"), lax.axis_index("z")
    return [(z + dz) % 4 * 4 + (y + dy) % 4 for dy, dz in places]


def shards(
    tokens, x_weight, z_weight, bc_weight, dt_weight, conv_x, conv_bc, dt_bias, decay_rate, skip,
    norm_gain,
):
    core = lax.axis_index("core")
    width = x_weight.shape[1] // 2
    heads = dt_weight.shape[1] // 2

    def mine(a, axis):
        size = a.shape[axis] // 2
        return lax.dynamic_slice_in_dim(a, core * size, size, axis)

    def others(a, axis):
        size = a.shape[axis] // 2
        return lax.dynamic_slice_in_dim(a, (1 - core) * size, size, axis)

    def per_lane(a):
        return jnp.pad(mine(a, 0), (0, LANES - heads))[None, :]

    narrow = jnp.concatenate(
        [bc_weight, dt_weight, jnp.zeros((bc_weight.shape[0], LANES - 2 * heads), BF16)], axis=1
    )
    narrow = lax.all_gather(narrow, ("z", "y", "core"), axis=0, tiled=True)
    own_block = jnp.concatenate([mine(x_weight, 1), swap_cores(others(x_weight, 1))], axis=0)
    place = jnp.stack([core, *block_order()]).astype(jnp.int32)
    slabs, sums, early, z_blocks, z_wholes = [], [], [], [], []

    def after_first(blocks):
        rows, z_rows = tied((tokens, z_weight), *blocks[1:])
        chips = lax.axis_size("z") * lax.axis_size("y")
        to_next = lambda target: lax.ppermute(
            rows[-HALO:], ("z", "y", "core"),
            [(2 * i + 1, 2 * i + 2 + target) for i in range(chips - 1)],
        )
        slabs.extend((rows, swap_cores(rows), to_next(0) + to_next(1)))
        z_blocks.append(
            in_core_order(core, mine(z_rows, 1), swap_cores(others(z_rows, 1)), 0)
        )
        sources = [(i, 0, blocks[0].shape[0]) for i in range(5)]
        sums.extend(first_products(place, slabs, blocks, sources, 5))

    def before_last(second):
        (z_block,) = tied((z_blocks[0],), *second)
        z_wholes.append(lax.all_gather(z_block, ("z", "y"), axis=0, tiled=True))
        early.extend(
            prepared(place, slabs, narrow, conv_bc, per_lane(dt_bias), per_lane(decay_rate), heads)
        )
        return early[:1]

    blocks, sources = travelling(own_block, after_first, lambda: sums[:1], before_last)
    bcc, cum, cum_slab, cum_t, step_t, weights_in, decays = early
    (z_whole,) = z_wholes
    xc, entering, final = local_states(
        place, slabs, blocks, sources, 5, 11, sums, bcc, weights_in, decays, mine(conv_x, 1)
    )
    before, before_decay, earlier = earlier_states(final)
    skip_lanes = jnp.repeat(mine(skip, 0), HEAD)[None, :]
    local = local_outputs(xc, bcc, cum, cum_t, step_t, entering, skip_lanes)
    gate = project_gate(place, slabs, z_whole)
    gated, send, squares = gate_outputs(place[:1], gate, local, bcc, cum_slab, before, before_decay, earlier)

    other = swap_cores(send)
    summed = mine(squares + swap_cores(squares), 1)
    across = [round_ring(summed, "x", distance) for distance in range(1, lax.axis_size("x"))]
    mean_squares = (summed + sum(across)) / (2 * width * lax.axis_size("x"))
    return normalized(core, gated, other, mean_squares, norm_gain[None, :])


def solution(mesh):
    fine = Mesh(mesh.devices.reshape(4, 4, 2, 4), ("z", "y", "core", "x"))
    ctx = ("z", "y", "core")
    placed = (
        P(ctx, None),
        P(ctx, "x"),
        P(ctx, "x"),
        P(ctx, None),
        P(ctx, "x"),
        P(None, "x"),
        P(),
        P("x"),
        P("x"),
        P("x"),
        P("x"),
    )
    return jax.shard_map(
        shards, mesh=fine, in_specs=placed, out_specs=P(ctx, "x"), check_vma=False
    )
```

```python
import functools

import jax
import jax.numpy as jnp
from jax import lax
from jax.experimental import pallas as pl
from jax.experimental.pallas import tpu as pltpu
from jax.sharding import Mesh, PartitionSpec as P

GROUP = 256
HALO = 16
LANES = 128
HEAD = 64
F32 = jnp.float32
BF16 = jnp.bfloat16


def swap_cores(a):
    return lax.ppermute(a, "core", [(0, 1), (1, 0)])


def round_ring(a, axis, distance):
    size = lax.axis_size(axis)
    return lax.ppermute(a, axis, [(i, (i + distance) % size) for i in range(size)])


def along_chips(a, distance):
    chips = lax.axis_size("z") * lax.axis_size("y")
    return lax.ppermute(a, ("z", "y"), [(i, i + distance) for i in range(chips - distance)])


def in_core_order(core, mine, other, axis):
    first = jnp.where(core == 0, mine, other)
    second = jnp.where(core == 0, other, mine)
    return jnp.concatenate([first, second], axis=axis)


def expand_heads(values, width):
    high = values.astype(BF16)
    rest = values - high.astype(F32)
    middle = rest.astype(BF16)
    low = (rest - middle.astype(F32)).astype(BF16)
    row = lax.broadcasted_iota(jnp.int32, (LANES, width), 0)
    col = lax.broadcasted_iota(jnp.int32, (LANES, width), 1)
    spread = ((col >= row * HEAD) & (col < row * HEAD + HEAD)).astype(BF16)
    dot = lambda part: jnp.dot(part, spread, preferred_element_type=F32)
    return dot(high) + dot(middle) + dot(low)


def silu(a):
    half = 0.5 * a
    return half + half * jnp.tanh(half)


def conv_rows(rows, kernel_ref):
    taps, count = kernel_ref.shape[0], rows.shape[0] - HALO
    first = HALO - (taps - 1)
    accum = kernel_ref[0:1, :] * rows[first : first + count]
    for tap in range(1, taps):
        accum = accum + kernel_ref[tap : tap + 1, :] * rows[first + tap : first + tap + count]
    return silu(accum).astype(BF16)


def prepare_kernel(
    place_ref, own_ref, other_ref, before_ref, weight_ref, conv_ref, bias_ref, rate_ref,
    bcc_ref, cum_ref, cum_slab_ref, cum_t_ref, step_t_ref, weights_in_ref, decays_ref,
    accum,
):
    step = pl.program_id(0)
    core = place_ref[0]
    slab = own_ref.shape[0]
    heads = cum_t_ref.shape[0]
    rows_own = pl.ds(pl.multiple_of(HALO + slab * core, HALO), slab)
    rows_other = pl.ds(pl.multiple_of(HALO + slab * (1 - core), HALO), slab)

    @pl.when(step == 0)
    def _():
        accum[...] = jnp.zeros_like(accum)

    weight = weight_ref[...]
    for rows, ref in ((slice(0, HALO), before_ref), (rows_own, own_ref), (rows_other, other_ref)):
        accum[rows, :] = accum[rows, :] + jnp.dot(ref[...], weight, preferred_element_type=F32)

    @pl.when(step == pl.num_programs(0) - 1)
    def _():
        total = jnp.zeros((1, LANES), F32)
        row = lax.broadcasted_iota(jnp.int32, (GROUP, GROUP), 0)
        col = lax.broadcasted_iota(jnp.int32, (GROUP, GROUP), 1)
        lower = (row >= col).astype(F32)
        for block in range(2 * slab // GROUP):
            part = slice(block * GROUP, (block + 1) * GROUP)
            narrow = accum[block * GROUP : (block + 1) * GROUP + HALO, : 2 * LANES]
            bcc_ref[part, :] = conv_rows(narrow.astype(BF16).astype(F32), conv_ref)
            raw = accum[block * GROUP + HALO : (block + 1) * GROUP + HALO, 2 * LANES :]
            raw = jnp.where(core == 0, raw, pltpu.roll(raw, LANES - heads, axis=1))
            raw = raw + bias_ref[...]
            step_size = jnp.maximum(raw, 0.0) + jnp.log1p(jnp.exp(-jnp.abs(raw)))
            log_decay = -rate_ref[...] * step_size
            cum = jnp.dot(
                lower, log_decay, preferred_element_type=F32, precision=lax.Precision.HIGHEST
            )
            last = cum[GROUP - 1 : GROUP, :]
            cum_ref[part, :] = cum
            cum_slab_ref[part, :] = cum + total
            cum_t_ref[:, part] = cum.T[:heads, :]
            step_t_ref[:, part] = step_size.T[:heads, :]
            weights_in_ref[part, :] = jnp.exp(last - cum) * step_size
            decays_ref[block * 8 : block * 8 + 8, :] = jnp.broadcast_to(jnp.exp(last), (8, LANES))
            total = total + last
        end = decays_ref.shape[0] - 8
        decays_ref[end:, :] = jnp.broadcast_to(jnp.exp(total), (8, LANES))


def block_columns(ref, place_ref, first, count):
    core = place_ref[0]
    parts = []
    for index in range(first, first + count):
        base = place_ref[1 + index] * (2 * LANES)
        for start in (base + LANES * core, base + LANES * (1 - core)):
            parts.append(ref[:, pl.ds(pl.multiple_of(start, LANES), LANES)])
    return jnp.concatenate(parts, axis=1)


def stacked(sources, refs):
    return jnp.concatenate([refs[ref][first : first + size, :] for ref, first, size in sources], axis=0)


def first_kernel(sources, count, place_ref, own_ref, other_ref, before_ref, *refs):
    weights, (out_ref, out_before_ref) = refs[:-2], refs[-2:]
    block = pl.program_id(0)
    is_own = block // 2 == place_ref[0]

    def product(ref):
        columns = block_columns(ref, place_ref, 0, count)
        return jnp.dot(columns, stacked(sources, weights), preferred_element_type=F32)

    @pl.when(block == 0)
    def _():
        out_before_ref[...] = product(before_ref)

    @pl.when(is_own)
    def _():
        out_ref[...] = product(own_ref)

    @pl.when(jnp.logical_not(is_own))
    def _():
        out_ref[...] = product(other_ref)


def states_kernel(
    sources, done, count, place_ref, own_ref, other_ref, before_ref, *refs
):
    weights = refs[:-13]
    (
        sum_ref, sum_before_ref, bcc_ref, weights_in_ref, decays_ref, conv_ref,
        xc_ref, entering_ref, final_ref,
        state, x_in, tail, wide,
    ) = refs[-13:]
    block = pl.program_id(0)
    width = x_in.shape[1]
    is_own = block // 2 == place_ref[0]

    def product(ref):
        columns = block_columns(ref, place_ref, done, count)
        return jnp.dot(columns, wide[...], preferred_element_type=F32)

    @pl.when(block == 0)
    def _():
        state[...] = jnp.zeros_like(state)
        row = 0
        for ref, first, size in sources:
            wide[row : row + size, :] = weights[ref][first : first + size, :]
            row += size
        tail[...] = (sum_before_ref[...] + product(before_ref)).astype(BF16).astype(F32)

    @pl.when(is_own)
    def _():
        x_in[...] = (sum_ref[...] + product(own_ref)).astype(BF16).astype(F32)

    @pl.when(jnp.logical_not(is_own))
    def _():
        x_in[...] = (sum_ref[...] + product(other_ref)).astype(BF16).astype(F32)

    rows = jnp.concatenate([tail[...], x_in[...]], axis=0)
    tail[...] = rows[GROUP:]
    xc = conv_rows(rows, conv_ref)
    xc_ref[...] = xc
    entering_ref[0] = state[...].astype(BF16)
    weighted = (expand_heads(weights_in_ref[...], width) * xc.astype(F32)).astype(BF16)
    contrib = lax.dot_general(
        bcc_ref[:, :LANES], weighted, (((0,), (0,)), ((), ())), preferred_element_type=F32
    )
    decay = expand_heads(decays_ref[pl.ds(pl.multiple_of(block * 8, 8), 8), :], width)
    state[...] = state[...] * decay[0:1] + contrib

    @pl.when(block == pl.num_programs(0) - 1)
    def _():
        end = decays_ref.shape[0] - 8
        final_ref[:LANES, :] = state[...].astype(BF16)
        final_ref[LANES:, :] = split_decay(expand_heads(decays_ref[end:, :], width)[0:1])


def split_decay(decay):
    high = decay.astype(BF16)
    low = decay - high.astype(F32)
    row = lax.broadcasted_iota(jnp.int32, (HALO, decay.shape[1]), 0)
    return jnp.where(row == 0, high.astype(F32), jnp.where(row == 1, low, 0.0)).astype(BF16)


def unpacked(sent):
    sent = sent.astype(F32)
    return sent[:LANES], sent[LANES : LANES + 1] + sent[LANES + 1 : LANES + 2]


def row_kernel(place_ref, *refs):
    size = len(refs) - 3
    parts, (total_ref, before_ref, before_decay_ref) = refs[:size], refs[size:]
    place = place_ref[0]
    width = total_ref.shape[1]
    total, decay = jnp.zeros((LANES, width), F32), jnp.ones((1, width), F32)
    before_ref[...] = total
    before_decay_ref[...] = jnp.broadcast_to(decay, before_decay_ref.shape)
    for index in range(size):
        if index > 0:

            @pl.when(place == index)
            def _():
                before_ref[...] = total
                before_decay_ref[...] = jnp.broadcast_to(decay, before_decay_ref.shape)

        distance = (place - index + size) % size
        chosen = parts[0][...]
        for other in range(1, size):
            chosen = jnp.where(distance == other, parts[other][...], chosen)
        state, state_decay = unpacked(chosen)
        total = total * state_decay + state
        decay = decay * state_decay
    total_ref[:LANES, :] = total.astype(BF16)
    total_ref[LANES:, :] = split_decay(decay)


def outputs_kernel(xc_ref, bcc_ref, cum_ref, cum_t_ref, step_t_ref, entering_ref, skip_ref, out_ref, carried):
    width = xc_ref.shape[1]
    b_rows, c_rows = bcc_ref[:, :LANES], bcc_ref[:, LANES:]
    scores = lax.dot_general(c_rows, b_rows, (((1,), (1,)), ((), ())), preferred_element_type=F32)
    row = lax.broadcasted_iota(jnp.int32, (GROUP, GROUP), 0)
    col = lax.broadcasted_iota(jnp.int32, (GROUP, GROUP), 1)
    scores = jnp.where(row >= col, scores, 0.0)
    cum = cum_ref[...]
    grown = expand_heads(jnp.exp(cum), width)
    carried[...] = grown * jnp.dot(c_rows, entering_ref[0], preferred_element_type=F32)
    lane = lax.broadcasted_iota(jnp.int32, (GROUP, LANES), 1)

    def mixing(head):
        gaps = cum[:, head : head + 1] - cum_t_ref[head : head + 1, :]
        return (
            scores * jnp.exp(jnp.minimum(gaps, 0.0)) * step_t_ref[head : head + 1, :]
        ).astype(BF16)

    for pair in range(width // LANES):
        lanes = slice(pair * LANES, (pair + 1) * LANES)
        inputs = xc_ref[:, lanes]
        zero = jnp.zeros_like(inputs)
        both = jnp.concatenate([mixing(2 * pair), mixing(2 * pair + 1)], axis=1)
        stacked = jnp.concatenate(
            [jnp.where(lane < HEAD, inputs, zero), jnp.where(lane < HEAD, zero, inputs)], axis=0
        )
        out_ref[:, lanes] = (
            carried[:, lanes]
            + jnp.dot(both, stacked, preferred_element_type=F32)
            + skip_ref[:, lanes] * inputs.astype(F32)
        ).astype(BF16)


def z_kernel(place_ref, own_ref, other_ref, weight_ref, gate_ref, accum):
    step = pl.program_id(0)
    slab = own_ref.shape[0]
    core = place_ref[0]

    def product(ref):
        return jnp.dot(ref[...], weight_ref[...], preferred_element_type=F32)

    for index, ref in enumerate((own_ref, other_ref)):
        rows = slice(index * slab, (index + 1) * slab)
        target = pl.ds(pl.multiple_of(slab * (core if index == 0 else 1 - core), slab), slab)

        @pl.when(step == 0)
        def _():
            accum[rows, :] = product(ref)

        @pl.when((step > 0) & (step < pl.num_programs(0) - 1))
        def _():
            accum[rows, :] = accum[rows, :] + product(ref)

        @pl.when(step == pl.num_programs(0) - 1)
        def _():
            gate_ref[target, :] = (accum[rows, :] + product(ref)).astype(BF16)


def gate_kernel(
    core_ref, gate_ref, local_ref, bcc_ref, cum_ref, before_ref, before_decay_ref, *refs
):
    earlier, (mine_ref, send_ref, squares_ref, incoming) = refs[:-4], refs[-4:]
    width = local_ref.shape[1]

    @pl.when(pl.program_id(0) == 0)
    def _():
        carried = jnp.zeros((LANES, width), F32)
        for part in earlier:
            state, decay = unpacked(part[...])
            carried = carried * decay + state
        incoming[...] = (carried * before_decay_ref[0:1, :] + before_ref[...]).astype(BF16)

    grown = expand_heads(jnp.exp(cum_ref[...]), width)
    carried = jnp.dot(bcc_ref[:, LANES:], incoming[...], preferred_element_type=F32)
    gated = (local_ref[...].astype(F32) + grown * carried) * silu(gate_ref[...].astype(F32))
    is_own = pl.program_id(0) // 2 == core_ref[0]

    @pl.when(is_own)
    def _():
        mine_ref[...] = gated.astype(BF16)

    @pl.when(jnp.logical_not(is_own))
    def _():
        send_ref[...] = gated.astype(BF16)

    squares = gated * gated
    high = squares.astype(BF16)
    low = (squares - high.astype(F32)).astype(BF16)
    ones = jnp.ones((8, width), BF16)
    across = (((1,), (1,)), ((), ()))
    summed = lax.dot_general(ones, high, across, preferred_element_type=F32) + lax.dot_general(
        ones, low, across, preferred_element_type=F32
    )
    squares_ref[...] = summed[0:1, :]


def norm_kernel(core_ref, mine_ref, other_ref, squares_ref, gain_ref, out_ref):
    half = pl.program_id(0)
    across = jnp.broadcast_to(squares_ref[...], (8, squares_ref.shape[1]))
    scale = lax.rsqrt(across + 1e-05).T[:, 0:1]

    @pl.when(half == core_ref[0])
    def _():
        out_ref[...] = (mine_ref[...].astype(F32) * scale * gain_ref[...]).astype(BF16)

    @pl.when(half != core_ref[0])
    def _():
        out_ref[...] = (other_ref[...].astype(F32) * scale * gain_ref[...]).astype(BF16)


def whole(shape):
    return pl.BlockSpec(shape, lambda i: (0,) * len(shape))


def rows_of(width):
    return pl.BlockSpec((GROUP, width), lambda i: (i, 0))


def params(flops, megabytes, vmem=32):
    return dict(
        compiler_params=pltpu.CompilerParams(vmem_limit_bytes=vmem * 2**20),
        cost_estimate=pl.CostEstimate(
            flops=int(flops), bytes_accessed=megabytes * 2**20, transcendentals=0
        ),
    )


def fixed(a):
    return pl.BlockSpec(a.shape, lambda i, place: (0,) * len(a.shape))


def row_block(width):
    return pl.BlockSpec((GROUP, width), lambda i, place: (i, 0))


def slab_blocks(depth):
    own = pl.BlockSpec((GROUP, depth), lambda i, place: (jnp.clip(i - 2 * place[0], 0, 1), 0))
    other = pl.BlockSpec((GROUP, depth), lambda i, place: (jnp.clip(i - 2 + 2 * place[0], 0, 1), 0))
    return [own, other]


def prepared(place, slabs, weight, conv_bc, bias, rate, heads):
    own, other, before = slabs
    slab, rows, depth = own.shape[0], 2 * own.shape[0], 512
    shape = jax.ShapeDtypeStruct
    outs = [
        shape((rows, 2 * LANES), BF16), shape((rows, LANES), F32), shape((rows, LANES), F32),
        shape((heads, rows), F32), shape((heads, rows), F32), shape((rows, LANES), F32),
        shape((rows // GROUP * 8 + 8, LANES), F32),
    ]
    columns = lambda a: pl.BlockSpec((a.shape[0], depth), lambda i, place: (0, i))
    return pl.pallas_call(
        prepare_kernel,
        grid_spec=pltpu.PrefetchScalarGridSpec(
            num_scalar_prefetch=1,
            grid=(own.shape[1] // depth,),
            in_specs=[columns(a) for a in slabs]
            + [pl.BlockSpec((depth, weight.shape[1]), lambda i, place: (i, 0))]
            + [fixed(a) for a in (conv_bc, bias, rate)],
            out_specs=[fixed(a) for a in outs],
            scratch_shapes=[pltpu.VMEM((HALO + rows, weight.shape[1]), F32)],
        ),
        out_shape=outs,
        name="prepared",
        **params(4e9, 14, 48),
    )(place, *slabs, weight, conv_bc, bias, rate)


def first_products(place, slabs, weights, sources, count):
    own, other, before = slabs
    width = weights[0].shape[1]
    outs = [
        jax.ShapeDtypeStruct((2 * own.shape[0], width), F32), jax.ShapeDtypeStruct((HALO, width), F32),
    ]
    return pl.pallas_call(
        functools.partial(first_kernel, sources, count),
        grid_spec=pltpu.PrefetchScalarGridSpec(
            num_scalar_prefetch=1,
            grid=(2 * own.shape[0] // GROUP,),
            in_specs=slab_blocks(own.shape[1]) + [fixed(a) for a in (before, *weights)],
            out_specs=[row_block(width), fixed(outs[1])],
        ),
        out_shape=outs,
        name="first_products",
        **params(6e9, 18, 48),
    )(place, *slabs, *weights)


def local_states(place, slabs, weights, sources, done, count, sums, bcc, weights_in, decays, conv_x):
    own, other, before = slabs
    rows, width = sums[0].shape
    blocks = rows // GROUP
    outs = [
        jax.ShapeDtypeStruct((rows, width), BF16),
        jax.ShapeDtypeStruct((blocks, LANES, width), BF16),
        jax.ShapeDtypeStruct((LANES + HALO, width), BF16),
    ]
    return pl.pallas_call(
        functools.partial(states_kernel, sources, done, count),
        grid_spec=pltpu.PrefetchScalarGridSpec(
            num_scalar_prefetch=1,
            grid=(blocks,),
            in_specs=slab_blocks(own.shape[1])
            + [fixed(a) for a in (before, *weights)]
            + [
                row_block(width), fixed(sums[1]), row_block(2 * LANES), row_block(LANES),
                fixed(decays), fixed(conv_x),
            ],
            out_specs=[
                row_block(width),
                pl.BlockSpec((1, LANES, width), lambda i, place: (i, 0, 0)),
                fixed(outs[2]),
            ],
            scratch_shapes=[
                pltpu.VMEM((LANES, width), F32), pltpu.VMEM((GROUP, width), F32),
                pltpu.VMEM((HALO, width), F32),
                pltpu.VMEM((sum(size for _, _, size in sources), width), BF16),
            ],
        ),
        out_shape=outs,
        name="states",
        **params(11e9, 18, 40),
    )(place, *slabs, *weights, *sums, bcc, weights_in, decays, conv_x)


def local_outputs(xc, bcc, cum, cum_t, step_t, entering, skip):
    rows, width = xc.shape
    heads = cum_t.shape[0]
    by_lane = pl.BlockSpec((heads, GROUP), lambda i: (0, i))
    return pl.pallas_call(
        outputs_kernel,
        grid=(rows // GROUP,),
        in_specs=[
            rows_of(width), rows_of(2 * LANES), rows_of(LANES), by_lane, by_lane,
            pl.BlockSpec((1, LANES, width), lambda i: (i, 0, 0)), whole((1, width)),
        ],
        out_specs=rows_of(width),
        out_shape=jax.ShapeDtypeStruct((rows, width), BF16),
        scratch_shapes=[pltpu.VMEM((GROUP, width), F32)],
        compiler_params=pltpu.CompilerParams(vmem_limit_bytes=32 * 2**20),
        cost_estimate=pl.CostEstimate(flops=10**10, bytes_accessed=10 * 2**20, transcendentals=4 * 2**20),
        name="outputs",
    )(xc, bcc, cum, cum_t, step_t, entering, skip)


def project_gate(place, slabs, weight):
    own, other, _ = slabs
    rows, width, depth = 2 * own.shape[0], weight.shape[1] // 2, 1024
    columns = pl.BlockSpec((own.shape[0], depth), lambda i, place: (0, i))
    out = jax.ShapeDtypeStruct((rows, width), BF16)
    return pl.pallas_call(
        z_kernel,
        grid_spec=pltpu.PrefetchScalarGridSpec(
            num_scalar_prefetch=1,
            grid=(weight.shape[0] // depth,),
            in_specs=[columns, columns, pl.BlockSpec((depth, width), lambda i, place: (i, place[0]))],
            out_specs=fixed(out),
            scratch_shapes=[pltpu.VMEM((rows, width), F32)],
        ),
        out_shape=out,
        name="project_gate",
        **params(9e9, 20, 48),
    )(place, own, other, weight)


def gate_outputs(core, gate, local, bcc, cum_slab, before, before_decay, earlier):
    rows, width = local.shape
    half = jax.ShapeDtypeStruct((rows // 2, width), BF16)
    return pl.pallas_call(
        gate_kernel,
        grid_spec=pltpu.PrefetchScalarGridSpec(
            num_scalar_prefetch=1,
            grid=(rows // GROUP,),
            in_specs=[row_block(width), row_block(width), row_block(2 * LANES), row_block(LANES)]
            + [fixed(a) for a in (before, before_decay, *earlier)],
            out_specs=slab_blocks(width) + [pl.BlockSpec((1, GROUP), lambda i, place: (0, i))],
            scratch_shapes=[pltpu.VMEM((LANES, width), BF16)],
        ),
        out_shape=[half, half, jax.ShapeDtypeStruct((1, rows), F32)],
        name="gate",
        **params(1e9, 10, 60),
    )(core, gate, local, bcc, cum_slab, before, before_decay, *earlier)


def normalized(core, gated, other, mean_squares, gain):
    rows, width = other.shape
    return pl.pallas_call(
        norm_kernel,
        grid_spec=pltpu.PrefetchScalarGridSpec(
            num_scalar_prefetch=1,
            grid=(2,),
            in_specs=[
                pl.BlockSpec((rows, width), lambda j, core: (0, 0)),
                pl.BlockSpec((rows, width), lambda j, core: (0, 0)),
                pl.BlockSpec((1, rows), lambda j, core: (0, 0)),
                pl.BlockSpec((1, width), lambda j, core: (0, j)),
            ],
            out_specs=pl.BlockSpec((rows, width), lambda j, core: (0, j)),
        ),
        out_shape=jax.ShapeDtypeStruct((rows, 2 * width), BF16),
        compiler_params=pltpu.CompilerParams(vmem_limit_bytes=32 * 2**20),
        cost_estimate=pl.CostEstimate(flops=10**7, bytes_accessed=4 * 2**20, transcendentals=0),
        name="normalized",
    )(core.astype(jnp.int32)[None], gated, other, mean_squares, gain)


def earlier_states(final):
    size = lax.axis_size("y")
    parts = [final] + [round_ring(final, "y", distance) for distance in range(1, size)]
    width = final.shape[1]
    outs = [
        jax.ShapeDtypeStruct(final.shape, BF16),
        jax.ShapeDtypeStruct((LANES, width), F32),
        jax.ShapeDtypeStruct((8, width), F32),
    ]
    total, before, before_decay = pl.pallas_call(
        row_kernel,
        grid_spec=pltpu.PrefetchScalarGridSpec(
            num_scalar_prefetch=1,
            grid=(1,),
            in_specs=[fixed(a) for a in parts],
            out_specs=[fixed(a) for a in outs],
        ),
        out_shape=outs,
        name="row_states",
        **params(1e7, 2),
    )(lax.axis_index("y").astype(jnp.int32)[None], *parts)
    rows = lax.axis_size("z")
    earlier = [
        lax.ppermute(total, "z", [(i, i + distance) for i in range(rows - distance)])
        for distance in range(rows - 1, 0, -1)
    ]
    return before, before_decay, earlier


def tied(values, *to):
    return lax.optimization_barrier((*values, *to))[: len(values)]


def travelling(own, after_first, before_last):
    y_less, y_more = round_ring(own, "y", 1), round_ring(own, "y", -1)
    z_less, z_more = round_ring(own, "z", 1), round_ring(own, "z", -1)
    after_first([y_less, y_more, z_less, z_more])
    y_far, z_far = round_ring(y_less, "y", 1), round_ring(z_more, "z", -1)
    more_more, more_less = round_ring(z_more, "y", -1), round_ring(y_more, "z", 1)
    y_far, z_far = tied((y_far, z_far), more_more, more_less)
    far = [
        round_ring(z_far, "y", -1), round_ring(z_far, "y", 1),
        round_ring(y_far, "z", 1), round_ring(y_far, "z", -1),
    ]
    early = [own, y_less, y_more, z_less, z_more, y_far, z_far, more_more, more_less]
    held_z, held_y, last, *_ = tied((z_less, y_less, *far), *before_last(early))
    less_less, less_more = round_ring(held_z, "y", 1), round_ring(held_y, "z", -1)
    return [*far, less_less, less_more, round_ring(last, "y", -1)]


def all_rows(blocks):
    return [(index, 0, block.shape[0]) for index, block in enumerate(blocks)]


def block_order():
    places = (
        ((0, 0), (-1, 0), (1, 0), (0, -1), (0, 1), (2, 0), (0, 2), (1, 1), (1, -1))
        + ((1, 2), (-1, 2), (2, -1), (2, 1), (-1, -1), (-1, 1), (2, 2))
    )
    y, z = lax.axis_index("y"), lax.axis_index("z")
    return [(z + dz) % 4 * 4 + (y + dy) % 4 for dy, dz in places]


def shards(
    tokens, x_weight, z_weight, bc_weight, dt_weight, conv_x, conv_bc, dt_bias, decay_rate, skip,
    norm_gain,
):
    core = lax.axis_index("core")
    width = x_weight.shape[1] // 2
    heads = dt_weight.shape[1] // 2

    def mine(a, axis):
        size = a.shape[axis] // 2
        return lax.dynamic_slice_in_dim(a, core * size, size, axis)

    def others(a, axis):
        size = a.shape[axis] // 2
        return lax.dynamic_slice_in_dim(a, (1 - core) * size, size, axis)

    def per_lane(a):
        return jnp.pad(mine(a, 0), (0, LANES - heads))[None, :]

    narrow = jnp.concatenate(
        [bc_weight, dt_weight, jnp.zeros((bc_weight.shape[0], LANES - 2 * heads), BF16)], axis=1
    )
    narrow = lax.all_gather(narrow, ("z", "y", "core"), axis=0, tiled=True)
    own_block = jnp.concatenate([mine(x_weight, 1), swap_cores(others(x_weight, 1))], axis=0)
    place = jnp.stack([core, *block_order()]).astype(jnp.int32)
    slabs, sums = [], []

    def after_first(blocks):
        (rows,) = tied((tokens,), *blocks)
        chips = lax.axis_size("z") * lax.axis_size("y")
        to_next = lambda target: lax.ppermute(
            rows[-HALO:], ("z", "y", "core"),
            [(2 * i + 1, 2 * i + 2 + target) for i in range(chips - 1)],
        )
        slabs.extend((rows, swap_cores(rows), to_next(0) + to_next(1)))

    def before_last(blocks):
        sums.extend(first_products(place, slabs, blocks, all_rows(blocks), len(blocks)))
        return sums[:1]

    blocks = travelling(own_block, after_first, before_last)
    (z_rows,) = tied((z_weight,), own_block)
    z_whole = lax.all_gather(z_rows, ("z", "y", "core"), axis=0, tiled=True)
    bcc, cum, cum_slab, cum_t, step_t, weights_in, decays = prepared(
        place, slabs, narrow, conv_bc, per_lane(dt_bias), per_lane(decay_rate), heads
    )
    xc, entering, final = local_states(
        place, slabs, blocks, all_rows(blocks), 9, 7, sums, bcc, weights_in, decays, mine(conv_x, 1)
    )
    before, before_decay, earlier = earlier_states(final)
    skip_lanes = jnp.repeat(mine(skip, 0), HEAD)[None, :]
    local = local_outputs(xc, bcc, cum, cum_t, step_t, entering, skip_lanes)
    gate = project_gate(place, slabs, z_whole)
    gated, send, squares = gate_outputs(place[:1], gate, local, bcc, cum_slab, before, before_decay, earlier)

    other = swap_cores(send)
    summed = mine(squares + swap_cores(squares), 1)
    across = [round_ring(summed, "x", distance) for distance in range(1, lax.axis_size("x"))]
    mean_squares = (summed + sum(across)) / (2 * width * lax.axis_size("x"))
    return normalized(core, gated, other, mean_squares, norm_gain[None, :])


def solution(mesh):
    fine = Mesh(mesh.devices.reshape(4, 4, 2, 4), ("z", "y", "core", "x"))
    ctx = ("z", "y", "core")
    placed = (
        P(ctx, None),
        P(ctx, "x"),
        P(ctx, "x"),
        P(ctx, None),
        P(ctx, "x"),
        P(None, "x"),
        P(),
        P("x"),
        P("x"),
        P("x"),
        P("x"),
    )
    return jax.shard_map(
        shards, mesh=fine, in_specs=placed, out_specs=P(ctx, "x"), check_vma=False
    )
```

```python
import functools

import jax
import jax.numpy as jnp
from jax import lax
from jax.experimental import pallas as pl
from jax.experimental.pallas import tpu as pltpu
from jax.sharding import Mesh, PartitionSpec as P

GROUP = 256
HALO = 16
LANES = 128
HEAD = 64
F32 = jnp.float32
BF16 = jnp.bfloat16


def swap_cores(a):
    return lax.ppermute(a, "core", [(0, 1), (1, 0)])


def round_ring(a, axis, distance):
    size = lax.axis_size(axis)
    return lax.ppermute(a, axis, [(i, (i + distance) % size) for i in range(size)])


def along_chips(a, distance):
    chips = lax.axis_size("z") * lax.axis_size("y")
    return lax.ppermute(a, ("z", "y"), [(i, i + distance) for i in range(chips - distance)])


def in_core_order(core, mine, other, axis):
    first = jnp.where(core == 0, mine, other)
    second = jnp.where(core == 0, other, mine)
    return jnp.concatenate([first, second], axis=axis)


def expand_heads(values, width):
    heads = width // HEAD
    high = values.astype(BF16).astype(F32)
    rest = values - high
    middle = rest.astype(BF16).astype(F32)
    low = rest - middle
    lane = lax.broadcasted_iota(jnp.int32, values.shape, 1)
    parts = jnp.where(lane < heads, high, pltpu.roll(middle, heads, axis=1))
    parts = jnp.where(lane < 2 * heads, parts, pltpu.roll(low, 2 * heads, axis=1))
    parts = jnp.where(lane < 3 * heads, parts, 0.0).astype(BF16)
    row = lax.broadcasted_iota(jnp.int32, (LANES, width), 0)
    col = lax.broadcasted_iota(jnp.int32, (LANES, width), 1)
    head = row % heads
    spread = (col >= head * HEAD) & (col < head * HEAD + HEAD) & (row < 3 * heads)
    return jnp.dot(parts, spread.astype(BF16), preferred_element_type=F32)


def silu(a):
    half = 0.5 * a
    return half + half * jnp.tanh(half)


def conv_rows(rows, kernel_ref):
    taps, count = kernel_ref.shape[0], rows.shape[0] - HALO
    first = HALO - (taps - 1)
    accum = kernel_ref[0:1, :] * rows[first : first + count]
    for tap in range(1, taps):
        accum = accum + kernel_ref[tap : tap + 1, :] * rows[first + tap : first + tap + count]
    return silu(accum).astype(BF16)


def prepare_kernel(
    place_ref, own_ref, other_ref, before_ref, weight_ref, conv_ref, bias_ref, rate_ref,
    bcc_ref, cum_ref, cum_slab_ref, cum_t_ref, step_t_ref, weights_in_ref, decays_ref,
    accum,
):
    step = pl.program_id(0)
    core = place_ref[0]
    slab = own_ref.shape[0]
    heads = cum_t_ref.shape[0]
    rows_own = pl.ds(pl.multiple_of(HALO + slab * core, HALO), slab)
    rows_other = pl.ds(pl.multiple_of(HALO + slab * (1 - core), HALO), slab)

    @pl.when(step == 0)
    def _():
        accum[...] = jnp.zeros_like(accum)

    weight = weight_ref[...]
    for rows, ref in ((slice(0, HALO), before_ref), (rows_own, own_ref), (rows_other, other_ref)):
        accum[rows, :] = accum[rows, :] + jnp.dot(ref[...], weight, preferred_element_type=F32)

    @pl.when(step == pl.num_programs(0) - 1)
    def _():
        total = jnp.zeros((1, LANES), F32)
        row = lax.broadcasted_iota(jnp.int32, (GROUP, GROUP), 0)
        col = lax.broadcasted_iota(jnp.int32, (GROUP, GROUP), 1)
        lower = (row >= col).astype(F32)
        for block in range(2 * slab // GROUP):
            part = slice(block * GROUP, (block + 1) * GROUP)
            narrow = accum[block * GROUP : (block + 1) * GROUP + HALO, : 2 * LANES]
            bcc_ref[part, :] = conv_rows(narrow.astype(BF16).astype(F32), conv_ref)
            raw = accum[block * GROUP + HALO : (block + 1) * GROUP + HALO, 2 * LANES :]
            raw = jnp.where(core == 0, raw, pltpu.roll(raw, LANES - heads, axis=1))
            raw = raw + bias_ref[...]
            step_size = jnp.maximum(raw, 0.0) + jnp.log1p(jnp.exp(-jnp.abs(raw)))
            log_decay = -rate_ref[...] * step_size
            cum = jnp.dot(
                lower, log_decay, preferred_element_type=F32, precision=lax.Precision.HIGHEST
            )
            last = cum[GROUP - 1 : GROUP, :]
            cum_ref[part, :] = cum
            cum_slab_ref[part, :] = cum + total
            cum_t_ref[:, part] = cum.T[:heads, :]
            step_t_ref[:, part] = step_size.T[:heads, :]
            weights_in_ref[part, :] = jnp.exp(last - cum) * step_size
            decays_ref[block * 8 : block * 8 + 8, :] = jnp.broadcast_to(jnp.exp(last), (8, LANES))
            total = total + last
        end = decays_ref.shape[0] - 8
        decays_ref[end:, :] = jnp.broadcast_to(jnp.exp(total), (8, LANES))


def block_columns(ref, place_ref, first, count):
    core = place_ref[0]
    parts = []
    for index in range(first, first + count):
        base = place_ref[1 + index] * (2 * LANES)
        for start in (base + LANES * core, base + LANES * (1 - core)):
            parts.append(ref[:, pl.ds(pl.multiple_of(start, LANES), LANES)])
    return jnp.concatenate(parts, axis=1)


def stacked(sources, refs):
    return jnp.concatenate([refs[ref][first : first + size, :] for ref, first, size in sources], axis=0)


def products_kernel(sources, done, count, started, place_ref, own_ref, other_ref, before_ref, *refs):
    weights, sums, (out_ref, out_before_ref, wide) = refs[: -3 - 2 * started], refs[-3 - 2 * started : -3], refs[-3:]
    block = pl.program_id(0)
    is_own = block // 2 == place_ref[0]

    def product(ref):
        columns = block_columns(ref, place_ref, done, count)
        return jnp.dot(columns, wide[...], preferred_element_type=F32)

    @pl.when(block == 0)
    def _():
        row = 0
        for ref, first, size in sources:
            wide[row : row + size, :] = weights[ref][first : first + size, :]
            row += size
        added = product(before_ref)
        out_before_ref[...] = sums[1][...] + added if started else added

    @pl.when(is_own)
    def _():
        added = product(own_ref)
        out_ref[...] = sums[0][...] + added if started else added

    @pl.when(jnp.logical_not(is_own))
    def _():
        added = product(other_ref)
        out_ref[...] = sums[0][...] + added if started else added


def states_kernel(
    sources, done, count, place_ref, own_ref, other_ref, before_ref, *refs
):
    weights = refs[:-13]
    (
        sum_ref, sum_before_ref, bcc_ref, weights_in_ref, decays_ref, conv_ref,
        xc_ref, entering_ref, final_ref,
        state, x_in, tail, wide,
    ) = refs[-13:]
    block = pl.program_id(0)
    width = x_in.shape[1]
    is_own = block // 2 == place_ref[0]

    def product(ref):
        columns = block_columns(ref, place_ref, done, count)
        return jnp.dot(columns, wide[...], preferred_element_type=F32)

    @pl.when(block == 0)
    def _():
        state[...] = jnp.zeros_like(state)
        row = 0
        for ref, first, size in sources:
            wide[row : row + size, :] = weights[ref][first : first + size, :]
            row += size
        tail[...] = (sum_before_ref[...] + product(before_ref)).astype(BF16).astype(F32)

    @pl.when(is_own)
    def _():
        x_in[...] = (sum_ref[...] + product(own_ref)).astype(BF16).astype(F32)

    @pl.when(jnp.logical_not(is_own))
    def _():
        x_in[...] = (sum_ref[...] + product(other_ref)).astype(BF16).astype(F32)

    rows = jnp.concatenate([tail[...], x_in[...]], axis=0)
    tail[...] = rows[GROUP:]
    xc = conv_rows(rows, conv_ref)
    xc_ref[...] = xc
    entering_ref[0] = state[...].astype(BF16)
    weighted = (expand_heads(weights_in_ref[...], width) * xc.astype(F32)).astype(BF16)
    contrib = lax.dot_general(
        bcc_ref[:, :LANES], weighted, (((0,), (0,)), ((), ())), preferred_element_type=F32
    )
    decay = expand_heads(decays_ref[pl.ds(pl.multiple_of(block * 8, 8), 8), :], width)
    state[...] = state[...] * decay[0:1] + contrib

    @pl.when(block == pl.num_programs(0) - 1)
    def _():
        end = decays_ref.shape[0] - 8
        final_ref[:LANES, :] = state[...].astype(BF16)
        final_ref[LANES:, :] = split_decay(expand_heads(decays_ref[end:, :], width)[0:1])


def split_decay(decay):
    high = decay.astype(BF16)
    low = decay - high.astype(F32)
    row = lax.broadcasted_iota(jnp.int32, (HALO, decay.shape[1]), 0)
    return jnp.where(row == 0, high.astype(F32), jnp.where(row == 1, low, 0.0)).astype(BF16)


def unpacked(sent):
    sent = sent.astype(F32)
    return sent[:LANES], sent[LANES : LANES + 1] + sent[LANES + 1 : LANES + 2]


def row_kernel(place_ref, *refs):
    size = len(refs) - 3
    parts, (total_ref, before_ref, before_decay_ref) = refs[:size], refs[size:]
    place = place_ref[0]
    width = total_ref.shape[1]
    total, decay = jnp.zeros((LANES, width), F32), jnp.ones((1, width), F32)
    before_ref[...] = total
    before_decay_ref[...] = jnp.broadcast_to(decay, before_decay_ref.shape)
    for index in range(size):
        if index > 0:

            @pl.when(place == index)
            def _():
                before_ref[...] = total
                before_decay_ref[...] = jnp.broadcast_to(decay, before_decay_ref.shape)

        distance = (place - index + size) % size
        chosen = parts[0][...]
        for other in range(1, size):
            chosen = jnp.where(distance == other, parts[other][...], chosen)
        state, state_decay = unpacked(chosen)
        total = total * state_decay + state
        decay = decay * state_decay
    total_ref[:LANES, :] = total.astype(BF16)
    total_ref[LANES:, :] = split_decay(decay)


def outputs_kernel(xc_ref, bcc_ref, cum_ref, cum_t_ref, step_t_ref, entering_ref, skip_ref, out_ref, carried):
    width = xc_ref.shape[1]
    b_rows, c_rows = bcc_ref[:, :LANES], bcc_ref[:, LANES:]
    scores = lax.dot_general(c_rows, b_rows, (((1,), (1,)), ((), ())), preferred_element_type=F32)
    row = lax.broadcasted_iota(jnp.int32, (GROUP, GROUP), 0)
    col = lax.broadcasted_iota(jnp.int32, (GROUP, GROUP), 1)
    scores = jnp.where(row >= col, scores, 0.0)
    cum = cum_ref[...]
    grown = expand_heads(jnp.exp(cum), width)
    carried[...] = grown * jnp.dot(c_rows, entering_ref[0], preferred_element_type=F32)
    lane = lax.broadcasted_iota(jnp.int32, (GROUP, LANES), 1)

    def mixing(head):
        gaps = cum[:, head : head + 1] - cum_t_ref[head : head + 1, :]
        return (
            scores * jnp.exp(jnp.minimum(gaps, 0.0)) * step_t_ref[head : head + 1, :]
        ).astype(BF16)

    for pair in range(width // LANES):
        lanes = slice(pair * LANES, (pair + 1) * LANES)
        inputs = xc_ref[:, lanes]
        zero = jnp.zeros_like(inputs)
        both = jnp.concatenate([mixing(2 * pair), mixing(2 * pair + 1)], axis=1)
        stacked = jnp.concatenate(
            [jnp.where(lane < HEAD, inputs, zero), jnp.where(lane < HEAD, zero, inputs)], axis=0
        )
        out_ref[:, lanes] = (
            carried[:, lanes]
            + jnp.dot(both, stacked, preferred_element_type=F32)
            + skip_ref[:, lanes] * inputs.astype(F32)
        ).astype(BF16)


def z_kernel(place_ref, own_ref, other_ref, weight_ref, gate_ref, accum):
    step = pl.program_id(0)
    slab = own_ref.shape[0]
    core = place_ref[0]

    def product(ref):
        return jnp.dot(ref[...], weight_ref[...], preferred_element_type=F32)

    for index, ref in enumerate((own_ref, other_ref)):
        rows = slice(index * slab, (index + 1) * slab)
        target = pl.ds(pl.multiple_of(slab * (core if index == 0 else 1 - core), slab), slab)

        @pl.when(step == 0)
        def _():
            accum[rows, :] = product(ref)

        @pl.when((step > 0) & (step < pl.num_programs(0) - 1))
        def _():
            accum[rows, :] = accum[rows, :] + product(ref)

        @pl.when(step == pl.num_programs(0) - 1)
        def _():
            gate_ref[target, :] = (accum[rows, :] + product(ref)).astype(BF16)


def gate_kernel(
    core_ref, gate_ref, local_ref, bcc_ref, cum_ref, before_ref, before_decay_ref, *refs
):
    earlier, (mine_ref, send_ref, squares_ref, incoming) = refs[:-4], refs[-4:]
    width = local_ref.shape[1]

    @pl.when(pl.program_id(0) == 0)
    def _():
        carried = jnp.zeros((LANES, width), F32)
        for part in earlier:
            state, decay = unpacked(part[...])
            carried = carried * decay + state
        incoming[...] = (carried * before_decay_ref[0:1, :] + before_ref[...]).astype(BF16)

    grown = expand_heads(jnp.exp(cum_ref[...]), width)
    carried = jnp.dot(bcc_ref[:, LANES:], incoming[...], preferred_element_type=F32)
    gated = (local_ref[...].astype(F32) + grown * carried) * silu(gate_ref[...].astype(F32))
    is_own = pl.program_id(0) // 2 == core_ref[0]

    @pl.when(is_own)
    def _():
        mine_ref[...] = gated.astype(BF16)

    @pl.when(jnp.logical_not(is_own))
    def _():
        send_ref[...] = gated.astype(BF16)

    squares = gated * gated
    high = squares.astype(BF16)
    low = (squares - high.astype(F32)).astype(BF16)
    ones = jnp.ones((8, width), BF16)
    across = (((1,), (1,)), ((), ()))
    summed = lax.dot_general(ones, high, across, preferred_element_type=F32) + lax.dot_general(
        ones, low, across, preferred_element_type=F32
    )
    squares_ref[...] = summed[0:1, :]


def norm_kernel(core_ref, mine_ref, other_ref, squares_ref, gain_ref, out_ref):
    half = pl.program_id(0)
    across = jnp.broadcast_to(squares_ref[...], (8, squares_ref.shape[1]))
    scale = lax.rsqrt(across + 1e-05).T[:, 0:1]

    @pl.when(half == core_ref[0])
    def _():
        out_ref[...] = (mine_ref[...].astype(F32) * scale * gain_ref[...]).astype(BF16)

    @pl.when(half != core_ref[0])
    def _():
        out_ref[...] = (other_ref[...].astype(F32) * scale * gain_ref[...]).astype(BF16)


def whole(shape):
    return pl.BlockSpec(shape, lambda i: (0,) * len(shape))


def rows_of(width):
    return pl.BlockSpec((GROUP, width), lambda i: (i, 0))


def params(flops, megabytes, vmem=32):
    return dict(
        compiler_params=pltpu.CompilerParams(vmem_limit_bytes=vmem * 2**20),
        cost_estimate=pl.CostEstimate(
            flops=int(flops), bytes_accessed=megabytes * 2**20, transcendentals=0
        ),
    )


def fixed(a):
    return pl.BlockSpec(a.shape, lambda i, place: (0,) * len(a.shape))


def row_block(width):
    return pl.BlockSpec((GROUP, width), lambda i, place: (i, 0))


def slab_blocks(depth):
    own = pl.BlockSpec((GROUP, depth), lambda i, place: (jnp.clip(i - 2 * place[0], 0, 1), 0))
    other = pl.BlockSpec((GROUP, depth), lambda i, place: (jnp.clip(i - 2 + 2 * place[0], 0, 1), 0))
    return [own, other]


def prepared(place, slabs, weight, conv_bc, bias, rate, heads):
    own, other, before = slabs
    slab, rows, depth = own.shape[0], 2 * own.shape[0], 512
    shape = jax.ShapeDtypeStruct
    outs = [
        shape((rows, 2 * LANES), BF16), shape((rows, LANES), F32), shape((rows, LANES), F32),
        shape((heads, rows), F32), shape((heads, rows), F32), shape((rows, LANES), F32),
        shape((rows // GROUP * 8 + 8, LANES), F32),
    ]
    columns = lambda a: pl.BlockSpec((a.shape[0], depth), lambda i, place: (0, i))
    return pl.pallas_call(
        prepare_kernel,
        grid_spec=pltpu.PrefetchScalarGridSpec(
            num_scalar_prefetch=1,
            grid=(own.shape[1] // depth,),
            in_specs=[columns(a) for a in slabs]
            + [pl.BlockSpec((depth, weight.shape[1]), lambda i, place: (i, 0))]
            + [fixed(a) for a in (conv_bc, bias, rate)],
            out_specs=[fixed(a) for a in outs],
            scratch_shapes=[pltpu.VMEM((HALO + rows, weight.shape[1]), F32)],
        ),
        out_shape=outs,
        name="prepared",
        **params(4e9, 14, 48),
    )(place, *slabs, weight, conv_bc, bias, rate)


def products(place, slabs, weights, done, sums=()):
    own, other, before = slabs
    width, count = weights[0].shape[1], len(weights)
    outs = [
        jax.ShapeDtypeStruct((2 * own.shape[0], width), F32), jax.ShapeDtypeStruct((HALO, width), F32),
    ]
    specs = [row_block(width), fixed(outs[1])]
    sources = all_rows(weights)
    return pl.pallas_call(
        functools.partial(products_kernel, sources, done, count, len(sums) // 2),
        grid_spec=pltpu.PrefetchScalarGridSpec(
            num_scalar_prefetch=1,
            grid=(2 * own.shape[0] // GROUP,),
            in_specs=slab_blocks(own.shape[1])
            + [fixed(a) for a in (before, *weights)]
            + specs[: len(sums)],
            out_specs=specs,
            scratch_shapes=[pltpu.VMEM((sum(size for _, _, size in sources), width), BF16)],
        ),
        out_shape=outs,
        name="more_products" if sums else "first_products",
        **params(5e9, 16, 48),
    )(place, *slabs, *weights, *sums)


def local_states(place, slabs, weights, sources, done, count, sums, bcc, weights_in, decays, conv_x):
    own, other, before = slabs
    rows, width = sums[0].shape
    blocks = rows // GROUP
    outs = [
        jax.ShapeDtypeStruct((rows, width), BF16),
        jax.ShapeDtypeStruct((blocks, LANES, width), BF16),
        jax.ShapeDtypeStruct((LANES + HALO, width), BF16),
    ]
    return pl.pallas_call(
        functools.partial(states_kernel, sources, done, count),
        grid_spec=pltpu.PrefetchScalarGridSpec(
            num_scalar_prefetch=1,
            grid=(blocks,),
            in_specs=slab_blocks(own.shape[1])
            + [fixed(a) for a in (before, *weights)]
            + [
                row_block(width), fixed(sums[1]), row_block(2 * LANES), row_block(LANES),
                fixed(decays), fixed(conv_x),
            ],
            out_specs=[
                row_block(width),
                pl.BlockSpec((1, LANES, width), lambda i, place: (i, 0, 0)),
                fixed(outs[2]),
            ],
            scratch_shapes=[
                pltpu.VMEM((LANES, width), F32), pltpu.VMEM((GROUP, width), F32),
                pltpu.VMEM((HALO, width), F32),
                pltpu.VMEM((sum(size for _, _, size in sources), width), BF16),
            ],
        ),
        out_shape=outs,
        name="states",
        **params(11e9, 18, 40),
    )(place, *slabs, *weights, *sums, bcc, weights_in, decays, conv_x)


def local_outputs(xc, bcc, cum, cum_t, step_t, entering, skip):
    rows, width = xc.shape
    heads = cum_t.shape[0]
    by_lane = pl.BlockSpec((heads, GROUP), lambda i: (0, i))
    return pl.pallas_call(
        outputs_kernel,
        grid=(rows // GROUP,),
        in_specs=[
            rows_of(width), rows_of(2 * LANES), rows_of(LANES), by_lane, by_lane,
            pl.BlockSpec((1, LANES, width), lambda i: (i, 0, 0)), whole((1, width)),
        ],
        out_specs=rows_of(width),
        out_shape=jax.ShapeDtypeStruct((rows, width), BF16),
        scratch_shapes=[pltpu.VMEM((GROUP, width), F32)],
        compiler_params=pltpu.CompilerParams(vmem_limit_bytes=32 * 2**20),
        cost_estimate=pl.CostEstimate(flops=10**10, bytes_accessed=10 * 2**20, transcendentals=4 * 2**20),
        name="outputs",
    )(xc, bcc, cum, cum_t, step_t, entering, skip)


def project_gate(place, slabs, weight):
    own, other, _ = slabs
    rows, width, depth = 2 * own.shape[0], weight.shape[1] // 2, 1024
    columns = pl.BlockSpec((own.shape[0], depth), lambda i, place: (0, i))
    out = jax.ShapeDtypeStruct((rows, width), BF16)
    return pl.pallas_call(
        z_kernel,
        grid_spec=pltpu.PrefetchScalarGridSpec(
            num_scalar_prefetch=1,
            grid=(weight.shape[0] // depth,),
            in_specs=[columns, columns, pl.BlockSpec((depth, width), lambda i, place: (i, place[0]))],
            out_specs=fixed(out),
            scratch_shapes=[pltpu.VMEM((rows, width), F32)],
        ),
        out_shape=out,
        name="project_gate",
        **params(9e9, 20, 48),
    )(place, own, other, weight)


def gate_outputs(core, gate, local, bcc, cum_slab, before, before_decay, earlier):
    rows, width = local.shape
    half = jax.ShapeDtypeStruct((rows // 2, width), BF16)
    return pl.pallas_call(
        gate_kernel,
        grid_spec=pltpu.PrefetchScalarGridSpec(
            num_scalar_prefetch=1,
            grid=(rows // GROUP,),
            in_specs=[row_block(width), row_block(width), row_block(2 * LANES), row_block(LANES)]
            + [fixed(a) for a in (before, before_decay, *earlier)],
            out_specs=slab_blocks(width) + [pl.BlockSpec((1, GROUP), lambda i, place: (0, i))],
            scratch_shapes=[pltpu.VMEM((LANES, width), BF16)],
        ),
        out_shape=[half, half, jax.ShapeDtypeStruct((1, rows), F32)],
        name="gate",
        **params(1e9, 10, 60),
    )(core, gate, local, bcc, cum_slab, before, before_decay, *earlier)


def normalized(core, gated, other, mean_squares, gain):
    rows, width = other.shape
    return pl.pallas_call(
        norm_kernel,
        grid_spec=pltpu.PrefetchScalarGridSpec(
            num_scalar_prefetch=1,
            grid=(2,),
            in_specs=[
                pl.BlockSpec((rows, width), lambda j, core: (0, 0)),
                pl.BlockSpec((rows, width), lambda j, core: (0, 0)),
                pl.BlockSpec((1, rows), lambda j, core: (0, 0)),
                pl.BlockSpec((1, width), lambda j, core: (0, j)),
            ],
            out_specs=pl.BlockSpec((rows, width), lambda j, core: (0, j)),
        ),
        out_shape=jax.ShapeDtypeStruct((rows, 2 * width), BF16),
        compiler_params=pltpu.CompilerParams(vmem_limit_bytes=32 * 2**20),
        cost_estimate=pl.CostEstimate(flops=10**7, bytes_accessed=4 * 2**20, transcendentals=0),
        name="normalized",
    )(core.astype(jnp.int32)[None], gated, other, mean_squares, gain)


def earlier_states(final):
    size = lax.axis_size("y")
    parts = [final] + [round_ring(final, "y", distance) for distance in range(1, size)]
    width = final.shape[1]
    outs = [
        jax.ShapeDtypeStruct(final.shape, BF16),
        jax.ShapeDtypeStruct((LANES, width), F32),
        jax.ShapeDtypeStruct((8, width), F32),
    ]
    total, before, before_decay = pl.pallas_call(
        row_kernel,
        grid_spec=pltpu.PrefetchScalarGridSpec(
            num_scalar_prefetch=1,
            grid=(1,),
            in_specs=[fixed(a) for a in parts],
            out_specs=[fixed(a) for a in outs],
        ),
        out_shape=outs,
        name="row_states",
        **params(1e7, 2),
    )(lax.axis_index("y").astype(jnp.int32)[None], *parts)
    rows = lax.axis_size("z")
    earlier = [
        lax.ppermute(total, "z", [(i, i + distance) for i in range(rows - distance)])
        for distance in range(rows - 1, 0, -1)
    ]
    return before, before_decay, earlier


def tied(values, *to):
    return lax.optimization_barrier((*values, *to))[: len(values)]


def travelling(own, before_third, before_last):
    y_less, y_more = round_ring(own, "y", 1), round_ring(own, "y", -1)
    z_less, z_more = round_ring(own, "z", 1), round_ring(own, "z", -1)
    nearest = [own, y_less, y_more, z_less, z_more]
    second = [
        round_ring(y_less, "y", 1), round_ring(z_more, "z", -1),
        round_ring(z_more, "y", -1), round_ring(y_more, "z", 1),
    ]
    y_far, z_far, *_ = tied(second, *before_third(nearest))
    far = [
        round_ring(z_far, "y", -1), round_ring(z_far, "y", 1),
        round_ring(y_far, "z", 1), round_ring(y_far, "z", -1),
    ]
    held_z, held_y, last, *_ = tied((z_less, y_less, *far), *before_last())
    less_less, less_more = round_ring(held_z, "y", 1), round_ring(held_y, "z", -1)
    return nearest, second, [*far, less_less, less_more, round_ring(last, "y", -1)]


def all_rows(blocks):
    return [(index, 0, block.shape[0]) for index, block in enumerate(blocks)]


def block_order():
    places = (
        ((0, 0), (-1, 0), (1, 0), (0, -1), (0, 1), (2, 0), (0, 2), (1, 1), (1, -1))
        + ((1, 2), (-1, 2), (2, -1), (2, 1), (-1, -1), (-1, 1), (2, 2))
    )
    y, z = lax.axis_index("y"), lax.axis_index("z")
    return [(z + dz) % 4 * 4 + (y + dy) % 4 for dy, dz in places]


def shards(
    tokens, x_weight, z_weight, bc_weight, dt_weight, conv_x, conv_bc, dt_bias, decay_rate, skip,
    norm_gain,
):
    core = lax.axis_index("core")
    width = x_weight.shape[1] // 2
    heads = dt_weight.shape[1] // 2

    def mine(a, axis):
        size = a.shape[axis] // 2
        return lax.dynamic_slice_in_dim(a, core * size, size, axis)

    def others(a, axis):
        size = a.shape[axis] // 2
        return lax.dynamic_slice_in_dim(a, (1 - core) * size, size, axis)

    def per_lane(a):
        return jnp.pad(mine(a, 0), (0, LANES - heads))[None, :]

    narrow = jnp.concatenate(
        [bc_weight, dt_weight, jnp.zeros((bc_weight.shape[0], LANES - 2 * heads), BF16)], axis=1
    )
    narrow = lax.all_gather(narrow, ("z", "y", "core"), axis=0, tiled=True)
    own_block = jnp.concatenate([mine(x_weight, 1), swap_cores(others(x_weight, 1))], axis=0)
    place = jnp.stack([core, *block_order()]).astype(jnp.int32)
    slabs, sums, early = [], [], []

    def before_third(blocks):
        (rows,) = tied((tokens,), *blocks[1:])
        chips = lax.axis_size("z") * lax.axis_size("y")
        to_next = lambda target: lax.ppermute(
            rows[-HALO:], ("z", "y", "core"),
            [(2 * i + 1, 2 * i + 2 + target) for i in range(chips - 1)],
        )
        slabs.extend((rows, swap_cores(rows), to_next(0) + to_next(1)))
        sums.extend(products(place, slabs, blocks, 0))
        return sums[:1]

    def before_last():
        early.extend(
            prepared(place, slabs, narrow, conv_bc, per_lane(dt_bias), per_lane(decay_rate), heads)
        )
        return early[:1]

    nearest, second, blocks = travelling(own_block, before_third, before_last)
    (z_rows,) = tied((z_weight,), own_block)
    z_whole = lax.all_gather(z_rows, ("z", "y", "core"), axis=0, tiled=True)
    sums = products(place, slabs, second, len(nearest), sums)
    bcc, cum, cum_slab, cum_t, step_t, weights_in, decays = early
    xc, entering, final = local_states(
        place, slabs, blocks, all_rows(blocks), 9, 7, sums, bcc, weights_in, decays, mine(conv_x, 1)
    )
    before, before_decay, earlier = earlier_states(final)
    skip_lanes = jnp.repeat(mine(skip, 0), HEAD)[None, :]
    local = local_outputs(xc, bcc, cum, cum_t, step_t, entering, skip_lanes)
    gate = project_gate(place, slabs, z_whole)
    gated, send, squares = gate_outputs(place[:1], gate, local, bcc, cum_slab, before, before_decay, earlier)

    other = swap_cores(send)
    summed = mine(squares + swap_cores(squares), 1)
    across = [round_ring(summed, "x", distance) for distance in range(1, lax.axis_size("x"))]
    mean_squares = (summed + sum(across)) / (2 * width * lax.axis_size("x"))
    return normalized(core, gated, other, mean_squares, norm_gain[None, :])


def solution(mesh):
    fine = Mesh(mesh.devices.reshape(4, 4, 2, 4), ("z", "y", "core", "x"))
    ctx = ("z", "y", "core")
    placed = (
        P(ctx, None),
        P(ctx, "x"),
        P(ctx, "x"),
        P(ctx, None),
        P(ctx, "x"),
        P(None, "x"),
        P(),
        P("x"),
        P("x"),
        P("x"),
        P("x"),
    )
    return jax.shard_map(
        shards, mesh=fine, in_specs=placed, out_specs=P(ctx, "x"), check_vma=False
    )
```

```python
import functools

import jax
import jax.numpy as jnp
from jax import lax
from jax.experimental import pallas as pl
from jax.experimental.pallas import tpu as pltpu
from jax.sharding import Mesh, PartitionSpec as P

GROUP = 256
HALO = 16
LANES = 128
HEAD = 64
F32 = jnp.float32
BF16 = jnp.bfloat16


def swap_cores(a):
    return lax.ppermute(a, "core", [(0, 1), (1, 0)])


def round_ring(a, axis, distance):
    size = lax.axis_size(axis)
    return lax.ppermute(a, axis, [(i, (i + distance) % size) for i in range(size)])


def along_chips(a, distance):
    chips = lax.axis_size("z") * lax.axis_size("y")
    return lax.ppermute(a, ("z", "y"), [(i, i + distance) for i in range(chips - distance)])


def in_core_order(core, mine, other, axis):
    first = jnp.where(core == 0, mine, other)
    second = jnp.where(core == 0, other, mine)
    return jnp.concatenate([first, second], axis=axis)


def expand_heads(values, width):
    heads = width // HEAD
    high = values.astype(BF16).astype(F32)
    rest = values - high
    middle = rest.astype(BF16).astype(F32)
    low = rest - middle
    lane = lax.broadcasted_iota(jnp.int32, values.shape, 1)
    parts = jnp.where(lane < heads, high, pltpu.roll(middle, heads, axis=1))
    parts = jnp.where(lane < 2 * heads, parts, pltpu.roll(low, 2 * heads, axis=1))
    parts = jnp.where(lane < 3 * heads, parts, 0.0).astype(BF16)
    row = lax.broadcasted_iota(jnp.int32, (LANES, width), 0)
    col = lax.broadcasted_iota(jnp.int32, (LANES, width), 1)
    head = row % heads
    spread = (col >= head * HEAD) & (col < head * HEAD + HEAD) & (row < 3 * heads)
    return jnp.dot(parts, spread.astype(BF16), preferred_element_type=F32)


def silu(a):
    half = 0.5 * a
    return half + half * jnp.tanh(half)


def conv_rows(rows, kernel_ref):
    taps, count = kernel_ref.shape[0], rows.shape[0] - HALO
    first = HALO - (taps - 1)
    accum = kernel_ref[0:1, :] * rows[first : first + count]
    for tap in range(1, taps):
        accum = accum + kernel_ref[tap : tap + 1, :] * rows[first + tap : first + tap + count]
    return silu(accum).astype(BF16)


def prepare_kernel(
    place_ref, own_ref, other_ref, before_ref, weight_ref, conv_ref, bias_ref, rate_ref,
    bcc_ref, cum_ref, cum_slab_ref, cum_t_ref, step_t_ref, weights_in_ref, decays_ref,
    accum,
):
    step = pl.program_id(0)
    core = place_ref[0]
    slab = own_ref.shape[0]
    heads = cum_t_ref.shape[0]
    rows_own = pl.ds(pl.multiple_of(HALO + slab * core, HALO), slab)
    rows_other = pl.ds(pl.multiple_of(HALO + slab * (1 - core), HALO), slab)

    @pl.when(step == 0)
    def _():
        accum[...] = jnp.zeros_like(accum)

    weight = weight_ref[...]
    for rows, ref in ((slice(0, HALO), before_ref), (rows_own, own_ref), (rows_other, other_ref)):
        accum[rows, :] = accum[rows, :] + jnp.dot(ref[...], weight, preferred_element_type=F32)

    @pl.when(step == pl.num_programs(0) - 1)
    def _():
        total = jnp.zeros((1, LANES), F32)
        row = lax.broadcasted_iota(jnp.int32, (GROUP, GROUP), 0)
        col = lax.broadcasted_iota(jnp.int32, (GROUP, GROUP), 1)
        lower = (row >= col).astype(F32)
        for block in range(2 * slab // GROUP):
            part = slice(block * GROUP, (block + 1) * GROUP)
            narrow = accum[block * GROUP : (block + 1) * GROUP + HALO, : 2 * LANES]
            bcc_ref[part, :] = conv_rows(narrow.astype(BF16).astype(F32), conv_ref)
            raw = accum[block * GROUP + HALO : (block + 1) * GROUP + HALO, 2 * LANES :]
            raw = jnp.where(core == 0, raw, pltpu.roll(raw, LANES - heads, axis=1))
            raw = raw + bias_ref[...]
            step_size = jnp.maximum(raw, 0.0) + jnp.log1p(jnp.exp(-jnp.abs(raw)))
            log_decay = -rate_ref[...] * step_size
            cum = jnp.dot(
                lower, log_decay, preferred_element_type=F32, precision=lax.Precision.HIGHEST
            )
            last = cum[GROUP - 1 : GROUP, :]
            cum_ref[part, :] = cum
            cum_slab_ref[part, :] = cum + total
            cum_t_ref[:, part] = cum.T[:heads, :]
            step_t_ref[:, part] = step_size.T[:heads, :]
            weights_in_ref[part, :] = jnp.exp(last - cum) * step_size
            decays_ref[block * 8 : block * 8 + 8, :] = jnp.broadcast_to(jnp.exp(last), (8, LANES))
            total = total + last
        end = decays_ref.shape[0] - 8
        decays_ref[end:, :] = jnp.broadcast_to(jnp.exp(total), (8, LANES))


def block_columns(ref, place_ref, first, count):
    core = place_ref[0]
    parts = []
    for index in range(first, first + count):
        base = place_ref[1 + index] * (2 * LANES)
        for start in (base + LANES * core, base + LANES * (1 - core)):
            parts.append(ref[:, pl.ds(pl.multiple_of(start, LANES), LANES)])
    return jnp.concatenate(parts, axis=1)


def stacked(sources, refs):
    return jnp.concatenate([refs[ref][first : first + size, :] for ref, first, size in sources], axis=0)


def products_kernel(sources, done, count, started, place_ref, own_ref, other_ref, before_ref, *refs):
    weights, sums, (out_ref, out_before_ref, wide) = refs[: -3 - 2 * started], refs[-3 - 2 * started : -3], refs[-3:]
    block = pl.program_id(0)
    is_own = block // 2 == place_ref[0]

    def product(ref):
        columns = block_columns(ref, place_ref, done, count)
        return jnp.dot(columns, wide[...], preferred_element_type=F32)

    @pl.when(block == 0)
    def _():
        row = 0
        for ref, first, size in sources:
            wide[row : row + size, :] = weights[ref][first : first + size, :]
            row += size
        added = product(before_ref)
        out_before_ref[...] = sums[1][...] + added if started else added

    @pl.when(is_own)
    def _():
        added = product(own_ref)
        out_ref[...] = sums[0][...] + added if started else added

    @pl.when(jnp.logical_not(is_own))
    def _():
        added = product(other_ref)
        out_ref[...] = sums[0][...] + added if started else added


def states_kernel(
    sources, done, count, place_ref, own_ref, other_ref, before_ref, *refs
):
    weights = refs[:-13]
    (
        sum_ref, sum_before_ref, bcc_ref, weights_in_ref, decays_ref, conv_ref,
        xc_ref, entering_ref, final_ref,
        state, x_in, tail, wide,
    ) = refs[-13:]
    block = pl.program_id(0)
    width = x_in.shape[1]
    is_own = block // 2 == place_ref[0]

    def product(ref):
        columns = block_columns(ref, place_ref, done, count)
        return jnp.dot(columns, wide[...], preferred_element_type=F32)

    @pl.when(block == 0)
    def _():
        state[...] = jnp.zeros_like(state)
        row = 0
        for ref, first, size in sources:
            wide[row : row + size, :] = weights[ref][first : first + size, :]
            row += size
        tail[...] = (sum_before_ref[...] + product(before_ref)).astype(BF16).astype(F32)

    @pl.when(is_own)
    def _():
        x_in[...] = (sum_ref[...] + product(own_ref)).astype(BF16).astype(F32)

    @pl.when(jnp.logical_not(is_own))
    def _():
        x_in[...] = (sum_ref[...] + product(other_ref)).astype(BF16).astype(F32)

    rows = jnp.concatenate([tail[...], x_in[...]], axis=0)
    tail[...] = rows[GROUP:]
    xc = conv_rows(rows, conv_ref)
    xc_ref[...] = xc
    entering_ref[0] = state[...].astype(BF16)
    weighted = (expand_heads(weights_in_ref[...], width) * xc.astype(F32)).astype(BF16)
    contrib = lax.dot_general(
        bcc_ref[:, :LANES], weighted, (((0,), (0,)), ((), ())), preferred_element_type=F32
    )
    decay = expand_heads(decays_ref[pl.ds(pl.multiple_of(block * 8, 8), 8), :], width)
    state[...] = state[...] * decay[0:1] + contrib

    @pl.when(block == pl.num_programs(0) - 1)
    def _():
        end = decays_ref.shape[0] - 8
        final_ref[:LANES, :] = state[...].astype(BF16)
        final_ref[LANES:, :] = split_decay(expand_heads(decays_ref[end:, :], width)[0:1])


def split_decay(decay):
    high = decay.astype(BF16)
    low = decay - high.astype(F32)
    row = lax.broadcasted_iota(jnp.int32, (HALO, decay.shape[1]), 0)
    return jnp.where(row == 0, high.astype(F32), jnp.where(row == 1, low, 0.0)).astype(BF16)


def unpacked(sent):
    sent = sent.astype(F32)
    return sent[:LANES], sent[LANES : LANES + 1] + sent[LANES + 1 : LANES + 2]


def row_kernel(place_ref, *refs):
    size = len(refs) - 3
    parts, (total_ref, before_ref, before_decay_ref) = refs[:size], refs[size:]
    place = place_ref[0]
    width = total_ref.shape[1]
    total, decay = jnp.zeros((LANES, width), F32), jnp.ones((1, width), F32)
    before_ref[...] = total
    before_decay_ref[...] = jnp.broadcast_to(decay, before_decay_ref.shape)
    for index in range(size):
        if index > 0:

            @pl.when(place == index)
            def _():
                before_ref[...] = total
                before_decay_ref[...] = jnp.broadcast_to(decay, before_decay_ref.shape)

        distance = (place - index + size) % size
        chosen = parts[0][...]
        for other in range(1, size):
            chosen = jnp.where(distance == other, parts[other][...], chosen)
        state, state_decay = unpacked(chosen)
        total = total * state_decay + state
        decay = decay * state_decay
    total_ref[:LANES, :] = total.astype(BF16)
    total_ref[LANES:, :] = split_decay(decay)


def outputs_kernel(xc_ref, bcc_ref, cum_ref, cum_t_ref, step_t_ref, entering_ref, skip_ref, out_ref, carried):
    width = xc_ref.shape[1]
    b_rows, c_rows = bcc_ref[:, :LANES], bcc_ref[:, LANES:]
    scores = lax.dot_general(c_rows, b_rows, (((1,), (1,)), ((), ())), preferred_element_type=F32)
    row = lax.broadcasted_iota(jnp.int32, (GROUP, GROUP), 0)
    col = lax.broadcasted_iota(jnp.int32, (GROUP, GROUP), 1)
    scores = jnp.where(row >= col, scores, 0.0)
    cum = cum_ref[...]
    grown = expand_heads(jnp.exp(cum), width)
    carried[...] = grown * jnp.dot(c_rows, entering_ref[0], preferred_element_type=F32)
    lane = lax.broadcasted_iota(jnp.int32, (GROUP, LANES), 1)

    def mixing(head):
        gaps = cum[:, head : head + 1] - cum_t_ref[head : head + 1, :]
        return (
            scores * jnp.exp(jnp.minimum(gaps, 0.0)) * step_t_ref[head : head + 1, :]
        ).astype(BF16)

    for pair in range(width // LANES):
        lanes = slice(pair * LANES, (pair + 1) * LANES)
        inputs = xc_ref[:, lanes]
        zero = jnp.zeros_like(inputs)
        both = jnp.concatenate([mixing(2 * pair), mixing(2 * pair + 1)], axis=1)
        stacked = jnp.concatenate(
            [jnp.where(lane < HEAD, inputs, zero), jnp.where(lane < HEAD, zero, inputs)], axis=0
        )
        out_ref[:, lanes] = (
            carried[:, lanes]
            + jnp.dot(both, stacked, preferred_element_type=F32)
            + skip_ref[:, lanes] * inputs.astype(F32)
        ).astype(BF16)


def z_kernel(place_ref, own_ref, other_ref, weight_ref, gate_ref, accum):
    step = pl.program_id(0)
    slab = own_ref.shape[0]
    core = place_ref[0]

    def product(ref):
        return jnp.dot(ref[...], weight_ref[...], preferred_element_type=F32)

    for index, ref in enumerate((own_ref, other_ref)):
        rows = slice(index * slab, (index + 1) * slab)
        target = pl.ds(pl.multiple_of(slab * (core if index == 0 else 1 - core), slab), slab)

        @pl.when(step == 0)
        def _():
            accum[rows, :] = product(ref)

        @pl.when((step > 0) & (step < pl.num_programs(0) - 1))
        def _():
            accum[rows, :] = accum[rows, :] + product(ref)

        @pl.when(step == pl.num_programs(0) - 1)
        def _():
            gate_ref[target, :] = (accum[rows, :] + product(ref)).astype(BF16)


def gate_kernel(
    core_ref, gate_ref, local_ref, bcc_ref, cum_ref, before_ref, before_decay_ref, *refs
):
    earlier, (mine_ref, send_ref, squares_ref, incoming) = refs[:-4], refs[-4:]
    width = local_ref.shape[1]

    @pl.when(pl.program_id(0) == 0)
    def _():
        carried = jnp.zeros((LANES, width), F32)
        for part in earlier:
            state, decay = unpacked(part[...])
            carried = carried * decay + state
        incoming[...] = (carried * before_decay_ref[0:1, :] + before_ref[...]).astype(BF16)

    grown = expand_heads(jnp.exp(cum_ref[...]), width)
    carried = jnp.dot(bcc_ref[:, LANES:], incoming[...], preferred_element_type=F32)
    gated = (local_ref[...].astype(F32) + grown * carried) * silu(gate_ref[...].astype(F32))
    is_own = pl.program_id(0) // 2 == core_ref[0]

    @pl.when(is_own)
    def _():
        mine_ref[...] = gated.astype(BF16)

    @pl.when(jnp.logical_not(is_own))
    def _():
        send_ref[...] = gated.astype(BF16)

    squares = gated * gated
    high = squares.astype(BF16)
    low = (squares - high.astype(F32)).astype(BF16)
    ones = jnp.ones((8, width), BF16)
    across = (((1,), (1,)), ((), ()))
    summed = lax.dot_general(ones, high, across, preferred_element_type=F32) + lax.dot_general(
        ones, low, across, preferred_element_type=F32
    )
    squares_ref[...] = summed[0:1, :]


def norm_kernel(core_ref, mine_ref, other_ref, squares_ref, gain_ref, out_ref):
    half = pl.program_id(0)
    across = jnp.broadcast_to(squares_ref[...], (8, squares_ref.shape[1]))
    scale = lax.rsqrt(across + 1e-05).T[:, 0:1]

    @pl.when(half == core_ref[0])
    def _():
        out_ref[...] = (mine_ref[...].astype(F32) * scale * gain_ref[...]).astype(BF16)

    @pl.when(half != core_ref[0])
    def _():
        out_ref[...] = (other_ref[...].astype(F32) * scale * gain_ref[...]).astype(BF16)


def whole(shape):
    return pl.BlockSpec(shape, lambda i: (0,) * len(shape))


def rows_of(width):
    return pl.BlockSpec((GROUP, width), lambda i: (i, 0))


def params(flops, megabytes, vmem=32):
    return dict(
        compiler_params=pltpu.CompilerParams(vmem_limit_bytes=vmem * 2**20),
        cost_estimate=pl.CostEstimate(
            flops=int(flops), bytes_accessed=megabytes * 2**20, transcendentals=0
        ),
    )


def fixed(a):
    return pl.BlockSpec(a.shape, lambda i, place: (0,) * len(a.shape))


def row_block(width):
    return pl.BlockSpec((GROUP, width), lambda i, place: (i, 0))


def slab_blocks(depth):
    own = pl.BlockSpec((GROUP, depth), lambda i, place: (jnp.clip(i - 2 * place[0], 0, 1), 0))
    other = pl.BlockSpec((GROUP, depth), lambda i, place: (jnp.clip(i - 2 + 2 * place[0], 0, 1), 0))
    return [own, other]


def prepared(place, slabs, weight, conv_bc, bias, rate, heads):
    own, other, before = slabs
    slab, rows, depth = own.shape[0], 2 * own.shape[0], 512
    shape = jax.ShapeDtypeStruct
    outs = [
        shape((rows, 2 * LANES), BF16), shape((rows, LANES), F32), shape((rows, LANES), F32),
        shape((heads, rows), F32), shape((heads, rows), F32), shape((rows, LANES), F32),
        shape((rows // GROUP * 8 + 8, LANES), F32),
    ]
    columns = lambda a: pl.BlockSpec((a.shape[0], depth), lambda i, place: (0, i))
    return pl.pallas_call(
        prepare_kernel,
        grid_spec=pltpu.PrefetchScalarGridSpec(
            num_scalar_prefetch=1,
            grid=(own.shape[1] // depth,),
            in_specs=[columns(a) for a in slabs]
            + [pl.BlockSpec((depth, weight.shape[1]), lambda i, place: (i, 0))]
            + [fixed(a) for a in (conv_bc, bias, rate)],
            out_specs=[fixed(a) for a in outs],
            scratch_shapes=[pltpu.VMEM((HALO + rows, weight.shape[1]), F32)],
        ),
        out_shape=outs,
        name="prepared",
        **params(4e9, 14, 60),
    )(place, *slabs, weight, conv_bc, bias, rate)


def products(place, slabs, weights, done, sums=()):
    own, other, before = slabs
    width, count = weights[0].shape[1], len(weights)
    outs = [
        jax.ShapeDtypeStruct((2 * own.shape[0], width), F32), jax.ShapeDtypeStruct((HALO, width), F32),
    ]
    specs = [row_block(width), fixed(outs[1])]
    sources = all_rows(weights)
    return pl.pallas_call(
        functools.partial(products_kernel, sources, done, count, len(sums) // 2),
        grid_spec=pltpu.PrefetchScalarGridSpec(
            num_scalar_prefetch=1,
            grid=(2 * own.shape[0] // GROUP,),
            in_specs=slab_blocks(own.shape[1])
            + [fixed(a) for a in (before, *weights)]
            + specs[: len(sums)],
            out_specs=specs,
            scratch_shapes=[pltpu.VMEM((sum(size for _, _, size in sources), width), BF16)],
        ),
        out_shape=outs,
        name="more_products" if sums else "first_products",
        **params(5e9, 16, 48),
    )(place, *slabs, *weights, *sums)


def local_states(place, slabs, weights, sources, done, count, sums, bcc, weights_in, decays, conv_x):
    own, other, before = slabs
    rows, width = sums[0].shape
    blocks = rows // GROUP
    outs = [
        jax.ShapeDtypeStruct((rows, width), BF16),
        jax.ShapeDtypeStruct((blocks, LANES, width), BF16),
        jax.ShapeDtypeStruct((LANES + HALO, width), BF16),
    ]
    return pl.pallas_call(
        functools.partial(states_kernel, sources, done, count),
        grid_spec=pltpu.PrefetchScalarGridSpec(
            num_scalar_prefetch=1,
            grid=(blocks,),
            in_specs=slab_blocks(own.shape[1])
            + [fixed(a) for a in (before, *weights)]
            + [
                row_block(width), fixed(sums[1]), row_block(2 * LANES), row_block(LANES),
                fixed(decays), fixed(conv_x),
            ],
            out_specs=[
                row_block(width),
                pl.BlockSpec((1, LANES, width), lambda i, place: (i, 0, 0)),
                fixed(outs[2]),
            ],
            scratch_shapes=[
                pltpu.VMEM((LANES, width), F32), pltpu.VMEM((GROUP, width), F32),
                pltpu.VMEM((HALO, width), F32),
                pltpu.VMEM((sum(size for _, _, size in sources), width), BF16),
            ],
        ),
        out_shape=outs,
        name="states",
        **params(11e9, 18, 40),
    )(place, *slabs, *weights, *sums, bcc, weights_in, decays, conv_x)


def local_outputs(xc, bcc, cum, cum_t, step_t, entering, skip):
    rows, width = xc.shape
    heads = cum_t.shape[0]
    by_lane = pl.BlockSpec((heads, GROUP), lambda i: (0, i))
    return pl.pallas_call(
        outputs_kernel,
        grid=(rows // GROUP,),
        in_specs=[
            rows_of(width), rows_of(2 * LANES), rows_of(LANES), by_lane, by_lane,
            pl.BlockSpec((1, LANES, width), lambda i: (i, 0, 0)), whole((1, width)),
        ],
        out_specs=rows_of(width),
        out_shape=jax.ShapeDtypeStruct((rows, width), BF16),
        scratch_shapes=[pltpu.VMEM((GROUP, width), F32)],
        compiler_params=pltpu.CompilerParams(vmem_limit_bytes=32 * 2**20),
        cost_estimate=pl.CostEstimate(flops=10**10, bytes_accessed=10 * 2**20, transcendentals=4 * 2**20),
        name="outputs",
    )(xc, bcc, cum, cum_t, step_t, entering, skip)


def project_gate(place, slabs, weight):
    own, other, _ = slabs
    rows, width, depth = 2 * own.shape[0], weight.shape[1] // 2, 1024
    columns = pl.BlockSpec((own.shape[0], depth), lambda i, place: (0, i))
    out = jax.ShapeDtypeStruct((rows, width), BF16)
    return pl.pallas_call(
        z_kernel,
        grid_spec=pltpu.PrefetchScalarGridSpec(
            num_scalar_prefetch=1,
            grid=(weight.shape[0] // depth,),
            in_specs=[columns, columns, pl.BlockSpec((depth, width), lambda i, place: (i, place[0]))],
            out_specs=fixed(out),
            scratch_shapes=[pltpu.VMEM((rows, width), F32)],
        ),
        out_shape=out,
        name="project_gate",
        **params(9e9, 20, 48),
    )(place, own, other, weight)


def gate_outputs(core, gate, local, bcc, cum_slab, before, before_decay, earlier):
    rows, width = local.shape
    half = jax.ShapeDtypeStruct((rows // 2, width), BF16)
    return pl.pallas_call(
        gate_kernel,
        grid_spec=pltpu.PrefetchScalarGridSpec(
            num_scalar_prefetch=1,
            grid=(rows // GROUP,),
            in_specs=[row_block(width), row_block(width), row_block(2 * LANES), row_block(LANES)]
            + [fixed(a) for a in (before, before_decay, *earlier)],
            out_specs=slab_blocks(width) + [pl.BlockSpec((1, GROUP), lambda i, place: (0, i))],
            scratch_shapes=[pltpu.VMEM((LANES, width), BF16)],
        ),
        out_shape=[half, half, jax.ShapeDtypeStruct((1, rows), F32)],
        name="gate",
        **params(1e9, 10, 60),
    )(core, gate, local, bcc, cum_slab, before, before_decay, *earlier)


def normalized(core, gated, other, mean_squares, gain):
    rows, width = other.shape
    return pl.pallas_call(
        norm_kernel,
        grid_spec=pltpu.PrefetchScalarGridSpec(
            num_scalar_prefetch=1,
            grid=(2,),
            in_specs=[
                pl.BlockSpec((rows, width), lambda j, core: (0, 0)),
                pl.BlockSpec((rows, width), lambda j, core: (0, 0)),
                pl.BlockSpec((1, rows), lambda j, core: (0, 0)),
                pl.BlockSpec((1, width), lambda j, core: (0, j)),
            ],
            out_specs=pl.BlockSpec((rows, width), lambda j, core: (0, j)),
        ),
        out_shape=jax.ShapeDtypeStruct((rows, 2 * width), BF16),
        compiler_params=pltpu.CompilerParams(vmem_limit_bytes=32 * 2**20),
        cost_estimate=pl.CostEstimate(flops=10**7, bytes_accessed=4 * 2**20, transcendentals=0),
        name="normalized",
    )(core.astype(jnp.int32)[None], gated, other, mean_squares, gain)


def earlier_states(final):
    size = lax.axis_size("y")
    parts = [final] + [round_ring(final, "y", distance) for distance in range(1, size)]
    width = final.shape[1]
    outs = [
        jax.ShapeDtypeStruct(final.shape, BF16),
        jax.ShapeDtypeStruct((LANES, width), F32),
        jax.ShapeDtypeStruct((8, width), F32),
    ]
    total, before, before_decay = pl.pallas_call(
        row_kernel,
        grid_spec=pltpu.PrefetchScalarGridSpec(
            num_scalar_prefetch=1,
            grid=(1,),
            in_specs=[fixed(a) for a in parts],
            out_specs=[fixed(a) for a in outs],
        ),
        out_shape=outs,
        name="row_states",
        **params(1e7, 2),
    )(lax.axis_index("y").astype(jnp.int32)[None], *parts)
    rows = lax.axis_size("z")
    earlier = [
        lax.ppermute(total, "z", [(i, i + distance) for i in range(rows - distance)])
        for distance in range(rows - 1, 0, -1)
    ]
    return before, before_decay, earlier


def tied(values, *to):
    return lax.optimization_barrier((*values, *to))[: len(values)]


def travelling(own, before_third, before_last):
    y_less, y_more = round_ring(own, "y", 1), round_ring(own, "y", -1)
    z_less, z_more = round_ring(own, "z", 1), round_ring(own, "z", -1)
    nearest = [own, y_less, y_more, z_less, z_more]
    second = [
        round_ring(y_less, "y", 1), round_ring(z_more, "z", -1),
        round_ring(z_more, "y", -1), round_ring(y_more, "z", 1),
    ]
    y_far, z_far, _, _, held_z, held_y = tied((*second, z_less, y_less), *before_third(nearest))
    less_less = round_ring(held_z, "y", 1)
    far = [
        round_ring(z_far, "y", -1), round_ring(z_far, "y", 1),
        round_ring(y_far, "z", 1), round_ring(y_far, "z", -1),
    ]
    held_y, last, *_ = tied((held_y, *far), *before_last())
    less_more = round_ring(held_y, "z", -1)
    return nearest, second, [*far, less_less, less_more, round_ring(last, "y", -1)]


def all_rows(blocks):
    return [(index, 0, block.shape[0]) for index, block in enumerate(blocks)]


def block_order():
    places = (
        ((0, 0), (-1, 0), (1, 0), (0, -1), (0, 1), (2, 0), (0, 2), (1, 1), (1, -1))
        + ((1, 2), (-1, 2), (2, -1), (2, 1), (-1, -1), (-1, 1), (2, 2))
    )
    y, z = lax.axis_index("y"), lax.axis_index("z")
    return [(z + dz) % 4 * 4 + (y + dy) % 4 for dy, dz in places]


def shards(
    tokens, x_weight, z_weight, bc_weight, dt_weight, conv_x, conv_bc, dt_bias, decay_rate, skip,
    norm_gain,
):
    core = lax.axis_index("core")
    width = x_weight.shape[1] // 2
    heads = dt_weight.shape[1] // 2

    def mine(a, axis):
        size = a.shape[axis] // 2
        return lax.dynamic_slice_in_dim(a, core * size, size, axis)

    def others(a, axis):
        size = a.shape[axis] // 2
        return lax.dynamic_slice_in_dim(a, (1 - core) * size, size, axis)

    def per_lane(a):
        return jnp.pad(mine(a, 0), (0, LANES - heads))[None, :]

    narrow = jnp.concatenate(
        [bc_weight, dt_weight, jnp.zeros((bc_weight.shape[0], LANES - 2 * heads), BF16)], axis=1
    )
    narrow = lax.all_gather(narrow, ("z", "y", "core"), axis=0, tiled=True)
    own_block = jnp.concatenate([mine(x_weight, 1), swap_cores(others(x_weight, 1))], axis=0)
    place = jnp.stack([core, *block_order()]).astype(jnp.int32)
    slabs, sums, early = [], [], []

    def before_third(blocks):
        (rows,) = tied((tokens,), *blocks[1:])
        chips = lax.axis_size("z") * lax.axis_size("y")
        to_next = lambda target: lax.ppermute(
            rows[-HALO:], ("z", "y", "core"),
            [(2 * i + 1, 2 * i + 2 + target) for i in range(chips - 1)],
        )
        slabs.extend((rows, swap_cores(rows), to_next(0) + to_next(1)))
        sums.extend(products(place, slabs, blocks, 0))
        return sums[:1]

    def before_last():
        early.extend(
            prepared(place, slabs, narrow, conv_bc, per_lane(dt_bias), per_lane(decay_rate), heads)
        )
        return early[:1]

    nearest, second, blocks = travelling(own_block, before_third, before_last)
    (z_rows,) = tied((z_weight,), own_block)
    z_whole = lax.all_gather(z_rows, ("z", "y", "core"), axis=0, tiled=True)
    sums = products(place, slabs, second, len(nearest), sums)
    bcc, cum, cum_slab, cum_t, step_t, weights_in, decays = early
    xc, entering, final = local_states(
        place, slabs, blocks, all_rows(blocks), 9, 7, sums, bcc, weights_in, decays, mine(conv_x, 1)
    )
    before, before_decay, earlier = earlier_states(final)
    skip_lanes = jnp.repeat(mine(skip, 0), HEAD)[None, :]
    local = local_outputs(xc, bcc, cum, cum_t, step_t, entering, skip_lanes)
    gate = project_gate(place, slabs, z_whole)
    gated, send, squares = gate_outputs(place[:1], gate, local, bcc, cum_slab, before, before_decay, earlier)

    other = swap_cores(send)
    summed = mine(squares + swap_cores(squares), 1)
    across = [round_ring(summed, "x", distance) for distance in range(1, lax.axis_size("x"))]
    mean_squares = (summed + sum(across)) / (2 * width * lax.axis_size("x"))
    return normalized(core, gated, other, mean_squares, norm_gain[None, :])


def solution(mesh):
    fine = Mesh(mesh.devices.reshape(4, 4, 2, 4), ("z", "y", "core", "x"))
    ctx = ("z", "y", "core")
    placed = (
        P(ctx, None),
        P(ctx, "x"),
        P(ctx, "x"),
        P(ctx, None),
        P(ctx, "x"),
        P(None, "x"),
        P(),
        P("x"),
        P("x"),
        P("x"),
        P("x"),
    )
    return jax.shard_map(
        shards, mesh=fine, in_specs=placed, out_specs=P(ctx, "x"), check_vma=False
    )
```

```python
import functools

import jax
import jax.numpy as jnp
from jax import lax
from jax.experimental import pallas as pl
from jax.experimental.pallas import tpu as pltpu
from jax.sharding import Mesh, PartitionSpec as P

GROUP = 256
HALO = 16
LANES = 128
HEAD = 64
F32 = jnp.float32
BF16 = jnp.bfloat16


def swap_cores(a):
    return lax.ppermute(a, "core", [(0, 1), (1, 0)])


def round_ring(a, axis, distance):
    size = lax.axis_size(axis)
    return lax.ppermute(a, axis, [(i, (i + distance) % size) for i in range(size)])


def along_chips(a, distance):
    chips = lax.axis_size("z") * lax.axis_size("y")
    return lax.ppermute(a, ("z", "y"), [(i, i + distance) for i in range(chips - distance)])


def in_core_order(core, mine, other, axis):
    first = jnp.where(core == 0, mine, other)
    second = jnp.where(core == 0, other, mine)
    return jnp.concatenate([first, second], axis=axis)


def expand_heads(values, width):
    heads = width // HEAD
    high = values.astype(BF16).astype(F32)
    rest = values - high
    middle = rest.astype(BF16).astype(F32)
    low = rest - middle
    lane = lax.broadcasted_iota(jnp.int32, values.shape, 1)
    parts = jnp.where(lane < heads, high, pltpu.roll(middle, heads, axis=1))
    parts = jnp.where(lane < 2 * heads, parts, pltpu.roll(low, 2 * heads, axis=1))
    parts = jnp.where(lane < 3 * heads, parts, 0.0).astype(BF16)
    row = lax.broadcasted_iota(jnp.int32, (LANES, width), 0)
    col = lax.broadcasted_iota(jnp.int32, (LANES, width), 1)
    head = row % heads
    spread = (col >= head * HEAD) & (col < head * HEAD + HEAD) & (row < 3 * heads)
    return jnp.dot(parts, spread.astype(BF16), preferred_element_type=F32)


def silu(a):
    half = 0.5 * a
    return half + half * jnp.tanh(half)


def conv_rows(rows, kernel_ref):
    taps, count = kernel_ref.shape[0], rows.shape[0] - HALO
    first = HALO - (taps - 1)
    accum = kernel_ref[0:1, :] * rows[first : first + count]
    for tap in range(1, taps):
        accum = accum + kernel_ref[tap : tap + 1, :] * rows[first + tap : first + tap + count]
    return silu(accum).astype(BF16)


def prepare_kernel(
    place_ref, own_ref, other_ref, before_ref, weight_ref, conv_ref, bias_ref, rate_ref,
    bcc_ref, cum_ref, cum_slab_ref, cum_t_ref, step_t_ref, weights_in_ref, decays_ref,
    accum,
):
    step = pl.program_id(0)
    core = place_ref[0]
    slab = own_ref.shape[0]
    heads = cum_t_ref.shape[0]
    rows_own = pl.ds(pl.multiple_of(HALO + slab * core, HALO), slab)
    rows_other = pl.ds(pl.multiple_of(HALO + slab * (1 - core), HALO), slab)

    @pl.when(step == 0)
    def _():
        accum[...] = jnp.zeros_like(accum)

    weight = weight_ref[...]
    for rows, ref in ((slice(0, HALO), before_ref), (rows_own, own_ref), (rows_other, other_ref)):
        accum[rows, :] = accum[rows, :] + jnp.dot(ref[...], weight, preferred_element_type=F32)

    @pl.when(step == pl.num_programs(0) - 1)
    def _():
        total = jnp.zeros((1, LANES), F32)
        row = lax.broadcasted_iota(jnp.int32, (GROUP, GROUP), 0)
        col = lax.broadcasted_iota(jnp.int32, (GROUP, GROUP), 1)
        lower = (row >= col).astype(F32)
        for block in range(2 * slab // GROUP):
            part = slice(block * GROUP, (block + 1) * GROUP)
            narrow = accum[block * GROUP : (block + 1) * GROUP + HALO, : 2 * LANES]
            bcc_ref[part, :] = conv_rows(narrow.astype(BF16).astype(F32), conv_ref)
            raw = accum[block * GROUP + HALO : (block + 1) * GROUP + HALO, 2 * LANES :]
            raw = jnp.where(core == 0, raw, pltpu.roll(raw, LANES - heads, axis=1))
            raw = raw + bias_ref[...]
            step_size = jnp.maximum(raw, 0.0) + jnp.log1p(jnp.exp(-jnp.abs(raw)))
            log_decay = -rate_ref[...] * step_size
            cum = jnp.dot(
                lower, log_decay, preferred_element_type=F32, precision=lax.Precision.HIGHEST
            )
            last = cum[GROUP - 1 : GROUP, :]
            cum_ref[part, :] = cum
            cum_slab_ref[part, :] = cum + total
            cum_t_ref[:, part] = cum.T[:heads, :]
            step_t_ref[:, part] = step_size.T[:heads, :]
            weights_in_ref[part, :] = jnp.exp(last - cum) * step_size
            decays_ref[block * 8 : block * 8 + 8, :] = jnp.broadcast_to(jnp.exp(last), (8, LANES))
            total = total + last
        end = decays_ref.shape[0] - 8
        decays_ref[end:, :] = jnp.broadcast_to(jnp.exp(total), (8, LANES))


def block_columns(ref, place_ref, first, count):
    core = place_ref[0]
    parts = []
    for index in range(first, first + count):
        base = place_ref[1 + index] * (2 * LANES)
        for start in (base + LANES * core, base + LANES * (1 - core)):
            parts.append(ref[:, pl.ds(pl.multiple_of(start, LANES), LANES)])
    return jnp.concatenate(parts, axis=1)


def stacked(sources, refs):
    return jnp.concatenate([refs[ref][first : first + size, :] for ref, first, size in sources], axis=0)


def products_kernel(sources, done, count, started, place_ref, own_ref, other_ref, before_ref, *refs):
    weights, sums, (out_ref, out_before_ref, wide) = refs[: -3 - 2 * started], refs[-3 - 2 * started : -3], refs[-3:]
    block = pl.program_id(0)
    is_own = block // 2 == place_ref[0]

    def product(ref):
        columns = block_columns(ref, place_ref, done, count)
        return jnp.dot(columns, wide[...], preferred_element_type=F32)

    @pl.when(block == 0)
    def _():
        row = 0
        for ref, first, size in sources:
            wide[row : row + size, :] = weights[ref][first : first + size, :]
            row += size
        added = product(before_ref)
        out_before_ref[...] = sums[1][...] + added if started else added

    @pl.when(is_own)
    def _():
        added = product(own_ref)
        out_ref[...] = sums[0][...] + added if started else added

    @pl.when(jnp.logical_not(is_own))
    def _():
        added = product(other_ref)
        out_ref[...] = sums[0][...] + added if started else added


def states_kernel(
    sources, done, count, place_ref, own_ref, other_ref, before_ref, *refs
):
    weights = refs[:-13]
    (
        sum_ref, sum_before_ref, bcc_ref, weights_in_ref, decays_ref, conv_ref,
        xc_ref, entering_ref, final_ref,
        state, x_in, tail, wide,
    ) = refs[-13:]
    block = pl.program_id(0)
    width = x_in.shape[1]
    is_own = block // 2 == place_ref[0]

    def product(ref):
        columns = block_columns(ref, place_ref, done, count)
        return jnp.dot(columns, wide[...], preferred_element_type=F32)

    @pl.when(block == 0)
    def _():
        state[...] = jnp.zeros_like(state)
        row = 0
        for ref, first, size in sources:
            wide[row : row + size, :] = weights[ref][first : first + size, :]
            row += size
        tail[...] = (sum_before_ref[...] + product(before_ref)).astype(BF16).astype(F32)

    @pl.when(is_own)
    def _():
        x_in[...] = (sum_ref[...] + product(own_ref)).astype(BF16).astype(F32)

    @pl.when(jnp.logical_not(is_own))
    def _():
        x_in[...] = (sum_ref[...] + product(other_ref)).astype(BF16).astype(F32)

    rows = jnp.concatenate([tail[...], x_in[...]], axis=0)
    tail[...] = rows[GROUP:]
    xc = conv_rows(rows, conv_ref)
    xc_ref[...] = xc
    entering_ref[0] = state[...].astype(BF16)
    weighted = (expand_heads(weights_in_ref[...], width) * xc.astype(F32)).astype(BF16)
    contrib = lax.dot_general(
        bcc_ref[:, :LANES], weighted, (((0,), (0,)), ((), ())), preferred_element_type=F32
    )
    decay = expand_heads(decays_ref[pl.ds(pl.multiple_of(block * 8, 8), 8), :], width)
    state[...] = state[...] * decay[0:1] + contrib

    @pl.when(block == pl.num_programs(0) - 1)
    def _():
        end = decays_ref.shape[0] - 8
        final_ref[:LANES, :] = state[...].astype(BF16)
        final_ref[LANES:, :] = split_decay(expand_heads(decays_ref[end:, :], width)[0:1])


def split_decay(decay):
    high = decay.astype(BF16)
    low = decay - high.astype(F32)
    row = lax.broadcasted_iota(jnp.int32, (HALO, decay.shape[1]), 0)
    return jnp.where(row == 0, high.astype(F32), jnp.where(row == 1, low, 0.0)).astype(BF16)


def unpacked(sent):
    sent = sent.astype(F32)
    return sent[:LANES], sent[LANES : LANES + 1] + sent[LANES + 1 : LANES + 2]


def row_kernel(place_ref, *refs):
    size = len(refs) - 3
    parts, (total_ref, before_ref, before_decay_ref) = refs[:size], refs[size:]
    place = place_ref[0]
    width = total_ref.shape[1]
    total, decay = jnp.zeros((LANES, width), F32), jnp.ones((1, width), F32)
    before_ref[...] = total
    before_decay_ref[...] = jnp.broadcast_to(decay, before_decay_ref.shape)
    for index in range(size):
        if index > 0:

            @pl.when(place == index)
            def _():
                before_ref[...] = total
                before_decay_ref[...] = jnp.broadcast_to(decay, before_decay_ref.shape)

        distance = (place - index + size) % size
        chosen = parts[0][...]
        for other in range(1, size):
            chosen = jnp.where(distance == other, parts[other][...], chosen)
        state, state_decay = unpacked(chosen)
        total = total * state_decay + state
        decay = decay * state_decay
    total_ref[:LANES, :] = total.astype(BF16)
    total_ref[LANES:, :] = split_decay(decay)


def outputs_kernel(xc_ref, bcc_ref, cum_ref, cum_t_ref, step_t_ref, entering_ref, skip_ref, out_ref, carried):
    width = xc_ref.shape[1]
    b_rows, c_rows = bcc_ref[:, :LANES], bcc_ref[:, LANES:]
    scores = lax.dot_general(c_rows, b_rows, (((1,), (1,)), ((), ())), preferred_element_type=F32)
    row = lax.broadcasted_iota(jnp.int32, (GROUP, GROUP), 0)
    col = lax.broadcasted_iota(jnp.int32, (GROUP, GROUP), 1)
    scores = jnp.where(row >= col, scores, 0.0)
    cum = cum_ref[...]
    grown = expand_heads(jnp.exp(cum), width)
    carried[...] = grown * jnp.dot(c_rows, entering_ref[0], preferred_element_type=F32)
    lane = lax.broadcasted_iota(jnp.int32, (GROUP, LANES), 1)

    def mixing(head):
        gaps = cum[:, head : head + 1] - cum_t_ref[head : head + 1, :]
        return (
            scores * jnp.exp(jnp.minimum(gaps, 0.0)) * step_t_ref[head : head + 1, :]
        ).astype(BF16)

    for pair in range(width // LANES):
        lanes = slice(pair * LANES, (pair + 1) * LANES)
        inputs = xc_ref[:, lanes]
        zero = jnp.zeros_like(inputs)
        both = jnp.concatenate([mixing(2 * pair), mixing(2 * pair + 1)], axis=1)
        stacked = jnp.concatenate(
            [jnp.where(lane < HEAD, inputs, zero), jnp.where(lane < HEAD, zero, inputs)], axis=0
        )
        out_ref[:, lanes] = (
            carried[:, lanes]
            + jnp.dot(both, stacked, preferred_element_type=F32)
            + skip_ref[:, lanes] * inputs.astype(F32)
        ).astype(BF16)


def z_kernel(place_ref, own_ref, other_ref, weight_ref, gate_ref, accum):
    step = pl.program_id(0)
    slab = own_ref.shape[0]
    core = place_ref[0]

    def product(ref):
        return jnp.dot(ref[...], weight_ref[...], preferred_element_type=F32)

    for index, ref in enumerate((own_ref, other_ref)):
        rows = slice(index * slab, (index + 1) * slab)
        target = pl.ds(pl.multiple_of(slab * (core if index == 0 else 1 - core), slab), slab)

        @pl.when(step == 0)
        def _():
            accum[rows, :] = product(ref)

        @pl.when((step > 0) & (step < pl.num_programs(0) - 1))
        def _():
            accum[rows, :] = accum[rows, :] + product(ref)

        @pl.when(step == pl.num_programs(0) - 1)
        def _():
            gate_ref[target, :] = (accum[rows, :] + product(ref)).astype(BF16)


def gate_kernel(
    core_ref, gate_ref, local_ref, bcc_ref, cum_ref, before_ref, before_decay_ref, *refs
):
    earlier, (mine_ref, send_ref, squares_ref, incoming) = refs[:-4], refs[-4:]
    width = local_ref.shape[1]

    @pl.when(pl.program_id(0) == 0)
    def _():
        carried = jnp.zeros((LANES, width), F32)
        for part in earlier:
            state, decay = unpacked(part[...])
            carried = carried * decay + state
        incoming[...] = (carried * before_decay_ref[0:1, :] + before_ref[...]).astype(BF16)

    grown = expand_heads(jnp.exp(cum_ref[...]), width)
    carried = jnp.dot(bcc_ref[:, LANES:], incoming[...], preferred_element_type=F32)
    gated = (local_ref[...].astype(F32) + grown * carried) * silu(gate_ref[...].astype(F32))
    is_own = pl.program_id(0) // 2 == core_ref[0]

    @pl.when(is_own)
    def _():
        mine_ref[...] = gated.astype(BF16)

    @pl.when(jnp.logical_not(is_own))
    def _():
        send_ref[...] = gated.astype(BF16)

    squares = gated * gated
    high = squares.astype(BF16)
    low = (squares - high.astype(F32)).astype(BF16)
    ones = jnp.ones((8, width), BF16)
    across = (((1,), (1,)), ((), ()))
    summed = lax.dot_general(ones, high, across, preferred_element_type=F32) + lax.dot_general(
        ones, low, across, preferred_element_type=F32
    )
    squares_ref[...] = summed[0:1, :]


def norm_kernel(core_ref, mine_ref, other_ref, squares_ref, gain_ref, out_ref):
    half = pl.program_id(0)
    across = jnp.broadcast_to(squares_ref[...], (8, squares_ref.shape[1]))
    scale = lax.rsqrt(across + 1e-05).T[:, 0:1]

    @pl.when(half == core_ref[0])
    def _():
        out_ref[...] = (mine_ref[...].astype(F32) * scale * gain_ref[...]).astype(BF16)

    @pl.when(half != core_ref[0])
    def _():
        out_ref[...] = (other_ref[...].astype(F32) * scale * gain_ref[...]).astype(BF16)


def whole(shape):
    return pl.BlockSpec(shape, lambda i: (0,) * len(shape))


def rows_of(width):
    return pl.BlockSpec((GROUP, width), lambda i: (i, 0))


def params(flops, megabytes, vmem=32):
    return dict(
        compiler_params=pltpu.CompilerParams(vmem_limit_bytes=vmem * 2**20),
        cost_estimate=pl.CostEstimate(
            flops=int(flops), bytes_accessed=megabytes * 2**20, transcendentals=0
        ),
    )


def fixed(a):
    return pl.BlockSpec(a.shape, lambda i, place: (0,) * len(a.shape))


def row_block(width):
    return pl.BlockSpec((GROUP, width), lambda i, place: (i, 0))


def slab_blocks(depth):
    own = pl.BlockSpec((GROUP, depth), lambda i, place: (jnp.clip(i - 2 * place[0], 0, 1), 0))
    other = pl.BlockSpec((GROUP, depth), lambda i, place: (jnp.clip(i - 2 + 2 * place[0], 0, 1), 0))
    return [own, other]


def prepared(place, slabs, weight, conv_bc, bias, rate, heads):
    own, other, before = slabs
    slab, rows, depth = own.shape[0], 2 * own.shape[0], 512
    shape = jax.ShapeDtypeStruct
    outs = [
        shape((rows, 2 * LANES), BF16), shape((rows, LANES), F32), shape((rows, LANES), F32),
        shape((heads, rows), F32), shape((heads, rows), F32), shape((rows, LANES), F32),
        shape((rows // GROUP * 8 + 8, LANES), F32),
    ]
    columns = lambda a: pl.BlockSpec((a.shape[0], depth), lambda i, place: (0, i))
    return pl.pallas_call(
        prepare_kernel,
        grid_spec=pltpu.PrefetchScalarGridSpec(
            num_scalar_prefetch=1,
            grid=(own.shape[1] // depth,),
            in_specs=[columns(a) for a in slabs]
            + [pl.BlockSpec((depth, weight.shape[1]), lambda i, place: (i, 0))]
            + [fixed(a) for a in (conv_bc, bias, rate)],
            out_specs=[fixed(a) for a in outs],
            scratch_shapes=[pltpu.VMEM((HALO + rows, weight.shape[1]), F32)],
        ),
        out_shape=outs,
        name="prepared",
        **params(4e9, 14, 60),
    )(place, *slabs, weight, conv_bc, bias, rate)


def products(place, slabs, weights, done, sums=()):
    own, other, before = slabs
    width, count = weights[0].shape[1], len(weights)
    outs = [
        jax.ShapeDtypeStruct((2 * own.shape[0], width), F32), jax.ShapeDtypeStruct((HALO, width), F32),
    ]
    specs = [row_block(width), fixed(outs[1])]
    sources = all_rows(weights)
    return pl.pallas_call(
        functools.partial(products_kernel, sources, done, count, len(sums) // 2),
        grid_spec=pltpu.PrefetchScalarGridSpec(
            num_scalar_prefetch=1,
            grid=(2 * own.shape[0] // GROUP,),
            in_specs=slab_blocks(own.shape[1])
            + [fixed(a) for a in (before, *weights)]
            + specs[: len(sums)],
            out_specs=specs,
            scratch_shapes=[pltpu.VMEM((sum(size for _, _, size in sources), width), BF16)],
        ),
        out_shape=outs,
        name="more_products" if sums else "first_products",
        **params(5e9, 16, 48),
    )(place, *slabs, *weights, *sums)


def local_states(place, slabs, weights, sources, done, count, sums, bcc, weights_in, decays, conv_x):
    own, other, before = slabs
    rows, width = sums[0].shape
    blocks = rows // GROUP
    outs = [
        jax.ShapeDtypeStruct((rows, width), BF16),
        jax.ShapeDtypeStruct((blocks, LANES, width), BF16),
        jax.ShapeDtypeStruct((LANES + HALO, width), BF16),
    ]
    return pl.pallas_call(
        functools.partial(states_kernel, sources, done, count),
        grid_spec=pltpu.PrefetchScalarGridSpec(
            num_scalar_prefetch=1,
            grid=(blocks,),
            in_specs=slab_blocks(own.shape[1])
            + [fixed(a) for a in (before, *weights)]
            + [
                row_block(width), fixed(sums[1]), row_block(2 * LANES), row_block(LANES),
                fixed(decays), fixed(conv_x),
            ],
            out_specs=[
                row_block(width),
                pl.BlockSpec((1, LANES, width), lambda i, place: (i, 0, 0)),
                fixed(outs[2]),
            ],
            scratch_shapes=[
                pltpu.VMEM((LANES, width), F32), pltpu.VMEM((GROUP, width), F32),
                pltpu.VMEM((HALO, width), F32),
                pltpu.VMEM((sum(size for _, _, size in sources), width), BF16),
            ],
        ),
        out_shape=outs,
        name="states",
        **params(11e9, 18, 40),
    )(place, *slabs, *weights, *sums, bcc, weights_in, decays, conv_x)


def local_outputs(xc, bcc, cum, cum_t, step_t, entering, skip):
    rows, width = xc.shape
    heads = cum_t.shape[0]
    by_lane = pl.BlockSpec((heads, GROUP), lambda i: (0, i))
    return pl.pallas_call(
        outputs_kernel,
        grid=(rows // GROUP,),
        in_specs=[
            rows_of(width), rows_of(2 * LANES), rows_of(LANES), by_lane, by_lane,
            pl.BlockSpec((1, LANES, width), lambda i: (i, 0, 0)), whole((1, width)),
        ],
        out_specs=rows_of(width),
        out_shape=jax.ShapeDtypeStruct((rows, width), BF16),
        scratch_shapes=[pltpu.VMEM((GROUP, width), F32)],
        compiler_params=pltpu.CompilerParams(vmem_limit_bytes=32 * 2**20),
        cost_estimate=pl.CostEstimate(flops=10**10, bytes_accessed=10 * 2**20, transcendentals=4 * 2**20),
        name="outputs",
    )(xc, bcc, cum, cum_t, step_t, entering, skip)


def project_gate(place, slabs, weight):
    own, other, _ = slabs
    rows, width, depth = 2 * own.shape[0], weight.shape[1], 1024
    columns = pl.BlockSpec((own.shape[0], depth), lambda i, place: (0, i))
    out = jax.ShapeDtypeStruct((rows, width), BF16)
    return pl.pallas_call(
        z_kernel,
        grid_spec=pltpu.PrefetchScalarGridSpec(
            num_scalar_prefetch=1,
            grid=(weight.shape[0] // depth,),
            in_specs=[columns, columns, pl.BlockSpec((depth, width), lambda i, place: (i, 0))],
            out_specs=fixed(out),
            scratch_shapes=[pltpu.VMEM((rows, width), F32)],
        ),
        out_shape=out,
        name="project_gate",
        **params(9e9, 20, 48),
    )(place, own, other, weight)


def gate_outputs(core, gate, local, bcc, cum_slab, before, before_decay, earlier):
    rows, width = local.shape
    half = jax.ShapeDtypeStruct((rows // 2, width), BF16)
    return pl.pallas_call(
        gate_kernel,
        grid_spec=pltpu.PrefetchScalarGridSpec(
            num_scalar_prefetch=1,
            grid=(rows // GROUP,),
            in_specs=[row_block(width), row_block(width), row_block(2 * LANES), row_block(LANES)]
            + [fixed(a) for a in (before, before_decay, *earlier)],
            out_specs=slab_blocks(width) + [pl.BlockSpec((1, GROUP), lambda i, place: (0, i))],
            scratch_shapes=[pltpu.VMEM((LANES, width), BF16)],
        ),
        out_shape=[half, half, jax.ShapeDtypeStruct((1, rows), F32)],
        name="gate",
        **params(1e9, 10, 60),
    )(core, gate, local, bcc, cum_slab, before, before_decay, *earlier)


def normalized(core, gated, other, mean_squares, gain):
    rows, width = other.shape
    return pl.pallas_call(
        norm_kernel,
        grid_spec=pltpu.PrefetchScalarGridSpec(
            num_scalar_prefetch=1,
            grid=(2,),
            in_specs=[
                pl.BlockSpec((rows, width), lambda j, core: (0, 0)),
                pl.BlockSpec((rows, width), lambda j, core: (0, 0)),
                pl.BlockSpec((1, rows), lambda j, core: (0, 0)),
                pl.BlockSpec((1, width), lambda j, core: (0, j)),
            ],
            out_specs=pl.BlockSpec((rows, width), lambda j, core: (0, j)),
        ),
        out_shape=jax.ShapeDtypeStruct((rows, 2 * width), BF16),
        compiler_params=pltpu.CompilerParams(vmem_limit_bytes=32 * 2**20),
        cost_estimate=pl.CostEstimate(flops=10**7, bytes_accessed=4 * 2**20, transcendentals=0),
        name="normalized",
    )(core.astype(jnp.int32)[None], gated, other, mean_squares, gain)


def earlier_states(final):
    size = lax.axis_size("y")
    parts = [final] + [round_ring(final, "y", distance) for distance in range(1, size)]
    width = final.shape[1]
    outs = [
        jax.ShapeDtypeStruct(final.shape, BF16),
        jax.ShapeDtypeStruct((LANES, width), F32),
        jax.ShapeDtypeStruct((8, width), F32),
    ]
    total, before, before_decay = pl.pallas_call(
        row_kernel,
        grid_spec=pltpu.PrefetchScalarGridSpec(
            num_scalar_prefetch=1,
            grid=(1,),
            in_specs=[fixed(a) for a in parts],
            out_specs=[fixed(a) for a in outs],
        ),
        out_shape=outs,
        name="row_states",
        **params(1e7, 2),
    )(lax.axis_index("y").astype(jnp.int32)[None], *parts)
    rows = lax.axis_size("z")
    earlier = [
        lax.ppermute(total, "z", [(i, i + distance) for i in range(rows - distance)])
        for distance in range(rows - 1, 0, -1)
    ]
    return before, before_decay, earlier


def tied(values, *to):
    return lax.optimization_barrier((*values, *to))[: len(values)]


def travelling(own, before_third, before_last):
    y_less, y_more = round_ring(own, "y", 1), round_ring(own, "y", -1)
    z_less, z_more = round_ring(own, "z", 1), round_ring(own, "z", -1)
    nearest = [own, y_less, y_more, z_less, z_more]
    second = [
        round_ring(y_less, "y", 1), round_ring(z_more, "z", -1),
        round_ring(z_more, "y", -1), round_ring(y_more, "z", 1),
    ]
    y_far, z_far, _, _, held_z, held_y = tied((*second, z_less, y_less), *before_third(nearest))
    less_less = round_ring(held_z, "y", 1)
    far = [
        round_ring(z_far, "y", -1), round_ring(z_far, "y", 1),
        round_ring(y_far, "z", 1), round_ring(y_far, "z", -1),
    ]
    held_y, last, *_ = tied((held_y, *far), *before_last())
    less_more = round_ring(held_y, "z", -1)
    return nearest, second, [*far, less_less, less_more, round_ring(last, "y", -1)]


def all_rows(blocks):
    return [(index, 0, block.shape[0]) for index, block in enumerate(blocks)]


def block_order():
    places = (
        ((0, 0), (-1, 0), (1, 0), (0, -1), (0, 1), (2, 0), (0, 2), (1, 1), (1, -1))
        + ((1, 2), (-1, 2), (2, -1), (2, 1), (-1, -1), (-1, 1), (2, 2))
    )
    y, z = lax.axis_index("y"), lax.axis_index("z")
    return [(z + dz) % 4 * 4 + (y + dy) % 4 for dy, dz in places]


def shards(
    tokens, x_weight, z_weight, bc_weight, dt_weight, conv_x, conv_bc, dt_bias, decay_rate, skip,
    norm_gain,
):
    core = lax.axis_index("core")
    width = x_weight.shape[1] // 2
    heads = dt_weight.shape[1] // 2

    def mine(a, axis):
        size = a.shape[axis] // 2
        return lax.dynamic_slice_in_dim(a, core * size, size, axis)

    def others(a, axis):
        size = a.shape[axis] // 2
        return lax.dynamic_slice_in_dim(a, (1 - core) * size, size, axis)

    def per_lane(a):
        return jnp.pad(mine(a, 0), (0, LANES - heads))[None, :]

    narrow = jnp.concatenate(
        [bc_weight, dt_weight, jnp.zeros((bc_weight.shape[0], LANES - 2 * heads), BF16)], axis=1
    )
    narrow = lax.all_gather(narrow, ("z", "y", "core"), axis=0, tiled=True)
    own_block = jnp.concatenate([mine(x_weight, 1), swap_cores(others(x_weight, 1))], axis=0)
    place = jnp.stack([core, *block_order()]).astype(jnp.int32)
    slabs, sums, early = [], [], []

    def before_third(blocks):
        (rows,) = tied((tokens,), *blocks[1:])
        chips = lax.axis_size("z") * lax.axis_size("y")
        to_next = lambda target: lax.ppermute(
            rows[-HALO:], ("z", "y", "core"),
            [(2 * i + 1, 2 * i + 2 + target) for i in range(chips - 1)],
        )
        slabs.extend((rows, swap_cores(rows), to_next(0) + to_next(1)))
        sums.extend(products(place, slabs, blocks, 0))
        return sums[:1]

    def before_last():
        early.extend(
            prepared(place, slabs, narrow, conv_bc, per_lane(dt_bias), per_lane(decay_rate), heads)
        )
        return early[:1]

    nearest, second, blocks = travelling(own_block, before_third, before_last)
    (z_rows,) = tied((z_weight,), own_block)
    z_block = in_core_order(core, mine(z_rows, 1), swap_cores(others(z_rows, 1)), 0)
    z_whole = lax.all_gather(z_block, ("z", "y"), axis=0, tiled=True)
    sums = products(place, slabs, second, len(nearest), sums)
    bcc, cum, cum_slab, cum_t, step_t, weights_in, decays = early
    xc, entering, final = local_states(
        place, slabs, blocks, all_rows(blocks), 9, 7, sums, bcc, weights_in, decays, mine(conv_x, 1)
    )
    before, before_decay, earlier = earlier_states(final)
    skip_lanes = jnp.repeat(mine(skip, 0), HEAD)[None, :]
    local = local_outputs(xc, bcc, cum, cum_t, step_t, entering, skip_lanes)
    gate = project_gate(place, slabs, z_whole)
    gated, send, squares = gate_outputs(place[:1], gate, local, bcc, cum_slab, before, before_decay, earlier)

    other = swap_cores(send)
    summed = mine(squares + swap_cores(squares), 1)
    across = [round_ring(summed, "x", distance) for distance in range(1, lax.axis_size("x"))]
    mean_squares = (summed + sum(across)) / (2 * width * lax.axis_size("x"))
    return normalized(core, gated, other, mean_squares, norm_gain[None, :])


def solution(mesh):
    fine = Mesh(mesh.devices.reshape(4, 4, 2, 4), ("z", "y", "core", "x"))
    ctx = ("z", "y", "core")
    placed = (
        P(ctx, None),
        P(ctx, "x"),
        P(ctx, "x"),
        P(ctx, None),
        P(ctx, "x"),
        P(None, "x"),
        P(),
        P("x"),
        P("x"),
        P("x"),
        P("x"),
    )
    return jax.shard_map(
        shards, mesh=fine, in_specs=placed, out_specs=P(ctx, "x"), check_vma=False
    )
```

```python
import functools

import jax
import jax.numpy as jnp
from jax import lax
from jax.experimental import pallas as pl
from jax.experimental.pallas import tpu as pltpu
from jax.sharding import Mesh, PartitionSpec as P

GROUP = 256
HALO = 16
LANES = 128
HEAD = 64
F32 = jnp.float32
BF16 = jnp.bfloat16


def swap_cores(a):
    return lax.ppermute(a, "core", [(0, 1), (1, 0)])


def round_ring(a, axis, distance):
    size = lax.axis_size(axis)
    return lax.ppermute(a, axis, [(i, (i + distance) % size) for i in range(size)])


def along_chips(a, distance):
    chips = lax.axis_size("z") * lax.axis_size("y")
    return lax.ppermute(a, ("z", "y"), [(i, i + distance) for i in range(chips - distance)])


def in_core_order(core, mine, other, axis):
    first = jnp.where(core == 0, mine, other)
    second = jnp.where(core == 0, other, mine)
    return jnp.concatenate([first, second], axis=axis)


def expand_heads(values, width):
    heads = width // HEAD
    high = values.astype(BF16).astype(F32)
    rest = values - high
    middle = rest.astype(BF16).astype(F32)
    low = rest - middle
    lane = lax.broadcasted_iota(jnp.int32, values.shape, 1)
    parts = jnp.where(lane < heads, high, pltpu.roll(middle, heads, axis=1))
    parts = jnp.where(lane < 2 * heads, parts, pltpu.roll(low, 2 * heads, axis=1))
    parts = jnp.where(lane < 3 * heads, parts, 0.0).astype(BF16)
    row = lax.broadcasted_iota(jnp.int32, (LANES, width), 0)
    col = lax.broadcasted_iota(jnp.int32, (LANES, width), 1)
    head = row % heads
    spread = (col >= head * HEAD) & (col < head * HEAD + HEAD) & (row < 3 * heads)
    return jnp.dot(parts, spread.astype(BF16), preferred_element_type=F32)


def silu(a):
    half = 0.5 * a
    return half + half * jnp.tanh(half)


def conv_rows(rows, kernel_ref):
    taps, count = kernel_ref.shape[0], rows.shape[0] - HALO
    first = HALO - (taps - 1)
    accum = kernel_ref[0:1, :] * rows[first : first + count]
    for tap in range(1, taps):
        accum = accum + kernel_ref[tap : tap + 1, :] * rows[first + tap : first + tap + count]
    return silu(accum).astype(BF16)


def prepare_kernel(
    place_ref, own_ref, other_ref, before_ref, weight_ref, conv_ref, bias_ref, rate_ref,
    bcc_ref, cum_ref, cum_slab_ref, cum_t_ref, step_t_ref, weights_in_ref, decays_ref,
    accum,
):
    step = pl.program_id(0)
    core = place_ref[0]
    slab = own_ref.shape[0]
    heads = cum_t_ref.shape[0]
    rows_own = pl.ds(pl.multiple_of(HALO + slab * core, HALO), slab)
    rows_other = pl.ds(pl.multiple_of(HALO + slab * (1 - core), HALO), slab)

    @pl.when(step == 0)
    def _():
        accum[...] = jnp.zeros_like(accum)

    weight = weight_ref[...]
    for rows, ref in ((slice(0, HALO), before_ref), (rows_own, own_ref), (rows_other, other_ref)):
        accum[rows, :] = accum[rows, :] + jnp.dot(ref[...], weight, preferred_element_type=F32)

    @pl.when(step == pl.num_programs(0) - 1)
    def _():
        total = jnp.zeros((1, LANES), F32)
        row = lax.broadcasted_iota(jnp.int32, (GROUP, GROUP), 0)
        col = lax.broadcasted_iota(jnp.int32, (GROUP, GROUP), 1)
        lower = (row >= col).astype(F32)
        for block in range(2 * slab // GROUP):
            part = slice(block * GROUP, (block + 1) * GROUP)
            narrow = accum[block * GROUP : (block + 1) * GROUP + HALO, : 2 * LANES]
            bcc_ref[part, :] = conv_rows(narrow.astype(BF16).astype(F32), conv_ref)
            raw = accum[block * GROUP + HALO : (block + 1) * GROUP + HALO, 2 * LANES :]
            raw = jnp.where(core == 0, raw, pltpu.roll(raw, LANES - heads, axis=1))
            raw = raw + bias_ref[...]
            step_size = jnp.maximum(raw, 0.0) + jnp.log1p(jnp.exp(-jnp.abs(raw)))
            log_decay = -rate_ref[...] * step_size
            cum = jnp.dot(
                lower, log_decay, preferred_element_type=F32, precision=lax.Precision.HIGHEST
            )
            last = cum[GROUP - 1 : GROUP, :]
            cum_ref[part, :] = cum
            cum_slab_ref[part, :] = cum + total
            cum_t_ref[:, part] = cum.T[:heads, :]
            step_t_ref[:, part] = step_size.T[:heads, :]
            weights_in_ref[part, :] = jnp.exp(last - cum) * step_size
            decays_ref[block * 8 : block * 8 + 8, :] = jnp.broadcast_to(jnp.exp(last), (8, LANES))
            total = total + last
        end = decays_ref.shape[0] - 8
        decays_ref[end:, :] = jnp.broadcast_to(jnp.exp(total), (8, LANES))


def block_columns(ref, place_ref, first, count):
    core = place_ref[0]
    parts = []
    for index in range(first, first + count):
        base = place_ref[1 + index] * (2 * LANES)
        for start in (base + LANES * core, base + LANES * (1 - core)):
            parts.append(ref[:, pl.ds(pl.multiple_of(start, LANES), LANES)])
    return jnp.concatenate(parts, axis=1)


def stacked(sources, refs):
    return jnp.concatenate([refs[ref][first : first + size, :] for ref, first, size in sources], axis=0)


def products_kernel(sources, done, count, started, place_ref, own_ref, other_ref, before_ref, *refs):
    weights, sums, (out_ref, out_before_ref, wide) = refs[: -3 - 2 * started], refs[-3 - 2 * started : -3], refs[-3:]
    block = pl.program_id(0)
    is_own = block // 2 == place_ref[0]

    def product(ref):
        columns = block_columns(ref, place_ref, done, count)
        return jnp.dot(columns, wide[...], preferred_element_type=F32)

    @pl.when(block == 0)
    def _():
        row = 0
        for ref, first, size in sources:
            wide[row : row + size, :] = weights[ref][first : first + size, :]
            row += size
        added = product(before_ref)
        out_before_ref[...] = sums[1][...] + added if started else added

    @pl.when(is_own)
    def _():
        added = product(own_ref)
        out_ref[...] = sums[0][...] + added if started else added

    @pl.when(jnp.logical_not(is_own))
    def _():
        added = product(other_ref)
        out_ref[...] = sums[0][...] + added if started else added


def states_kernel(
    sources, done, count, place_ref, own_ref, other_ref, before_ref, *refs
):
    weights = refs[:-13]
    (
        sum_ref, sum_before_ref, bcc_ref, weights_in_ref, decays_ref, conv_ref,
        xc_ref, entering_ref, final_ref,
        state, x_in, tail, wide,
    ) = refs[-13:]
    block = pl.program_id(0)
    width = x_in.shape[1]
    is_own = block // 2 == place_ref[0]

    def product(ref):
        columns = block_columns(ref, place_ref, done, count)
        return jnp.dot(columns, wide[...], preferred_element_type=F32)

    @pl.when(block == 0)
    def _():
        state[...] = jnp.zeros_like(state)
        row = 0
        for ref, first, size in sources:
            wide[row : row + size, :] = weights[ref][first : first + size, :]
            row += size
        tail[...] = (sum_before_ref[...] + product(before_ref)).astype(BF16).astype(F32)

    @pl.when(is_own)
    def _():
        x_in[...] = (sum_ref[...] + product(own_ref)).astype(BF16).astype(F32)

    @pl.when(jnp.logical_not(is_own))
    def _():
        x_in[...] = (sum_ref[...] + product(other_ref)).astype(BF16).astype(F32)

    rows = jnp.concatenate([tail[...], x_in[...]], axis=0)
    tail[...] = rows[GROUP:]
    xc = conv_rows(rows, conv_ref)
    xc_ref[...] = xc
    entering_ref[0] = state[...].astype(BF16)
    weighted = (expand_heads(weights_in_ref[...], width) * xc.astype(F32)).astype(BF16)
    contrib = lax.dot_general(
        bcc_ref[:, :LANES], weighted, (((0,), (0,)), ((), ())), preferred_element_type=F32
    )
    decay = expand_heads(decays_ref[pl.ds(pl.multiple_of(block * 8, 8), 8), :], width)
    state[...] = state[...] * decay[0:1] + contrib

    @pl.when(block == pl.num_programs(0) - 1)
    def _():
        end = decays_ref.shape[0] - 8
        final_ref[:LANES, :] = state[...].astype(BF16)
        final_ref[LANES:, :] = split_decay(expand_heads(decays_ref[end:, :], width)[0:1])


def split_decay(decay):
    high = decay.astype(BF16)
    low = decay - high.astype(F32)
    row = lax.broadcasted_iota(jnp.int32, (HALO, decay.shape[1]), 0)
    return jnp.where(row == 0, high.astype(F32), jnp.where(row == 1, low, 0.0)).astype(BF16)


def unpacked(sent):
    sent = sent.astype(F32)
    return sent[:LANES], sent[LANES : LANES + 1] + sent[LANES + 1 : LANES + 2]


def row_kernel(place_ref, *refs):
    size = len(refs) - 3
    parts, (total_ref, before_ref, before_decay_ref) = refs[:size], refs[size:]
    place = place_ref[0]
    width = total_ref.shape[1]
    total, decay = jnp.zeros((LANES, width), F32), jnp.ones((1, width), F32)
    before_ref[...] = total
    before_decay_ref[...] = jnp.broadcast_to(decay, before_decay_ref.shape)
    for index in range(size):
        if index > 0:

            @pl.when(place == index)
            def _():
                before_ref[...] = total
                before_decay_ref[...] = jnp.broadcast_to(decay, before_decay_ref.shape)

        distance = (place - index + size) % size
        chosen = parts[0][...]
        for other in range(1, size):
            chosen = jnp.where(distance == other, parts[other][...], chosen)
        state, state_decay = unpacked(chosen)
        total = total * state_decay + state
        decay = decay * state_decay
    total_ref[:LANES, :] = total.astype(BF16)
    total_ref[LANES:, :] = split_decay(decay)


def outputs_kernel(xc_ref, bcc_ref, cum_ref, cum_t_ref, step_t_ref, entering_ref, skip_ref, out_ref, carried):
    width = xc_ref.shape[1]
    b_rows, c_rows = bcc_ref[:, :LANES], bcc_ref[:, LANES:]
    scores = lax.dot_general(c_rows, b_rows, (((1,), (1,)), ((), ())), preferred_element_type=F32)
    row = lax.broadcasted_iota(jnp.int32, (GROUP, GROUP), 0)
    col = lax.broadcasted_iota(jnp.int32, (GROUP, GROUP), 1)
    scores = jnp.where(row >= col, scores, 0.0)
    cum = cum_ref[...]
    grown = expand_heads(jnp.exp(cum), width)
    carried[...] = grown * jnp.dot(c_rows, entering_ref[0], preferred_element_type=F32)
    lane = lax.broadcasted_iota(jnp.int32, (GROUP, LANES), 1)

    def mixing(head):
        gaps = cum[:, head : head + 1] - cum_t_ref[head : head + 1, :]
        return (
            scores * jnp.exp(jnp.minimum(gaps, 0.0)) * step_t_ref[head : head + 1, :]
        ).astype(BF16)

    for pair in range(width // LANES):
        lanes = slice(pair * LANES, (pair + 1) * LANES)
        inputs = xc_ref[:, lanes]
        zero = jnp.zeros_like(inputs)
        both = jnp.concatenate([mixing(2 * pair), mixing(2 * pair + 1)], axis=1)
        stacked = jnp.concatenate(
            [jnp.where(lane < HEAD, inputs, zero), jnp.where(lane < HEAD, zero, inputs)], axis=0
        )
        out_ref[:, lanes] = (
            carried[:, lanes]
            + jnp.dot(both, stacked, preferred_element_type=F32)
            + skip_ref[:, lanes] * inputs.astype(F32)
        ).astype(BF16)


def z_kernel(place_ref, own_ref, other_ref, weight_ref, gate_ref, accum):
    step = pl.program_id(0)
    slab = own_ref.shape[0]
    core = place_ref[0]

    def product(ref):
        return jnp.dot(ref[...], weight_ref[...], preferred_element_type=F32)

    for index, ref in enumerate((own_ref, other_ref)):
        rows = slice(index * slab, (index + 1) * slab)
        target = pl.ds(pl.multiple_of(slab * (core if index == 0 else 1 - core), slab), slab)

        @pl.when(step == 0)
        def _():
            accum[rows, :] = product(ref)

        @pl.when((step > 0) & (step < pl.num_programs(0) - 1))
        def _():
            accum[rows, :] = accum[rows, :] + product(ref)

        @pl.when(step == pl.num_programs(0) - 1)
        def _():
            gate_ref[target, :] = (accum[rows, :] + product(ref)).astype(BF16)


def gate_kernel(
    core_ref, gate_ref, local_ref, bcc_ref, cum_ref, before_ref, before_decay_ref, *refs
):
    earlier, (mine_ref, send_ref, squares_ref, incoming) = refs[:-4], refs[-4:]
    width = local_ref.shape[1]

    @pl.when(pl.program_id(0) == 0)
    def _():
        carried = jnp.zeros((LANES, width), F32)
        for part in earlier:
            state, decay = unpacked(part[...])
            carried = carried * decay + state
        incoming[...] = (carried * before_decay_ref[0:1, :] + before_ref[...]).astype(BF16)

    grown = expand_heads(jnp.exp(cum_ref[...]), width)
    carried = jnp.dot(bcc_ref[:, LANES:], incoming[...], preferred_element_type=F32)
    gated = (local_ref[...].astype(F32) + grown * carried) * silu(gate_ref[...].astype(F32))
    is_own = pl.program_id(0) // 2 == core_ref[0]

    @pl.when(is_own)
    def _():
        mine_ref[...] = gated.astype(BF16)

    @pl.when(jnp.logical_not(is_own))
    def _():
        send_ref[...] = gated.astype(BF16)

    squares = gated * gated
    high = squares.astype(BF16)
    low = (squares - high.astype(F32)).astype(BF16)
    ones = jnp.ones((8, width), BF16)
    across = (((1,), (1,)), ((), ()))
    summed = lax.dot_general(ones, high, across, preferred_element_type=F32) + lax.dot_general(
        ones, low, across, preferred_element_type=F32
    )
    squares_ref[...] = summed[0:1, :]


def norm_kernel(core_ref, mine_ref, other_ref, squares_ref, gain_ref, out_ref):
    half = pl.program_id(0)
    across = jnp.broadcast_to(squares_ref[...], (8, squares_ref.shape[1]))
    scale = lax.rsqrt(across + 1e-05).T[:, 0:1]

    @pl.when(half == core_ref[0])
    def _():
        out_ref[...] = (mine_ref[...].astype(F32) * scale * gain_ref[...]).astype(BF16)

    @pl.when(half != core_ref[0])
    def _():
        out_ref[...] = (other_ref[...].astype(F32) * scale * gain_ref[...]).astype(BF16)


def whole(shape):
    return pl.BlockSpec(shape, lambda i: (0,) * len(shape))


def rows_of(width):
    return pl.BlockSpec((GROUP, width), lambda i: (i, 0))


def params(flops, megabytes, vmem=32):
    return dict(
        compiler_params=pltpu.CompilerParams(vmem_limit_bytes=vmem * 2**20),
        cost_estimate=pl.CostEstimate(
            flops=int(flops), bytes_accessed=megabytes * 2**20, transcendentals=0
        ),
    )


def fixed(a):
    return pl.BlockSpec(a.shape, lambda i, place: (0,) * len(a.shape))


def row_block(width):
    return pl.BlockSpec((GROUP, width), lambda i, place: (i, 0))


def slab_blocks(depth):
    own = pl.BlockSpec((GROUP, depth), lambda i, place: (jnp.clip(i - 2 * place[0], 0, 1), 0))
    other = pl.BlockSpec((GROUP, depth), lambda i, place: (jnp.clip(i - 2 + 2 * place[0], 0, 1), 0))
    return [own, other]


def prepared(place, slabs, weight, conv_bc, bias, rate, heads):
    own, other, before = slabs
    slab, rows, depth = own.shape[0], 2 * own.shape[0], 512
    shape = jax.ShapeDtypeStruct
    outs = [
        shape((rows, 2 * LANES), BF16), shape((rows, LANES), F32), shape((rows, LANES), F32),
        shape((heads, rows), F32), shape((heads, rows), F32), shape((rows, LANES), F32),
        shape((rows // GROUP * 8 + 8, LANES), F32),
    ]
    columns = lambda a: pl.BlockSpec((a.shape[0], depth), lambda i, place: (0, i))
    return pl.pallas_call(
        prepare_kernel,
        grid_spec=pltpu.PrefetchScalarGridSpec(
            num_scalar_prefetch=1,
            grid=(own.shape[1] // depth,),
            in_specs=[columns(a) for a in slabs]
            + [pl.BlockSpec((depth, weight.shape[1]), lambda i, place: (i, 0))]
            + [fixed(a) for a in (conv_bc, bias, rate)],
            out_specs=[fixed(a) for a in outs],
            scratch_shapes=[pltpu.VMEM((HALO + rows, weight.shape[1]), F32)],
        ),
        out_shape=outs,
        name="prepared",
        **params(4e9, 14, 60),
    )(place, *slabs, weight, conv_bc, bias, rate)


def products(place, slabs, weights, done, sums=()):
    own, other, before = slabs
    width, count = weights[0].shape[1], len(weights)
    outs = [
        jax.ShapeDtypeStruct((2 * own.shape[0], width), F32), jax.ShapeDtypeStruct((HALO, width), F32),
    ]
    specs = [row_block(width), fixed(outs[1])]
    sources = all_rows(weights)
    return pl.pallas_call(
        functools.partial(products_kernel, sources, done, count, len(sums) // 2),
        grid_spec=pltpu.PrefetchScalarGridSpec(
            num_scalar_prefetch=1,
            grid=(2 * own.shape[0] // GROUP,),
            in_specs=slab_blocks(own.shape[1])
            + [fixed(a) for a in (before, *weights)]
            + specs[: len(sums)],
            out_specs=specs,
            scratch_shapes=[pltpu.VMEM((sum(size for _, _, size in sources), width), BF16)],
        ),
        out_shape=outs,
        name="more_products" if sums else "first_products",
        **params(5e9, 16, 48),
    )(place, *slabs, *weights, *sums)


def local_states(place, slabs, weights, sources, done, count, sums, bcc, weights_in, decays, conv_x):
    own, other, before = slabs
    rows, width = sums[0].shape
    blocks = rows // GROUP
    outs = [
        jax.ShapeDtypeStruct((rows, width), BF16),
        jax.ShapeDtypeStruct((blocks, LANES, width), BF16),
        jax.ShapeDtypeStruct((LANES + HALO, width), BF16),
    ]
    return pl.pallas_call(
        functools.partial(states_kernel, sources, done, count),
        grid_spec=pltpu.PrefetchScalarGridSpec(
            num_scalar_prefetch=1,
            grid=(blocks,),
            in_specs=slab_blocks(own.shape[1])
            + [fixed(a) for a in (before, *weights)]
            + [
                row_block(width), fixed(sums[1]), row_block(2 * LANES), row_block(LANES),
                fixed(decays), fixed(conv_x),
            ],
            out_specs=[
                row_block(width),
                pl.BlockSpec((1, LANES, width), lambda i, place: (i, 0, 0)),
                fixed(outs[2]),
            ],
            scratch_shapes=[
                pltpu.VMEM((LANES, width), F32), pltpu.VMEM((GROUP, width), F32),
                pltpu.VMEM((HALO, width), F32),
                pltpu.VMEM((sum(size for _, _, size in sources), width), BF16),
            ],
        ),
        out_shape=outs,
        name="states",
        **params(11e9, 18, 40),
    )(place, *slabs, *weights, *sums, bcc, weights_in, decays, conv_x)


def local_outputs(xc, bcc, cum, cum_t, step_t, entering, skip):
    rows, width = xc.shape
    heads = cum_t.shape[0]
    by_lane = pl.BlockSpec((heads, GROUP), lambda i: (0, i))
    return pl.pallas_call(
        outputs_kernel,
        grid=(rows // GROUP,),
        in_specs=[
            rows_of(width), rows_of(2 * LANES), rows_of(LANES), by_lane, by_lane,
            pl.BlockSpec((1, LANES, width), lambda i: (i, 0, 0)), whole((1, width)),
        ],
        out_specs=rows_of(width),
        out_shape=jax.ShapeDtypeStruct((rows, width), BF16),
        scratch_shapes=[pltpu.VMEM((GROUP, width), F32)],
        compiler_params=pltpu.CompilerParams(vmem_limit_bytes=32 * 2**20),
        cost_estimate=pl.CostEstimate(flops=10**10, bytes_accessed=10 * 2**20, transcendentals=4 * 2**20),
        name="outputs",
    )(xc, bcc, cum, cum_t, step_t, entering, skip)


def project_gate(place, slabs, weight):
    own, other, _ = slabs
    rows, width, depth = 2 * own.shape[0], weight.shape[1] // 2, 1024
    columns = pl.BlockSpec((own.shape[0], depth), lambda i, place: (0, i))
    out = jax.ShapeDtypeStruct((rows, width), BF16)
    return pl.pallas_call(
        z_kernel,
        grid_spec=pltpu.PrefetchScalarGridSpec(
            num_scalar_prefetch=1,
            grid=(weight.shape[0] // depth,),
            in_specs=[columns, columns, pl.BlockSpec((depth, width), lambda i, place: (i, place[0]))],
            out_specs=fixed(out),
            scratch_shapes=[pltpu.VMEM((rows, width), F32)],
        ),
        out_shape=out,
        name="project_gate",
        **params(9e9, 20, 48),
    )(place, own, other, weight)


def gate_outputs(core, gate, local, bcc, cum_slab, before, before_decay, earlier):
    rows, width = local.shape
    half = jax.ShapeDtypeStruct((rows // 2, width), BF16)
    return pl.pallas_call(
        gate_kernel,
        grid_spec=pltpu.PrefetchScalarGridSpec(
            num_scalar_prefetch=1,
            grid=(rows // GROUP,),
            in_specs=[row_block(width), row_block(width), row_block(2 * LANES), row_block(LANES)]
            + [fixed(a) for a in (before, before_decay, *earlier)],
            out_specs=slab_blocks(width) + [pl.BlockSpec((1, GROUP), lambda i, place: (0, i))],
            scratch_shapes=[pltpu.VMEM((LANES, width), BF16)],
        ),
        out_shape=[half, half, jax.ShapeDtypeStruct((1, rows), F32)],
        name="gate",
        **params(1e9, 10, 60),
    )(core, gate, local, bcc, cum_slab, before, before_decay, *earlier)


def normalized(core, gated, other, mean_squares, gain):
    rows, width = other.shape
    return pl.pallas_call(
        norm_kernel,
        grid_spec=pltpu.PrefetchScalarGridSpec(
            num_scalar_prefetch=1,
            grid=(2,),
            in_specs=[
                pl.BlockSpec((rows, width), lambda j, core: (0, 0)),
                pl.BlockSpec((rows, width), lambda j, core: (0, 0)),
                pl.BlockSpec((1, rows), lambda j, core: (0, 0)),
                pl.BlockSpec((1, width), lambda j, core: (0, j)),
            ],
            out_specs=pl.BlockSpec((rows, width), lambda j, core: (0, j)),
        ),
        out_shape=jax.ShapeDtypeStruct((rows, 2 * width), BF16),
        compiler_params=pltpu.CompilerParams(vmem_limit_bytes=32 * 2**20),
        cost_estimate=pl.CostEstimate(flops=10**7, bytes_accessed=4 * 2**20, transcendentals=0),
        name="normalized",
    )(core.astype(jnp.int32)[None], gated, other, mean_squares, gain)


def earlier_states(final):
    size = lax.axis_size("y")
    less, more = round_ring(final, "y", 1), round_ring(final, "y", size - 1)
    cut = final.shape[0] // 2 // HALO * HALO
    opposite = [round_ring(less[:cut], "y", 1), round_ring(more[cut:], "y", size - 1)]
    parts = [final, less, jnp.concatenate(opposite, axis=0), more]
    width = final.shape[1]
    outs = [
        jax.ShapeDtypeStruct(final.shape, BF16),
        jax.ShapeDtypeStruct((LANES, width), F32),
        jax.ShapeDtypeStruct((8, width), F32),
    ]
    total, before, before_decay = pl.pallas_call(
        row_kernel,
        grid_spec=pltpu.PrefetchScalarGridSpec(
            num_scalar_prefetch=1,
            grid=(1,),
            in_specs=[fixed(a) for a in parts],
            out_specs=[fixed(a) for a in outs],
        ),
        out_shape=outs,
        name="row_states",
        **params(1e7, 2),
    )(lax.axis_index("y").astype(jnp.int32)[None], *parts)
    rows = lax.axis_size("z")
    earlier = [
        lax.ppermute(total, "z", [(i, i + distance) for i in range(rows - distance)])
        for distance in range(rows - 1, 0, -1)
    ]
    return before, before_decay, earlier


def tied(values, *to):
    return lax.optimization_barrier((*values, *to))[: len(values)]


def travelling(own, before_third, before_last):
    y_less, y_more = round_ring(own, "y", 1), round_ring(own, "y", -1)
    z_less, z_more = round_ring(own, "z", 1), round_ring(own, "z", -1)
    nearest = [own, y_less, y_more, z_less, z_more]
    second = [
        round_ring(y_less, "y", 1), round_ring(z_more, "z", -1),
        round_ring(z_more, "y", -1), round_ring(y_more, "z", 1),
    ]
    y_far, z_far, _, _, held_z, held_y = tied((*second, z_less, y_less), *before_third(nearest))
    less_less = round_ring(held_z, "y", 1)
    far = [
        round_ring(z_far, "y", -1), round_ring(z_far, "y", 1),
        round_ring(y_far, "z", 1), round_ring(y_far, "z", -1),
    ]
    held_y, last, *_ = tied((held_y, *far), *before_last())
    less_more = round_ring(held_y, "z", -1)
    return nearest, second, [*far, less_less, less_more, round_ring(last, "y", -1)]


def all_rows(blocks):
    return [(index, 0, block.shape[0]) for index, block in enumerate(blocks)]


def block_order():
    places = (
        ((0, 0), (-1, 0), (1, 0), (0, -1), (0, 1), (2, 0), (0, 2), (1, 1), (1, -1))
        + ((1, 2), (-1, 2), (2, -1), (2, 1), (-1, -1), (-1, 1), (2, 2))
    )
    y, z = lax.axis_index("y"), lax.axis_index("z")
    return [(z + dz) % 4 * 4 + (y + dy) % 4 for dy, dz in places]


def shards(
    tokens, x_weight, z_weight, bc_weight, dt_weight, conv_x, conv_bc, dt_bias, decay_rate, skip,
    norm_gain,
):
    core = lax.axis_index("core")
    width = x_weight.shape[1] // 2
    heads = dt_weight.shape[1] // 2

    def mine(a, axis):
        size = a.shape[axis] // 2
        return lax.dynamic_slice_in_dim(a, core * size, size, axis)

    def others(a, axis):
        size = a.shape[axis] // 2
        return lax.dynamic_slice_in_dim(a, (1 - core) * size, size, axis)

    def per_lane(a):
        return jnp.pad(mine(a, 0), (0, LANES - heads))[None, :]

    narrow = jnp.concatenate(
        [bc_weight, dt_weight, jnp.zeros((bc_weight.shape[0], LANES - 2 * heads), BF16)], axis=1
    )
    narrow = lax.all_gather(narrow, ("z", "y", "core"), axis=0, tiled=True)
    own_block = jnp.concatenate([mine(x_weight, 1), swap_cores(others(x_weight, 1))], axis=0)
    place = jnp.stack([core, *block_order()]).astype(jnp.int32)
    slabs, sums, early = [], [], []

    def before_third(blocks):
        (rows,) = tied((tokens,), *blocks[1:])
        chips = lax.axis_size("z") * lax.axis_size("y")
        to_next = lambda target: lax.ppermute(
            rows[-HALO:], ("z", "y", "core"),
            [(2 * i + 1, 2 * i + 2 + target) for i in range(chips - 1)],
        )
        slabs.extend((rows, swap_cores(rows), to_next(0) + to_next(1)))
        sums.extend(products(place, slabs, blocks, 0))
        return sums[:1]

    def before_last():
        early.extend(
            prepared(place, slabs, narrow, conv_bc, per_lane(dt_bias), per_lane(decay_rate), heads)
        )
        return early[:1]

    nearest, second, blocks = travelling(own_block, before_third, before_last)
    (z_rows,) = tied((z_weight,), own_block)
    z_whole = lax.all_gather(z_rows, ("z", "y", "core"), axis=0, tiled=True)
    sums = products(place, slabs, second, len(nearest), sums)
    bcc, cum, cum_slab, cum_t, step_t, weights_in, decays = early
    xc, entering, final = local_states(
        place, slabs, blocks, all_rows(blocks), 9, 7, sums, bcc, weights_in, decays, mine(conv_x, 1)
    )
    before, before_decay, earlier = earlier_states(final)
    skip_lanes = jnp.repeat(mine(skip, 0), HEAD)[None, :]
    local = local_outputs(xc, bcc, cum, cum_t, step_t, entering, skip_lanes)
    gate = project_gate(place, slabs, z_whole)
    gated, send, squares = gate_outputs(place[:1], gate, local, bcc, cum_slab, before, before_decay, earlier)

    other = swap_cores(send)
    summed = mine(squares + swap_cores(squares), 1)
    across = [round_ring(summed, "x", distance) for distance in range(1, lax.axis_size("x"))]
    mean_squares = (summed + sum(across)) / (2 * width * lax.axis_size("x"))
    return normalized(core, gated, other, mean_squares, norm_gain[None, :])


def solution(mesh):
    fine = Mesh(mesh.devices.reshape(4, 4, 2, 4), ("z", "y", "core", "x"))
    ctx = ("z", "y", "core")
    placed = (
        P(ctx, None),
        P(ctx, "x"),
        P(ctx, "x"),
        P(ctx, None),
        P(ctx, "x"),
        P(None, "x"),
        P(),
        P("x"),
        P("x"),
        P("x"),
        P("x"),
    )
    return jax.shard_map(
        shards, mesh=fine, in_specs=placed, out_specs=P(ctx, "x"), check_vma=False
    )
```

```python
import functools

import jax
import jax.numpy as jnp
from jax import lax
from jax.experimental import pallas as pl
from jax.experimental.pallas import tpu as pltpu
from jax.sharding import Mesh, PartitionSpec as P

GROUP = 256
HALO = 16
LANES = 128
HEAD = 64
F32 = jnp.float32
BF16 = jnp.bfloat16


def swap_cores(a):
    return lax.ppermute(a, "core", [(0, 1), (1, 0)])


def round_ring(a, axis, distance):
    size = lax.axis_size(axis)
    return lax.ppermute(a, axis, [(i, (i + distance) % size) for i in range(size)])


def along_chips(a, distance):
    chips = lax.axis_size("z") * lax.axis_size("y")
    return lax.ppermute(a, ("z", "y"), [(i, i + distance) for i in range(chips - distance)])


def in_core_order(core, mine, other, axis):
    first = jnp.where(core == 0, mine, other)
    second = jnp.where(core == 0, other, mine)
    return jnp.concatenate([first, second], axis=axis)


def expand_heads(values, width):
    heads = width // HEAD
    high = values.astype(BF16).astype(F32)
    rest = values - high
    middle = rest.astype(BF16).astype(F32)
    low = rest - middle
    lane = lax.broadcasted_iota(jnp.int32, values.shape, 1)
    parts = jnp.where(lane < heads, high, pltpu.roll(middle, heads, axis=1))
    parts = jnp.where(lane < 2 * heads, parts, pltpu.roll(low, 2 * heads, axis=1))
    parts = jnp.where(lane < 3 * heads, parts, 0.0).astype(BF16)
    row = lax.broadcasted_iota(jnp.int32, (LANES, width), 0)
    col = lax.broadcasted_iota(jnp.int32, (LANES, width), 1)
    head = row % heads
    spread = (col >= head * HEAD) & (col < head * HEAD + HEAD) & (row < 3 * heads)
    return jnp.dot(parts, spread.astype(BF16), preferred_element_type=F32)


def silu(a):
    half = 0.5 * a
    return half + half * jnp.tanh(half)


def conv_rows(rows, kernel_ref):
    taps, count = kernel_ref.shape[0], rows.shape[0] - HALO
    first = HALO - (taps - 1)
    accum = kernel_ref[0:1, :] * rows[first : first + count]
    for tap in range(1, taps):
        accum = accum + kernel_ref[tap : tap + 1, :] * rows[first + tap : first + tap + count]
    return silu(accum).astype(BF16)


def prepare_kernel(
    place_ref, own_ref, other_ref, before_ref, weight_ref, conv_ref, bias_ref, rate_ref,
    bcc_ref, cum_ref, cum_slab_ref, cum_t_ref, step_t_ref, weights_in_ref, decays_ref,
    accum,
):
    step = pl.program_id(0)
    core = place_ref[0]
    slab = own_ref.shape[0]
    heads = cum_t_ref.shape[0]
    rows_own = pl.ds(pl.multiple_of(HALO + slab * core, HALO), slab)
    rows_other = pl.ds(pl.multiple_of(HALO + slab * (1 - core), HALO), slab)

    @pl.when(step == 0)
    def _():
        accum[...] = jnp.zeros_like(accum)

    weight = weight_ref[...]
    for rows, ref in ((slice(0, HALO), before_ref), (rows_own, own_ref), (rows_other, other_ref)):
        accum[rows, :] = accum[rows, :] + jnp.dot(ref[...], weight, preferred_element_type=F32)

    @pl.when(step == pl.num_programs(0) - 1)
    def _():
        total = jnp.zeros((1, LANES), F32)
        row = lax.broadcasted_iota(jnp.int32, (GROUP, GROUP), 0)
        col = lax.broadcasted_iota(jnp.int32, (GROUP, GROUP), 1)
        lower = (row >= col).astype(F32)
        for block in range(2 * slab // GROUP):
            part = slice(block * GROUP, (block + 1) * GROUP)
            narrow = accum[block * GROUP : (block + 1) * GROUP + HALO, : 2 * LANES]
            bcc_ref[part, :] = conv_rows(narrow.astype(BF16).astype(F32), conv_ref)
            raw = accum[block * GROUP + HALO : (block + 1) * GROUP + HALO, 2 * LANES :]
            raw = jnp.where(core == 0, raw, pltpu.roll(raw, LANES - heads, axis=1))
            raw = raw + bias_ref[...]
            step_size = jnp.maximum(raw, 0.0) + jnp.log1p(jnp.exp(-jnp.abs(raw)))
            log_decay = -rate_ref[...] * step_size
            cum = jnp.dot(
                lower, log_decay, preferred_element_type=F32, precision=lax.Precision.HIGHEST
            )
            last = cum[GROUP - 1 : GROUP, :]
            cum_ref[part, :] = cum
            cum_slab_ref[part, :] = cum + total
            cum_t_ref[:, part] = cum.T[:heads, :]
            step_t_ref[:, part] = step_size.T[:heads, :]
            weights_in_ref[part, :] = jnp.exp(last - cum) * step_size
            decays_ref[block * 8 : block * 8 + 8, :] = jnp.broadcast_to(jnp.exp(last), (8, LANES))
            total = total + last
        end = decays_ref.shape[0] - 8
        decays_ref[end:, :] = jnp.broadcast_to(jnp.exp(total), (8, LANES))


def block_columns(ref, place_ref, first, count):
    core = place_ref[0]
    parts = []
    for index in range(first, first + count):
        base = place_ref[1 + index] * (2 * LANES)
        for start in (base + LANES * core, base + LANES * (1 - core)):
            parts.append(ref[:, pl.ds(pl.multiple_of(start, LANES), LANES)])
    return jnp.concatenate(parts, axis=1)


def stacked(sources, refs):
    return jnp.concatenate([refs[ref][first : first + size, :] for ref, first, size in sources], axis=0)


def products_kernel(sources, done, count, started, place_ref, own_ref, other_ref, before_ref, *refs):
    weights, sums, (out_ref, out_before_ref, wide) = refs[: -3 - 2 * started], refs[-3 - 2 * started : -3], refs[-3:]
    block = pl.program_id(0)
    is_own = block // 2 == place_ref[0]

    def product(ref):
        columns = block_columns(ref, place_ref, done, count)
        return jnp.dot(columns, wide[...], preferred_element_type=F32)

    @pl.when(block == 0)
    def _():
        row = 0
        for ref, first, size in sources:
            wide[row : row + size, :] = weights[ref][first : first + size, :]
            row += size
        added = product(before_ref)
        out_before_ref[...] = sums[1][...] + added if started else added

    @pl.when(is_own)
    def _():
        added = product(own_ref)
        out_ref[...] = sums[0][...] + added if started else added

    @pl.when(jnp.logical_not(is_own))
    def _():
        added = product(other_ref)
        out_ref[...] = sums[0][...] + added if started else added


def states_kernel(
    sources, done, count, place_ref, own_ref, other_ref, before_ref, *refs
):
    weights = refs[:-13]
    (
        sum_ref, sum_before_ref, bcc_ref, weights_in_ref, decays_ref, conv_ref,
        xc_ref, entering_ref, final_ref,
        state, x_in, tail, wide,
    ) = refs[-13:]
    block = pl.program_id(0)
    width = x_in.shape[1]
    is_own = block // 2 == place_ref[0]

    def product(ref):
        columns = block_columns(ref, place_ref, done, count)
        return jnp.dot(columns, wide[...], preferred_element_type=F32)

    @pl.when(block == 0)
    def _():
        state[...] = jnp.zeros_like(state)
        row = 0
        for ref, first, size in sources:
            wide[row : row + size, :] = weights[ref][first : first + size, :]
            row += size
        tail[...] = (sum_before_ref[...] + product(before_ref)).astype(BF16).astype(F32)

    @pl.when(is_own)
    def _():
        x_in[...] = (sum_ref[...] + product(own_ref)).astype(BF16).astype(F32)

    @pl.when(jnp.logical_not(is_own))
    def _():
        x_in[...] = (sum_ref[...] + product(other_ref)).astype(BF16).astype(F32)

    rows = jnp.concatenate([tail[...], x_in[...]], axis=0)
    tail[...] = rows[GROUP:]
    xc = conv_rows(rows, conv_ref)
    xc_ref[...] = xc
    entering_ref[0] = state[...].astype(BF16)
    weighted = (expand_heads(weights_in_ref[...], width) * xc.astype(F32)).astype(BF16)
    contrib = lax.dot_general(
        bcc_ref[:, :LANES], weighted, (((0,), (0,)), ((), ())), preferred_element_type=F32
    )
    decay = expand_heads(decays_ref[pl.ds(pl.multiple_of(block * 8, 8), 8), :], width)
    state[...] = state[...] * decay[0:1] + contrib

    @pl.when(block == pl.num_programs(0) - 1)
    def _():
        end = decays_ref.shape[0] - 8
        final_ref[:LANES, :] = state[...].astype(BF16)
        final_ref[LANES:, :] = split_decay(expand_heads(decays_ref[end:, :], width)[0:1])


def split_decay(decay):
    high = decay.astype(BF16)
    low = decay - high.astype(F32)
    row = lax.broadcasted_iota(jnp.int32, (HALO, decay.shape[1]), 0)
    return jnp.where(row == 0, high.astype(F32), jnp.where(row == 1, low, 0.0)).astype(BF16)


def unpacked(sent):
    sent = sent.astype(F32)
    return sent[:LANES], sent[LANES : LANES + 1] + sent[LANES + 1 : LANES + 2]


def row_kernel(place_ref, *refs):
    size = len(refs) - 3
    parts, (total_ref, before_ref, before_decay_ref) = refs[:size], refs[size:]
    place = place_ref[0]
    width = total_ref.shape[1]
    total, decay = jnp.zeros((LANES, width), F32), jnp.ones((1, width), F32)
    before_ref[...] = total
    before_decay_ref[...] = jnp.broadcast_to(decay, before_decay_ref.shape)
    for index in range(size):
        if index > 0:

            @pl.when(place == index)
            def _():
                before_ref[...] = total
                before_decay_ref[...] = jnp.broadcast_to(decay, before_decay_ref.shape)

        distance = (place - index + size) % size
        chosen = parts[0][...]
        for other in range(1, size):
            chosen = jnp.where(distance == other, parts[other][...], chosen)
        state, state_decay = unpacked(chosen)
        total = total * state_decay + state
        decay = decay * state_decay
    total_ref[:LANES, :] = total.astype(BF16)
    total_ref[LANES:, :] = split_decay(decay)


def outputs_kernel(xc_ref, bcc_ref, cum_ref, cum_t_ref, step_t_ref, entering_ref, skip_ref, out_ref, carried):
    width = xc_ref.shape[1]
    b_rows, c_rows = bcc_ref[:, :LANES], bcc_ref[:, LANES:]
    scores = lax.dot_general(c_rows, b_rows, (((1,), (1,)), ((), ())), preferred_element_type=F32)
    row = lax.broadcasted_iota(jnp.int32, (GROUP, GROUP), 0)
    col = lax.broadcasted_iota(jnp.int32, (GROUP, GROUP), 1)
    scores = jnp.where(row >= col, scores, 0.0)
    cum = cum_ref[...]
    grown = expand_heads(jnp.exp(cum), width)
    carried[...] = grown * jnp.dot(c_rows, entering_ref[0], preferred_element_type=F32)
    lane = lax.broadcasted_iota(jnp.int32, (GROUP, LANES), 1)

    def mixing(head):
        gaps = cum[:, head : head + 1] - cum_t_ref[head : head + 1, :]
        return (
            scores * jnp.exp(jnp.minimum(gaps, 0.0)) * step_t_ref[head : head + 1, :]
        ).astype(BF16)

    for pair in range(width // LANES):
        lanes = slice(pair * LANES, (pair + 1) * LANES)
        inputs = xc_ref[:, lanes]
        zero = jnp.zeros_like(inputs)
        both = jnp.concatenate([mixing(2 * pair), mixing(2 * pair + 1)], axis=1)
        stacked = jnp.concatenate(
            [jnp.where(lane < HEAD, inputs, zero), jnp.where(lane < HEAD, zero, inputs)], axis=0
        )
        out_ref[:, lanes] = (
            carried[:, lanes]
            + jnp.dot(both, stacked, preferred_element_type=F32)
            + skip_ref[:, lanes] * inputs.astype(F32)
        ).astype(BF16)


def z_kernel(place_ref, own_ref, other_ref, weight_ref, gate_ref, accum):
    step = pl.program_id(0)
    slab = own_ref.shape[0]
    core = place_ref[0]

    def product(ref):
        return jnp.dot(ref[...], weight_ref[...], preferred_element_type=F32)

    for index, ref in enumerate((own_ref, other_ref)):
        rows = slice(index * slab, (index + 1) * slab)
        target = pl.ds(pl.multiple_of(slab * (core if index == 0 else 1 - core), slab), slab)

        @pl.when(step == 0)
        def _():
            accum[rows, :] = product(ref)

        @pl.when((step > 0) & (step < pl.num_programs(0) - 1))
        def _():
            accum[rows, :] = accum[rows, :] + product(ref)

        @pl.when(step == pl.num_programs(0) - 1)
        def _():
            gate_ref[target, :] = (accum[rows, :] + product(ref)).astype(BF16)


def gate_kernel(
    core_ref, gate_ref, local_ref, bcc_ref, cum_ref, before_ref, before_decay_ref, *refs
):
    earlier, (mine_ref, send_ref, squares_ref, incoming) = refs[:-4], refs[-4:]
    width = local_ref.shape[1]

    @pl.when(pl.program_id(0) == 0)
    def _():
        carried = jnp.zeros((LANES, width), F32)
        for part in earlier:
            state, decay = unpacked(part[...])
            carried = carried * decay + state
        incoming[...] = (carried * before_decay_ref[0:1, :] + before_ref[...]).astype(BF16)

    grown = expand_heads(jnp.exp(cum_ref[...]), width)
    carried = jnp.dot(bcc_ref[:, LANES:], incoming[...], preferred_element_type=F32)
    gated = (local_ref[...].astype(F32) + grown * carried) * silu(gate_ref[...].astype(F32))
    is_own = pl.program_id(0) // 2 == core_ref[0]

    @pl.when(is_own)
    def _():
        mine_ref[...] = gated.astype(BF16)

    @pl.when(jnp.logical_not(is_own))
    def _():
        send_ref[...] = gated.astype(BF16)

    squares = gated * gated
    high = squares.astype(BF16)
    low = (squares - high.astype(F32)).astype(BF16)
    ones = jnp.ones((8, width), BF16)
    across = (((1,), (1,)), ((), ()))
    summed = lax.dot_general(ones, high, across, preferred_element_type=F32) + lax.dot_general(
        ones, low, across, preferred_element_type=F32
    )
    squares_ref[...] = summed[0:1, :]


def norm_kernel(core_ref, mine_ref, other_ref, squares_ref, gain_ref, out_ref):
    half = pl.program_id(0)
    across = jnp.broadcast_to(squares_ref[...], (8, squares_ref.shape[1]))
    scale = lax.rsqrt(across + 1e-05).T[:, 0:1]

    @pl.when(half == core_ref[0])
    def _():
        out_ref[...] = (mine_ref[...].astype(F32) * scale * gain_ref[...]).astype(BF16)

    @pl.when(half != core_ref[0])
    def _():
        out_ref[...] = (other_ref[...].astype(F32) * scale * gain_ref[...]).astype(BF16)


def whole(shape):
    return pl.BlockSpec(shape, lambda i: (0,) * len(shape))


def rows_of(width):
    return pl.BlockSpec((GROUP, width), lambda i: (i, 0))


def params(flops, megabytes, vmem=32):
    return dict(
        compiler_params=pltpu.CompilerParams(vmem_limit_bytes=vmem * 2**20),
        cost_estimate=pl.CostEstimate(
            flops=int(flops), bytes_accessed=megabytes * 2**20, transcendentals=0
        ),
    )


def fixed(a):
    return pl.BlockSpec(a.shape, lambda i, place: (0,) * len(a.shape))


def row_block(width):
    return pl.BlockSpec((GROUP, width), lambda i, place: (i, 0))


def slab_blocks(depth):
    own = pl.BlockSpec((GROUP, depth), lambda i, place: (jnp.clip(i - 2 * place[0], 0, 1), 0))
    other = pl.BlockSpec((GROUP, depth), lambda i, place: (jnp.clip(i - 2 + 2 * place[0], 0, 1), 0))
    return [own, other]


def prepared(place, slabs, weight, conv_bc, bias, rate, heads):
    own, other, before = slabs
    slab, rows, depth = own.shape[0], 2 * own.shape[0], 512
    shape = jax.ShapeDtypeStruct
    outs = [
        shape((rows, 2 * LANES), BF16), shape((rows, LANES), F32), shape((rows, LANES), F32),
        shape((heads, rows), F32), shape((heads, rows), F32), shape((rows, LANES), F32),
        shape((rows // GROUP * 8 + 8, LANES), F32),
    ]
    columns = lambda a: pl.BlockSpec((a.shape[0], depth), lambda i, place: (0, i))
    return pl.pallas_call(
        prepare_kernel,
        grid_spec=pltpu.PrefetchScalarGridSpec(
            num_scalar_prefetch=1,
            grid=(own.shape[1] // depth,),
            in_specs=[columns(a) for a in slabs]
            + [pl.BlockSpec((depth, weight.shape[1]), lambda i, place: (i, 0))]
            + [fixed(a) for a in (conv_bc, bias, rate)],
            out_specs=[fixed(a) for a in outs],
            scratch_shapes=[pltpu.VMEM((HALO + rows, weight.shape[1]), F32)],
        ),
        out_shape=outs,
        name="prepared",
        **params(4e9, 14, 60),
    )(place, *slabs, weight, conv_bc, bias, rate)


def products(place, slabs, weights, done, sums=()):
    own, other, before = slabs
    width, count = weights[0].shape[1], len(weights)
    outs = [
        jax.ShapeDtypeStruct((2 * own.shape[0], width), F32), jax.ShapeDtypeStruct((HALO, width), F32),
    ]
    specs = [row_block(width), fixed(outs[1])]
    sources = all_rows(weights)
    return pl.pallas_call(
        functools.partial(products_kernel, sources, done, count, len(sums) // 2),
        grid_spec=pltpu.PrefetchScalarGridSpec(
            num_scalar_prefetch=1,
            grid=(2 * own.shape[0] // GROUP,),
            in_specs=slab_blocks(own.shape[1])
            + [fixed(a) for a in (before, *weights)]
            + specs[: len(sums)],
            out_specs=specs,
            scratch_shapes=[pltpu.VMEM((sum(size for _, _, size in sources), width), BF16)],
        ),
        out_shape=outs,
        name="more_products" if sums else "first_products",
        **params(5e9, 16, 48),
    )(place, *slabs, *weights, *sums)


def local_states(place, slabs, weights, sources, done, count, sums, bcc, weights_in, decays, conv_x):
    own, other, before = slabs
    rows, width = sums[0].shape
    blocks = rows // GROUP
    outs = [
        jax.ShapeDtypeStruct((rows, width), BF16),
        jax.ShapeDtypeStruct((blocks, LANES, width), BF16),
        jax.ShapeDtypeStruct((LANES + HALO, width), BF16),
    ]
    return pl.pallas_call(
        functools.partial(states_kernel, sources, done, count),
        grid_spec=pltpu.PrefetchScalarGridSpec(
            num_scalar_prefetch=1,
            grid=(blocks,),
            in_specs=slab_blocks(own.shape[1])
            + [fixed(a) for a in (before, *weights)]
            + [
                row_block(width), fixed(sums[1]), row_block(2 * LANES), row_block(LANES),
                fixed(decays), fixed(conv_x),
            ],
            out_specs=[
                row_block(width),
                pl.BlockSpec((1, LANES, width), lambda i, place: (i, 0, 0)),
                fixed(outs[2]),
            ],
            scratch_shapes=[
                pltpu.VMEM((LANES, width), F32), pltpu.VMEM((GROUP, width), F32),
                pltpu.VMEM((HALO, width), F32),
                pltpu.VMEM((sum(size for _, _, size in sources), width), BF16),
            ],
        ),
        out_shape=outs,
        name="states",
        **params(11e9, 18, 40),
    )(place, *slabs, *weights, *sums, bcc, weights_in, decays, conv_x)


def local_outputs(xc, bcc, cum, cum_t, step_t, entering, skip):
    rows, width = xc.shape
    heads = cum_t.shape[0]
    by_lane = pl.BlockSpec((heads, GROUP), lambda i: (0, i))
    return pl.pallas_call(
        outputs_kernel,
        grid=(rows // GROUP,),
        in_specs=[
            rows_of(width), rows_of(2 * LANES), rows_of(LANES), by_lane, by_lane,
            pl.BlockSpec((1, LANES, width), lambda i: (i, 0, 0)), whole((1, width)),
        ],
        out_specs=rows_of(width),
        out_shape=jax.ShapeDtypeStruct((rows, width), BF16),
        scratch_shapes=[pltpu.VMEM((GROUP, width), F32)],
        compiler_params=pltpu.CompilerParams(vmem_limit_bytes=32 * 2**20),
        cost_estimate=pl.CostEstimate(flops=10**10, bytes_accessed=10 * 2**20, transcendentals=4 * 2**20),
        name="outputs",
    )(xc, bcc, cum, cum_t, step_t, entering, skip)


def project_gate(place, slabs, weight):
    own, other, _ = slabs
    rows, width, depth = 2 * own.shape[0], weight.shape[1] // 2, 1024
    columns = pl.BlockSpec((own.shape[0], depth), lambda i, place: (0, i))
    out = jax.ShapeDtypeStruct((rows, width), BF16)
    return pl.pallas_call(
        z_kernel,
        grid_spec=pltpu.PrefetchScalarGridSpec(
            num_scalar_prefetch=1,
            grid=(weight.shape[0] // depth,),
            in_specs=[columns, columns, pl.BlockSpec((depth, width), lambda i, place: (i, place[0]))],
            out_specs=fixed(out),
            scratch_shapes=[pltpu.VMEM((rows, width), F32)],
        ),
        out_shape=out,
        name="project_gate",
        **params(9e9, 20, 48),
    )(place, own, other, weight)


def gate_outputs(core, gate, local, bcc, cum_slab, before, before_decay, earlier):
    rows, width = local.shape
    half = jax.ShapeDtypeStruct((rows // 2, width), BF16)
    return pl.pallas_call(
        gate_kernel,
        grid_spec=pltpu.PrefetchScalarGridSpec(
            num_scalar_prefetch=1,
            grid=(rows // GROUP,),
            in_specs=[row_block(width), row_block(width), row_block(2 * LANES), row_block(LANES)]
            + [fixed(a) for a in (before, before_decay, *earlier)],
            out_specs=slab_blocks(width) + [pl.BlockSpec((1, GROUP), lambda i, place: (0, i))],
            scratch_shapes=[pltpu.VMEM((LANES, width), BF16)],
        ),
        out_shape=[half, half, jax.ShapeDtypeStruct((1, rows), F32)],
        name="gate",
        **params(1e9, 10, 60),
    )(core, gate, local, bcc, cum_slab, before, before_decay, *earlier)


def normalized(core, gated, other, mean_squares, gain):
    rows, width = other.shape
    return pl.pallas_call(
        norm_kernel,
        grid_spec=pltpu.PrefetchScalarGridSpec(
            num_scalar_prefetch=1,
            grid=(2,),
            in_specs=[
                pl.BlockSpec((rows, width), lambda j, core: (0, 0)),
                pl.BlockSpec((rows, width), lambda j, core: (0, 0)),
                pl.BlockSpec((1, rows), lambda j, core: (0, 0)),
                pl.BlockSpec((1, width), lambda j, core: (0, j)),
            ],
            out_specs=pl.BlockSpec((rows, width), lambda j, core: (0, j)),
        ),
        out_shape=jax.ShapeDtypeStruct((rows, 2 * width), BF16),
        compiler_params=pltpu.CompilerParams(vmem_limit_bytes=32 * 2**20),
        cost_estimate=pl.CostEstimate(flops=10**7, bytes_accessed=4 * 2**20, transcendentals=0),
        name="normalized",
    )(core.astype(jnp.int32)[None], gated, other, mean_squares, gain)


def earlier_states(final):
    size = lax.axis_size("y")
    parts = [final] + [round_ring(final, "y", distance) for distance in range(1, size)]
    width = final.shape[1]
    outs = [
        jax.ShapeDtypeStruct(final.shape, BF16),
        jax.ShapeDtypeStruct((LANES, width), F32),
        jax.ShapeDtypeStruct((8, width), F32),
    ]
    total, before, before_decay = pl.pallas_call(
        row_kernel,
        grid_spec=pltpu.PrefetchScalarGridSpec(
            num_scalar_prefetch=1,
            grid=(1,),
            in_specs=[fixed(a) for a in parts],
            out_specs=[fixed(a) for a in outs],
        ),
        out_shape=outs,
        name="row_states",
        **params(1e7, 2),
    )(lax.axis_index("y").astype(jnp.int32)[None], *parts)
    rows = lax.axis_size("z")
    earlier = [
        lax.ppermute(total, "z", [(i, i + distance) for i in range(rows - distance)])
        for distance in range(rows - 1, 0, -1)
    ]
    return before, before_decay, earlier


def tied(values, *to):
    return lax.optimization_barrier((*values, *to))[: len(values)]


def travelling(own, before_third, before_last):
    y_less, y_more = round_ring(own, "y", 1), round_ring(own, "y", -1)
    z_less, z_more = round_ring(own, "z", 1), round_ring(own, "z", -1)
    nearest = [own, y_less, y_more, z_less, z_more]
    second = [
        round_ring(y_less, "y", 1), round_ring(z_more, "z", -1),
        round_ring(z_more, "y", -1), round_ring(y_more, "z", 1),
    ]
    y_far, z_far, _, _, held_z, held_y = tied((*second, z_less, y_less), *before_third(nearest))
    less_less = round_ring(held_z, "y", 1)
    far = [
        round_ring(z_far, "y", -1), round_ring(z_far, "y", 1),
        round_ring(y_far, "z", 1), round_ring(y_far, "z", -1),
    ]
    held_y, last, *_ = tied((held_y, *far), *before_last())
    less_more = round_ring(held_y, "z", -1)
    return nearest, second, [*far, less_less, less_more, round_ring(last, "y", -1)]


def all_rows(blocks):
    return [(index, 0, block.shape[0]) for index, block in enumerate(blocks)]


def block_order():
    places = (
        ((0, 0), (-1, 0), (1, 0), (0, -1), (0, 1), (2, 0), (0, 2), (1, 1), (1, -1))
        + ((1, 2), (-1, 2), (2, -1), (2, 1), (-1, -1), (-1, 1), (2, 2))
    )
    y, z = lax.axis_index("y"), lax.axis_index("z")
    return [(z + dz) % 4 * 4 + (y + dy) % 4 for dy, dz in places]


def shards(
    tokens, x_weight, z_weight, bc_weight, dt_weight, conv_x, conv_bc, dt_bias, decay_rate, skip,
    norm_gain,
):
    core = lax.axis_index("core")
    width = x_weight.shape[1] // 2
    heads = dt_weight.shape[1] // 2

    def mine(a, axis):
        size = a.shape[axis] // 2
        return lax.dynamic_slice_in_dim(a, core * size, size, axis)

    def others(a, axis):
        size = a.shape[axis] // 2
        return lax.dynamic_slice_in_dim(a, (1 - core) * size, size, axis)

    def per_lane(a):
        return jnp.pad(mine(a, 0), (0, LANES - heads))[None, :]

    send = others(x_weight, 1)
    bc_weight, dt_weight = tied((bc_weight, dt_weight), send)
    narrow = jnp.concatenate(
        [bc_weight, dt_weight, jnp.zeros((bc_weight.shape[0], LANES - 2 * heads), BF16)], axis=1
    )
    narrow = lax.all_gather(narrow, ("z", "y", "core"), axis=0, tiled=True)
    own_block = jnp.concatenate([mine(x_weight, 1), swap_cores(send)], axis=0)
    place = jnp.stack([core, *block_order()]).astype(jnp.int32)
    slabs, sums, early = [], [], []

    def before_third(blocks):
        (rows,) = tied((tokens,), *blocks[1:])
        chips = lax.axis_size("z") * lax.axis_size("y")
        to_next = lambda target: lax.ppermute(
            rows[-HALO:], ("z", "y", "core"),
            [(2 * i + 1, 2 * i + 2 + target) for i in range(chips - 1)],
        )
        slabs.extend((rows, swap_cores(rows), to_next(0) + to_next(1)))
        sums.extend(products(place, slabs, blocks, 0))
        return sums[:1]

    def before_last():
        early.extend(
            prepared(place, slabs, narrow, conv_bc, per_lane(dt_bias), per_lane(decay_rate), heads)
        )
        return early[:1]

    nearest, second, blocks = travelling(own_block, before_third, before_last)
    (z_rows,) = tied((z_weight,), own_block)
    z_whole = lax.all_gather(z_rows, ("z", "y", "core"), axis=0, tiled=True)
    sums = products(place, slabs, second, len(nearest), sums)
    bcc, cum, cum_slab, cum_t, step_t, weights_in, decays = early
    xc, entering, final = local_states(
        place, slabs, blocks, all_rows(blocks), 9, 7, sums, bcc, weights_in, decays, mine(conv_x, 1)
    )
    before, before_decay, earlier = earlier_states(final)
    skip_lanes = jnp.repeat(mine(skip, 0), HEAD)[None, :]
    local = local_outputs(xc, bcc, cum, cum_t, step_t, entering, skip_lanes)
    gate = project_gate(place, slabs, z_whole)
    gated, send, squares = gate_outputs(place[:1], gate, local, bcc, cum_slab, before, before_decay, earlier)

    other = swap_cores(send)
    summed = mine(squares + swap_cores(squares), 1)
    across = [round_ring(summed, "x", distance) for distance in range(1, lax.axis_size("x"))]
    mean_squares = (summed + sum(across)) / (2 * width * lax.axis_size("x"))
    return normalized(core, gated, other, mean_squares, norm_gain[None, :])


def solution(mesh):
    fine = Mesh(mesh.devices.reshape(4, 4, 2, 4), ("z", "y", "core", "x"))
    ctx = ("z", "y", "core")
    placed = (
        P(ctx, None),
        P(ctx, "x"),
        P(ctx, "x"),
        P(ctx, None),
        P(ctx, "x"),
        P(None, "x"),
        P(),
        P("x"),
        P("x"),
        P("x"),
        P("x"),
    )
    return jax.shard_map(
        shards, mesh=fine, in_specs=placed, out_specs=P(ctx, "x"), check_vma=False
    )
```
